32 devices in a mesh: row: 4 (over z), col: 8 (over y, x, core).
Axes of the slice: x: 2, y: 2, z: 4, core: 2. Of those that a mesh axis runs over, the one named last changes fastest.
Arguments:
- points: float32 [4, 4, 262144], P(None, None, ('row', 'col')), may hold values from -0.4 to 1.4, as said below
- density: float32 [262144], P(('row', 'col')), may hold values from -6 to 6
- near_pairs: int32 [192, 2], P(('row', 'col')), may hold values from 0 to 127, as said below
- far_pairs: int32 [512, 2], P(('row', 'col')), may hold values from 0 to 127, as said below
- near_count: int32 [32], P(('row', 'col')), may hold values from 1 to 6
- far_count: int32 [32], P(('row', 'col')), may hold values from 1 to 16
Outputs:
- potential: float32 [262144], P(('row', 'col'))
The draws below stay inside these ranges and needn't reach their ends.
Inputs may be any that keep to these rules, and one draw needn't show every extreme that they name: `near_pairs`: the first column indexes target band blocks and the second source band blocks (below 64). On device (r, c) the first column lies in c * 16 to c * 16 + 15, so every near target block is one of the device's own blocks. The first slot of each device names one of its own blocks k as (c * 16 + k, r * 16 + k). `far_pairs`: the first column indexes target band blocks (below 128), the second source band blocks (below 64). `points`: weights (entry 3) lie in 0.01 to 0.04; coordinates in -0.4 to 1.4.
All inputs are finite; a program needn't handle non-finite values.
Results may differ from the reference program's by a relative error of at most 0.0003.
Values sent between devices are 32-bit elements; how exact they have to be, the bound alone decides.
No kernel may reach another device: no remote copies, remote signals or barrier semaphores. Data moves between devices by JAX's collectives and lax.ppermute only.
A program may use at most 64 MiB of HBM per device.

```python
import jax
import jax.numpy as jnp
from jax import lax

BLK = 512
QUAD = 4
BPD = 16
NNEAR = 6
NFAR = 16
PANELS = 262144
N_ROW = 4
N_COL = 8
DEVICES = 32


def draw_points(key, part):
    first, second, third = jax.random.split(key, 3)
    center = jax.random.uniform(first, (3, 1, PANELS), jnp.float32, 0.0, 1.0)
    weight = jnp.exp(jax.random.uniform(third, (1, QUAD, PANELS), jnp.float32, jnp.log(0.01), jnp.log(0.04)))
    offset = jnp.clip(0.08 * jax.random.normal(second, (3, QUAD, PANELS), jnp.float32), -0.4, 0.4)
    return jnp.concatenate([center + offset, weight], axis=0).astype(jnp.float32)


def near_list(key):
    first, second, third = jax.random.split(key, 3)
    dev = jnp.arange(DEVICES, dtype=jnp.int32)
    own = jax.random.randint(first, (DEVICES, NNEAR), 0, BPD)
    col_a = (dev % N_COL)[:, None] * BPD + own
    col_b = jax.random.randint(second, (DEVICES, NNEAR), 0, N_ROW * BPD)
    which = jax.random.randint(third, (DEVICES,), 0, BPD)
    col_a = col_a.at[:, 0].set(dev % N_COL * BPD + which)
    col_b = col_b.at[:, 0].set(dev // N_COL * BPD + which)
    col_a = col_a.at[N_COL - 1, 1].set(N_COL * BPD - 1)
    col_b = col_b.at[N_COL - 1, 1].set(0)
    return jnp.stack([col_a.reshape(-1), col_b.reshape(-1)], axis=1).astype(jnp.int32)


def far_list(key):
    first, second = jax.random.split(key, 2)
    col_a = jax.random.randint(first, (DEVICES, NFAR), 0, N_COL * BPD)
    col_b = jax.random.randint(second, (DEVICES, NFAR), 0, N_ROW * BPD)
    col_a = col_a.at[0, 0].set(N_COL * BPD - 1)
    col_b = col_b.at[0, 0].set(0)
    return jnp.stack([col_a.reshape(-1), col_b.reshape(-1)], axis=1).astype(jnp.int32)


def draw_near_pairs(key, part):
    return near_list(jax.random.fold_in(key, 11))


def draw_far_pairs(key, part):
    return far_list(jax.random.fold_in(key, 12))


def skewed_counts(key, slots):
    first, second, third = jax.random.split(key, 3)
    left = jax.random.randint(first, (DEVICES,), 0, slots)
    right = jax.random.randint(second, (DEVICES,), 0, slots)
    counts = 1 + left * right // (slots - 1)
    busy = jax.random.randint(third, (), 0, DEVICES)
    return counts.at[busy].set(slots).astype(jnp.int32)


def draw_near_count(key, part):
    return skewed_counts(jax.random.fold_in(key, 21), NNEAR)


def draw_far_count(key, part):
    return skewed_counts(jax.random.fold_in(key, 22), NFAR)


def block_levels(key, extent, cuts, low, top_value):
    factor_of = 1.0
    for position, parts in cuts:
        draws = jax.random.uniform(jax.random.fold_in(jax.random.fold_in(key, 6), position), (parts,), jnp.float32, low / len(cuts), top_value / len(cuts))
        factor_of = factor_of * jnp.repeat(jnp.exp(draws), extent[position] // parts).reshape((-1,) + (1,) * (len(extent) - 1 - position))
    return factor_of


def noise(own_key, dims, spread, reach, cuts=(), held_as=jnp.bfloat16):
    values = jax.random.normal(own_key, dims, jnp.float32) * spread
    if len(cuts) > 0:
        values = block_levels(own_key, dims, cuts, -0.22, 0.18) * values
    return jnp.clip(values, min=-reach, max=reach).astype(held_as)


def setup_inputs(seed: int = 0) -> dict:
    key_of = jax.random.split(jax.random.key(seed), 7)
    return {
        "points": draw_points(jax.random.fold_in(key_of[6], 71), 0),
        "density": noise(key_of[1], (PANELS,), 1.0, 6.0, ((0, 32),), jnp.float32),
        "near_pairs": draw_near_pairs(jax.random.fold_in(key_of[6], 71), 0),
        "far_pairs": draw_far_pairs(jax.random.fold_in(key_of[6], 71), 0),
        "near_count": draw_near_count(jax.random.fold_in(key_of[6], 71), 0),
        "far_count": draw_far_count(jax.random.fold_in(key_of[6], 71), 0),
    }


soft_sq = 0.0004

def centroid(block):
    weight = lax.optimization_barrier(jnp.sum(block[3], axis=0))
    place = lax.optimization_barrier(jnp.sum(block[:3] * block[3][None], axis=1)) / weight[None]
    return (place, weight)

def far_tile(left, right):
    place_i, weight_i = centroid(left)
    place_j, weight_j = centroid(right)
    dist = jnp.zeros((left.shape[2], right.shape[2]), jnp.float32)
    for k in range(3):
        diff = place_i[k][:, None] - place_j[k][None, :]
        dist = dist + diff * diff
    return weight_i[:, None] * weight_j[None, :] * lax.rsqrt(dist + soft_sq)

def near_tile(left, right):
    total = jnp.zeros((left.shape[2], right.shape[2]), jnp.float32)
    for u in range(left.shape[1]):
        for v in range(right.shape[1]):
            dist = jnp.zeros((left.shape[2], right.shape[2]), jnp.float32)
            for k in range(3):
                diff = left[k, u][:, None] - right[k, v][None, :]
                dist = dist + diff * diff
            total = total + left[3, u][:, None] * right[3, v][None, :] * lax.rsqrt(dist + soft_sq)
    return total

def run_list(field, blocked, dens, pairs, counts, slots, tile_fn):

    def step(acc, s):
        dev = s // slots
        r = dev // N_COL
        c = dev % N_COL
        a = pairs[s, 0]
        b = pairs[s, 1]
        big_i = ((r * N_COL + a // BPD) * BPD + a % BPD).astype(jnp.int32)
        big_j = ((b // BPD * N_COL + c) * BPD + b % BPD).astype(jnp.int32)
        valid = s % slots < counts[dev]
        mirror = jnp.where(big_i == big_j, 0.0, 1.0).astype(jnp.float32)

        def compute(acc_in):
            left = lax.dynamic_index_in_dim(blocked, big_i, 2, keepdims=False)
            right = lax.dynamic_index_in_dim(blocked, big_j, 2, keepdims=False)
            tile = tile_fn(left, right)
            dens_i = lax.dynamic_index_in_dim(dens, big_i, 0, keepdims=False)
            dens_j = lax.dynamic_index_in_dim(dens, big_j, 0, keepdims=False)
            to_rows = jnp.dot(tile, dens_j, precision=lax.Precision.HIGHEST)
            to_cols = mirror * jnp.dot(dens_i, tile, precision=lax.Precision.HIGHEST)
            acc_in = acc_in.at[big_i].add(to_rows)
            return acc_in.at[big_j].add(to_cols)
        return (lax.cond(valid, compute, lambda x: x, acc), None)
    field, _ = lax.scan(step, field, jnp.arange(pairs.shape[0], dtype=jnp.int32))
    return field

def reference(points, density, near_pairs, far_pairs, near_count, far_count):
    nblk = PANELS // BLK
    blocked = points.reshape(4, points.shape[1], nblk, BLK)
    dens = density.reshape(nblk, BLK)
    field = jnp.zeros((nblk, BLK), jnp.float32)
    field = run_list(field, blocked, dens, near_pairs, near_count, NNEAR, near_tile)
    field = run_list(field, blocked, dens, far_pairs, far_count, NFAR, far_tile)
    return field.reshape(PANELS)
```

```python
import functools

import jax
import jax.numpy as jnp
from jax import lax
from jax.experimental import pallas as pl
from jax.experimental.pallas import tpu as pltpu
from jax.sharding import PartitionSpec as P

BLK = 512
LANES = 128
SOFT_SQ = 0.0004
TERMS = 48
VMEM = pl.BlockSpec(memory_space=pltpu.VMEM)
SMEM = pl.BlockSpec(memory_space=pltpu.SMEM)
ANY = pl.BlockSpec(memory_space=pl.ANY)
HIGH = lax.Precision.HIGHEST
PARAMS = pltpu.CompilerParams(vmem_limit_bytes=40 * 1024 * 1024)


def prep_kernel(far_ref, near_ref, pts_ref, dens_ref, far_out, near_out, weight_out):
    blocks = near_out.shape[0]
    quad = pts_ref.shape[1]
    for k in range(blocks):
        cols = slice(k * BLK, (k + 1) * BLK)
        w = pts_ref[3, :, cols]
        total = jnp.sum(w, axis=0, keepdims=True)
        dens = jnp.concatenate([dens_ref[4 * k + q : 4 * k + q + 1, :] for q in range(4)], axis=1)
        for c in range(3):
            x = pts_ref[c, :, cols]
            far_out[k, c : c + 1, :] = jnp.sum(x * w, axis=0, keepdims=True) / total
            near_out[k, quad * c : quad * c + quad, :] = x
        near_out[k, quad * 3 : quad * 4, :] = w
        near_out[k, quad * 4 : quad * 4 + 8, :] = jnp.broadcast_to(dens, (8, BLK))
        far_out[k, 3:4, :] = total * dens
        weight_out[k : k + 1, :] = total
    lane = lax.broadcasted_iota(jnp.int32, (1, BLK), 1)
    rows = [jnp.full((1, BLK), -1.0, jnp.float32) for _ in range(4)]
    for s in range(far_ref.shape[0]):
        for j in range(2):
            rows[j] = jnp.where(lane == s, far_ref[s, j].astype(jnp.float32), rows[j])
    for s in range(near_ref.shape[0]):
        for j in range(2):
            rows[2 + j] = jnp.where(lane == s, near_ref[s, j].astype(jnp.float32), rows[2 + j])
    for j in range(4):
        far_out[blocks, j : j + 1, :] = rows[j]


def pack_kernel(*refs, peers):
    asks, near_ref, outs = refs[:peers], refs[peers], refs[peers + 1 :]
    blocks, rows, _ = near_ref.shape
    body = rows - 8
    for ask, out in zip(asks, outs):
        slots = ask.shape[0] - 1
        for s in range(slots):
            k = lax.rem(ask[s + 1, 1], blocks)
            out[s * body : (s + 1) * body, :] = near_ref[k, 0:body, :]
            out[slots * body + s : slots * body + s + 1, :] = near_ref[k, body : body + 1, :]


def expand(x):
    row = lax.broadcasted_iota(jnp.int32, x.shape, 0)
    live = row < 3
    centred = jnp.where(live, x - 0.5, 0.0)
    head = jnp.round(centred * 256.0) * (1.0 / 256.0)
    rest = centred - head
    rest1 = rest.astype(jnp.bfloat16).astype(jnp.float32)
    rest2 = rest - rest1

    def three(value):
        one = value.astype(jnp.bfloat16).astype(jnp.float32)
        two = (value - one).astype(jnp.bfloat16).astype(jnp.float32)
        return jnp.where(row == 0, one, jnp.where(row == 1, two, jnp.where(row == 2, value - one - two, 0.0)))

    big = three(jnp.sum(head * head, axis=0, keepdims=True))
    small = three(jnp.sum(rest * (2.0 * head + rest), axis=0, keepdims=True) + 0.5 * SOFT_SQ)
    ones = jnp.where(live, 1.0, 0.0)
    h2, a2, b2 = -2.0 * head, -2.0 * rest1, -2.0 * rest2
    left = [h2, big, ones, small, ones, h2, h2, a2, b2, a2, a2, b2]
    right = [head, ones, big, ones, small, rest1, rest2, head, head, rest1, rest2, rest1]
    return jnp.concatenate(left, axis=0), jnp.concatenate(right, axis=0)


def as_column(row):
    return jnp.transpose(jnp.broadcast_to(row, (LANES, row.shape[1])))


def fold_lanes(tile, row):
    part = tile[:, :LANES] * row[:, :LANES]
    for q in range(1, BLK // LANES):
        part = part + tile[:, q * LANES : (q + 1) * LANES] * row[:, q * LANES : (q + 1) * LANES]
    return part


def fold_rows(tile, col):
    wide = jnp.concatenate([tile[:, q * LANES : (q + 1) * LANES] * col for q in range(BLK // LANES)], axis=1)
    return jnp.sum(wide.reshape(-1, 8, BLK), axis=0)


def far_kernel(pairs, count, *refs, n_row, n_col, blocks):
    row_in, col_in = refs[:n_col], refs[n_col : n_col + n_row - 1]
    rows_out, cols_out, row_buf, col_buf, sems = refs[n_col + n_row - 1 :]
    copies = []
    for p in range(n_col):
        src = row_in[p].at[pl.ds(0, blocks)]
        copies.append(pltpu.make_async_copy(src, row_buf.at[pl.ds(p * blocks, blocks)], sems.at[p]))
    for p in range(n_row):
        src = (row_in[0] if p == 0 else col_in[p - 1]).at[pl.ds(0, blocks)]
        copies.append(pltpu.make_async_copy(src, col_buf.at[pl.ds(p * blocks, blocks)], sems.at[n_col + p]))
    for copy in copies:
        copy.start()
    rows_out[...] = jnp.zeros_like(rows_out)
    cols_out[...] = jnp.zeros_like(cols_out)
    my_row, my_col = lax.axis_index("row"), lax.axis_index("col")
    for copy in copies:
        copy.wait()

    def step(s, _):
        a, b = pairs[s, 0], pairs[s, 1]
        at = jnp.bitwise_xor(lax.div(a, blocks), my_col) * blocks + lax.rem(a, blocks)
        bt = jnp.bitwise_xor(lax.div(b, blocks), my_row) * blocks + lax.rem(b, blocks)
        same = (at < blocks) & (bt < blocks) & (at == bt)
        left, right = row_buf[at], col_buf[bt]
        lhs = jnp.transpose(expand(left)[0]).astype(jnp.bfloat16)
        rhs = expand(right)[1].astype(jnp.bfloat16)
        tile = lax.rsqrt(jnp.dot(lhs, rhs, preferred_element_type=jnp.float32))
        part = fold_lanes(tile, right[3:4])
        rows_out[pl.ds(s, 1), :] = jnp.sum(jnp.transpose(part), axis=0, keepdims=True)
        cols = jnp.sum(fold_rows(tile, as_column(left[3:4])), axis=0, keepdims=True)
        cols_out[pl.ds(s, 1), :] = cols * jnp.where(same, 0.0, 1.0)
        return 0

    lax.fori_loop(0, count[0], step, 0)


def near_kernel(pairs, count, near_ref, *refs, peers, first, last, chunk):
    got = refs[:peers]
    rows_out, cols_out, right_buf, lhs_buf, rhs_buf, w_buf, z_buf, row_buf = refs[peers:]
    blocks, depth, _ = near_ref.shape
    body = depth - 8
    quad = body // 4
    my_row, my_col = lax.axis_index("row"), lax.axis_index("col")
    rows_out[...] = jnp.zeros_like(rows_out)
    if cols_out is not None:
        cols_out[...] = jnp.zeros_like(cols_out)

    def points(ref):
        sides = [[ref[quad * c + u : quad * c + u + 1, :] for c in range(4)] for u in range(quad)]
        return jnp.concatenate([jnp.concatenate(side, axis=0) for side in sides], axis=1)

    def step(s, _):
        a, b = pairs[s, 0], pairs[s, 1]
        ka, kb = a - my_col * blocks, lax.rem(b, blocks)
        where = jnp.bitwise_xor(lax.div(b, blocks), my_row)

        @pl.when(where == 0)
        def _():
            right_buf[...] = near_ref[kb]

        for p in range(peers):
            slots = pairs.shape[0] - 1

            @pl.when(where == p + 1)
            def _():
                at = pl.multiple_of((s - 1) * body, 8)
                right_buf[0:body, :] = got[p][pl.ds(at, body), :]
                right_buf[body : body + 1, :] = got[p][pl.ds(slots * body + s - 1, 1), :]

        left, right = points(near_ref.at[ka]), points(right_buf)
        dens_i, dens_j = near_ref[ka, body : body + 1, :], right_buf[body : body + 1, :]
        lhs_buf[...] = jnp.transpose(expand(left)[0]).astype(jnp.bfloat16)
        rhs_buf[...] = expand(right)[1].astype(jnp.bfloat16)
        w_buf[...] = as_column(left[3:4])
        z_buf[...] = as_column(left[3:4] * jnp.concatenate([dens_i] * quad, axis=1))
        row_buf[...] = jnp.zeros_like(row_buf)
        weights = right[3:4]

        def part(i, acc):
            at = pl.multiple_of(i * chunk, chunk)
            lhs = lhs_buf[pl.ds(at, chunk), :]
            tile = None
            for v in range(quad):
                cols = slice(v * BLK, (v + 1) * BLK)
                dist = jnp.dot(lhs, rhs_buf[:, cols], preferred_element_type=jnp.float32)
                term = weights[:, cols] * lax.rsqrt(dist)
                tile = term if tile is None else tile + term
            to = pl.multiple_of(lax.rem(i, BLK // chunk) * chunk, chunk)
            row_buf[pl.ds(to, chunk), :] += w_buf[pl.ds(at, chunk), :] * fold_lanes(tile, dens_j)
            return acc + fold_rows(tile, z_buf[pl.ds(at, chunk), :])

        acc = lax.fori_loop(0, quad * BLK // chunk, part, jnp.zeros((8, BLK), jnp.float32))
        rows_out[pl.ds(ka, 1), :] += jnp.sum(jnp.transpose(row_buf[...]), axis=0, keepdims=True)
        if cols_out is not None:
            same = (where == 0) & (ka == kb)
            cols_out[pl.ds(s, 1), :] = jnp.sum(acc, axis=0, keepdims=True) * jnp.where(same, 0.0, 1.0)
        return 0

    lax.fori_loop(first, jnp.minimum(count[0], last), step, 0)


def final_kernel(*refs, n_row, n_col, blocks):
    refs = list(refs)
    out = refs.pop()
    take = lambda n: [refs.pop(0) for _ in range(n)]
    weight, near0, near1 = take(3)
    tags, rows, cols, near_cols = take(n_col + n_row - 1), take(n_col), take(n_row), take(n_row)
    my_row, my_col = lax.axis_index("row"), lax.axis_index("col")

    def hot(tag, line, slots, base):
        index = tag[blocks, line : line + 1, 0:slots]
        want = lax.broadcasted_iota(jnp.int32, (blocks, slots), 0) + base * blocks
        return jnp.where(index == want.astype(jnp.float32), 1.0, 0.0)

    def gather(pick, slots):
        return jnp.dot(
            jnp.concatenate(pick, axis=1),
            jnp.concatenate(slots, axis=0),
            precision=HIGH,
            preferred_element_type=jnp.float32,
        )

    far = rows[0].shape[0]
    near = near_cols[0].shape[0]
    row_tags = [tags[0]] + tags[n_col:]
    pick = [hot(tags[p], 0, far, my_col) for p in range(n_col)]
    pick += [hot(row_tags[p], 1, far, my_row) for p in range(n_row)]
    field = gather(pick, [r[...] for r in rows + cols]) * weight[...]
    pick = [hot(row_tags[p], 3, near, my_row) for p in range(n_row)]
    field = field + gather(pick, [r[...] for r in near_cols]) + near0[...] + near1[...]
    for q in range(BLK // LANES):
        out[pl.ds(q, blocks, stride=BLK // LANES), :] = field[:, q * LANES : (q + 1) * LANES]


def f32(*shape):
    return jax.ShapeDtypeStruct(shape, jnp.float32)


def body(points, density, near_pairs, far_pairs, near_count, far_count, *, n_row, n_col):
    quad = points.shape[1]
    blocks = points.shape[2] // BLK
    nnear, nfar = near_pairs.shape[0], far_pairs.shape[0]
    depth = 4 * quad
    peers = n_row - 1

    def from_peer(x, axis, n, d):
        return lax.ppermute(x, axis, [(i, i ^ d) for i in range(n)])

    asks = [from_peer(near_pairs, "row", n_row, d) for d in range(1, n_row)]
    far_own, near_own, weight = pl.pallas_call(
        prep_kernel,
        out_shape=(f32(blocks + 1, 4, BLK), f32(blocks, depth + 8, BLK), f32(blocks, BLK)),
        in_specs=[SMEM, SMEM, VMEM, VMEM],
        out_specs=(VMEM, VMEM, VMEM),
        compiler_params=PARAMS,
        name="prep",
    )(far_pairs, near_pairs, points, density.reshape(-1, LANES))

    row_far = {0: far_own}
    for d in range(2, n_col, 2):
        row_far[d] = from_peer(far_own, "col", n_col, d)
    row_far[1] = from_peer(far_own, "col", n_col, 1)
    col_far = [from_peer(far_own, "row", n_row, d) for d in range(1, n_row)]
    for d in range(2, n_col, 2):
        row_far[d + 1] = from_peer(row_far[d], "col", n_col, 1)
    row_far = [row_far[d] for d in range(n_col)]

    slots = nnear - 1
    pack_rows = -(-(slots * depth + slots) // 8) * 8
    packs = pl.pallas_call(
        functools.partial(pack_kernel, peers=peers),
        out_shape=tuple(f32(pack_rows, BLK) for _ in range(peers)),
        in_specs=[SMEM] * peers + [VMEM],
        out_specs=tuple(VMEM for _ in range(peers)),
        compiler_params=PARAMS,
        name="pack",
    )(*asks, near_own)
    got = [from_peer(x, "row", n_row, d + 1) for d, x in enumerate(packs)]

    def near_call(peer_data, first, last, with_cols, name):
        chunk = 256
        kernel = functools.partial(near_kernel, peers=len(peer_data), first=first, last=last, chunk=chunk)
        outs = [f32(blocks, BLK)] + [f32(8, BLK)] * with_cols
        if not with_cols:
            inner, n_in = kernel, 3 + len(peer_data)
            kernel = lambda *refs: inner(*refs[: n_in + 1], None, *refs[n_in + 1 :])
        return pl.pallas_call(
            kernel,
            out_shape=tuple(outs),
            in_specs=[SMEM, SMEM] + [VMEM] * (1 + len(peer_data)),
            out_specs=tuple(VMEM for _ in outs),
            scratch_shapes=[
                pltpu.VMEM((depth + 8, BLK), jnp.float32),
                pltpu.VMEM((quad * BLK, TERMS), jnp.bfloat16),
                pltpu.VMEM((TERMS, quad * BLK), jnp.bfloat16),
                pltpu.VMEM((quad * BLK, LANES), jnp.float32),
                pltpu.VMEM((quad * BLK, LANES), jnp.float32),
                pltpu.VMEM((BLK, LANES), jnp.float32),
            ],
            compiler_params=PARAMS,
            name=name,
        )(near_pairs, near_count, near_own, *peer_data)

    (near0,) = near_call([], 0, 1, 0, "near_own")

    far_rows, far_cols = pl.pallas_call(
        functools.partial(far_kernel, n_row=n_row, n_col=n_col, blocks=blocks),
        out_shape=(f32(nfar, BLK), f32(nfar, BLK)),
        in_specs=[SMEM, SMEM] + [ANY] * (n_col + n_row - 1),
        out_specs=(VMEM, VMEM),
        scratch_shapes=[
            pltpu.VMEM((n_col * blocks, 4, BLK), jnp.float32),
            pltpu.VMEM((n_row * blocks, 4, BLK), jnp.float32),
            pltpu.SemaphoreType.DMA((n_col + n_row,)),
        ],
        compiler_params=PARAMS,
        name="far",
    )(far_pairs, far_count, *row_far, *col_far)

    near1, near_cols = near_call(got, 1, nnear, 1, "near_rest")

    all_rows = [far_rows] + [from_peer(far_rows, "col", n_col, d) for d in range(1, n_col)]
    all_cols = [far_cols] + [from_peer(far_cols, "row", n_row, d) for d in range(1, n_row)]
    all_near = [near_cols] + [from_peer(near_cols, "row", n_row, d) for d in range(1, n_row)]
    args = [weight, near0, near1, *row_far, *col_far, *all_rows, *all_cols, *all_near]
    out = pl.pallas_call(
        functools.partial(final_kernel, n_row=n_row, n_col=n_col, blocks=blocks),
        out_shape=f32(blocks * BLK // LANES, LANES),
        in_specs=[VMEM] * len(args),
        out_specs=VMEM,
        compiler_params=PARAMS,
        name="final",
    )(*args)
    return out.reshape(-1)


def solution(mesh):
    in_specs = (
        P(None, None, ("row", "col")),
        P(("row", "col")),
        P(("row", "col"), None),
        P(("row", "col"), None),
        P(("row", "col")),
        P(("row", "col")),
    )
    out_specs = P(("row", "col"))
    kernel = functools.partial(body, n_row=mesh.shape["row"], n_col=mesh.shape["col"])
    return jax.shard_map(kernel, mesh=mesh, in_specs=in_specs, out_specs=out_specs, check_vma=False)
```

```python
import functools

import jax
import jax.numpy as jnp
from jax import lax
from jax.experimental import pallas as pl
from jax.experimental.pallas import tpu as pltpu
from jax.sharding import PartitionSpec as P

BLK = 512
LANES = 128
SOFT_SQ = 0.0004
TERMS = 64
SPLIT = 48
HALF = 256
GROUP = 16
CHUNK = 128
VMEM = pl.BlockSpec(memory_space=pltpu.VMEM)
SMEM = pl.BlockSpec(memory_space=pltpu.SMEM)
HIGH = lax.Precision.HIGHEST
PARAMS = pltpu.CompilerParams(vmem_limit_bytes=40 * 1024 * 1024)


def prep_kernel(far_ref, near_ref, pts_ref, dens_ref, far_out, near_out, weight_out):
    blocks = near_out.shape[0]
    quad = pts_ref.shape[1]
    for k in range(blocks):
        cols = slice(k * BLK, (k + 1) * BLK)
        w = pts_ref[3, :, cols]
        total = jnp.sum(w, axis=0, keepdims=True)
        dens = jnp.concatenate([dens_ref[4 * k + q : 4 * k + q + 1, :] for q in range(4)], axis=1)
        for c in range(3):
            x = pts_ref[c, :, cols]
            far_out[k, c : c + 1, :] = jnp.sum(x * w, axis=0, keepdims=True) / total
            near_out[k, quad * c : quad * c + quad, :] = x
        near_out[k, quad * 3 : quad * 4, :] = w
        near_out[k, quad * 4 : quad * 4 + 8, :] = jnp.broadcast_to(dens, (8, BLK))
        far_out[k, 3:4, :] = total * dens
        weight_out[k : k + 1, :] = total
    lane = lax.broadcasted_iota(jnp.int32, (1, BLK), 1)
    rows = [jnp.full((1, BLK), -1.0, jnp.float32) for _ in range(4)]
    for s in range(far_ref.shape[0]):
        for j in range(2):
            rows[j] = jnp.where(lane == s, far_ref[s, j].astype(jnp.float32), rows[j])
    for s in range(near_ref.shape[0]):
        for j in range(2):
            rows[2 + j] = jnp.where(lane == s, near_ref[s, j].astype(jnp.float32), rows[2 + j])
    for j in range(4):
        far_out[blocks, j : j + 1, :] = rows[j]


def pack_kernel(asks, near_ref, out):
    blocks, rows, _ = near_ref.shape
    body, slots = rows - 8, asks.shape[1] - 1
    for p in range(out.shape[0]):
        for s in range(slots):
            k = lax.rem(asks[p, s + 1], blocks)
            out[p, s * body : (s + 1) * body, :] = near_ref[k, 0:body, :]
            out[p, slots * body + s : slots * body + s + 1, :] = near_ref[k, body : body + 1, :]


def three(value):
    one = value.astype(jnp.bfloat16).astype(jnp.float32)
    two = (value - one).astype(jnp.bfloat16).astype(jnp.float32)
    return one, two, value - one - two


def pick_row(row, values):
    out = jnp.zeros(row.shape, jnp.float32)
    for k, value in enumerate(values):
        out = jnp.where(row == k, value, out)
    return out


def parts(x):
    row = lax.broadcasted_iota(jnp.int32, x.shape, 0)
    live = row < 3
    centred = jnp.where(live, x - 0.5, 0.0)
    head = jnp.round(centred * 256.0) * (1.0 / 256.0)
    rest = centred - head
    rest1 = rest.astype(jnp.bfloat16).astype(jnp.float32)
    big = pick_row(row, three(jnp.sum(head * head, axis=0, keepdims=True)))
    small = pick_row(row, three(jnp.sum(rest * (2.0 * head + rest), axis=0, keepdims=True) + 0.5 * SOFT_SQ))
    return head, rest1, rest - rest1, big, small, jnp.where(live, 1.0, 0.0)


def left_terms(x, columns):
    head, rest1, rest2, big, small, ones = parts(x)
    h2, a2, b2 = -2.0 * head, -2.0 * rest1, -2.0 * rest2
    groups = [h2, big, ones, small, ones, h2, h2, a2, b2, a2, a2, b2]
    row = lax.broadcasted_iota(jnp.int32, (TERMS - SPLIT, x.shape[1]), 0)
    groups.append(pick_row(row, [part for column in columns for part in three(column)]))
    return jnp.concatenate(groups, axis=0)


def right_terms(x):
    head, rest1, rest2, big, small, ones = parts(x)
    groups = [head, ones, big, ones, small, rest1, rest2, head, head, rest1, rest2, rest1]
    groups.append(jnp.zeros((TERMS - SPLIT, x.shape[1]), jnp.float32))
    return jnp.concatenate(groups, axis=0).astype(jnp.bfloat16)


def column_of(lhs, which):
    row = lax.broadcasted_iota(jnp.int32, (TERMS, LANES), 0) - SPLIT - 3 * which
    pick = jnp.where((row >= 0) & (row < 3), 1.0, 0.0).astype(jnp.bfloat16)
    return jnp.dot(lhs, pick, preferred_element_type=jnp.float32)


def fold_lanes(tile, row):
    part = tile[:, :LANES] * row[:, :LANES]
    for q in range(1, tile.shape[1] // LANES):
        part = part + tile[:, q * LANES : (q + 1) * LANES] * row[:, q * LANES : (q + 1) * LANES]
    return part


def twice(col):
    return jnp.concatenate([col] * (HALF // LANES), axis=1)


def far_kernel(pairs, count, row_in, col_in, rows_out, cols_out, lhs_buf, rhs_buf, part_buf, *, blocks):
    rows_out[...] = jnp.zeros_like(rows_out)
    cols_out[...] = jnp.zeros_like(cols_out)
    my_row, my_col = lax.axis_index("row"), lax.axis_index("col")

    def step(s, _):
        a, b = pairs[s, 0], pairs[s, 1]
        a_dev, b_dev = lax.div(a, blocks), lax.div(b, blocks)
        ka, kb = lax.rem(a, blocks), lax.rem(b, blocks)
        same = (a_dev == my_col) & (b_dev == my_row) & (ka == kb)
        left, right = row_in[a_dev, ka], col_in[b_dev, kb]
        lhs_buf[...] = jnp.transpose(left_terms(left, [left[3:4]])).astype(jnp.bfloat16)
        rhs_buf[...] = right_terms(right)
        lhs = lhs_buf[...]
        zcol = column_of(lhs, 0)
        total = []
        for h in range(BLK // HALF):
            cols = slice(h * HALF, (h + 1) * HALF)
            dist = jnp.dot(lhs, rhs_buf[:, cols], preferred_element_type=jnp.float32)
            acc = jnp.zeros((8, HALF), jnp.float32)
            for g in range(BLK // 8):
                rows = slice(g * 8, (g + 1) * 8)
                tile = lax.rsqrt(dist[rows, :])
                part = fold_lanes(tile, right[3:4, cols])
                part_buf[rows, :] = part if h == 0 else part_buf[rows, :] + part
                acc = acc + tile * twice(zcol[rows, :])
            total.append(jnp.sum(acc, axis=0, keepdims=True))
        rows_out[pl.ds(s, 1), :] = jnp.sum(jnp.transpose(part_buf[...]), axis=0, keepdims=True)
        cols_out[pl.ds(s, 1), :] = jnp.concatenate(total, axis=1) * jnp.where(same, 0.0, 1.0)
        return 0

    lax.fori_loop(0, count[0], step, 0)


def near_kernel(pairs, count, near_ref, *refs, first, last):
    refs = list(refs)
    lhs_buf, rhs_buf, part_buf, acc_buf = refs[-4:]
    got = None
    if first > 0:
        got, far_cols, rows_out, cols_out = refs[:4]
        nfar = far_cols.shape[0]
        cols_out[0:nfar, :] = far_cols[...]
        cols_out[nfar : nfar + 8, :] = jnp.zeros((8, BLK), jnp.float32)
    else:
        rows_out = refs[0]
    blocks, depth, _ = near_ref.shape
    body = depth - 8
    quad = body // 4
    my_row, my_col = lax.axis_index("row"), lax.axis_index("col")
    rows_out[...] = jnp.zeros_like(rows_out)

    def points(tall):
        sides = [[tall[quad * c + u : quad * c + u + 1, :] for c in range(4)] for u in range(quad)]
        return jnp.concatenate([jnp.concatenate(side, axis=0) for side in sides], axis=1)

    def step(s, _):
        a, b = pairs[s, 0], pairs[s, 1]
        ka, kb = a - my_col * blocks, lax.rem(b, blocks)
        b_dev = lax.div(b, blocks)
        left, dens_i = points(near_ref[ka, 0:body, :]), near_ref[ka, body : body + 1, :]
        if first > 0:
            slots = pairs.shape[0] - 1
            at = pl.multiple_of((s - 1) * body, 8)
            right = points(got[b_dev, pl.ds(at, body), :])
            dens_j = got[b_dev, pl.ds(slots * body + s - 1, 1), :]
        else:
            right, dens_j = left, dens_i
        terms = jnp.transpose(left_terms(left, [left[3:4], jnp.concatenate([dens_i] * quad, axis=1)]))
        terms = terms.astype(jnp.bfloat16)
        for g in range(BLK // GROUP):
            for u in range(quad):
                to, at = (g * quad + u) * GROUP, u * BLK + g * GROUP
                lhs_buf[to : to + GROUP, :] = terms[at : at + GROUP, :]
        rhs_buf[...] = right_terms(right)
        weights = right[3:4]
        acc_buf[...] = jnp.zeros_like(acc_buf)

        def chunk(i, _):
            at = pl.multiple_of(i * CHUNK * quad, CHUNK * quad)
            lhs = lhs_buf[pl.ds(at, CHUNK * quad), :]
            wcol = column_of(lhs, 0)
            groups = CHUNK // GROUP
            first_rows = [lhs[g * quad * GROUP : g * quad * GROUP + GROUP, :] for g in range(groups)]
            dcol = column_of(jnp.concatenate(first_rows, axis=0), 1)
            part = None
            for h in range(BLK // HALF):
                tiles = [None] * groups
                for v in range(quad):
                    cols = slice(v * BLK + h * HALF, v * BLK + (h + 1) * HALF)
                    dist = jnp.dot(lhs, rhs_buf[:, cols], preferred_element_type=jnp.float32)
                    for g in range(groups):
                        inner = None
                        for u in range(quad):
                            rows = slice((g * quad + u) * GROUP, (g * quad + u + 1) * GROUP)
                            term = lax.rsqrt(dist[rows, :]) * twice(wcol[rows, :])
                            inner = term if inner is None else inner + term
                        inner = inner * weights[:, cols]
                        tiles[g] = inner if tiles[g] is None else tiles[g] + inner
                tile = jnp.concatenate(tiles, axis=0)
                cols = slice(h * HALF, (h + 1) * HALF)
                more = fold_lanes(tile, dens_j[:, cols])
                part = more if part is None else part + more
                acc_buf[:, cols] += jnp.sum((tile * twice(dcol)).reshape(-1, 8, HALF), axis=0)
            part_buf[pl.ds(pl.multiple_of(i * CHUNK, CHUNK), CHUNK), :] = part
            return 0

        lax.fori_loop(0, BLK // CHUNK, chunk, 0)
        rows_out[pl.ds(ka, 1), :] += jnp.sum(jnp.transpose(part_buf[...]), axis=0, keepdims=True)
        if first > 0:
            same = (b_dev == my_row) & (ka == kb)
            cols = jnp.sum(acc_buf[...], axis=0, keepdims=True)
            cols_out[pl.ds(nfar + s, 1), :] = cols * jnp.where(same, 0.0, 1.0)
        return 0

    lax.fori_loop(first, jnp.minimum(count[0], last), step, 0)


def final_kernel(weight, near0, near1, row_far, col_far, rows, cols, out):
    n_col, n_row = rows.shape[0], cols.shape[0]
    blocks, nfar = weight.shape[0], rows.shape[1]
    my_row, my_col = lax.axis_index("row"), lax.axis_index("col")

    def hot(index, slots, base):
        want = lax.broadcasted_iota(jnp.int32, (blocks, slots), 0) + base * blocks
        return jnp.where(index[:, 0:slots] == want.astype(jnp.float32), 1.0, 0.0)

    def gather(pick, slots):
        return jnp.dot(
            jnp.concatenate(pick, axis=1),
            jnp.concatenate(slots, axis=0),
            precision=HIGH,
            preferred_element_type=jnp.float32,
        )

    pick = [hot(row_far[p, blocks, 0:1, :], nfar, my_col) for p in range(n_col)]
    pick += [hot(col_far[p, blocks, 1:2, :], nfar, my_row) for p in range(n_row)]
    slots = [rows[p] for p in range(n_col)] + [cols[p, 0:nfar, :] for p in range(n_row)]
    field = gather(pick, slots) * weight[...]
    near = cols.shape[1] - nfar
    pick = [hot(col_far[p, blocks, 3:4, :], near, my_row) for p in range(n_row)]
    field = field + gather(pick, [cols[p, nfar:, :] for p in range(n_row)]) + near0[...] + near1[...]
    for q in range(BLK // LANES):
        out[pl.ds(q, blocks, stride=BLK // LANES), :] = field[:, q * LANES : (q + 1) * LANES]


def f32(*shape):
    return jax.ShapeDtypeStruct(shape, jnp.float32)


def cost(micros):
    return pl.CostEstimate(flops=int(micros * 1.1e9), bytes_accessed=1 << 16, transcendentals=0)


def body(points, density, near_pairs, far_pairs, near_count, far_count, *, n_row, n_col):
    quad = points.shape[1]
    blocks = points.shape[2] // BLK
    nnear, nfar = near_pairs.shape[0], far_pairs.shape[0]
    depth = 4 * quad

    def everywhere(x, axis, n):
        return lax.all_to_all(jnp.broadcast_to(x[None], (n,) + x.shape), axis, 0, 0)

    far_own, near_own, weight = pl.pallas_call(
        prep_kernel,
        out_shape=(f32(blocks + 1, 4, BLK), f32(blocks, depth + 8, BLK), f32(blocks, BLK)),
        in_specs=[SMEM, SMEM, VMEM, VMEM],
        out_specs=(VMEM, VMEM, VMEM),
        compiler_params=PARAMS,
        name="prep",
    )(far_pairs, near_pairs, points, density.reshape(-1, LANES))

    col_far = lax.all_gather(far_own, "row")
    row_far = lax.all_gather(far_own, "col")
    asks = col_far[:, blocks, 3, :nnear].astype(jnp.int32)

    slots = nnear - 1
    pack_rows = -(-(slots * depth + slots) // 8) * 8
    packs = pl.pallas_call(
        pack_kernel,
        out_shape=f32(n_row, pack_rows, BLK),
        in_specs=[SMEM, VMEM],
        out_specs=VMEM,
        compiler_params=PARAMS,
        name="pack",
    )(asks, near_own)
    got = lax.all_to_all(packs, "row", 0, 0)

    def near_call(extra, first, last, outs, name):
        return pl.pallas_call(
            functools.partial(near_kernel, first=first, last=last),
            out_shape=outs,
            in_specs=[SMEM, SMEM] + [VMEM] * (1 + len(extra)),
            out_specs=tuple(VMEM for _ in outs),
            scratch_shapes=[
                pltpu.VMEM((quad * BLK, TERMS), jnp.bfloat16),
                pltpu.VMEM((TERMS, quad * BLK), jnp.bfloat16),
                pltpu.VMEM((BLK, LANES), jnp.float32),
                pltpu.VMEM((8, BLK), jnp.float32),
            ],
            compiler_params=PARAMS,
            cost_estimate=cost(3.0),
            name=name,
        )(near_pairs, near_count, near_own, *extra)

    (near0,) = near_call([], 0, 1, (f32(blocks, BLK),), "near_own")

    far_rows, far_cols = pl.pallas_call(
        functools.partial(far_kernel, blocks=blocks),
        out_shape=(f32(nfar, BLK), f32(nfar, BLK)),
        in_specs=[SMEM, SMEM, VMEM, VMEM],
        out_specs=(VMEM, VMEM),
        scratch_shapes=[
            pltpu.VMEM((BLK, TERMS), jnp.bfloat16),
            pltpu.VMEM((TERMS, BLK), jnp.bfloat16),
            pltpu.VMEM((BLK, LANES), jnp.float32),
        ],
        compiler_params=PARAMS,
        cost_estimate=cost(3.0),
        name="far",
    )(far_pairs, far_count, row_far, col_far)

    near1, cols = near_call([got, far_cols], 1, nnear, (f32(blocks, BLK), f32(nfar + 8, BLK)), "near_rest")

    all_rows = lax.all_gather(far_rows, "col")
    all_cols = everywhere(cols, "row", n_row)
    out = pl.pallas_call(
        final_kernel,
        out_shape=f32(blocks * BLK // LANES, LANES),
        in_specs=[VMEM] * 7,
        out_specs=VMEM,
        compiler_params=PARAMS,
        name="final",
    )(weight, near0, near1, row_far, col_far, all_rows, all_cols)
    return out.reshape(-1)


def solution(mesh):
    in_specs = (
        P(None, None, ("row", "col")),
        P(("row", "col")),
        P(("row", "col"), None),
        P(("row", "col"), None),
        P(("row", "col")),
        P(("row", "col")),
    )
    out_specs = P(("row", "col"))
    kernel = functools.partial(body, n_row=mesh.shape["row"], n_col=mesh.shape["col"])
    return jax.shard_map(kernel, mesh=mesh, in_specs=in_specs, out_specs=out_specs, check_vma=False)
```

```python
import functools

import jax
import jax.numpy as jnp
from jax import lax
from jax.experimental import pallas as pl
from jax.experimental.pallas import tpu as pltpu
from jax.sharding import PartitionSpec as P

BLK = 512
LANES = 128
SOFT_SQ = 0.0004
TERMS = 64
SPLIT = 48
HALF = 256
GROUP = 16
CHUNK = 128
VMEM = pl.BlockSpec(memory_space=pltpu.VMEM)
SMEM = pl.BlockSpec(memory_space=pltpu.SMEM)
HIGH = lax.Precision.HIGHEST
PARAMS = pltpu.CompilerParams(vmem_limit_bytes=40 * 1024 * 1024)


def prep_kernel(far_ref, pts_ref, dens_ref, row_out, col_out, near_out, weight_out):
    blocks = near_out.shape[0]
    quad = pts_ref.shape[1]

    def to_all(k, value):
        for out in (row_out, col_out):
            for p in range(out.shape[0]):
                out[p, k] = value

    for k in range(blocks):
        cols = slice(k * BLK, (k + 1) * BLK)
        w = pts_ref[3, :, cols]
        total = jnp.sum(w, axis=0, keepdims=True)
        dens = jnp.concatenate([dens_ref[4 * k + q : 4 * k + q + 1, :] for q in range(4)], axis=1)
        lines = []
        for c in range(3):
            x = pts_ref[c, :, cols]
            lines.append(jnp.sum(x * w, axis=0, keepdims=True) / total)
            near_out[k, quad * c : quad * c + quad, :] = x
        near_out[k, quad * 3 : quad * 4, :] = w
        near_out[k, quad * 4 : quad * 4 + 8, :] = jnp.broadcast_to(dens, (8, BLK))
        to_all(k, jnp.concatenate(lines + [total * dens], axis=0))
        weight_out[k : k + 1, :] = total
    lane = lax.broadcasted_iota(jnp.int32, (4, BLK), 1)
    line = lax.broadcasted_iota(jnp.int32, (4, BLK), 0)
    tags = jnp.full((4, BLK), -1.0, jnp.float32)
    for s in range(far_ref.shape[1]):
        for j in range(2):
            tags = jnp.where((lane == s) & (line == j), far_ref[j, s].astype(jnp.float32), tags)
    to_all(blocks, tags)


def pack_kernel(lists, near_ref, out, sent, runs, load, edge):
    blocks, rows, _ = near_ref.shape
    n_row, slots = sent.shape[0], sent.shape[1] - 1
    body = rows - 8
    me = lax.axis_index("row")
    for p in range(n_row):
        load[p] = 0
        for q in range(n_row):
            edge[p, q] = 0
        for t in range(slots + 1):
            sent[p, t] = 0
            runs[p, t] = 0
    for q in range(n_row):
        for s in range(slots + 1):
            b = lists[q, slots + 1 + s]
            own = (b >= 0) & (lax.div(jnp.maximum(b, 0), blocks) == q)
            load[q] += own.astype(jnp.int32)

    def share(i, _):
        s, q = lax.div(i, n_row) + 1, lax.rem(i, n_row)
        a, b = lists[q, s], lists[q, slots + 1 + s]
        r = lax.div(jnp.maximum(b, 0), blocks)

        @pl.when((b >= 0) & (r != q))
        def _():
            here = load[q] <= load[r]
            here = jnp.where(edge[r, q] >= slots, False, here)
            here = jnp.where(edge[q, r] >= slots, True, here)
            run, src = jnp.where(here, q, r), jnp.where(here, r, q)
            ka, kb = lax.rem(a, blocks), lax.rem(b, blocks)
            t = edge[src, run]
            edge[src, run] = t + 1
            load[run] += 1

            @pl.when(src == me)
            def _():
                sent[run, t] = jnp.where(here, kb, ka)

            @pl.when(run == me)
            def _():
                runs[src, t] = jnp.where(here, ka, kb)
                runs[src, slots] = t + 1

        return 0

    lax.fori_loop(0, slots * n_row, share, 0)
    for p in range(n_row):
        for s in range(slots):
            k = sent[p, s]
            out[p, s * body : (s + 1) * body, :] = near_ref[k, 0:body, :]
            out[p, slots * body + s : slots * body + s + 1, :] = near_ref[k, body : body + 1, :]


def three(value):
    one = value.astype(jnp.bfloat16).astype(jnp.float32)
    two = (value - one).astype(jnp.bfloat16).astype(jnp.float32)
    return one, two, value - one - two


def pick_row(row, values):
    out = jnp.zeros(row.shape, jnp.float32)
    for k, value in enumerate(values):
        out = jnp.where(row == k, value, out)
    return out


def parts(x):
    row = lax.broadcasted_iota(jnp.int32, x.shape, 0)
    live = row < 3
    centred = jnp.where(live, x - 0.5, 0.0)
    head = jnp.round(centred * 256.0) * (1.0 / 256.0)
    rest = centred - head
    rest1 = rest.astype(jnp.bfloat16).astype(jnp.float32)
    big = pick_row(row, three(jnp.sum(head * head, axis=0, keepdims=True)))
    small = pick_row(row, three(jnp.sum(rest * (2.0 * head + rest), axis=0, keepdims=True) + 0.5 * SOFT_SQ))
    return head, rest1, rest - rest1, big, small, jnp.where(live, 1.0, 0.0)


def left_terms(x, columns):
    head, rest1, rest2, big, small, ones = parts(x)
    h2, a2, b2 = -2.0 * head, -2.0 * rest1, -2.0 * rest2
    groups = [h2, big, ones, small, ones, h2, h2, a2, b2, a2, a2, b2]
    row = lax.broadcasted_iota(jnp.int32, (TERMS - SPLIT, x.shape[1]), 0)
    groups.append(pick_row(row, [part for column in columns for part in three(column)]))
    return jnp.concatenate(groups, axis=0)


def right_terms(x):
    head, rest1, rest2, big, small, ones = parts(x)
    groups = [head, ones, big, ones, small, rest1, rest2, head, head, rest1, rest2, rest1]
    groups.append(jnp.zeros((TERMS - SPLIT, x.shape[1]), jnp.float32))
    return jnp.concatenate(groups, axis=0).astype(jnp.bfloat16)


def column_of(lhs, which):
    row = lax.broadcasted_iota(jnp.int32, (TERMS, LANES), 0) - SPLIT - 3 * which
    pick = jnp.where((row >= 0) & (row < 3), 1.0, 0.0).astype(jnp.bfloat16)
    return jnp.dot(lhs, pick, preferred_element_type=jnp.float32)


def fold_lanes(tile, row):
    part = tile[:, :LANES] * row[:, :LANES]
    for q in range(1, tile.shape[1] // LANES):
        part = part + tile[:, q * LANES : (q + 1) * LANES] * row[:, q * LANES : (q + 1) * LANES]
    return part


def twice(col):
    return jnp.concatenate([col] * (HALF // LANES), axis=1)


def far_kernel(pairs, count, row_in, col_in, _, rows_out, cols_out, lhs_buf, rhs_buf, part_buf, *, blocks):
    rows_out[...] = jnp.zeros_like(rows_out)
    cols_out[...] = jnp.zeros_like(cols_out)
    my_row, my_col = lax.axis_index("row"), lax.axis_index("col")

    def step(s, _):
        a, b = pairs[0, s], pairs[1, s]
        a_dev, b_dev = lax.div(a, blocks), lax.div(b, blocks)
        ka, kb = lax.rem(a, blocks), lax.rem(b, blocks)
        same = (a_dev == my_col) & (b_dev == my_row) & (ka == kb)
        left, right = row_in[a_dev, ka], col_in[b_dev, kb]
        lhs_buf[...] = jnp.transpose(left_terms(left, [left[3:4]])).astype(jnp.bfloat16)
        rhs_buf[...] = right_terms(right)
        lhs = lhs_buf[...]
        zcol = column_of(lhs, 0)
        total = []
        for h in range(BLK // HALF):
            cols = slice(h * HALF, (h + 1) * HALF)
            dist = jnp.dot(lhs, rhs_buf[:, cols], preferred_element_type=jnp.float32)
            acc = jnp.zeros((8, HALF), jnp.float32)
            for g in range(BLK // 8):
                rows = slice(g * 8, (g + 1) * 8)
                tile = lax.rsqrt(dist[rows, :])
                part = fold_lanes(tile, right[3:4, cols])
                part_buf[rows, :] = part if h == 0 else part_buf[rows, :] + part
                acc = acc + tile * twice(zcol[rows, :])
            total.append(jnp.sum(acc, axis=0, keepdims=True))
        rows_out[pl.ds(s, 1), :] = jnp.sum(jnp.transpose(part_buf[...]), axis=0, keepdims=True)
        cols_out[pl.ds(s, 1), :] = jnp.concatenate(total, axis=1) * jnp.where(same, 0.0, 1.0)
        return 0

    lax.fori_loop(0, count[0], step, 0)


def points(tall):
    quad = tall.shape[0] // 4
    sides = [[tall[quad * c + u : quad * c + u + 1, :] for c in range(4)] for u in range(quad)]
    return jnp.concatenate([jnp.concatenate(side, axis=0) for side in sides], axis=1)


def near_tile(left, dens_i, right, dens_j, lhs_buf, rhs_buf, part_buf, acc_buf):
    quad = left.shape[1] // BLK
    terms = jnp.transpose(left_terms(left, [left[3:4], jnp.concatenate([dens_i] * quad, axis=1)]))
    terms = terms.astype(jnp.bfloat16)
    for g in range(BLK // GROUP):
        for u in range(quad):
            to, at = (g * quad + u) * GROUP, u * BLK + g * GROUP
            lhs_buf[to : to + GROUP, :] = terms[at : at + GROUP, :]
    rhs_buf[...] = right_terms(right)
    weights = right[3:4]
    acc_buf[...] = jnp.zeros_like(acc_buf)

    def chunk(i, _):
        at = pl.multiple_of(i * CHUNK * quad, CHUNK * quad)
        lhs = lhs_buf[pl.ds(at, CHUNK * quad), :]
        wcol = column_of(lhs, 0)
        groups = CHUNK // GROUP
        first_rows = [lhs[g * quad * GROUP : g * quad * GROUP + GROUP, :] for g in range(groups)]
        dcol = column_of(jnp.concatenate(first_rows, axis=0), 1)
        part = None
        for h in range(BLK // HALF):
            tiles = [None] * groups
            for v in range(quad):
                cols = slice(v * BLK + h * HALF, v * BLK + (h + 1) * HALF)
                dist = jnp.dot(lhs, rhs_buf[:, cols], preferred_element_type=jnp.float32)
                for g in range(groups):
                    inner = None
                    for u in range(quad):
                        rows = slice((g * quad + u) * GROUP, (g * quad + u + 1) * GROUP)
                        term = lax.rsqrt(dist[rows, :]) * twice(wcol[rows, :])
                        inner = term if inner is None else inner + term
                    inner = inner * weights[:, cols]
                    tiles[g] = inner if tiles[g] is None else tiles[g] + inner
            tile = jnp.concatenate(tiles, axis=0)
            cols = slice(h * HALF, (h + 1) * HALF)
            more = fold_lanes(tile, dens_j[:, cols])
            part = more if part is None else part + more
            acc_buf[:, cols] += jnp.sum((tile * twice(dcol)).reshape(-1, 8, HALF), axis=0)
        part_buf[pl.ds(pl.multiple_of(i * CHUNK, CHUNK), CHUNK), :] = part
        return 0

    lax.fori_loop(0, BLK // CHUNK, chunk, 0)
    rows = jnp.sum(jnp.transpose(part_buf[...]), axis=0, keepdims=True)
    return rows, jnp.sum(acc_buf[...], axis=0, keepdims=True)


def near_own_kernel(pairs, count, near_ref, field, *bufs):
    blocks, depth, _ = near_ref.shape
    body = depth - 8
    my_row, my_col = lax.axis_index("row"), lax.axis_index("col")
    field[...] = jnp.zeros_like(field)

    def step(s, _):
        ka = pairs[0, s] - my_col * blocks
        kb = pairs[1, s] - my_row * blocks

        @pl.when((kb >= 0) & (kb < blocks))
        def _():
            left, right = points(near_ref[ka, 0:body, :]), points(near_ref[kb, 0:body, :])
            dens_i, dens_j = near_ref[ka, body : body + 1, :], near_ref[kb, body : body + 1, :]
            rows, cols = near_tile(left, dens_i, right, dens_j, *bufs)
            field[pl.ds(ka, 1), :] += rows
            field[pl.ds(kb, 1), :] += cols * jnp.where(ka == kb, 0.0, 1.0)

        return 0

    lax.fori_loop(0, count[0], step, 0)


def near_kernel(runs, near_ref, got, start, _, field, back, *bufs):
    depth = near_ref.shape[1]
    n_row, slots = runs.shape[0], runs.shape[1] - 1
    body = depth - 8
    field[...] = start[...]
    back[...] = jnp.zeros_like(back)

    def peer(p, _):
        def step(t, _):
            ka = runs[p, t]
            at = pl.multiple_of(t * body, 8)
            left, right = points(near_ref[ka, 0:body, :]), points(got[p, pl.ds(at, body), :])
            dens_i = near_ref[ka, body : body + 1, :]
            dens_j = got[p, pl.ds(slots * body + t, 1), :]
            rows, cols = near_tile(left, dens_i, right, dens_j, *bufs)
            field[pl.ds(ka, 1), :] += rows
            back[p, pl.ds(t, 1), :] = cols
            return 0

        lax.fori_loop(0, runs[p, slots], step, 0)
        return 0

    lax.fori_loop(0, n_row, peer, 0)


def final_kernel(sent, weight, near, row_far, col_far, rows, cols, back, out, field):
    n_col, n_row = rows.shape[0], cols.shape[0]
    blocks, nfar = weight.shape[0], rows.shape[1]
    my_row, my_col = lax.axis_index("row"), lax.axis_index("col")
    field[...] = near[...]
    for p in range(n_row):
        for t in range(sent.shape[1] - 1):
            field[pl.ds(sent[p, t], 1), :] += back[p, t : t + 1, :]

    def hot(index, slots, base):
        want = lax.broadcasted_iota(jnp.int32, (blocks, slots), 0) + base * blocks
        return jnp.where(index[:, 0:slots] == want.astype(jnp.float32), 1.0, 0.0)

    pick = [hot(row_far[p, blocks, 0:1, :], nfar, my_col) for p in range(n_col)]
    pick += [hot(col_far[p, blocks, 1:2, :], nfar, my_row) for p in range(n_row)]
    far = jnp.dot(
        jnp.concatenate(pick, axis=1),
        jnp.concatenate([rows[p] for p in range(n_col)] + [cols[p] for p in range(n_row)], axis=0),
        precision=HIGH,
        preferred_element_type=jnp.float32,
    )
    total = field[...] + far * weight[...]
    for q in range(BLK // LANES):
        out[pl.ds(q, blocks, stride=BLK // LANES), :] = total[:, q * LANES : (q + 1) * LANES]


def f32(*shape):
    return jax.ShapeDtypeStruct(shape, jnp.float32)


def cost(micros):
    return pl.CostEstimate(flops=int(micros * 1.1e9), bytes_accessed=1 << 16, transcendentals=0)


def body(points, density, near_pairs, far_pairs, near_count, far_count, *, n_row, n_col):
    quad = points.shape[1]
    blocks = points.shape[2] // BLK
    nnear, nfar = near_pairs.shape[0], far_pairs.shape[0]
    depth, slots = 4 * quad, nnear - 1
    near_pairs, far_pairs = near_pairs.T, far_pairs.T

    def swap(x, axis):
        return lax.all_to_all(x, axis, 0, 0)

    def everywhere(x, n):
        return jnp.broadcast_to(x[None], (n,) + x.shape)

    used = jnp.arange(nnear) < near_count[0]
    lists = jnp.concatenate([near_pairs[0], jnp.where(used, near_pairs[1], -1)])
    lists = swap(everywhere(lists, n_row), "row")

    col_far, row_far, near_own, weight = pl.pallas_call(
        prep_kernel,
        out_shape=(
            f32(n_row, blocks + 1, 4, BLK),
            f32(n_col, blocks + 1, 4, BLK),
            f32(blocks, depth + 8, BLK),
            f32(blocks, BLK),
        ),
        in_specs=[SMEM, VMEM, VMEM],
        out_specs=(VMEM, VMEM, VMEM, VMEM),
        compiler_params=PARAMS,
        cost_estimate=cost(1.7),
        name="prep",
    )(far_pairs, points, density.reshape(-1, LANES))
    col_far = swap(col_far, "row")
    row_far = swap(row_far, "col")

    ints = jax.ShapeDtypeStruct((n_row, slots + 1), jnp.int32)
    pack_rows = -(-(slots * depth + slots) // 8) * 8
    packs, sent, runs = pl.pallas_call(
        pack_kernel,
        out_shape=(f32(n_row, pack_rows, BLK), ints, ints),
        in_specs=[SMEM, VMEM],
        out_specs=(VMEM, SMEM, SMEM),
        scratch_shapes=[pltpu.SMEM((n_row,), jnp.int32), pltpu.SMEM((n_row, n_row), jnp.int32)],
        compiler_params=PARAMS,
        cost_estimate=cost(2.0),
        name="pack",
    )(lists, near_own)
    got = swap(packs, "row")

    bufs = [
        pltpu.VMEM((quad * BLK, TERMS), jnp.bfloat16),
        pltpu.VMEM((TERMS, quad * BLK), jnp.bfloat16),
        pltpu.VMEM((BLK, LANES), jnp.float32),
        pltpu.VMEM((8, BLK), jnp.float32),
    ]
    near0 = pl.pallas_call(
        near_own_kernel,
        out_shape=f32(blocks, BLK),
        in_specs=[SMEM, SMEM, VMEM],
        out_specs=VMEM,
        scratch_shapes=bufs,
        compiler_params=PARAMS,
        cost_estimate=cost(5.0),
        name="near_own",
    )(near_pairs, near_count, near_own)

    far_rows, far_cols = pl.pallas_call(
        functools.partial(far_kernel, blocks=blocks),
        out_shape=(f32(nfar, BLK), f32(nfar, BLK)),
        in_specs=[SMEM, SMEM, VMEM, VMEM, pl.BlockSpec(memory_space=pl.ANY)],
        out_specs=(VMEM, VMEM),
        scratch_shapes=[
            pltpu.VMEM((BLK, TERMS), jnp.bfloat16),
            pltpu.VMEM((TERMS, BLK), jnp.bfloat16),
            pltpu.VMEM((BLK, LANES), jnp.float32),
        ],
        compiler_params=PARAMS,
        cost_estimate=cost(4.0),
        name="far",
    )(far_pairs, far_count, row_far, col_far, near0)

    near1, back = pl.pallas_call(
        near_kernel,
        out_shape=(f32(blocks, BLK), f32(n_row, 8, BLK)),
        in_specs=[SMEM, VMEM, VMEM, VMEM, pl.BlockSpec(memory_space=pl.ANY)],
        out_specs=(VMEM, VMEM),
        scratch_shapes=bufs,
        compiler_params=PARAMS,
        cost_estimate=cost(10.0),
        name="near_rest",
    )(runs, near_own, got, near0, far_cols)

    all_rows = swap(everywhere(far_rows, n_col), "col")
    all_cols = swap(everywhere(far_cols, n_row), "row")
    back = swap(back, "row")
    out = pl.pallas_call(
        final_kernel,
        out_shape=f32(blocks * BLK // LANES, LANES),
        in_specs=[SMEM] + [VMEM] * 7,
        out_specs=VMEM,
        scratch_shapes=[pltpu.VMEM((blocks, BLK), jnp.float32)],
        compiler_params=PARAMS,
        name="final",
    )(sent, weight, near1, row_far, col_far, all_rows, all_cols, back)
    return out.reshape(-1)


def solution(mesh):
    in_specs = (
        P(None, None, ("row", "col")),
        P(("row", "col")),
        P(("row", "col"), None),
        P(("row", "col"), None),
        P(("row", "col")),
        P(("row", "col")),
    )
    out_specs = P(("row", "col"))
    kernel = functools.partial(body, n_row=mesh.shape["row"], n_col=mesh.shape["col"])
    return jax.shard_map(kernel, mesh=mesh, in_specs=in_specs, out_specs=out_specs, check_vma=False)
```

```python
import functools

import jax
import jax.numpy as jnp
from jax import lax
from jax.experimental import pallas as pl
from jax.experimental.pallas import tpu as pltpu
from jax.sharding import PartitionSpec as P

BLK = 512
LANES = 128
SOFT_SQ = 0.0004
TERMS = 64
SPLIT = 48
HALF = 512
GROUP = 16
CHUNK = 128
VMEM = pl.BlockSpec(memory_space=pltpu.VMEM)
SMEM = pl.BlockSpec(memory_space=pltpu.SMEM)
HIGH = lax.Precision.HIGHEST
PARAMS = pltpu.CompilerParams(vmem_limit_bytes=40 * 1024 * 1024)


def prep_kernel(far_ref, pts_ref, dens_ref, far_out, near_out, weight_out):
    blocks = near_out.shape[0]
    quad = pts_ref.shape[1]

    for k in range(blocks):
        cols = slice(k * BLK, (k + 1) * BLK)
        w = pts_ref[3, :, cols]
        total = jnp.sum(w, axis=0, keepdims=True)
        dens = jnp.concatenate([dens_ref[4 * k + q : 4 * k + q + 1, :] for q in range(4)], axis=1)
        lines = []
        for c in range(3):
            x = pts_ref[c, :, cols]
            lines.append(jnp.sum(x * w, axis=0, keepdims=True) / total)
            near_out[k, quad * c : quad * c + quad, :] = x
        near_out[k, quad * 3 : quad * 4, :] = w
        near_out[k, quad * 4 : quad * 4 + 8, :] = jnp.broadcast_to(dens, (8, BLK))
        far_out[k] = jnp.concatenate(lines + [total * dens], axis=0)
        weight_out[k : k + 1, :] = total
    lane = lax.broadcasted_iota(jnp.int32, (4, BLK), 1)
    line = lax.broadcasted_iota(jnp.int32, (4, BLK), 0)
    tags = jnp.full((4, BLK), -1.0, jnp.float32)
    for s in range(far_ref.shape[1]):
        for j in range(2):
            tags = jnp.where((lane == s) & (line == j), far_ref[j, s].astype(jnp.float32), tags)
    far_out[blocks] = tags


def pack_kernel(*refs, n_row):
    lists, near_ref = refs[:n_row], refs[n_row]
    outs, (sent, runs, table, load, edge) = refs[n_row + 1 : 2 * n_row], refs[2 * n_row :]
    blocks, rows, _ = near_ref.shape
    slots = sent.shape[1] - 1
    body = rows - 8
    me = lax.axis_index("row")
    for d in range(n_row):
        q = jnp.bitwise_xor(me, d)
        own = jnp.int32(0)
        for s in range(slots + 1):
            b = lists[d][1, s]
            table[q, s] = lists[d][0, s]
            table[q, slots + 1 + s] = b
            own = own + jnp.where((b >= q * blocks) & (b < (q + 1) * blocks), 1, 0)
        load[q] = own
        for r in range(n_row):
            edge[d, r] = 0
        for t in range(slots + 1):
            sent[d, t] = 0
            runs[d, t] = 0

    def share(i, _):
        s, q = lax.div(i, n_row) + 1, lax.rem(i, n_row)
        a, b = table[q, s], table[q, slots + 1 + s]
        r = lax.div(jnp.maximum(b, 0), blocks)

        @pl.when((b >= 0) & (r != q))
        def _():
            here = load[q] <= load[r]
            here = jnp.where(edge[r, q] >= slots, False, here)
            here = jnp.where(edge[q, r] >= slots, True, here)
            run, src = jnp.where(here, q, r), jnp.where(here, r, q)
            ka, kb = lax.rem(a, blocks), lax.rem(b, blocks)
            t = edge[src, run]
            edge[src, run] = t + 1
            load[run] += 1

            @pl.when(src == me)
            def _():
                sent[run, t] = jnp.where(here, kb, ka)

            @pl.when(run == me)
            def _():
                runs[src, t] = jnp.where(here, ka, kb)
                runs[src, slots] = t + 1

        return 0

    lax.fori_loop(0, slots * n_row, share, 0)
    for d, out in enumerate(outs):
        for s in range(slots):
            k = sent[jnp.bitwise_xor(me, d + 1), s]
            out[s * body : (s + 1) * body, :] = near_ref[k, 0:body, :]
            out[slots * body + s : slots * body + s + 1, :] = near_ref[k, body : body + 1, :]


def three(value):
    one = value.astype(jnp.bfloat16).astype(jnp.float32)
    two = (value - one).astype(jnp.bfloat16).astype(jnp.float32)
    return one, two, value - one - two


def pick_row(row, values):
    out = jnp.zeros(row.shape, jnp.float32)
    for k, value in enumerate(values):
        out = jnp.where(row == k, value, out)
    return out


def parts(x):
    row = lax.broadcasted_iota(jnp.int32, x.shape, 0)
    live = row < 3
    centred = jnp.where(live, x - 0.5, 0.0)
    head = jnp.round(centred * 256.0) * (1.0 / 256.0)
    rest = centred - head
    rest1 = rest.astype(jnp.bfloat16).astype(jnp.float32)
    big = pick_row(row, three(jnp.sum(head * head, axis=0, keepdims=True)))
    small = pick_row(row, three(jnp.sum(rest * (2.0 * head + rest), axis=0, keepdims=True) + 0.5 * SOFT_SQ))
    return head, rest1, rest - rest1, big, small, jnp.where(live, 1.0, 0.0)


def left_terms(x, columns):
    head, rest1, rest2, big, small, ones = parts(x)
    h2, a2, b2 = -2.0 * head, -2.0 * rest1, -2.0 * rest2
    groups = [h2, big, ones, small, ones, h2, h2, a2, b2, a2, a2, b2]
    row = lax.broadcasted_iota(jnp.int32, (TERMS - SPLIT, x.shape[1]), 0)
    groups.append(pick_row(row, [part for column in columns for part in three(column)]))
    return jnp.concatenate(groups, axis=0)


def right_terms(x):
    head, rest1, rest2, big, small, ones = parts(x)
    groups = [head, ones, big, ones, small, rest1, rest2, head, head, rest1, rest2, rest1]
    groups.append(jnp.zeros((TERMS - SPLIT, x.shape[1]), jnp.float32))
    return jnp.concatenate(groups, axis=0).astype(jnp.bfloat16)


def column_of(lhs, which):
    row = lax.broadcasted_iota(jnp.int32, (TERMS, LANES), 0) - SPLIT - 3 * which
    pick = jnp.where((row >= 0) & (row < 3), 1.0, 0.0).astype(jnp.bfloat16)
    return jnp.dot(lhs, pick, preferred_element_type=jnp.float32)


def fold_lanes(tile, row):
    part = tile[:, :LANES] * row[:, :LANES]
    for q in range(1, tile.shape[1] // LANES):
        part = part + tile[:, q * LANES : (q + 1) * LANES] * row[:, q * LANES : (q + 1) * LANES]
    return part


def twice(col):
    return jnp.concatenate([col] * (HALF // LANES), axis=1)


def far_kernel(*refs, blocks, n_row):
    pairs, count, back, row_in = refs[:4]
    col_in = refs[4 : 4 + n_row]
    rows_out, cols_out = refs[4 + n_row : 6 + n_row]
    messages = refs[6 + n_row : 5 + 2 * n_row]
    right_buf, lhs_buf, rhs_buf, part_buf = refs[5 + 2 * n_row :]
    rows_out[...] = jnp.zeros_like(rows_out)
    cols_out[...] = jnp.zeros_like(cols_out)
    my_row, my_col = lax.axis_index("row"), lax.axis_index("col")

    def step(s, _):
        a, b = pairs[0, s], pairs[1, s]
        a_dev, b_way = lax.div(a, blocks), jnp.bitwise_xor(lax.div(b, blocks), my_row)
        ka, kb = lax.rem(a, blocks), lax.rem(b, blocks)
        same = (a_dev == my_col) & (b_way == 0) & (ka == kb)
        for d in range(n_row):

            @pl.when(b_way == d)
            def _():
                right_buf[...] = col_in[d][kb]

        left, right = row_in[a_dev, ka], right_buf[...]
        lhs_buf[...] = jnp.transpose(left_terms(left, [left[3:4]])).astype(jnp.bfloat16)
        rhs_buf[...] = right_terms(right)
        lhs = lhs_buf[...]
        zcol = column_of(lhs, 0)
        total = []
        for h in range(BLK // HALF):
            cols = slice(h * HALF, (h + 1) * HALF)
            dist = jnp.dot(lhs, rhs_buf[:, cols], preferred_element_type=jnp.float32)
            acc = jnp.zeros((8, HALF), jnp.float32)
            for g in range(BLK // 8):
                rows = slice(g * 8, (g + 1) * 8)
                tile = lax.rsqrt(dist[rows, :])
                part = fold_lanes(tile, right[3:4, cols])
                part_buf[rows, :] = part if h == 0 else part_buf[rows, :] + part
                acc = acc + tile * twice(zcol[rows, :])
            total.append(jnp.sum(acc, axis=0, keepdims=True))
        rows_out[pl.ds(s, 1), :] = jnp.sum(jnp.transpose(part_buf[...]), axis=0, keepdims=True)
        cols_out[pl.ds(s, 1), :] = jnp.concatenate(total, axis=1) * jnp.where(same, 0.0, 1.0)
        return 0

    lax.fori_loop(0, count[0], step, 0)
    nfar = cols_out.shape[0]
    for d, message in enumerate(messages):
        message[0:nfar, :] = cols_out[...]
        message[nfar:, :] = back[d]


def points(tall):
    quad = tall.shape[0] // 4
    sides = [[tall[quad * c + u : quad * c + u + 1, :] for c in range(4)] for u in range(quad)]
    return jnp.concatenate([jnp.concatenate(side, axis=0) for side in sides], axis=1)


def near_tile(left, dens_i, right, dens_j, lhs_buf, rhs_buf, part_buf, acc_buf):
    quad = left.shape[1] // BLK
    terms = jnp.transpose(left_terms(left, [left[3:4], jnp.concatenate([dens_i] * quad, axis=1)]))
    terms = terms.astype(jnp.bfloat16)
    for g in range(BLK // GROUP):
        for u in range(quad):
            to, at = (g * quad + u) * GROUP, u * BLK + g * GROUP
            lhs_buf[to : to + GROUP, :] = terms[at : at + GROUP, :]
    rhs_buf[...] = right_terms(right)
    weights = right[3:4]
    acc_buf[...] = jnp.zeros_like(acc_buf)

    def chunk(i, _):
        at = pl.multiple_of(i * CHUNK * quad, CHUNK * quad)
        lhs = lhs_buf[pl.ds(at, CHUNK * quad), :]
        wcol = column_of(lhs, 0)
        groups = CHUNK // GROUP
        first_rows = [lhs[g * quad * GROUP : g * quad * GROUP + GROUP, :] for g in range(groups)]
        dcol = column_of(jnp.concatenate(first_rows, axis=0), 1)
        part = None
        for h in range(BLK // HALF):
            tiles = [None] * groups
            for v in range(quad):
                cols = slice(v * BLK + h * HALF, v * BLK + (h + 1) * HALF)
                dist = jnp.dot(lhs, rhs_buf[:, cols], preferred_element_type=jnp.float32)
                for g in range(groups):
                    inner = None
                    for u in range(quad):
                        rows = slice((g * quad + u) * GROUP, (g * quad + u + 1) * GROUP)
                        term = lax.rsqrt(dist[rows, :]) * twice(wcol[rows, :])
                        inner = term if inner is None else inner + term
                    inner = inner * weights[:, cols]
                    tiles[g] = inner if tiles[g] is None else tiles[g] + inner
            tile = jnp.concatenate(tiles, axis=0)
            cols = slice(h * HALF, (h + 1) * HALF)
            more = fold_lanes(tile, dens_j[:, cols])
            part = more if part is None else part + more
            acc_buf[:, cols] += jnp.sum((tile * twice(dcol)).reshape(-1, 8, HALF), axis=0)
        part_buf[pl.ds(pl.multiple_of(i * CHUNK, CHUNK), CHUNK), :] = part
        return 0

    lax.fori_loop(0, BLK // CHUNK, chunk, 0)
    rows = jnp.sum(jnp.transpose(part_buf[...]), axis=0, keepdims=True)
    return rows, jnp.sum(acc_buf[...], axis=0, keepdims=True)


def near_own_kernel(pairs, count, near_ref, field, *bufs):
    blocks, depth, _ = near_ref.shape
    body = depth - 8
    my_row, my_col = lax.axis_index("row"), lax.axis_index("col")
    field[...] = jnp.zeros_like(field)

    def step(s, _):
        ka = pairs[0, s] - my_col * blocks
        kb = pairs[1, s] - my_row * blocks

        @pl.when((kb >= 0) & (kb < blocks))
        def _():
            left, right = points(near_ref[ka, 0:body, :]), points(near_ref[kb, 0:body, :])
            dens_i, dens_j = near_ref[ka, body : body + 1, :], near_ref[kb, body : body + 1, :]
            rows, cols = near_tile(left, dens_i, right, dens_j, *bufs)
            field[pl.ds(ka, 1), :] += rows
            field[pl.ds(kb, 1), :] += cols * jnp.where(ka == kb, 0.0, 1.0)

        return 0

    lax.fori_loop(0, count[0], step, 0)


def near_kernel(*refs, n_row):
    runs, near_ref = refs[:2]
    got = refs[2 : n_row + 1]
    start, field, back, right_buf, *bufs = refs[n_row + 1 :]
    depth = near_ref.shape[1]
    slots = runs.shape[1] - 1
    body = depth - 8
    me = lax.axis_index("row")
    field[...] = start[...]
    back[...] = jnp.zeros_like(back)

    def step(i, _):
        way, t = lax.div(i, slots), lax.rem(i, slots)
        p = jnp.bitwise_xor(me, way + 1)

        @pl.when(t < runs[p, slots])
        def _():
            for d in range(n_row - 1):

                @pl.when(way == d)
                def _():
                    at = pl.multiple_of(t * body, 8)
                    right_buf[0:body, :] = got[d][pl.ds(at, body), :]
                    right_buf[body : body + 1, :] = got[d][pl.ds(slots * body + t, 1), :]

            ka = runs[p, t]
            left, right = points(near_ref[ka, 0:body, :]), points(right_buf[0:body, :])
            dens_i, dens_j = near_ref[ka, body : body + 1, :], right_buf[body : body + 1, :]
            rows, cols = near_tile(left, dens_i, right, dens_j, *bufs)
            field[pl.ds(ka, 1), :] += rows
            back[way, pl.ds(t, 1), :] = cols

        return 0

    lax.fori_loop(0, (n_row - 1) * slots, step, 0)


def final_kernel(*refs, n_row, n_col):
    refs = list(refs)
    take = lambda n: [refs.pop(0) for _ in range(n)]
    sent, weight, near, row_far = take(4)
    col_far, rows, (own_cols,), messages = take(n_row), take(n_col), take(1), take(n_row - 1)
    out, field = refs
    blocks, nfar = weight.shape[0], own_cols.shape[0]
    my_row, my_col = lax.axis_index("row"), lax.axis_index("col")
    field[...] = near[...]
    for d, message in enumerate(messages):
        for t in range(sent.shape[1] - 1):
            k = sent[jnp.bitwise_xor(my_row, d + 1), t]
            field[pl.ds(k, 1), :] += message[nfar + t : nfar + t + 1, :]

    def hot(index, base):
        want = lax.broadcasted_iota(jnp.int32, (blocks, nfar), 0) + base * blocks
        return jnp.where(index[:, 0:nfar] == want.astype(jnp.float32), 1.0, 0.0)

    pick = [hot(row_far[jnp.bitwise_xor(my_col, d), blocks, 0:1, :], my_col) for d in range(n_col)]
    pick += [hot(col_far[d][blocks, 1:2, :], my_row) for d in range(n_row)]
    far = jnp.dot(
        jnp.concatenate(pick, axis=1),
        jnp.concatenate([r[...] for r in rows] + [own_cols[...]] + [m[0:nfar, :] for m in messages], axis=0),
        precision=HIGH,
        preferred_element_type=jnp.float32,
    )
    total = field[...] + far * weight[...]
    for q in range(BLK // LANES):
        out[pl.ds(q, blocks, stride=BLK // LANES), :] = total[:, q * LANES : (q + 1) * LANES]


def f32(*shape):
    return jax.ShapeDtypeStruct(shape, jnp.float32)


def cost(micros):
    return pl.CostEstimate(flops=int(micros * 1.1e9), bytes_accessed=1 << 16, transcendentals=0)


def body(points, density, near_pairs, far_pairs, near_count, far_count, *, n_row, n_col):
    quad = points.shape[1]
    blocks = points.shape[2] // BLK
    nnear, nfar = near_pairs.shape[0], far_pairs.shape[0]
    depth, slots = 4 * quad, nnear - 1
    near_pairs, far_pairs = near_pairs.T, far_pairs.T

    def row_peers(x):
        xs = x if isinstance(x, (list, tuple)) else [x] * (n_row - 1)
        return [lax.ppermute(x, "row", [(i, i ^ (d + 1)) for i in range(n_row)]) for d, x in enumerate(xs)]

    used = jnp.arange(nnear)[None, :] < near_count[0]
    lists = jnp.where(used, near_pairs, -1)
    lists = [lists] + row_peers(lists)

    far_own, near_own, weight = pl.pallas_call(
        prep_kernel,
        out_shape=(f32(blocks + 1, 4, BLK), f32(blocks, depth + 8, BLK), f32(blocks, BLK)),
        in_specs=[SMEM, VMEM, VMEM],
        out_specs=(VMEM, VMEM, VMEM),
        compiler_params=PARAMS,
        cost_estimate=cost(1.2),
        name="prep",
    )(far_pairs, points, density.reshape(-1, LANES))
    row_far = lax.all_gather(far_own, "col")

    ints = jax.ShapeDtypeStruct((n_row, slots + 1), jnp.int32)
    pack_rows = -(-(slots * depth + slots) // 8) * 8
    *packs, sent, runs = pl.pallas_call(
        functools.partial(pack_kernel, n_row=n_row),
        out_shape=[f32(pack_rows, BLK)] * (n_row - 1) + [ints, ints],
        in_specs=[SMEM] * n_row + [VMEM],
        out_specs=[VMEM] * (n_row - 1) + [SMEM, SMEM],
        scratch_shapes=[
            pltpu.SMEM((n_row, 2 * nnear), jnp.int32),
            pltpu.SMEM((n_row,), jnp.int32),
            pltpu.SMEM((n_row, n_row), jnp.int32),
        ],
        compiler_params=PARAMS,
        cost_estimate=cost(2.0),
        name="pack",
    )(*lists, near_own)
    got = row_peers(packs)
    far_late, _ = lax.optimization_barrier((far_own, packs))
    col_far = [far_own] + row_peers(far_late)

    bufs = [
        pltpu.VMEM((quad * BLK, TERMS), jnp.bfloat16),
        pltpu.VMEM((TERMS, quad * BLK), jnp.bfloat16),
        pltpu.VMEM((BLK, LANES), jnp.float32),
        pltpu.VMEM((8, BLK), jnp.float32),
    ]
    near0 = pl.pallas_call(
        near_own_kernel,
        out_shape=f32(blocks, BLK),
        in_specs=[SMEM, SMEM, VMEM],
        out_specs=VMEM,
        scratch_shapes=bufs,
        compiler_params=PARAMS,
        cost_estimate=cost(5.0),
        name="near_own",
    )(near_pairs, near_count, near_own)

    near1, back = pl.pallas_call(
        functools.partial(near_kernel, n_row=n_row),
        out_shape=(f32(blocks, BLK), f32(n_row - 1, 8, BLK)),
        in_specs=[SMEM, VMEM] + [VMEM] * n_row,
        out_specs=(VMEM, VMEM),
        scratch_shapes=[pltpu.VMEM((depth + 8, BLK), jnp.float32)] + bufs,
        compiler_params=PARAMS,
        cost_estimate=cost(10.0),
        name="near_rest",
    )(runs, near_own, *got, near0)

    far_rows, far_cols, *messages = pl.pallas_call(
        functools.partial(far_kernel, blocks=blocks, n_row=n_row),
        out_shape=[f32(nfar, BLK), f32(nfar, BLK)] + [f32(nfar + 8, BLK)] * (n_row - 1),
        in_specs=[SMEM, SMEM] + [VMEM] * (n_row + 2),
        out_specs=[VMEM] * (n_row + 1),
        scratch_shapes=[
            pltpu.VMEM((4, BLK), jnp.float32),
            pltpu.VMEM((BLK, TERMS), jnp.bfloat16),
            pltpu.VMEM((TERMS, BLK), jnp.bfloat16),
            pltpu.VMEM((BLK, LANES), jnp.float32),
        ],
        compiler_params=PARAMS,
        cost_estimate=cost(4.0),
        name="far",
    )(far_pairs, far_count, back, row_far, *col_far)

    messages = row_peers(messages)
    rows = [far_rows]
    rows += [lax.ppermute(far_rows, "col", [(i, i ^ d) for i in range(n_col)]) for d in range(1, n_col)]
    args = [weight, near1, row_far, *col_far, *rows, far_cols, *messages]
    out = pl.pallas_call(
        functools.partial(final_kernel, n_row=n_row, n_col=n_col),
        out_shape=f32(blocks * BLK // LANES, LANES),
        in_specs=[SMEM] + [VMEM] * len(args),
        out_specs=VMEM,
        scratch_shapes=[pltpu.VMEM((blocks, BLK), jnp.float32)],
        compiler_params=PARAMS,
        name="final",
    )(sent, *args)
    return out.reshape(-1)


def solution(mesh):
    in_specs = (
        P(None, None, ("row", "col")),
        P(("row", "col")),
        P(("row", "col"), None),
        P(("row", "col"), None),
        P(("row", "col")),
        P(("row", "col")),
    )
    out_specs = P(("row", "col"))
    kernel = functools.partial(body, n_row=mesh.shape["row"], n_col=mesh.shape["col"])
    return jax.shard_map(kernel, mesh=mesh, in_specs=in_specs, out_specs=out_specs, check_vma=False)
```

```python
import functools

import jax
import jax.numpy as jnp
from jax import lax
from jax.experimental import pallas as pl
from jax.experimental.pallas import tpu as pltpu
from jax.sharding import PartitionSpec as P

BLK = 512
LANES = 128
SOFT_SQ = 0.0004
TERMS = 64
SPLIT = 48
HALF = 512
GROUP = 16
CHUNK = 128
VMEM = pl.BlockSpec(memory_space=pltpu.VMEM)
SMEM = pl.BlockSpec(memory_space=pltpu.SMEM)
HIGH = lax.Precision.HIGHEST
PARAMS = pltpu.CompilerParams(vmem_limit_bytes=40 * 1024 * 1024)


def prep_kernel(far_ref, near_ref, count, pts_ref, dens_ref, near_msg, far_out, near_out, weight_out):
    blocks = near_out.shape[0]
    quad = pts_ref.shape[1]

    for k in range(blocks):
        cols = slice(k * BLK, (k + 1) * BLK)
        w = pts_ref[3, :, cols]
        total = jnp.sum(w, axis=0, keepdims=True)
        dens = jnp.concatenate([dens_ref[4 * k + q : 4 * k + q + 1, :] for q in range(4)], axis=1)
        lines = []
        for c in range(3):
            x = pts_ref[c, :, cols]
            lines.append(jnp.sum(x * w, axis=0, keepdims=True) / total)
            near_out[k, quad * c : quad * c + quad, :] = x
        near_out[k, quad * 3 : quad * 4, :] = w
        near_out[k, quad * 4 : quad * 4 + 8, :] = jnp.broadcast_to(dens, (8, BLK))
        far_out[k] = jnp.concatenate(lines + [total * dens], axis=0)
        weight_out[k : k + 1, :] = total
    lane = lax.broadcasted_iota(jnp.int32, (4, BLK), 1)
    row = lax.broadcasted_iota(jnp.int32, (4, BLK), 0)
    tags = jnp.full((4, BLK), -1.0, jnp.float32)
    for s in range(far_ref.shape[1]):
        for j in range(2):
            tags = jnp.where((lane == s) & (row == j), far_ref[j, s].astype(jnp.float32), tags)
    far_out[blocks] = tags
    slots, body = near_ref.shape[1] - 1, quad * 4
    line = jnp.full((1, BLK), -1.0, jnp.float32)
    for t in range(slots):
        k = lax.rem(near_ref[0, t + 1], blocks)
        near_msg[t * body : (t + 1) * body, :] = near_out[k, 0:body, :]
        near_msg[slots * body + t : slots * body + t + 1, :] = near_out[k, body : body + 1, :]
        source = jnp.where(t + 1 < count[0], near_ref[1, t + 1], -1)
        line = jnp.where(lane[0:1] == t, source.astype(jnp.float32), line)
    rest = near_msg.shape[0] - slots * (body + 1)
    near_msg[slots * (body + 1) :, :] = jnp.broadcast_to(line, (rest, BLK))


def three(value):
    one = value.astype(jnp.bfloat16).astype(jnp.float32)
    two = (value - one).astype(jnp.bfloat16).astype(jnp.float32)
    return one, two, value - one - two


def pick_row(row, values):
    out = jnp.zeros(row.shape, jnp.float32)
    for k, value in enumerate(values):
        out = jnp.where(row == k, value, out)
    return out


def parts(x):
    row = lax.broadcasted_iota(jnp.int32, x.shape, 0)
    live = row < 3
    centred = jnp.where(live, x - 0.5, 0.0)
    head = jnp.round(centred * 256.0) * (1.0 / 256.0)
    rest = centred - head
    rest1 = rest.astype(jnp.bfloat16).astype(jnp.float32)
    big = pick_row(row, three(jnp.sum(head * head, axis=0, keepdims=True)))
    small = pick_row(row, three(jnp.sum(rest * (2.0 * head + rest), axis=0, keepdims=True) + 0.5 * SOFT_SQ))
    return head, rest1, rest - rest1, big, small, jnp.where(live, 1.0, 0.0)


def left_terms(x, columns):
    head, rest1, rest2, big, small, ones = parts(x)
    h2, a2, b2 = -2.0 * head, -2.0 * rest1, -2.0 * rest2
    groups = [h2, big, ones, small, ones, h2, h2, a2, b2, a2, a2, b2]
    row = lax.broadcasted_iota(jnp.int32, (TERMS - SPLIT, x.shape[1]), 0)
    groups.append(pick_row(row, [part for column in columns for part in three(column)]))
    return jnp.concatenate(groups, axis=0)


def right_terms(x):
    head, rest1, rest2, big, small, ones = parts(x)
    groups = [head, ones, big, ones, small, rest1, rest2, head, head, rest1, rest2, rest1]
    groups.append(jnp.zeros((TERMS - SPLIT, x.shape[1]), jnp.float32))
    return jnp.concatenate(groups, axis=0).astype(jnp.bfloat16)


def column_of(lhs, which):
    row = lax.broadcasted_iota(jnp.int32, (TERMS, LANES), 0) - SPLIT - 3 * which
    pick = jnp.where((row >= 0) & (row < 3), 1.0, 0.0).astype(jnp.bfloat16)
    return jnp.dot(lhs, pick, preferred_element_type=jnp.float32)


def fold_lanes(tile, row):
    part = tile[:, :LANES] * row[:, :LANES]
    for q in range(1, tile.shape[1] // LANES):
        part = part + tile[:, q * LANES : (q + 1) * LANES] * row[:, q * LANES : (q + 1) * LANES]
    return part


def twice(col):
    return jnp.concatenate([col] * (HALF // LANES), axis=1)


def place(x, n):
    bits = n.bit_length() - 1
    return sum(lax.rem(lax.div(x, 1 << (bits - 1 - j)), 2) * (1 << j) for j in range(bits))


def far_kernel(*refs, blocks, n_row, n_col):
    pairs, count, back, row_in = refs[:4]
    col_in = refs[4 : 4 + n_row]
    rows_out, cols_out = refs[4 + n_row : 6 + n_row]
    messages = refs[6 + n_row : 5 + 2 * n_row]
    right_buf, lhs_buf, rhs_buf, part_buf = refs[5 + 2 * n_row :]
    rows_out[...] = jnp.zeros_like(rows_out)
    cols_out[...] = jnp.zeros_like(cols_out)
    my_row, my_col = lax.axis_index("row"), lax.axis_index("col")

    def step(s, _):
        a, b = pairs[0, s], pairs[1, s]
        a_way, b_way = jnp.bitwise_xor(lax.div(a, blocks), my_col), jnp.bitwise_xor(lax.div(b, blocks), my_row)
        ka, kb = lax.rem(a, blocks), lax.rem(b, blocks)
        same = (a_way == 0) & (b_way == 0) & (ka == kb)
        for d in range(n_row):

            @pl.when(b_way == d)
            def _():
                right_buf[...] = col_in[d][kb]

        left, right = row_in[place(a_way, n_col) * (blocks + 1) + ka], right_buf[...]
        lhs_buf[...] = jnp.transpose(left_terms(left, [left[3:4]])).astype(jnp.bfloat16)
        rhs_buf[...] = right_terms(right)
        lhs = lhs_buf[...]
        zcol = column_of(lhs, 0)
        total = []
        for h in range(BLK // HALF):
            cols = slice(h * HALF, (h + 1) * HALF)
            dist = jnp.dot(lhs, rhs_buf[:, cols], preferred_element_type=jnp.float32)
            acc = jnp.zeros((8, HALF), jnp.float32)
            for g in range(BLK // 8):
                rows = slice(g * 8, (g + 1) * 8)
                tile = lax.rsqrt(dist[rows, :])
                part = fold_lanes(tile, right[3:4, cols])
                part_buf[rows, :] = part if h == 0 else part_buf[rows, :] + part
                acc = acc + tile * twice(zcol[rows, :])
            total.append(jnp.sum(acc, axis=0, keepdims=True))
        rows_out[pl.ds(s, 1), :] = jnp.sum(jnp.transpose(part_buf[...]), axis=0, keepdims=True)
        cols_out[pl.ds(s, 1), :] = jnp.concatenate(total, axis=1) * jnp.where(same, 0.0, 1.0)
        return 0

    lax.fori_loop(0, count[0], step, 0)
    nfar = cols_out.shape[0]
    for d, message in enumerate(messages):
        message[0:nfar, :] = cols_out[...]
        message[nfar:, :] = back[d]


def points(tall):
    quad = tall.shape[0] // 4
    sides = [[tall[quad * c + u : quad * c + u + 1, :] for c in range(4)] for u in range(quad)]
    return jnp.concatenate([jnp.concatenate(side, axis=0) for side in sides], axis=1)


def near_tile(left, dens_i, right, dens_j, lhs_buf, rhs_buf, part_buf, acc_buf):
    quad = left.shape[1] // BLK
    terms = jnp.transpose(left_terms(left, [left[3:4], jnp.concatenate([dens_i] * quad, axis=1)]))
    terms = terms.astype(jnp.bfloat16)
    for g in range(BLK // GROUP):
        for u in range(quad):
            to, at = (g * quad + u) * GROUP, u * BLK + g * GROUP
            lhs_buf[to : to + GROUP, :] = terms[at : at + GROUP, :]
    rhs_buf[...] = right_terms(right)
    weights = right[3:4]
    acc_buf[...] = jnp.zeros_like(acc_buf)

    def chunk(i, _):
        at = pl.multiple_of(i * CHUNK * quad, CHUNK * quad)
        lhs = lhs_buf[pl.ds(at, CHUNK * quad), :]
        wcol = column_of(lhs, 0)
        groups = CHUNK // GROUP
        first_rows = [lhs[g * quad * GROUP : g * quad * GROUP + GROUP, :] for g in range(groups)]
        dcol = column_of(jnp.concatenate(first_rows, axis=0), 1)
        part = None
        for h in range(BLK // HALF):
            tiles = [None] * groups
            for v in range(quad):
                cols = slice(v * BLK + h * HALF, v * BLK + (h + 1) * HALF)
                dist = jnp.dot(lhs, rhs_buf[:, cols], preferred_element_type=jnp.float32)
                for g in range(groups):
                    inner = None
                    for u in range(quad):
                        rows = slice((g * quad + u) * GROUP, (g * quad + u + 1) * GROUP)
                        term = lax.rsqrt(dist[rows, :]) * twice(wcol[rows, :])
                        inner = term if inner is None else inner + term
                    inner = inner * weights[:, cols]
                    tiles[g] = inner if tiles[g] is None else tiles[g] + inner
            tile = jnp.concatenate(tiles, axis=0)
            cols = slice(h * HALF, (h + 1) * HALF)
            more = fold_lanes(tile, dens_j[:, cols])
            part = more if part is None else part + more
            acc_buf[:, cols] += jnp.sum((tile * twice(dcol)).reshape(-1, 8, HALF), axis=0)
        part_buf[pl.ds(pl.multiple_of(i * CHUNK, CHUNK), CHUNK), :] = part
        return 0

    lax.fori_loop(0, BLK // CHUNK, chunk, 0)
    rows = jnp.sum(jnp.transpose(part_buf[...]), axis=0, keepdims=True)
    return rows, jnp.sum(acc_buf[...], axis=0, keepdims=True)


def near_own_kernel(pairs, near_ref, rows_out, *bufs):
    blocks, depth, _ = near_ref.shape
    k = lax.rem(pairs[0, 0], blocks)
    pts, dens = points(near_ref[k, 0 : depth - 8, :]), near_ref[k, depth - 8 : depth - 7, :]
    rows_out[...] = jnp.zeros_like(rows_out)
    rows_out[pl.ds(k, 1), :] = near_tile(pts, dens, pts, dens, *bufs)[0]


def near_kernel(*refs, n_row):
    pairs, count, near_ref = refs[:3]
    got = refs[3 : n_row + 2]
    start, field, back, right_buf, tags, sems, *bufs = refs[n_row + 2 :]
    blocks, depth, _ = near_ref.shape
    slots = pairs.shape[1] - 1
    body = depth - 8
    my_row = lax.axis_index("row")
    tail = slice(got[0].shape[0] - 8, got[0].shape[0])
    copies = [pltpu.make_async_copy(g.at[tail, 0:LANES], tags.at[d], sems.at[d]) for d, g in enumerate(got)]
    for copy in copies:
        copy.start()
    field[...] = start[...]
    back[...] = jnp.zeros_like(back)
    for copy in copies:
        copy.wait()

    def step(i, _):
        way, t = lax.div(i, slots), lax.rem(i, slots)
        sent = tags[jnp.maximum(way, 1) - 1, 7, t].astype(jnp.int32)
        own = jnp.where(t + 1 < count[0], pairs[1, t + 1], -1)
        b = jnp.where(way == 0, own, sent)

        @pl.when((b >= my_row * blocks) & (b < (my_row + 1) * blocks))
        def _():
            ka, kb = lax.rem(pairs[0, t + 1], blocks), b - my_row * blocks

            @pl.when(way == 0)
            def _():
                right_buf[...] = near_ref[ka]

            for d in range(n_row - 1):

                @pl.when(way == d + 1)
                def _():
                    at = pl.multiple_of(t * body, 8)
                    right_buf[0:body, :] = got[d][pl.ds(at, body), :]
                    right_buf[body : body + 1, :] = got[d][pl.ds(slots * body + t, 1), :]

            left, right = points(near_ref[kb, 0:body, :]), points(right_buf[0:body, :])
            dens_i, dens_j = near_ref[kb, body : body + 1, :], right_buf[body : body + 1, :]
            rows, cols = near_tile(left, dens_i, right, dens_j, *bufs)
            field[pl.ds(kb, 1), :] += rows

            @pl.when(way == 0)
            def _():
                field[pl.ds(ka, 1), :] += cols * jnp.where(ka == kb, 0.0, 1.0)

            @pl.when(way > 0)
            def _():
                back[way - 1, pl.ds(t, 1), :] = cols

        return 0

    lax.fori_loop(0, n_row * slots, step, 0)


def final_kernel(*refs, n_row, n_col):
    refs = list(refs)
    take = lambda n: [refs.pop(0) for _ in range(n)]
    pairs, weight, near, row_far = take(4)
    col_far, rows, own_cols, messages = take(n_row), *take(2), take(n_row - 1)
    out, field = refs
    blocks, nfar = weight.shape[0], own_cols.shape[0]
    my_row, my_col = lax.axis_index("row"), lax.axis_index("col")
    field[...] = near[...]
    for d, message in enumerate(messages):
        for t in range(pairs.shape[1] - 1):
            k = lax.rem(pairs[0, t + 1], blocks)
            field[pl.ds(k, 1), :] += message[nfar + t : nfar + t + 1, :]

    def hot(index, base):
        want = lax.broadcasted_iota(jnp.int32, (blocks, nfar), 0) + base * blocks
        return jnp.where(index[:, 0:nfar] == want.astype(jnp.float32), 1.0, 0.0)

    pick = [hot(row_far[p * (blocks + 1) + blocks, 0:1, :], my_col) for p in range(n_col)]
    pick += [hot(col_far[d][blocks, 1:2, :], my_row) for d in range(n_row)]
    far = jnp.dot(
        jnp.concatenate(pick, axis=1),
        jnp.concatenate([rows[...], own_cols[...]] + [m[0:nfar, :] for m in messages], axis=0),
        precision=HIGH,
        preferred_element_type=jnp.float32,
    )
    total = field[...] + far * weight[...]
    for q in range(BLK // LANES):
        out[pl.ds(q, blocks, stride=BLK // LANES), :] = total[:, q * LANES : (q + 1) * LANES]


def f32(*shape):
    return jax.ShapeDtypeStruct(shape, jnp.float32)


def cost(micros):
    return pl.CostEstimate(flops=int(micros * 1.1e9), bytes_accessed=1 << 16, transcendentals=0)


def body(points, density, near_pairs, far_pairs, near_count, far_count, *, n_row, n_col):
    quad = points.shape[1]
    blocks = points.shape[2] // BLK
    nnear, nfar = near_pairs.shape[0], far_pairs.shape[0]
    depth, slots = 4 * quad, nnear - 1
    near_pairs, far_pairs = near_pairs.T, far_pairs.T

    def swap(x, axis, d):
        n = {"row": n_row, "col": n_col}[axis]
        return lax.ppermute(x, axis, [(i, i ^ d) for i in range(n)])

    def halves(n):
        return [1 << j for j in reversed(range(n.bit_length() - 1))]

    def row_gather(x):
        known = {0: x}
        for d in halves(n_row):
            known.update({k ^ d: swap(v, "row", d) for k, v in known.items()})
        return [known[k] for k in range(n_row)]

    def col_gather(x):
        for d in halves(n_col):
            x = jnp.concatenate([x, swap(x, "col", d)], axis=0)
        return x

    msg_rows = -(-(slots * (depth + 1) + 1) // 8) * 8
    near_msg, far_own, near_own, weight = pl.pallas_call(
        prep_kernel,
        out_shape=(
            f32(msg_rows, BLK),
            f32(blocks + 1, 4, BLK),
            f32(blocks, depth + 8, BLK),
            f32(blocks, BLK),
        ),
        in_specs=[SMEM, SMEM, SMEM, VMEM, VMEM],
        out_specs=(VMEM, VMEM, VMEM, VMEM),
        compiler_params=PARAMS,
        cost_estimate=cost(1.2),
        name="prep",
    )(far_pairs, near_pairs, near_count, points, density.reshape(-1, LANES))
    got = row_gather(near_msg)[1:]
    row_far = col_gather(far_own)
    col_far = row_gather(far_own)

    bufs = [
        pltpu.VMEM((quad * BLK, TERMS), jnp.bfloat16),
        pltpu.VMEM((TERMS, quad * BLK), jnp.bfloat16),
        pltpu.VMEM((BLK, LANES), jnp.float32),
        pltpu.VMEM((8, BLK), jnp.float32),
    ]
    near0 = pl.pallas_call(
        near_own_kernel,
        out_shape=f32(blocks, BLK),
        in_specs=[SMEM, VMEM],
        out_specs=VMEM,
        scratch_shapes=bufs,
        compiler_params=PARAMS,
        cost_estimate=cost(5.0),
        name="near_own",
    )(near_pairs, near_own)

    near1, back = pl.pallas_call(
        functools.partial(near_kernel, n_row=n_row),
        out_shape=(f32(blocks, BLK), f32(n_row - 1, 8, BLK)),
        in_specs=[SMEM, SMEM, VMEM] + [VMEM] * n_row,
        out_specs=(VMEM, VMEM),
        scratch_shapes=[
            pltpu.VMEM((depth + 8, BLK), jnp.float32),
            pltpu.SMEM((n_row - 1, 8, LANES), jnp.float32),
            pltpu.SemaphoreType.DMA((n_row - 1,)),
        ]
        + bufs,
        compiler_params=PARAMS,
        cost_estimate=cost(10.0),
        name="near_rest",
    )(near_pairs, near_count, near_own, *got, near0)

    far_rows, far_cols, *messages = pl.pallas_call(
        functools.partial(far_kernel, blocks=blocks, n_row=n_row, n_col=n_col),
        out_shape=[f32(nfar, BLK), f32(nfar, BLK)] + [f32(nfar + 8, BLK)] * (n_row - 1),
        in_specs=[SMEM, SMEM] + [VMEM] * (n_row + 2),
        out_specs=[VMEM] * (n_row + 1),
        scratch_shapes=[
            pltpu.VMEM((4, BLK), jnp.float32),
            pltpu.VMEM((BLK, TERMS), jnp.bfloat16),
            pltpu.VMEM((TERMS, BLK), jnp.bfloat16),
            pltpu.VMEM((BLK, LANES), jnp.float32),
        ],
        compiler_params=PARAMS,
        cost_estimate=cost(4.0),
        name="far",
    )(far_pairs, far_count, back, row_far, *col_far)

    messages = [swap(x, "row", d + 1) for d, x in enumerate(messages)]
    args = [weight, near1, row_far, *col_far, col_gather(far_rows), far_cols, *messages]
    out = pl.pallas_call(
        functools.partial(final_kernel, n_row=n_row, n_col=n_col),
        out_shape=f32(blocks * BLK // LANES, LANES),
        in_specs=[SMEM] + [VMEM] * len(args),
        out_specs=VMEM,
        scratch_shapes=[pltpu.VMEM((blocks, BLK), jnp.float32)],
        compiler_params=PARAMS,
        name="final",
    )(near_pairs, *args)
    return out.reshape(-1)


def solution(mesh):
    in_specs = (
        P(None, None, ("row", "col")),
        P(("row", "col")),
        P(("row", "col"), None),
        P(("row", "col"), None),
        P(("row", "col")),
        P(("row", "col")),
    )
    out_specs = P(("row", "col"))
    kernel = functools.partial(body, n_row=mesh.shape["row"], n_col=mesh.shape["col"])
    return jax.shard_map(kernel, mesh=mesh, in_specs=in_specs, out_specs=out_specs, check_vma=False)
```

```python
import functools

import jax
import jax.numpy as jnp
from jax import lax
from jax.experimental import pallas as pl
from jax.experimental.pallas import tpu as pltpu
from jax.sharding import PartitionSpec as P

BLK = 512
LANES = 128
SOFT_SQ = 0.0004
TERMS = 64
SPLIT = 48
HALF = 512
GROUP = 16
CHUNK = 128
FAR_UNIT = 1024
NEAR_LOAD = 7
VMEM = pl.BlockSpec(memory_space=pltpu.VMEM)
SMEM = pl.BlockSpec(memory_space=pltpu.SMEM)
HIGH = lax.Precision.HIGHEST
PARAMS = pltpu.CompilerParams(vmem_limit_bytes=40 * 1024 * 1024)


def prep_kernel(far_ref, pts_ref, dens_ref, far_out, near_out, weight_out):
    blocks = near_out.shape[0]
    quad = pts_ref.shape[1]

    for k in range(blocks):
        cols = slice(k * BLK, (k + 1) * BLK)
        w = pts_ref[3, :, cols]
        total = jnp.sum(w, axis=0, keepdims=True)
        dens = jnp.concatenate([dens_ref[4 * k + q : 4 * k + q + 1, :] for q in range(4)], axis=1)
        lines = []
        for c in range(3):
            x = pts_ref[c, :, cols]
            lines.append(jnp.sum(x * w, axis=0, keepdims=True) / total)
            near_out[k, quad * c : quad * c + quad, :] = x
        near_out[k, quad * 3 : quad * 4, :] = w
        near_out[k, quad * 4 : quad * 4 + 8, :] = jnp.broadcast_to(dens, (8, BLK))
        far_out[k] = jnp.concatenate(lines + [total * dens], axis=0)
        weight_out[k : k + 1, :] = total
    lane = lax.broadcasted_iota(jnp.int32, (4, BLK), 1)
    row = lax.broadcasted_iota(jnp.int32, (4, BLK), 0)
    tags = jnp.full((4, BLK), -1.0, jnp.float32)
    for s in range(far_ref.shape[1]):
        for j in range(2):
            tags = jnp.where((lane == s) & (row == j), far_ref[j, s].astype(jnp.float32), tags)
    far_out[blocks] = tags


def plan_kernel(*refs, n_row):
    lists, near_ref = refs[:n_row], refs[n_row]
    msg, sent, runs, table, load, sends, pending = refs[n_row + 1 :]
    blocks, rows, _ = near_ref.shape
    slots, body = sent.shape[0], rows - 8
    me = lax.axis_index("row")
    for t in range(slots):
        sent[t] = 0
    runs[3, 0] = 0
    for d in range(n_row):
        q = jnp.bitwise_xor(me, d)
        inside, outside = jnp.int32(0), jnp.int32(0)
        for s in range(slots + 1):
            a, b = lists[d][0, s], lists[d][1, s]
            table[q, s] = lax.rem(a, FAR_UNIT)
            table[q, slots + 1 + s] = b
            if s > 0:
                own = (b >= q * blocks) & (b < (q + 1) * blocks)
                inside = inside + jnp.where(own, 1, 0)
                outside = outside + jnp.where((b >= 0) & jnp.logical_not(own), 1, 0)
        load[q] = inside * NEAR_LOAD + lax.div(lists[d][0, 0], FAR_UNIT)
        sends[q] = 0
        pending[q] = outside

    def add_run(own, way, slot):
        i = runs[3, 0]
        runs[0, i] = own
        runs[1, i] = way
        runs[2, i] = slot
        runs[3, 0] = i + 1

    def share(i, _):
        s, q = lax.div(i, n_row) + 1, lax.rem(i, n_row)
        a, b = table[q, s], table[q, slots + 1 + s]
        r = lax.div(jnp.maximum(b, 0), blocks)
        ka, kb = lax.rem(a, blocks), lax.rem(jnp.maximum(b, 0), blocks)

        @pl.when((b >= 0) & (r == q) & (q == me))
        def _():
            add_run(ka, 0, kb)

        @pl.when((b >= 0) & (r != q))
        def _():
            here = (load[q] < load[r]) & (sends[r] + pending[r] < slots)
            run, src = jnp.where(here, q, r), jnp.where(here, r, q)
            pending[q] -= 1
            t = sends[src]
            sends[src] = t + 1
            load[run] += NEAR_LOAD

            @pl.when(src == me)
            def _():
                sent[t] = jnp.where(here, kb, ka)

            @pl.when(run == me)
            def _():
                add_run(jnp.where(here, ka, kb), jnp.bitwise_xor(src, me), t)

        return 0

    lax.fori_loop(0, slots * n_row, share, 0)
    for t in range(slots):
        k = sent[t]
        msg[t * body : (t + 1) * body, :] = near_ref[k, 0:body, :]
        msg[slots * body + t : slots * body + t + 1, :] = near_ref[k, body : body + 1, :]
    rest = msg.shape[0] - slots * (body + 1)
    if rest > 0:
        msg[slots * (body + 1) :, :] = jnp.zeros((rest, BLK), jnp.float32)


def three(value):
    one = value.astype(jnp.bfloat16).astype(jnp.float32)
    two = (value - one).astype(jnp.bfloat16).astype(jnp.float32)
    return one, two, value - one - two


def pick_row(row, values):
    out = jnp.zeros(row.shape, jnp.float32)
    for k, value in enumerate(values):
        out = jnp.where(row == k, value, out)
    return out


def parts(x):
    row = lax.broadcasted_iota(jnp.int32, x.shape, 0)
    live = row < 3
    centred = jnp.where(live, x - 0.5, 0.0)
    head = jnp.round(centred * 256.0) * (1.0 / 256.0)
    rest = centred - head
    rest1 = rest.astype(jnp.bfloat16).astype(jnp.float32)
    big = pick_row(row, three(jnp.sum(head * head, axis=0, keepdims=True)))
    small = pick_row(row, three(jnp.sum(rest * (2.0 * head + rest), axis=0, keepdims=True) + 0.5 * SOFT_SQ))
    return head, rest1, rest - rest1, big, small, jnp.where(live, 1.0, 0.0)


def left_terms(x, columns):
    head, rest1, rest2, big, small, ones = parts(x)
    h2, a2, b2 = -2.0 * head, -2.0 * rest1, -2.0 * rest2
    groups = [h2, big, ones, small, ones, h2, h2, a2, b2, a2, a2, b2]
    row = lax.broadcasted_iota(jnp.int32, (TERMS - SPLIT, x.shape[1]), 0)
    groups.append(pick_row(row, [part for column in columns for part in three(column)]))
    return jnp.concatenate(groups, axis=0)


def right_terms(x):
    head, rest1, rest2, big, small, ones = parts(x)
    groups = [head, ones, big, ones, small, rest1, rest2, head, head, rest1, rest2, rest1]
    groups.append(jnp.zeros((TERMS - SPLIT, x.shape[1]), jnp.float32))
    return jnp.concatenate(groups, axis=0).astype(jnp.bfloat16)


def column_of(lhs, which):
    row = lax.broadcasted_iota(jnp.int32, (TERMS, LANES), 0) - SPLIT - 3 * which
    pick = jnp.where((row >= 0) & (row < 3), 1.0, 0.0).astype(jnp.bfloat16)
    return jnp.dot(lhs, pick, preferred_element_type=jnp.float32)


def fold_lanes(tile, row):
    part = tile[:, :LANES] * row[:, :LANES]
    for q in range(1, tile.shape[1] // LANES):
        part = part + tile[:, q * LANES : (q + 1) * LANES] * row[:, q * LANES : (q + 1) * LANES]
    return part


def twice(col):
    return jnp.concatenate([col] * (HALF // LANES), axis=1)


def place(x, n):
    bits = n.bit_length() - 1
    div, rem = (lambda a, b: a // b, lambda a, b: a % b) if isinstance(x, int) else (lax.div, lax.rem)
    return sum(rem(div(x, 1 << (bits - 1 - j)), 2) * (1 << j) for j in range(bits))


def far_kernel(*refs, blocks, n_row, n_col):
    pairs, count, back, row_in = refs[:4]
    col_in = refs[4 : 4 + n_row]
    rows_out, cols_out = refs[4 + n_row : 6 + n_row]
    messages = refs[6 + n_row : 5 + 2 * n_row]
    right_buf, lhs_buf, rhs_buf, part_buf = refs[5 + 2 * n_row :]
    rows_out[...] = jnp.zeros_like(rows_out)
    cols_out[...] = jnp.zeros_like(cols_out)
    my_row, my_col = lax.axis_index("row"), lax.axis_index("col")

    def step(s, _):
        a, b = pairs[0, s], pairs[1, s]
        a_way, b_way = jnp.bitwise_xor(lax.div(a, blocks), my_col), jnp.bitwise_xor(lax.div(b, blocks), my_row)
        ka, kb = lax.rem(a, blocks), lax.rem(b, blocks)
        same = (a_way == 0) & (b_way == 0) & (ka == kb)
        for d in range(n_row):

            @pl.when(b_way == d)
            def _():
                right_buf[...] = col_in[d][kb]

        left, right = row_in[place(a_way, n_col) * (blocks + 1) + ka], right_buf[...]
        lhs_buf[...] = jnp.transpose(left_terms(left, [left[3:4]])).astype(jnp.bfloat16)
        rhs_buf[...] = right_terms(right)
        lhs = lhs_buf[...]
        zcol = column_of(lhs, 0)
        total = []
        for h in range(BLK // HALF):
            cols = slice(h * HALF, (h + 1) * HALF)
            dist = jnp.dot(lhs, rhs_buf[:, cols], preferred_element_type=jnp.float32)
            acc = jnp.zeros((8, HALF), jnp.float32)
            for g in range(BLK // 8):
                rows = slice(g * 8, (g + 1) * 8)
                tile = lax.rsqrt(dist[rows, :])
                part = fold_lanes(tile, right[3:4, cols])
                part_buf[rows, :] = part if h == 0 else part_buf[rows, :] + part
                acc = acc + tile * twice(zcol[rows, :])
            total.append(jnp.sum(acc, axis=0, keepdims=True))
        rows_out[pl.ds(s, 1), :] = jnp.sum(jnp.transpose(part_buf[...]), axis=0, keepdims=True)
        cols_out[pl.ds(s, 1), :] = jnp.concatenate(total, axis=1) * jnp.where(same, 0.0, 1.0)
        return 0

    lax.fori_loop(0, count[0], step, 0)
    nfar = cols_out.shape[0]
    for d, message in enumerate(messages):
        message[0:nfar, :] = cols_out[...]
        message[nfar:, :] = back[d]


def points(tall):
    quad = tall.shape[0] // 4
    sides = [[tall[quad * c + u : quad * c + u + 1, :] for c in range(4)] for u in range(quad)]
    return jnp.concatenate([jnp.concatenate(side, axis=0) for side in sides], axis=1)


def near_tile(left, dens_i, right, dens_j, lhs_buf, rhs_buf, part_buf, acc_buf):
    quad = left.shape[1] // BLK
    terms = jnp.transpose(left_terms(left, [left[3:4], jnp.concatenate([dens_i] * quad, axis=1)]))
    terms = terms.astype(jnp.bfloat16)
    for g in range(BLK // GROUP):
        for u in range(quad):
            to, at = (g * quad + u) * GROUP, u * BLK + g * GROUP
            lhs_buf[to : to + GROUP, :] = terms[at : at + GROUP, :]
    rhs_buf[...] = right_terms(right)
    weights = right[3:4]
    acc_buf[...] = jnp.zeros_like(acc_buf)

    def chunk(i, _):
        at = pl.multiple_of(i * CHUNK * quad, CHUNK * quad)
        lhs = lhs_buf[pl.ds(at, CHUNK * quad), :]
        wcol = column_of(lhs, 0)
        groups = CHUNK // GROUP
        first_rows = [lhs[g * quad * GROUP : g * quad * GROUP + GROUP, :] for g in range(groups)]
        dcol = column_of(jnp.concatenate(first_rows, axis=0), 1)
        part = None
        for h in range(BLK // HALF):
            tiles = [None] * groups
            for v in range(quad):
                cols = slice(v * BLK + h * HALF, v * BLK + (h + 1) * HALF)
                dist = jnp.dot(lhs, rhs_buf[:, cols], preferred_element_type=jnp.float32)
                for g in range(groups):
                    inner = None
                    for u in range(quad):
                        rows = slice((g * quad + u) * GROUP, (g * quad + u + 1) * GROUP)
                        term = lax.rsqrt(dist[rows, :]) * twice(wcol[rows, :])
                        inner = term if inner is None else inner + term
                    inner = inner * weights[:, cols]
                    tiles[g] = inner if tiles[g] is None else tiles[g] + inner
            tile = jnp.concatenate(tiles, axis=0)
            cols = slice(h * HALF, (h + 1) * HALF)
            more = fold_lanes(tile, dens_j[:, cols])
            part = more if part is None else part + more
            acc_buf[:, cols] += jnp.sum((tile * twice(dcol)).reshape(-1, 8, HALF), axis=0)
        part_buf[pl.ds(pl.multiple_of(i * CHUNK, CHUNK), CHUNK), :] = part
        return 0

    lax.fori_loop(0, BLK // CHUNK, chunk, 0)
    rows = jnp.sum(jnp.transpose(part_buf[...]), axis=0, keepdims=True)
    return rows, jnp.sum(acc_buf[...], axis=0, keepdims=True)


def near_own_kernel(pairs, near_ref, rows_out, *bufs):
    blocks, depth, _ = near_ref.shape
    k = lax.rem(pairs[0, 0], blocks)
    pts, dens = points(near_ref[k, 0 : depth - 8, :]), near_ref[k, depth - 8 : depth - 7, :]
    rows_out[...] = jnp.zeros_like(rows_out)
    rows_out[pl.ds(k, 1), :] = near_tile(pts, dens, pts, dens, *bufs)[0]


def near_kernel(*refs, n_row, slots):
    runs, near_ref = refs[:2]
    got = refs[2 : n_row + 1]
    start, field, back, right_buf, *bufs = refs[n_row + 1 :]
    body = near_ref.shape[1] - 8
    field[...] = start[...]
    back[...] = jnp.zeros_like(back)

    def step(i, _):
        ka, way, t = runs[0, i], runs[1, i], runs[2, i]

        @pl.when(way == 0)
        def _():
            right_buf[...] = near_ref[t]

        for d in range(n_row - 1):

            @pl.when(way == d + 1)
            def _():
                at = pl.multiple_of(t * body, 8)
                right_buf[0:body, :] = got[d][pl.ds(at, body), :]
                right_buf[body : body + 1, :] = got[d][pl.ds(slots * body + t, 1), :]

        left, right = points(near_ref[ka, 0:body, :]), points(right_buf[0:body, :])
        dens_i, dens_j = near_ref[ka, body : body + 1, :], right_buf[body : body + 1, :]
        rows, cols = near_tile(left, dens_i, right, dens_j, *bufs)
        field[pl.ds(ka, 1), :] += rows

        @pl.when(way == 0)
        def _():
            field[pl.ds(t, 1), :] += cols * jnp.where(ka == t, 0.0, 1.0)

        @pl.when(way > 0)
        def _():
            back[way - 1, pl.ds(t, 1), :] = cols

        return 0

    lax.fori_loop(0, runs[3, 0], step, 0)


def final_kernel(*refs, n_row, n_col):
    refs = list(refs)
    take = lambda n: [refs.pop(0) for _ in range(n)]
    sent, weight, near, row_far = take(4)
    col_far, rows, (own_cols,), messages = take(n_row), take(n_col // 2), take(1), take(n_row - 1)
    out, field = refs
    blocks, nfar = weight.shape[0], own_cols.shape[0]
    my_row, my_col = lax.axis_index("row"), lax.axis_index("col")
    field[...] = near[...]
    for d, message in enumerate(messages):
        for t in range(sent.shape[0]):
            field[pl.ds(sent[t], 1), :] += message[nfar + t : nfar + t + 1, :]

    def hot(index, base):
        want = lax.broadcasted_iota(jnp.int32, (blocks, nfar), 0) + base * blocks
        return jnp.where(index[:, 0:nfar] == want.astype(jnp.float32), 1.0, 0.0)

    tags = [place(d, n_col) * (blocks + 1) + blocks for d in range(n_col)]
    pick = [hot(row_far[tag, 0:1, :], my_col) for tag in tags]
    pick += [hot(col_far[d][blocks, 1:2, :], my_row) for d in range(n_row)]
    far = jnp.dot(
        jnp.concatenate(pick, axis=1),
        jnp.concatenate([r[...] for r in rows] + [own_cols[...]] + [m[0:nfar, :] for m in messages], axis=0),
        precision=HIGH,
        preferred_element_type=jnp.float32,
    )
    total = field[...] + far * weight[...]
    for q in range(BLK // LANES):
        out[pl.ds(q, blocks, stride=BLK // LANES), :] = total[:, q * LANES : (q + 1) * LANES]


def f32(*shape):
    return jax.ShapeDtypeStruct(shape, jnp.float32)


def cost(micros):
    return pl.CostEstimate(flops=int(micros * 1.1e9), bytes_accessed=1 << 16, transcendentals=0)


def body(points, density, near_pairs, far_pairs, near_count, far_count, *, n_row, n_col):
    quad = points.shape[1]
    blocks = points.shape[2] // BLK
    nnear, nfar = near_pairs.shape[0], far_pairs.shape[0]
    depth, slots = 4 * quad, nnear - 1
    near_pairs, far_pairs = near_pairs.T, far_pairs.T

    def swap(x, axis, d):
        n = {"row": n_row, "col": n_col}[axis]
        return lax.ppermute(x, axis, [(i, i ^ d) for i in range(n)])

    def halves(n):
        return [1 << j for j in reversed(range(n.bit_length() - 1))]

    def row_gather(x):
        known = {0: x}
        for d in halves(n_row):
            known.update({k ^ d: swap(v, "row", d) for k, v in known.items()})
        return [known[k] for k in range(n_row)]

    def col_gather(x):
        for d in halves(n_col):
            x = jnp.concatenate([x, swap(x, "col", d)], axis=0)
        return x

    line = lax.broadcasted_iota(jnp.int32, near_pairs.shape, 0)
    used = lax.broadcasted_iota(jnp.int32, near_pairs.shape, 1) < near_count[0]
    lists = jnp.where(line == 0, near_pairs + FAR_UNIT * far_count[0], jnp.where(used, near_pairs, -1))
    lists = [lists] + [swap(lists, "row", d) for d in range(1, n_row)]

    far_own, near_own, weight = pl.pallas_call(
        prep_kernel,
        out_shape=(f32(blocks + 1, 4, BLK), f32(blocks, depth + 8, BLK), f32(blocks, BLK)),
        in_specs=[SMEM, VMEM, VMEM],
        out_specs=(VMEM, VMEM, VMEM),
        compiler_params=PARAMS,
        cost_estimate=cost(1.0),
        name="prep",
    )(far_pairs, points, density.reshape(-1, LANES))
    row_far = col_gather(far_own)

    msg_rows = -(-slots * (depth + 1) // 8) * 8
    near_msg, sent, runs = pl.pallas_call(
        functools.partial(plan_kernel, n_row=n_row),
        out_shape=(
            f32(msg_rows, BLK),
            jax.ShapeDtypeStruct((slots,), jnp.int32),
            jax.ShapeDtypeStruct((4, n_row * slots), jnp.int32),
        ),
        in_specs=[SMEM] * n_row + [VMEM],
        out_specs=(VMEM, SMEM, SMEM),
        scratch_shapes=[pltpu.SMEM((n_row, 2 * nnear), jnp.int32)] + [pltpu.SMEM((n_row,), jnp.int32)] * 3,
        compiler_params=PARAMS,
        cost_estimate=cost(1.5),
        name="plan",
    )(*lists, near_own)
    got = row_gather(near_msg)[1:]
    far_late, got = lax.optimization_barrier((far_own, got))
    col_far = [far_own] + [swap(far_late, "row", d) for d in range(1, n_row)]

    bufs = [
        pltpu.VMEM((quad * BLK, TERMS), jnp.bfloat16),
        pltpu.VMEM((TERMS, quad * BLK), jnp.bfloat16),
        pltpu.VMEM((BLK, LANES), jnp.float32),
        pltpu.VMEM((8, BLK), jnp.float32),
    ]
    near0 = pl.pallas_call(
        near_own_kernel,
        out_shape=f32(blocks, BLK),
        in_specs=[SMEM, VMEM],
        out_specs=VMEM,
        scratch_shapes=bufs,
        compiler_params=PARAMS,
        cost_estimate=cost(5.0),
        name="near_own",
    )(near_pairs, near_own)

    near1, back = pl.pallas_call(
        functools.partial(near_kernel, n_row=n_row, slots=slots),
        out_shape=(f32(blocks, BLK), f32(n_row - 1, 8, BLK)),
        in_specs=[SMEM, VMEM] + [VMEM] * n_row,
        out_specs=(VMEM, VMEM),
        scratch_shapes=[pltpu.VMEM((depth + 8, BLK), jnp.float32)] + bufs,
        compiler_params=PARAMS,
        cost_estimate=cost(10.0),
        name="near_rest",
    )(runs, near_own, *got, near0)

    far_rows, far_cols, *messages = pl.pallas_call(
        functools.partial(far_kernel, blocks=blocks, n_row=n_row, n_col=n_col),
        out_shape=[f32(nfar, BLK), f32(nfar, BLK)] + [f32(nfar + 8, BLK)] * (n_row - 1),
        in_specs=[SMEM, SMEM] + [VMEM] * (n_row + 2),
        out_specs=[VMEM] * (n_row + 1),
        scratch_shapes=[
            pltpu.VMEM((4, BLK), jnp.float32),
            pltpu.VMEM((BLK, TERMS), jnp.bfloat16),
            pltpu.VMEM((TERMS, BLK), jnp.bfloat16),
            pltpu.VMEM((BLK, LANES), jnp.float32),
        ],
        compiler_params=PARAMS,
        cost_estimate=cost(4.0),
        name="far",
    )(far_pairs, far_count, back, row_far, *col_far)

    messages = [swap(x, "row", d + 1) for d, x in enumerate(messages)]
    both = jnp.concatenate([far_rows, swap(far_rows, "col", 1)], axis=0)
    rows = [both] + [swap(both, "col", d) for d in range(2, n_col, 2)]
    args = [weight, near1, row_far, *col_far, *rows, far_cols, *messages]
    out = pl.pallas_call(
        functools.partial(final_kernel, n_row=n_row, n_col=n_col),
        out_shape=f32(blocks * BLK // LANES, LANES),
        in_specs=[SMEM] + [VMEM] * len(args),
        out_specs=VMEM,
        scratch_shapes=[pltpu.VMEM((blocks, BLK), jnp.float32)],
        compiler_params=PARAMS,
        name="final",
    )(sent, *args)
    return out.reshape(-1)


def solution(mesh):
    in_specs = (
        P(None, None, ("row", "col")),
        P(("row", "col")),
        P(("row", "col"), None),
        P(("row", "col"), None),
        P(("row", "col")),
        P(("row", "col")),
    )
    out_specs = P(("row", "col"))
    kernel = functools.partial(body, n_row=mesh.shape["row"], n_col=mesh.shape["col"])
    return jax.shard_map(kernel, mesh=mesh, in_specs=in_specs, out_specs=out_specs, check_vma=False)
```

```python
import functools

import jax
import jax.numpy as jnp
from jax import lax
from jax.experimental import pallas as pl
from jax.experimental.pallas import tpu as pltpu
from jax.sharding import PartitionSpec as P

BLK = 512
LANES = 128
SOFT_SQ = 0.0004
TERMS = 64
SPLIT = 48
HALF = 512
GROUP = 16
CHUNK = 128
QUARTERS = 4
FAR_UNIT = 1024
NEAR_LOAD = 7
VMEM = pl.BlockSpec(memory_space=pltpu.VMEM)
SMEM = pl.BlockSpec(memory_space=pltpu.SMEM)
ANY = pl.BlockSpec(memory_space=pl.ANY)
HBM = pl.BlockSpec(memory_space=pltpu.HBM)
HIGH = lax.Precision.HIGHEST
PARAMS = pltpu.CompilerParams(vmem_limit_bytes=40 * 1024 * 1024)


def prep_kernel(pairs_hbm, pts_hbm, dens_hbm, far_out, near_out, weight_out, pairs, pts_ref, dens_ref, sems):
    blocks = near_out.shape[0]
    quad = pts_ref.shape[1]
    width = pts_ref.shape[2] // QUARTERS
    copies = [
        pltpu.make_async_copy(dens_hbm, dens_ref, sems.at[QUARTERS]),
        pltpu.make_async_copy(pairs_hbm, pairs, sems.at[QUARTERS + 1]),
    ]
    for i in range(QUARTERS):
        part = slice(i * width, (i + 1) * width)
        copies.append(pltpu.make_async_copy(pts_hbm.at[:, :, part], pts_ref.at[:, :, part], sems.at[i]))
    for copy in copies:
        copy.start()
    copies.pop(0).wait()
    copies.pop(0).wait()
    for k in range(blocks):
        cols = slice(k * BLK, (k + 1) * BLK)
        if k % (blocks // QUARTERS) == 0:
            copies.pop(0).wait()
        w = pts_ref[3, :, cols]
        total = jnp.sum(w, axis=0, keepdims=True)
        dens = jnp.concatenate([dens_ref[4 * k + q : 4 * k + q + 1, :] for q in range(4)], axis=1)
        lines = []
        for c in range(3):
            x = pts_ref[c, :, cols]
            lines.append(jnp.sum(x * w, axis=0, keepdims=True) / total)
            near_out[k, quad * c : quad * c + quad, :] = x
        near_out[k, quad * 3 : quad * 4, :] = w
        near_out[k, quad * 4 : quad * 4 + 8, :] = jnp.broadcast_to(dens, (8, BLK))
        far_out[k] = jnp.concatenate(lines + [total * dens], axis=0)
        weight_out[k : k + 1, :] = total
    far_out[blocks] = jnp.full((4, BLK), -1.0, jnp.float32)
    far_out[blocks, 0:2, 0 : pairs.shape[1]] = pairs[...].astype(jnp.float32)


def plan_kernel(*refs, n_row):
    lists, near_ref = refs[:n_row], refs[n_row]
    msg, sent, runs, table, load, sends, pending = refs[n_row + 1 :]
    blocks, rows, _ = near_ref.shape
    slots, body = sent.shape[0], rows - 8
    me = lax.axis_index("row")
    for t in range(slots):
        sent[t] = 0
    runs[3, 0] = 0
    for d in range(n_row):
        q = jnp.bitwise_xor(me, d)
        inside, outside = jnp.int32(0), jnp.int32(0)
        for s in range(slots + 1):
            a, b = lists[d][0, s], lists[d][1, s]
            table[q, s] = lax.rem(a, FAR_UNIT)
            table[q, slots + 1 + s] = b
            if s > 0:
                own = (b >= q * blocks) & (b < (q + 1) * blocks)
                inside = inside + jnp.where(own, 1, 0)
                outside = outside + jnp.where((b >= 0) & jnp.logical_not(own), 1, 0)
        load[q] = inside * NEAR_LOAD + lax.div(lists[d][0, 0], FAR_UNIT)
        sends[q] = 0
        pending[q] = outside

    def add_run(own, way, slot):
        i = runs[3, 0]
        runs[0, i] = own
        runs[1, i] = way
        runs[2, i] = slot
        runs[3, 0] = i + 1

    def share(i, _):
        s, q = lax.div(i, n_row) + 1, lax.rem(i, n_row)
        a, b = table[q, s], table[q, slots + 1 + s]
        r = lax.div(jnp.maximum(b, 0), blocks)
        ka, kb = lax.rem(a, blocks), lax.rem(jnp.maximum(b, 0), blocks)

        @pl.when((b >= 0) & (r == q) & (q == me))
        def _():
            add_run(ka, 0, kb)

        @pl.when((b >= 0) & (r != q))
        def _():
            here = (load[q] < load[r]) & (sends[r] + pending[r] < slots)
            run, src = jnp.where(here, q, r), jnp.where(here, r, q)
            pending[q] -= 1
            t = sends[src]
            sends[src] = t + 1
            load[run] += NEAR_LOAD

            @pl.when(src == me)
            def _():
                sent[t] = jnp.where(here, kb, ka)

            @pl.when(run == me)
            def _():
                add_run(jnp.where(here, ka, kb), jnp.bitwise_xor(src, me), t)

        return 0

    lax.fori_loop(0, slots * n_row, share, 0)
    for t in range(slots):
        k = sent[t]
        msg[t * body : (t + 1) * body, :] = near_ref[k, 0:body, :]
        msg[slots * body + t : slots * body + t + 1, :] = near_ref[k, body : body + 1, :]
    rest = msg.shape[0] - slots * (body + 1)
    if rest > 0:
        msg[slots * (body + 1) :, :] = jnp.zeros((rest, BLK), jnp.float32)


def three(value):
    one = value.astype(jnp.bfloat16).astype(jnp.float32)
    two = (value - one).astype(jnp.bfloat16).astype(jnp.float32)
    return one, two, value - one - two


def pick_row(row, values):
    out = jnp.zeros(row.shape, jnp.float32)
    for k, value in enumerate(values):
        out = jnp.where(row == k, value, out)
    return out


def parts(x):
    row = lax.broadcasted_iota(jnp.int32, x.shape, 0)
    live = row < 3
    centred = jnp.where(live, x - 0.5, 0.0)
    head = jnp.round(centred * 256.0) * (1.0 / 256.0)
    rest = centred - head
    rest1 = rest.astype(jnp.bfloat16).astype(jnp.float32)
    big = pick_row(row, three(jnp.sum(head * head, axis=0, keepdims=True)))
    small = pick_row(row, three(jnp.sum(rest * (2.0 * head + rest), axis=0, keepdims=True) + 0.5 * SOFT_SQ))
    return head, rest1, rest - rest1, big, small, jnp.where(live, 1.0, 0.0)


def left_terms(x, columns):
    head, rest1, rest2, big, small, ones = parts(x)
    h2, a2, b2 = -2.0 * head, -2.0 * rest1, -2.0 * rest2
    groups = [h2, big, ones, small, ones, h2, h2, a2, b2, a2, a2, b2]
    row = lax.broadcasted_iota(jnp.int32, (TERMS - SPLIT, x.shape[1]), 0)
    groups.append(pick_row(row, [part for column in columns for part in three(column)]))
    return jnp.concatenate(groups, axis=0)


def right_terms(x):
    head, rest1, rest2, big, small, ones = parts(x)
    groups = [head, ones, big, ones, small, rest1, rest2, head, head, rest1, rest2, rest1]
    groups.append(jnp.zeros((TERMS - SPLIT, x.shape[1]), jnp.float32))
    return jnp.concatenate(groups, axis=0).astype(jnp.bfloat16)


def column_of(lhs, which):
    row = lax.broadcasted_iota(jnp.int32, (TERMS, LANES), 0) - SPLIT - 3 * which
    pick = jnp.where((row >= 0) & (row < 3), 1.0, 0.0).astype(jnp.bfloat16)
    return jnp.dot(lhs, pick, preferred_element_type=jnp.float32)


def fold_lanes(tile, row):
    part = tile[:, :LANES] * row[:, :LANES]
    for q in range(1, tile.shape[1] // LANES):
        part = part + tile[:, q * LANES : (q + 1) * LANES] * row[:, q * LANES : (q + 1) * LANES]
    return part


def twice(col):
    return jnp.concatenate([col] * (HALF // LANES), axis=1)


def place(x, n):
    bits = n.bit_length() - 1
    div, rem = (lambda a, b: a // b, lambda a, b: a % b) if isinstance(x, int) else (lax.div, lax.rem)
    return sum(rem(div(x, 1 << (bits - 1 - j)), 2) * (1 << j) for j in range(bits))


def far_kernel(*refs, blocks, n_row, n_col):
    pairs, count, _, row_in = refs[:4]
    col_in = refs[4 : 4 + n_row]
    rows_out, cols_out, right_buf, lhs_buf, rhs_buf, part_buf = refs[4 + n_row :]
    rows_out[...] = jnp.zeros_like(rows_out)
    cols_out[...] = jnp.zeros_like(cols_out)
    my_row, my_col = lax.axis_index("row"), lax.axis_index("col")

    def step(s, _):
        a, b = pairs[0, s], pairs[1, s]
        a_way, b_way = jnp.bitwise_xor(lax.div(a, blocks), my_col), jnp.bitwise_xor(lax.div(b, blocks), my_row)
        ka, kb = lax.rem(a, blocks), lax.rem(b, blocks)
        same = (a_way == 0) & (b_way == 0) & (ka == kb)
        for d in range(n_row):

            @pl.when(b_way == d)
            def _():
                right_buf[...] = col_in[d][kb]

        left, right = row_in[place(a_way, n_col) * (blocks + 1) + ka], right_buf[...]
        lhs_buf[...] = jnp.transpose(left_terms(left, [left[3:4]])).astype(jnp.bfloat16)
        rhs_buf[...] = right_terms(right)
        lhs = lhs_buf[...]
        zcol = column_of(lhs, 0)
        total = []
        for h in range(BLK // HALF):
            cols = slice(h * HALF, (h + 1) * HALF)
            dist = jnp.dot(lhs, rhs_buf[:, cols], preferred_element_type=jnp.float32)
            acc = jnp.zeros((8, HALF), jnp.float32)
            for g in range(BLK // 8):
                rows = slice(g * 8, (g + 1) * 8)
                tile = lax.rsqrt(dist[rows, :])
                part = fold_lanes(tile, right[3:4, cols])
                part_buf[rows, :] = part if h == 0 else part_buf[rows, :] + part
                acc = acc + tile * twice(zcol[rows, :])
            total.append(jnp.sum(acc, axis=0, keepdims=True))
        rows_out[pl.ds(s, 1), :] = jnp.sum(jnp.transpose(part_buf[...]), axis=0, keepdims=True)
        cols_out[pl.ds(s, 1), :] = jnp.concatenate(total, axis=1) * jnp.where(same, 0.0, 1.0)
        return 0

    lax.fori_loop(0, count[0], step, 0)


def points(tall):
    quad = tall.shape[0] // 4
    sides = [[tall[quad * c + u : quad * c + u + 1, :] for c in range(4)] for u in range(quad)]
    return jnp.concatenate([jnp.concatenate(side, axis=0) for side in sides], axis=1)


def near_tile(left, dens_i, right, dens_j, lhs_buf, rhs_buf, part_buf, acc_buf):
    quad = left.shape[1] // BLK
    terms = jnp.transpose(left_terms(left, [left[3:4], jnp.concatenate([dens_i] * quad, axis=1)]))
    terms = terms.astype(jnp.bfloat16)
    for g in range(BLK // GROUP):
        for u in range(quad):
            to, at = (g * quad + u) * GROUP, u * BLK + g * GROUP
            lhs_buf[to : to + GROUP, :] = terms[at : at + GROUP, :]
    rhs_buf[...] = right_terms(right)
    weights = right[3:4]
    acc_buf[...] = jnp.zeros_like(acc_buf)

    def chunk(i, _):
        at = pl.multiple_of(i * CHUNK * quad, CHUNK * quad)
        lhs = lhs_buf[pl.ds(at, CHUNK * quad), :]
        wcol = column_of(lhs, 0)
        groups = CHUNK // GROUP
        first_rows = [lhs[g * quad * GROUP : g * quad * GROUP + GROUP, :] for g in range(groups)]
        dcol = column_of(jnp.concatenate(first_rows, axis=0), 1)
        part = None
        for h in range(BLK // HALF):
            tiles = [None] * groups
            for v in range(quad):
                cols = slice(v * BLK + h * HALF, v * BLK + (h + 1) * HALF)
                dist = jnp.dot(lhs, rhs_buf[:, cols], preferred_element_type=jnp.float32)
                for g in range(groups):
                    inner = None
                    for u in range(quad):
                        rows = slice((g * quad + u) * GROUP, (g * quad + u + 1) * GROUP)
                        term = lax.rsqrt(dist[rows, :]) * twice(wcol[rows, :])
                        inner = term if inner is None else inner + term
                    inner = inner * weights[:, cols]
                    tiles[g] = inner if tiles[g] is None else tiles[g] + inner
            tile = jnp.concatenate(tiles, axis=0)
            cols = slice(h * HALF, (h + 1) * HALF)
            more = fold_lanes(tile, dens_j[:, cols])
            part = more if part is None else part + more
            acc_buf[:, cols] += jnp.sum((tile * twice(dcol)).reshape(-1, 8, HALF), axis=0)
        part_buf[pl.ds(pl.multiple_of(i * CHUNK, CHUNK), CHUNK), :] = part
        return 0

    lax.fori_loop(0, BLK // CHUNK, chunk, 0)
    rows = jnp.sum(jnp.transpose(part_buf[...]), axis=0, keepdims=True)
    return rows, jnp.sum(acc_buf[...], axis=0, keepdims=True)


def near_own_kernel(pairs, near_ref, rows_out, *bufs):
    blocks, depth, _ = near_ref.shape
    k = lax.rem(pairs[0, 0], blocks)
    pts, dens = points(near_ref[k, 0 : depth - 8, :]), near_ref[k, depth - 8 : depth - 7, :]
    rows_out[...] = jnp.zeros_like(rows_out)
    rows_out[pl.ds(k, 1), :] = near_tile(pts, dens, pts, dens, *bufs)[0]


def near_kernel(*refs, n_row, slots):
    runs, near_ref = refs[:2]
    got = refs[2 : n_row + 1]
    start, far_cols = refs[n_row + 1 : n_row + 3]
    field, *messages = refs[-n_row - 5 : -5]
    right_buf, *bufs = refs[-5:]
    body = near_ref.shape[1] - 8
    nfar = far_cols.shape[0]
    field[...] = start[...]
    for message in messages:
        message[0:nfar, :] = far_cols[...]
        message[nfar:, :] = jnp.zeros((8, BLK), jnp.float32)

    def step(i, _):
        ka, way, t = runs[0, i], runs[1, i], runs[2, i]

        @pl.when(way == 0)
        def _():
            right_buf[...] = near_ref[t]

        for d in range(n_row - 1):

            @pl.when(way == d + 1)
            def _():
                at = pl.multiple_of(t * body, 8)
                right_buf[0:body, :] = got[d][pl.ds(at, body), :]
                right_buf[body : body + 1, :] = got[d][pl.ds(slots * body + t, 1), :]

        left, right = points(near_ref[ka, 0:body, :]), points(right_buf[0:body, :])
        dens_i, dens_j = near_ref[ka, body : body + 1, :], right_buf[body : body + 1, :]
        rows, cols = near_tile(left, dens_i, right, dens_j, *bufs)
        field[pl.ds(ka, 1), :] += rows

        @pl.when(way == 0)
        def _():
            field[pl.ds(t, 1), :] += cols * jnp.where(ka == t, 0.0, 1.0)

        for d, message in enumerate(messages):

            @pl.when(way == d + 1)
            def _():
                message[pl.ds(nfar + t, 1), :] = cols

        return 0

    lax.fori_loop(0, runs[3, 0], step, 0)


def final_kernel(*refs, n_row, n_col):
    refs = list(refs)
    take = lambda n: [refs.pop(0) for _ in range(n)]
    sent, weight, near, row_far = take(4)
    col_far, rows, (own_cols,), messages = take(n_row), take(n_col // 2), take(1), take(n_row - 1)
    out, field = refs
    blocks, nfar = weight.shape[0], own_cols.shape[0]
    my_row, my_col = lax.axis_index("row"), lax.axis_index("col")
    field[...] = near[...]
    for d, message in enumerate(messages):
        for t in range(sent.shape[0]):
            field[pl.ds(sent[t], 1), :] += message[nfar + t : nfar + t + 1, :]

    def hot(index, base):
        want = lax.broadcasted_iota(jnp.int32, (blocks, nfar), 0) + base * blocks
        return jnp.where(index[:, 0:nfar] == want.astype(jnp.float32), 1.0, 0.0)

    tags = [place(d, n_col) * (blocks + 1) + blocks for d in range(n_col)]
    pick = [hot(row_far[tag, 0:1, :], my_col) for tag in tags]
    pick += [hot(col_far[d][blocks, 1:2, :], my_row) for d in range(n_row)]
    far = jnp.dot(
        jnp.concatenate(pick, axis=1),
        jnp.concatenate([r[...] for r in rows] + [own_cols[...]] + [m[0:nfar, :] for m in messages], axis=0),
        precision=HIGH,
        preferred_element_type=jnp.float32,
    )
    total = field[...] + far * weight[...]
    for q in range(BLK // LANES):
        out[pl.ds(q, blocks, stride=BLK // LANES), :] = total[:, q * LANES : (q + 1) * LANES]


def f32(*shape):
    return jax.ShapeDtypeStruct(shape, jnp.float32)


def cost(micros):
    return pl.CostEstimate(flops=int(micros * 1.1e9), bytes_accessed=1 << 16, transcendentals=0)


def body(points, density, near_pairs, far_pairs, near_count, far_count, *, n_row, n_col):
    quad = points.shape[1]
    blocks = points.shape[2] // BLK
    nnear, nfar = near_pairs.shape[0], far_pairs.shape[0]
    depth, slots = 4 * quad, nnear - 1
    near_pairs, far_pairs = near_pairs.T, far_pairs.T

    def swap(x, axis, d):
        n = {"row": n_row, "col": n_col}[axis]
        return lax.ppermute(x, axis, [(i, i ^ d) for i in range(n)])

    def halves(n):
        return [1 << j for j in reversed(range(n.bit_length() - 1))]

    def row_gather(x):
        known = {0: x}
        for d in halves(n_row):
            known.update({k ^ d: swap(v, "row", d) for k, v in known.items()})
        return [known[k] for k in range(n_row)]

    def col_gather(x):
        for d in halves(n_col):
            x = jnp.concatenate([x, swap(x, "col", d)], axis=0)
        return x

    line = lax.broadcasted_iota(jnp.int32, near_pairs.shape, 0)
    used = lax.broadcasted_iota(jnp.int32, near_pairs.shape, 1) < near_count[0]
    lists = jnp.where(line == 0, near_pairs + FAR_UNIT * far_count[0], jnp.where(used, near_pairs, -1))
    lists = [lists] + [swap(lists, "row", d) for d in range(1, n_row)]

    far_own, near_own, weight = pl.pallas_call(
        prep_kernel,
        out_shape=(f32(blocks + 1, 4, BLK), f32(blocks, depth + 8, BLK), f32(blocks, BLK)),
        in_specs=[HBM, HBM, HBM],
        out_specs=(VMEM, VMEM, VMEM),
        scratch_shapes=[
            pltpu.VMEM(far_pairs.shape, jnp.int32),
            pltpu.VMEM(points.shape, jnp.float32),
            pltpu.VMEM((density.shape[0] // LANES, LANES), jnp.float32),
            pltpu.SemaphoreType.DMA((QUARTERS + 2,)),
        ],
        compiler_params=PARAMS,
        cost_estimate=cost(1.0),
        name="prep",
    )(*[pltpu.with_memory_space_constraint(x, pltpu.HBM) for x in (far_pairs, points, density.reshape(-1, LANES))])
    row_far = col_gather(far_own)
    col_far = row_gather(far_own)

    msg_rows = -(-slots * (depth + 1) // 8) * 8
    near_msg, sent, runs = pl.pallas_call(
        functools.partial(plan_kernel, n_row=n_row),
        out_shape=(
            f32(msg_rows, BLK),
            jax.ShapeDtypeStruct((slots,), jnp.int32),
            jax.ShapeDtypeStruct((4, n_row * slots), jnp.int32),
        ),
        in_specs=[SMEM] * n_row + [VMEM],
        out_specs=(VMEM, SMEM, SMEM),
        scratch_shapes=[pltpu.SMEM((n_row, 2 * nnear), jnp.int32)] + [pltpu.SMEM((n_row,), jnp.int32)] * 3,
        compiler_params=PARAMS,
        cost_estimate=cost(1.5),
        name="plan",
    )(*lists, near_own)
    got = row_gather(near_msg)[1:]

    bufs = [
        pltpu.VMEM((quad * BLK, TERMS), jnp.bfloat16),
        pltpu.VMEM((TERMS, quad * BLK), jnp.bfloat16),
        pltpu.VMEM((BLK, LANES), jnp.float32),
        pltpu.VMEM((8, BLK), jnp.float32),
    ]
    near0 = pl.pallas_call(
        near_own_kernel,
        out_shape=f32(blocks, BLK),
        in_specs=[SMEM, VMEM],
        out_specs=VMEM,
        scratch_shapes=bufs,
        compiler_params=PARAMS,
        cost_estimate=cost(1.0),
        name="near_own",
    )(near_pairs, near_own)

    far_rows, far_cols = pl.pallas_call(
        functools.partial(far_kernel, blocks=blocks, n_row=n_row, n_col=n_col),
        out_shape=[f32(nfar, BLK), f32(nfar, BLK)],
        in_specs=[SMEM, SMEM, ANY] + [VMEM] * (n_row + 1),
        out_specs=[VMEM, VMEM],
        scratch_shapes=[
            pltpu.VMEM((4, BLK), jnp.float32),
            pltpu.VMEM((BLK, TERMS), jnp.bfloat16),
            pltpu.VMEM((TERMS, BLK), jnp.bfloat16),
            pltpu.VMEM((BLK, LANES), jnp.float32),
        ],
        compiler_params=PARAMS,
        cost_estimate=cost(4.0),
        name="far",
    )(far_pairs, far_count, near0, row_far, *col_far)
    both = jnp.concatenate([far_rows, swap(far_rows, "col", 1)], axis=0)
    rows = [both] + [swap(both, "col", d) for d in range(2, n_col, 2)]

    near1, *messages = pl.pallas_call(
        functools.partial(near_kernel, n_row=n_row, slots=slots),
        out_shape=[f32(blocks, BLK)] + [f32(nfar + 8, BLK)] * (n_row - 1),
        in_specs=[SMEM] + [VMEM] * (n_row + 2) + [ANY] * len(rows),
        out_specs=[VMEM] * n_row,
        scratch_shapes=[pltpu.VMEM((depth + 8, BLK), jnp.float32)] + bufs,
        compiler_params=PARAMS,
        cost_estimate=cost(10.0),
        name="near_rest",
    )(runs, near_own, *got, near0, far_cols, *rows)

    messages = [swap(x, "row", d + 1) for d, x in enumerate(messages)]
    args = [weight, near1, row_far, *col_far, *rows, far_cols, *messages]
    out = pl.pallas_call(
        functools.partial(final_kernel, n_row=n_row, n_col=n_col),
        out_shape=f32(blocks * BLK // LANES, LANES),
        in_specs=[SMEM] + [VMEM] * len(args),
        out_specs=VMEM,
        scratch_shapes=[pltpu.VMEM((blocks, BLK), jnp.float32)],
        compiler_params=PARAMS,
        name="final",
    )(sent, *args)
    return out.reshape(-1)


def solution(mesh):
    in_specs = (
        P(None, None, ("row", "col")),
        P(("row", "col")),
        P(("row", "col"), None),
        P(("row", "col"), None),
        P(("row", "col")),
        P(("row", "col")),
    )
    out_specs = P(("row", "col"))
    kernel = functools.partial(body, n_row=mesh.shape["row"], n_col=mesh.shape["col"])
    return jax.shard_map(kernel, mesh=mesh, in_specs=in_specs, out_specs=out_specs, check_vma=False)
```

```python
import functools

import jax
import jax.numpy as jnp
from jax import lax
from jax.experimental import pallas as pl
from jax.experimental.pallas import tpu as pltpu
from jax.sharding import PartitionSpec as P

BLK = 512
LANES = 128
SOFT_SQ = 0.0004
TERMS = 64
SPLIT = 48
HALF = 512
QUARTERS = 4
GROUP = 16
CHUNK = 512
VMEM = pl.BlockSpec(memory_space=pltpu.VMEM)
SMEM = pl.BlockSpec(memory_space=pltpu.SMEM)
ANY = pl.BlockSpec(memory_space=pl.ANY)
HBM = pl.BlockSpec(memory_space=pltpu.HBM)
HIGH = lax.Precision.HIGHEST
PARAMS = pltpu.CompilerParams(vmem_limit_bytes=40 * 1024 * 1024)


def prep_kernel(near_ref, count, far_hbm, pts_hbm, dens_hbm, msg, far_out, near_out, weight_out, *scratch):
    far_ref, pts_ref, dens_ref, sems = scratch
    blocks = near_out.shape[0]
    quad = pts_ref.shape[1]
    slots, body = near_ref.shape[1] - 1, quad * 4
    base = near_lines(slots, quad)
    width = pts_ref.shape[2] // QUARTERS
    copies = [
        pltpu.make_async_copy(dens_hbm, dens_ref, sems.at[QUARTERS]),
        pltpu.make_async_copy(far_hbm, far_ref, sems.at[QUARTERS + 1]),
    ]
    for i in range(QUARTERS):
        part = slice(i * width, (i + 1) * width)
        copies.append(pltpu.make_async_copy(pts_hbm.at[:, :, part], pts_ref.at[:, :, part], sems.at[i]))
    for copy in copies:
        copy.start()
    copies.pop(0).wait()
    copies.pop(0).wait()

    def put_far(k, value):
        far_out[k] = value
        msg[base + 4 * k : base + 4 * k + 4, :] = value

    for k in range(blocks):
        cols = slice(k * BLK, (k + 1) * BLK)
        if k % (blocks // QUARTERS) == 0:
            copies.pop(0).wait()
        w = pts_ref[3, :, cols]
        total = jnp.sum(w, axis=0, keepdims=True)
        dens = jnp.concatenate([dens_ref[4 * k + q : 4 * k + q + 1, :] for q in range(4)], axis=1)
        lines = []
        for c in range(3):
            x = pts_ref[c, :, cols]
            lines.append(jnp.sum(x * w, axis=0, keepdims=True) / total)
            near_out[k, quad * c : quad * c + quad, :] = x
        near_out[k, quad * 3 : quad * 4, :] = w
        near_out[k, quad * 4 : quad * 4 + 8, :] = jnp.broadcast_to(dens, (8, BLK))
        put_far(k, jnp.concatenate(lines + [total * dens], axis=0))
        weight_out[k : k + 1, :] = total
    pairs = jnp.concatenate([far_ref[...].astype(jnp.float32), jnp.full((2, LANES - far_ref.shape[1]), -1.0)], axis=1)
    pairs = jnp.concatenate([pairs] * (BLK // LANES), axis=1)
    put_far(blocks, jnp.concatenate([pairs, jnp.zeros((2, BLK), jnp.float32)], axis=0))
    lane = lax.broadcasted_iota(jnp.int32, (1, BLK), 1)
    line = jnp.full((1, BLK), -1.0, jnp.float32)
    for t in range(slots):
        k = lax.rem(near_ref[0, t + 1], blocks)
        msg[t * body : (t + 1) * body, :] = near_out[k, 0:body, :]
        msg[slots * body + t : slots * body + t + 1, :] = near_out[k, body : body + 1, :]
        source = jnp.where(t + 1 < count[0], near_ref[1, t + 1], -1)
        line = jnp.where(lane == t, source.astype(jnp.float32), line)
    first = slots * (body + 1)
    msg[first:base, :] = jnp.broadcast_to(line, (base - first, BLK))


def near_lines(slots, quad):
    return -(-(slots * (4 * quad + 1) + 1) // 8) * 8


def three(value):
    one = value.astype(jnp.bfloat16).astype(jnp.float32)
    two = (value - one).astype(jnp.bfloat16).astype(jnp.float32)
    return one, two, value - one - two


def pick_row(row, values):
    out = jnp.zeros(row.shape, jnp.float32)
    for k, value in enumerate(values):
        out = jnp.where(row == k, value, out)
    return out


def parts(x):
    row = lax.broadcasted_iota(jnp.int32, x.shape, 0)
    live = row < 3
    centred = jnp.where(live, x - 0.5, 0.0)
    head = jnp.round(centred * 256.0) * (1.0 / 256.0)
    rest = centred - head
    rest1 = rest.astype(jnp.bfloat16).astype(jnp.float32)
    big = pick_row(row, three(jnp.sum(head * head, axis=0, keepdims=True)))
    small = pick_row(row, three(jnp.sum(rest * (2.0 * head + rest), axis=0, keepdims=True) + 0.5 * SOFT_SQ))
    return head, rest1, rest - rest1, big, small, jnp.where(live, 1.0, 0.0)


def left_terms(x, columns):
    head, rest1, rest2, big, small, ones = parts(x)
    h2, a2, b2 = -2.0 * head, -2.0 * rest1, -2.0 * rest2
    groups = [h2, big, ones, small, ones, h2, h2, a2, b2, a2, a2, b2]
    row = lax.broadcasted_iota(jnp.int32, (TERMS - SPLIT, x.shape[1]), 0)
    groups.append(pick_row(row, [part for column in columns for part in three(column)]))
    return jnp.concatenate(groups, axis=0)


def right_terms(x):
    head, rest1, rest2, big, small, ones = parts(x)
    groups = [head, ones, big, ones, small, rest1, rest2, head, head, rest1, rest2, rest1]
    groups.append(jnp.zeros((TERMS - SPLIT, x.shape[1]), jnp.float32))
    return jnp.concatenate(groups, axis=0).astype(jnp.bfloat16)


def column_of(lhs, which):
    row = lax.broadcasted_iota(jnp.int32, (TERMS, LANES), 0) - SPLIT - 3 * which
    pick = jnp.where((row >= 0) & (row < 3), 1.0, 0.0).astype(jnp.bfloat16)
    return jnp.dot(lhs, pick, preferred_element_type=jnp.float32)


def fold_lanes(tile, row):
    part = tile[:, :LANES] * row[:, :LANES]
    for q in range(1, tile.shape[1] // LANES):
        part = part + tile[:, q * LANES : (q + 1) * LANES] * row[:, q * LANES : (q + 1) * LANES]
    return part


def twice(col):
    return jnp.concatenate([col] * (HALF // LANES), axis=1)


def place(x, n):
    bits = n.bit_length() - 1
    div, rem = (lambda a, b: a // b, lambda a, b: a % b) if isinstance(x, int) else (lax.div, lax.rem)
    return sum(rem(div(x, 1 << (bits - 1 - j)), 2) * (1 << j) for j in range(bits))


def far_kernel(*refs, blocks, n_row, n_col, base):
    pairs, count, row_in, own_in = refs[:4]
    col_in = refs[4 : 3 + n_row]
    backs = refs[3 + n_row : 2 + 2 * n_row]
    rows_out, cols_out, *messages = refs[2 + 2 * n_row : -4]
    right_buf, lhs_buf, rhs_buf, part_buf = refs[-4:]
    rows_out[...] = jnp.zeros_like(rows_out)
    cols_out[...] = jnp.zeros_like(cols_out)
    my_row, my_col = lax.axis_index("row"), lax.axis_index("col")

    def step(s, _):
        a, b = pairs[0, s], pairs[1, s]
        a_way, b_way = jnp.bitwise_xor(lax.div(a, blocks), my_col), jnp.bitwise_xor(lax.div(b, blocks), my_row)
        ka, kb = lax.rem(a, blocks), lax.rem(b, blocks)
        same = (a_way == 0) & (b_way == 0) & (ka == kb)

        @pl.when(b_way == 0)
        def _():
            right_buf[...] = own_in[kb]

        for d, other in enumerate(col_in):

            @pl.when(b_way == d + 1)
            def _():
                lines = [other[pl.ds(base + 4 * kb + c, 1), :] for c in range(4)]
                right_buf[...] = jnp.concatenate(lines, axis=0)

        left, right = row_in[place(a_way, n_col) * (blocks + 1) + ka], right_buf[...]
        lhs_buf[...] = jnp.transpose(left_terms(left, [left[3:4]])).astype(jnp.bfloat16)
        rhs_buf[...] = right_terms(right)
        lhs = lhs_buf[...]
        zcol = column_of(lhs, 0)
        total = []
        for h in range(BLK // HALF):
            cols = slice(h * HALF, (h + 1) * HALF)
            dist = jnp.dot(lhs, rhs_buf[:, cols], preferred_element_type=jnp.float32)
            acc = jnp.zeros((8, HALF), jnp.float32)
            for g in range(BLK // 8):
                rows = slice(g * 8, (g + 1) * 8)
                tile = lax.rsqrt(dist[rows, :])
                part = fold_lanes(tile, right[3:4, cols])
                part_buf[rows, :] = part if h == 0 else part_buf[rows, :] + part
                acc = acc + tile * twice(zcol[rows, :])
            total.append(jnp.sum(acc, axis=0, keepdims=True))
        rows_out[pl.ds(s, 1), :] = jnp.sum(jnp.transpose(part_buf[...]), axis=0, keepdims=True)
        cols_out[pl.ds(s, 1), :] = jnp.concatenate(total, axis=1) * jnp.where(same, 0.0, 1.0)
        return 0

    lax.fori_loop(0, count[0], step, 0)
    nfar = cols_out.shape[0]
    for message, back in zip(messages, backs):
        message[0:nfar, :] = cols_out[...]
        message[nfar:, :] = back[...]


def points(tall):
    quad = tall.shape[0] // 4
    sides = [[tall[quad * c + u : quad * c + u + 1, :] for c in range(4)] for u in range(quad)]
    return jnp.concatenate([jnp.concatenate(side, axis=0) for side in sides], axis=1)


def near_tile(left, dens_i, right, dens_j, lhs_buf, rhs_buf, part_buf, acc_buf):
    quad = left.shape[1] // BLK
    terms = jnp.transpose(left_terms(left, [left[3:4], jnp.concatenate([dens_i] * quad, axis=1)]))
    terms = terms.astype(jnp.bfloat16)
    for g in range(BLK // GROUP):
        for u in range(quad):
            to, at = (g * quad + u) * GROUP, u * BLK + g * GROUP
            lhs_buf[to : to + GROUP, :] = terms[at : at + GROUP, :]
    rhs_buf[...] = right_terms(right)
    weights = right[3:4]
    acc_buf[...] = jnp.zeros_like(acc_buf)

    def chunk(i, _):
        at = pl.multiple_of(i * CHUNK * quad, CHUNK * quad)
        lhs = lhs_buf[pl.ds(at, CHUNK * quad), :]
        wcol = column_of(lhs, 0)
        groups = CHUNK // GROUP
        first_rows = [lhs[g * quad * GROUP : g * quad * GROUP + GROUP, :] for g in range(groups)]
        dcol = column_of(jnp.concatenate(first_rows, axis=0), 1)
        part = None
        for h in range(BLK // HALF):
            tiles = [None] * groups
            for v in range(quad):
                cols = slice(v * BLK + h * HALF, v * BLK + (h + 1) * HALF)
                dist = jnp.dot(lhs, rhs_buf[:, cols], preferred_element_type=jnp.float32)
                for g in range(groups):
                    inner = None
                    for u in range(quad):
                        rows = slice((g * quad + u) * GROUP, (g * quad + u + 1) * GROUP)
                        term = lax.rsqrt(dist[rows, :]) * twice(wcol[rows, :])
                        inner = term if inner is None else inner + term
                    inner = inner * weights[:, cols]
                    tiles[g] = inner if tiles[g] is None else tiles[g] + inner
            tile = jnp.concatenate(tiles, axis=0)
            cols = slice(h * HALF, (h + 1) * HALF)
            more = fold_lanes(tile, dens_j[:, cols])
            part = more if part is None else part + more
            acc_buf[:, cols] += jnp.sum((tile * twice(dcol)).reshape(-1, 8, HALF), axis=0)
        part_buf[pl.ds(pl.multiple_of(i * CHUNK, CHUNK), CHUNK), :] = part
        return 0

    lax.fori_loop(0, BLK // CHUNK, chunk, 0)
    rows = jnp.sum(jnp.transpose(part_buf[...]), axis=0, keepdims=True)
    return rows, jnp.sum(acc_buf[...], axis=0, keepdims=True)


def near_own_kernel(pairs, near_ref, rows_out, *bufs):
    blocks, depth, _ = near_ref.shape
    k = lax.rem(pairs[0, 0], blocks)
    pts, dens = points(near_ref[k, 0 : depth - 8, :]), near_ref[k, depth - 8 : depth - 7, :]
    rows_out[...] = jnp.zeros_like(rows_out)
    rows_out[pl.ds(k, 1), :] = near_tile(pts, dens, pts, dens, *bufs)[0]


def near_kernel(*refs, ways, base):
    away = [d for d in ways if d > 0]
    pairs, count, near_ref, *refs = refs
    got, start, field = refs[: len(away)], refs[len(away)], refs[len(away) + 1]
    backs = refs[len(away) + 2 : 2 * len(away) + 2]
    right_buf, tags, sems, *bufs = refs[2 * len(away) + 2 :]
    blocks, depth, _ = near_ref.shape
    slots = pairs.shape[1] - 1
    body = depth - 8
    my_row = lax.axis_index("row")
    copies = [
        pltpu.make_async_copy(g.at[base - 8 : base, 0:LANES], tags.at[d], sems.at[d]) for d, g in enumerate(got)
    ]
    for copy in copies:
        copy.start()
    field[...] = start[...]
    for back in backs:
        back[...] = jnp.zeros_like(back)
    for copy in copies:
        copy.wait()
    lead = len(ways) - len(away)

    def step(i, _):
        way, t = lax.div(i, slots), lax.rem(i, slots)
        b = tags[jnp.maximum(way - lead, 0), 7, t].astype(jnp.int32)
        if lead:
            b = jnp.where(way == 0, jnp.where(t + 1 < count[0], pairs[1, t + 1], -1), b)

        @pl.when((b >= my_row * blocks) & (b < (my_row + 1) * blocks))
        def _():
            ka, kb = lax.rem(pairs[0, t + 1], blocks), b - my_row * blocks
            if lead:

                @pl.when(way == 0)
                def _():
                    right_buf[...] = near_ref[ka]

            for d, other in enumerate(got):

                @pl.when(way == d + lead)
                def _():
                    at = pl.multiple_of(t * body, 8)
                    right_buf[0:body, :] = other[pl.ds(at, body), :]
                    right_buf[body : body + 1, :] = other[pl.ds(slots * body + t, 1), :]

            left, right = points(near_ref[kb, 0:body, :]), points(right_buf[0:body, :])
            dens_i, dens_j = near_ref[kb, body : body + 1, :], right_buf[body : body + 1, :]
            rows, cols = near_tile(left, dens_i, right, dens_j, *bufs)
            field[pl.ds(kb, 1), :] += rows
            if lead:

                @pl.when(way == 0)
                def _():
                    field[pl.ds(ka, 1), :] += cols * jnp.where(ka == kb, 0.0, 1.0)

            for d, back in enumerate(backs):

                @pl.when(way == d + lead)
                def _():
                    back[pl.ds(t, 1), :] = cols

        return 0

    lax.fori_loop(0, len(ways) * slots, step, 0)


def final_kernel(*refs, n_row, n_col, base):
    refs = list(refs)
    take = lambda n: [refs.pop(0) for _ in range(n)]
    pairs, weight, near, row_far, own_far = take(5)
    col_far, rows, (own_cols,), messages = take(n_row - 1), take(n_col // 2), take(1), take(n_row - 1)
    out, field = refs
    blocks, nfar = weight.shape[0], own_cols.shape[0]
    my_row, my_col = lax.axis_index("row"), lax.axis_index("col")
    field[...] = near[...]
    for d, message in enumerate(messages):
        for t in range(pairs.shape[1] - 1):
            k = lax.rem(pairs[0, t + 1], blocks)
            field[pl.ds(k, 1), :] += message[nfar + t : nfar + t + 1, :]

    def hot(index, base):
        want = lax.broadcasted_iota(jnp.int32, (blocks, nfar), 0) + base * blocks
        return jnp.where(index[:, 0:nfar] == want.astype(jnp.float32), 1.0, 0.0)

    tags = [place(d, n_col) * (blocks + 1) + blocks for d in range(n_col)]
    pick = [hot(row_far[tag, 0:1, :], my_col) for tag in tags]
    pick += [hot(own_far[blocks, 1:2, :], my_row)]
    line = base + 4 * blocks + 1
    pick += [hot(other[line : line + 1, :], my_row) for other in col_far]
    far = jnp.dot(
        jnp.concatenate(pick, axis=1),
        jnp.concatenate([r[...] for r in rows] + [own_cols[...]] + [m[0:nfar, :] for m in messages], axis=0),
        precision=HIGH,
        preferred_element_type=jnp.float32,
    )
    total = field[...] + far * weight[...]
    for q in range(BLK // LANES):
        out[pl.ds(q, blocks, stride=BLK // LANES), :] = total[:, q * LANES : (q + 1) * LANES]


def f32(*shape):
    return jax.ShapeDtypeStruct(shape, jnp.float32)


def cost(micros):
    return pl.CostEstimate(flops=int(micros * 1.1e9), bytes_accessed=1 << 16, transcendentals=0)


def body(points, density, near_pairs, far_pairs, near_count, far_count, *, n_row, n_col):
    quad = points.shape[1]
    blocks = points.shape[2] // BLK
    nnear, nfar = near_pairs.shape[0], far_pairs.shape[0]
    depth, slots = 4 * quad, nnear - 1
    near_pairs, far_pairs = near_pairs.T, far_pairs.T

    def swap(x, axis, d):
        n = {"row": n_row, "col": n_col}[axis]
        return lax.ppermute(x, axis, [(i, i ^ d) for i in range(n)])

    def halves(n):
        return [1 << j for j in reversed(range(n.bit_length() - 1))]

    def row_gather(x):
        known = {0: x}
        for d in halves(n_row):
            known.update({k ^ d: swap(v, "row", d) for k, v in known.items()})
        return [known[k] for k in range(n_row)]

    def col_gather(x):
        for d in halves(n_col):
            x = jnp.concatenate([x, swap(x, "col", d)], axis=0)
        return x

    base = near_lines(slots, quad)
    msg_rows = -(-(base + 4 * (blocks + 1)) // 8) * 8
    hbm = [pltpu.with_memory_space_constraint(x, pltpu.HBM) for x in (far_pairs, points, density.reshape(-1, LANES))]
    msg, far_own, near_own, weight = pl.pallas_call(
        prep_kernel,
        out_shape=(
            f32(msg_rows, BLK),
            f32(blocks + 1, 4, BLK),
            f32(blocks, depth + 8, BLK),
            f32(blocks, BLK),
        ),
        in_specs=[SMEM, SMEM, HBM, HBM, HBM],
        out_specs=(VMEM, VMEM, VMEM, VMEM),
        scratch_shapes=[
            pltpu.VMEM(far_pairs.shape, jnp.int32),
            pltpu.VMEM(points.shape, jnp.float32),
            pltpu.VMEM((density.shape[0] // LANES, LANES), jnp.float32),
            pltpu.SemaphoreType.DMA((QUARTERS + 2,)),
        ],
        compiler_params=PARAMS,
        cost_estimate=cost(1.2),
        name="prep",
    )(near_pairs, near_count, *hbm)
    got = row_gather(msg)[1:]
    row_far = col_gather(far_own)

    bufs = [
        pltpu.VMEM((quad * BLK, TERMS), jnp.bfloat16),
        pltpu.VMEM((TERMS, quad * BLK), jnp.bfloat16),
        pltpu.VMEM((BLK, LANES), jnp.float32),
        pltpu.VMEM((8, BLK), jnp.float32),
    ]
    near0 = pl.pallas_call(
        near_own_kernel,
        out_shape=f32(blocks, BLK),
        in_specs=[SMEM, VMEM],
        out_specs=VMEM,
        scratch_shapes=bufs,
        compiler_params=PARAMS,
        cost_estimate=cost(5.0),
        name="near_own",
    )(near_pairs, near_own)

    def near_call(ways, start, name):
        away = [d for d in ways if d > 0]
        field, *backs = pl.pallas_call(
            functools.partial(near_kernel, ways=ways, base=base),
            out_shape=[f32(blocks, BLK)] + [f32(8, BLK)] * len(away),
            in_specs=[SMEM, SMEM] + [VMEM] * (len(away) + 2),
            out_specs=[VMEM] * (len(away) + 1),
            scratch_shapes=[
                pltpu.VMEM((depth + 8, BLK), jnp.float32),
                pltpu.SMEM((len(away), 8, LANES), jnp.float32),
                pltpu.SemaphoreType.DMA((len(away),)),
            ]
            + bufs,
            compiler_params=PARAMS,
            cost_estimate=cost(5.0),
            name=name,
        )(near_pairs, near_count, near_own, *[got[d - 1] for d in away], start)
        return field, dict(zip(away, backs))

    direct = [d for d in range(1, n_row) if d & (d - 1) == 0]
    late = [d for d in range(1, n_row) if d & (d - 1) != 0]
    field, backs = near_call([0] + direct, near0, "near_direct")
    field, more = near_call(late, field, "near_late")
    backs.update(more)

    far_rows, far_cols, *messages = pl.pallas_call(
        functools.partial(far_kernel, blocks=blocks, n_row=n_row, n_col=n_col, base=base),
        out_shape=[f32(nfar, BLK), f32(nfar, BLK)] + [f32(nfar + 8, BLK)] * (n_row - 1),
        in_specs=[SMEM, SMEM] + [VMEM] * (2 * n_row),
        out_specs=[VMEM] * (n_row + 1),
        scratch_shapes=[
            pltpu.VMEM((4, BLK), jnp.float32),
            pltpu.VMEM((BLK, TERMS), jnp.bfloat16),
            pltpu.VMEM((TERMS, BLK), jnp.bfloat16),
            pltpu.VMEM((BLK, LANES), jnp.float32),
        ],
        compiler_params=PARAMS,
        cost_estimate=cost(4.0),
        name="far",
    )(far_pairs, far_count, row_far, far_own, *got, *[backs[d] for d in range(1, n_row)])

    messages = [swap(x, "row", d + 1) for d, x in enumerate(messages)]
    both = jnp.concatenate([far_rows, swap(far_rows, "col", 1)], axis=0)
    rows = [both] + [swap(both, "col", d) for d in range(2, n_col, 2)]
    args = [weight, field, row_far, far_own, *got, *rows, far_cols, *messages]
    out = pl.pallas_call(
        functools.partial(final_kernel, n_row=n_row, n_col=n_col, base=base),
        out_shape=f32(blocks * BLK // LANES, LANES),
        in_specs=[SMEM] + [VMEM] * len(args),
        out_specs=VMEM,
        scratch_shapes=[pltpu.VMEM((blocks, BLK), jnp.float32)],
        compiler_params=PARAMS,
        name="final",
    )(near_pairs, *args)
    return out.reshape(-1)


def solution(mesh):
    in_specs = (
        P(None, None, ("row", "col")),
        P(("row", "col")),
        P(("row", "col"), None),
        P(("row", "col"), None),
        P(("row", "col")),
        P(("row", "col")),
    )
    out_specs = P(("row", "col"))
    kernel = functools.partial(body, n_row=mesh.shape["row"], n_col=mesh.shape["col"])
    return jax.shard_map(kernel, mesh=mesh, in_specs=in_specs, out_specs=out_specs, check_vma=False)
```

```python
import functools

import jax
import jax.numpy as jnp
from jax import lax
from jax.experimental import pallas as pl
from jax.experimental.pallas import tpu as pltpu
from jax.sharding import PartitionSpec as P

BLK = 512
LANES = 128
SOFT_SQ = 0.0004
TERMS = 64
SPLIT = 48
HALF = 512
QUARTERS = 4
BUFS = 4
GROUP = 16
CHUNK = 512
VMEM = pl.BlockSpec(memory_space=pltpu.VMEM)
SMEM = pl.BlockSpec(memory_space=pltpu.SMEM)
ANY = pl.BlockSpec(memory_space=pl.ANY)
HBM = pl.BlockSpec(memory_space=pltpu.HBM)
PARAMS = pltpu.CompilerParams(vmem_limit_bytes=40 * 1024 * 1024)


def prep_kernel(near_ref, count, far_hbm, pts_hbm, dens_hbm, msg, far_out, near_out, weight_out, *scratch):
    far_ref, pts_ref, dens_ref, sems = scratch
    blocks = near_out.shape[0]
    quad = pts_ref.shape[1]
    slots, body = near_ref.shape[1] - 1, quad * 4
    width = pts_ref.shape[2] // QUARTERS
    copies = [
        pltpu.make_async_copy(dens_hbm, dens_ref, sems.at[QUARTERS]),
        pltpu.make_async_copy(far_hbm, far_ref, sems.at[QUARTERS + 1]),
    ]
    for i in range(QUARTERS):
        part = slice(i * width, (i + 1) * width)
        copies.append(pltpu.make_async_copy(pts_hbm.at[:, :, part], pts_ref.at[:, :, part], sems.at[i]))
    for copy in copies:
        copy.start()
    copies.pop(0).wait()
    copies.pop(0).wait()

    for k in range(blocks):
        cols = slice(k * BLK, (k + 1) * BLK)
        if k % (blocks // QUARTERS) == 0:
            copies.pop(0).wait()
        w = pts_ref[3, :, cols]
        total = jnp.sum(w, axis=0, keepdims=True)
        dens = jnp.concatenate([dens_ref[4 * k + q : 4 * k + q + 1, :] for q in range(4)], axis=1)
        lines = []
        for c in range(3):
            x = pts_ref[c, :, cols]
            lines.append(jnp.sum(x * w, axis=0, keepdims=True) / total)
            near_out[k, quad * c : quad * c + quad, :] = x
        near_out[k, quad * 3 : quad * 4, :] = w
        near_out[k, quad * 4 : quad * 4 + 8, :] = jnp.broadcast_to(dens, (8, BLK))
        far_out[k] = jnp.concatenate(lines + [total * dens], axis=0)
        weight_out[k : k + 1, :] = total
    pairs = jnp.concatenate([far_ref[...].astype(jnp.float32), jnp.full((2, LANES - far_ref.shape[1]), -1.0)], axis=1)
    pairs = jnp.concatenate([pairs] * (BLK // LANES), axis=1)
    far_out[blocks] = jnp.concatenate([pairs, jnp.zeros((2, BLK), jnp.float32)], axis=0)
    lane = lax.broadcasted_iota(jnp.int32, (1, BLK), 1)
    line = jnp.full((1, BLK), -1.0, jnp.float32)
    for t in range(slots):
        k = lax.rem(near_ref[0, t + 1], blocks)
        msg[t * body : (t + 1) * body, :] = near_out[k, 0:body, :]
        msg[slots * body + t : slots * body + t + 1, :] = near_out[k, body : body + 1, :]
        source = jnp.where(t + 1 < count[0], near_ref[1, t + 1], -1)
        line = jnp.where(lane == t, source.astype(jnp.float32), line)
    first = slots * (body + 1)
    msg[first:, :] = jnp.broadcast_to(line, (msg.shape[0] - first, BLK))


def three(value):
    one = value.astype(jnp.bfloat16).astype(jnp.float32)
    two = (value - one).astype(jnp.bfloat16).astype(jnp.float32)
    return one, two, value - one - two


def pick_row(row, values):
    out = jnp.zeros(row.shape, jnp.float32)
    for k, value in enumerate(values):
        out = jnp.where(row == k, value, out)
    return out


def parts(x):
    row = lax.broadcasted_iota(jnp.int32, x.shape, 0)
    live = row < 3
    centred = jnp.where(live, x - 0.5, 0.0)
    head = jnp.round(centred * 256.0) * (1.0 / 256.0)
    rest = centred - head
    rest1 = rest.astype(jnp.bfloat16).astype(jnp.float32)
    big = pick_row(row, three(jnp.sum(head * head, axis=0, keepdims=True)))
    small = pick_row(row, three(jnp.sum(rest * (2.0 * head + rest), axis=0, keepdims=True) + 0.5 * SOFT_SQ))
    return head, rest1, rest - rest1, big, small, jnp.where(live, 1.0, 0.0)


def left_terms(x, columns):
    head, rest1, rest2, big, small, ones = parts(x)
    h2, a2, b2 = -2.0 * head, -2.0 * rest1, -2.0 * rest2
    groups = [h2, big, ones, small, ones, h2, h2, a2, b2, a2, a2, b2]
    row = lax.broadcasted_iota(jnp.int32, (TERMS - SPLIT, x.shape[1]), 0)
    groups.append(pick_row(row, [part for column in columns for part in three(column)]))
    return jnp.concatenate(groups, axis=0)


def right_terms(x):
    head, rest1, rest2, big, small, ones = parts(x)
    groups = [head, ones, big, ones, small, rest1, rest2, head, head, rest1, rest2, rest1]
    groups.append(jnp.zeros((TERMS - SPLIT, x.shape[1]), jnp.float32))
    return jnp.concatenate(groups, axis=0).astype(jnp.bfloat16)


def column_of(lhs, which):
    row = lax.broadcasted_iota(jnp.int32, (TERMS, LANES), 0) - SPLIT - 3 * which
    pick = jnp.where((row >= 0) & (row < 3), 1.0, 0.0).astype(jnp.bfloat16)
    return jnp.dot(lhs, pick, preferred_element_type=jnp.float32)


def fold_lanes(tile, row):
    part = tile[:, :LANES] * row[:, :LANES]
    for q in range(1, tile.shape[1] // LANES):
        part = part + tile[:, q * LANES : (q + 1) * LANES] * row[:, q * LANES : (q + 1) * LANES]
    return part


def twice(col):
    return jnp.concatenate([col] * (HALF // LANES), axis=1)


def place(x, n):
    if isinstance(x, int):
        return x % 2 * (n // 2) + x // 2
    return lax.rem(x, 2) * (n // 2) + lax.div(x, 2)


def far_kernel(*refs, blocks, n_row, n_col):
    pairs, count, row_in = refs[:3]
    col_in = refs[3 : 3 + n_row]
    rows_out, cols_out, right_buf, lhs_buf, rhs_buf, part_buf = refs[4 + n_row :]
    rows_out[...] = jnp.zeros_like(rows_out)
    cols_out[...] = jnp.zeros_like(cols_out)
    my_row, my_col = lax.axis_index("row"), lax.axis_index("col")

    def one(s, j):
        a, b = pairs[0, s], pairs[1, s]
        a_way, b_way = jnp.bitwise_xor(lax.div(a, blocks), my_col), jnp.bitwise_xor(lax.div(b, blocks), my_row)
        ka, kb = lax.rem(a, blocks), lax.rem(b, blocks)
        same = (a_way == 0) & (b_way == 0) & (ka == kb)
        for d in range(n_row):

            @pl.when(b_way == d)
            def _():
                right_buf[j] = col_in[d][kb]

        left, right = row_in[place(a_way, n_col) * (blocks + 1) + ka], right_buf[j]
        lhs_buf[j] = jnp.transpose(left_terms(left, [left[3:4]])).astype(jnp.bfloat16)
        rhs_buf[j] = right_terms(right)
        lhs = lhs_buf[j]
        zcol = column_of(lhs, 0)
        dist = jnp.dot(lhs, rhs_buf[j], preferred_element_type=jnp.float32)
        acc = jnp.zeros((8, BLK), jnp.float32)
        for g in range(BLK // 8):
            rows = slice(g * 8, (g + 1) * 8)
            tile = lax.rsqrt(dist[rows, :])
            part_buf[j, rows, :] = fold_lanes(tile, right[3:4])
            acc = acc + tile * twice(zcol[rows, :])
        rows = jnp.sum(jnp.transpose(part_buf[j]), axis=0, keepdims=True)
        return rows, jnp.sum(acc, axis=0, keepdims=True) * jnp.where(same, 0.0, 1.0)

    def step(i, _):
        first, second = 2 * i, 2 * i + 1
        used = jnp.where(second < count[0], 1.0, 0.0)
        rows, cols = one(first, 0)
        more_rows, more_cols = one(jnp.where(second < count[0], second, first), 1)
        rows_out[pl.ds(first, 1), :] = rows
        cols_out[pl.ds(first, 1), :] = cols
        rows_out[pl.ds(second, 1), :] = more_rows * used
        cols_out[pl.ds(second, 1), :] = more_cols * used
        return 0

    lax.fori_loop(0, lax.div(count[0] + 1, 2), step, 0)


def points(tall):
    quad = tall.shape[0] // 4
    sides = [[tall[quad * c + u : quad * c + u + 1, :] for c in range(4)] for u in range(quad)]
    return jnp.concatenate([jnp.concatenate(side, axis=0) for side in sides], axis=1)


def near_tile(left, dens_i, right, dens_j, lhs_buf, rhs_buf, part_buf, acc_buf):
    quad = left.shape[1] // BLK
    terms = jnp.transpose(left_terms(left, [left[3:4], jnp.concatenate([dens_i] * quad, axis=1)]))
    terms = terms.astype(jnp.bfloat16)
    for g in range(BLK // GROUP):
        for u in range(quad):
            to, at = (g * quad + u) * GROUP, u * BLK + g * GROUP
            lhs_buf[to : to + GROUP, :] = terms[at : at + GROUP, :]
    rhs_buf[...] = right_terms(right)
    weights = right[3:4]
    acc_buf[...] = jnp.zeros_like(acc_buf)

    def chunk(i, _):
        at = pl.multiple_of(i * CHUNK * quad, CHUNK * quad)
        lhs = lhs_buf[pl.ds(at, CHUNK * quad), :]
        wcol = column_of(lhs, 0)
        groups = CHUNK // GROUP
        first_rows = [lhs[g * quad * GROUP : g * quad * GROUP + GROUP, :] for g in range(groups)]
        dcol = column_of(jnp.concatenate(first_rows, axis=0), 1)
        part = None
        for h in range(BLK // HALF):
            tiles = [None] * groups
            for v in range(quad):
                cols = slice(v * BLK + h * HALF, v * BLK + (h + 1) * HALF)
                dist = jnp.dot(lhs, rhs_buf[:, cols], preferred_element_type=jnp.float32)
                for g in range(groups):
                    inner = None
                    for u in range(quad):
                        rows = slice((g * quad + u) * GROUP, (g * quad + u + 1) * GROUP)
                        term = lax.rsqrt(dist[rows, :]) * twice(wcol[rows, :])
                        inner = term if inner is None else inner + term
                    inner = inner * weights[:, cols]
                    tiles[g] = inner if tiles[g] is None else tiles[g] + inner
            tile = jnp.concatenate(tiles, axis=0)
            cols = slice(h * HALF, (h + 1) * HALF)
            more = fold_lanes(tile, dens_j[:, cols])
            part = more if part is None else part + more
            acc_buf[:, cols] += jnp.sum((tile * twice(dcol)).reshape(-1, 8, HALF), axis=0)
        part_buf[pl.ds(pl.multiple_of(i * CHUNK, CHUNK), CHUNK), :] = part
        return 0

    lax.fori_loop(0, BLK // CHUNK, chunk, 0)
    rows = jnp.sum(jnp.transpose(part_buf[...]), axis=0, keepdims=True)
    return rows, jnp.sum(acc_buf[...], axis=0, keepdims=True)


def near_own_kernel(pairs, near_ref, rows_out, *bufs):
    blocks, depth, _ = near_ref.shape
    k = lax.rem(pairs[0, 0], blocks)
    pts, dens = points(near_ref[k, 0 : depth - 8, :]), near_ref[k, depth - 8 : depth - 7, :]
    rows_out[...] = jnp.zeros_like(rows_out)
    rows_out[pl.ds(k, 1), :] = near_tile(pts, dens, pts, dens, *bufs)[0]


def near_kernel(*refs, ways, merge=0):
    away = [d for d in ways if d > 0]
    pairs, count, near_ref, *refs = refs
    got, start = refs[: len(away)], refs[len(away)]
    field, *backs = refs[-(merge or len(away)) - BUFS - 4 : -BUFS - 3]
    right_buf, tags, sems, *bufs = refs[-BUFS - 3 :]
    done = refs[len(away) + 1 : -merge - BUFS - 4] if merge else []
    blocks, depth, _ = near_ref.shape
    slots = pairs.shape[1] - 1
    body = depth - 8
    my_row = lax.axis_index("row")
    tail = slice(got[0].shape[0] - 8, got[0].shape[0])
    copies = [
        pltpu.make_async_copy(g.at[tail, 0:LANES], tags.at[d], sems.at[d]) for d, g in enumerate(got)
    ]
    for copy in copies:
        copy.start()
    field[...] = start[...]
    base = 0
    if merge:
        far_cols, *done = done
        base = far_cols.shape[0]
        for back in backs:
            back[0:base, :] = far_cols[...]
        for back in backs[len(done) :]:
            back[base:, :] = jnp.zeros((8, BLK), jnp.float32)
        for back, value in zip(backs, done):
            back[base:, :] = value[...]
        backs = backs[len(done) :]
    else:
        for back in backs:
            back[...] = jnp.zeros_like(back)
    for copy in copies:
        copy.wait()
    lead = len(ways) - len(away)

    def step(i, _):
        way, t = lax.div(i, slots), lax.rem(i, slots)
        b = tags[jnp.maximum(way - lead, 0), 7, t].astype(jnp.int32)
        if lead:
            b = jnp.where(way == 0, jnp.where(t + 1 < count[0], pairs[1, t + 1], -1), b)

        @pl.when((b >= my_row * blocks) & (b < (my_row + 1) * blocks))
        def _():
            ka, kb = lax.rem(pairs[0, t + 1], blocks), b - my_row * blocks
            if lead:

                @pl.when(way == 0)
                def _():
                    right_buf[...] = near_ref[ka]

            for d, other in enumerate(got):

                @pl.when(way == d + lead)
                def _():
                    at = pl.multiple_of(t * body, 8)
                    right_buf[0:body, :] = other[pl.ds(at, body), :]
                    right_buf[body : body + 1, :] = other[pl.ds(slots * body + t, 1), :]

            left, right = points(near_ref[kb, 0:body, :]), points(right_buf[0:body, :])
            dens_i, dens_j = near_ref[kb, body : body + 1, :], right_buf[body : body + 1, :]
            rows, cols = near_tile(left, dens_i, right, dens_j, *bufs)
            field[pl.ds(kb, 1), :] += rows
            if lead:

                @pl.when(way == 0)
                def _():
                    field[pl.ds(ka, 1), :] += cols * jnp.where(ka == kb, 0.0, 1.0)

            for d, back in enumerate(backs):

                @pl.when(way == d + lead)
                def _():
                    back[pl.ds(base + t, 1), :] = cols

        return 0

    lax.fori_loop(0, len(ways) * slots, step, 0)


def final_kernel(*refs, n_row, n_col):
    refs = list(refs)
    take = lambda n: [refs.pop(0) for _ in range(n)]
    pairs, weight, near, row_far = take(4)
    col_far, rows, (own_cols,), messages = take(n_row), take(n_col // 2), take(1), take(n_row - 1)
    out, field = refs
    blocks, nfar = weight.shape[0], own_cols.shape[0]
    my_row, my_col = lax.axis_index("row"), lax.axis_index("col")
    field[...] = near[...]
    for message in messages:
        for t in range(pairs.shape[1] - 1):
            k = lax.rem(pairs[0, t + 1], blocks)
            field[pl.ds(k, 1), :] += message[nfar + t : nfar + t + 1, :]

    def hot(index, base):
        want = lax.broadcasted_iota(jnp.int32, (blocks, nfar), 0) + base * blocks
        return jnp.where(index[:, 0:nfar] == want.astype(jnp.float32), 1.0, 0.0)

    tags = [place(d, n_col) * (blocks + 1) + blocks for d in range(n_col)]
    pick = [hot(row_far[tag, 0:1, :], my_col) for tag in tags]
    pick += [hot(other[blocks, 1:2, :], my_row) for other in col_far]
    pick = jnp.concatenate(pick * 3, axis=1).astype(jnp.bfloat16)
    slots = jnp.concatenate([r[...] for r in rows] + [own_cols[...]] + [m[0:nfar, :] for m in messages], axis=0)
    slots = jnp.concatenate(three(slots), axis=0).astype(jnp.bfloat16)
    far = jnp.dot(pick, slots, preferred_element_type=jnp.float32)
    total = field[...] + far * weight[...]
    for q in range(BLK // LANES):
        out[pl.ds(q, blocks, stride=BLK // LANES), :] = total[:, q * LANES : (q + 1) * LANES]


def f32(*shape):
    return jax.ShapeDtypeStruct(shape, jnp.float32)


def cost(micros):
    return pl.CostEstimate(flops=int(micros * 1.1e9), bytes_accessed=1 << 16, transcendentals=0)


def body(points, density, near_pairs, far_pairs, near_count, far_count, *, n_row, n_col):
    quad = points.shape[1]
    blocks = points.shape[2] // BLK
    nnear, nfar = near_pairs.shape[0], far_pairs.shape[0]
    depth, slots = 4 * quad, nnear - 1
    near_pairs, far_pairs = near_pairs.T, far_pairs.T

    def swap(x, axis, d):
        n = {"row": n_row, "col": n_col}[axis]
        return lax.ppermute(x, axis, [(i, i ^ d) for i in range(n)])

    direct = [d for d in range(1, n_row) if d & (d - 1) == 0]
    late = [d for d in range(1, n_row) if d & (d - 1) != 0]

    def halves(n):
        return [1 << j for j in reversed(range(n.bit_length() - 1))]

    def row_gather(x):
        known = {0: x}
        for d in halves(n_row):
            known.update({k ^ d: swap(v, "row", d) for k, v in known.items()})
        return [known[k] for k in range(n_row)]

    def col_gather(x):
        x = jnp.concatenate([x] + [swap(x, "col", d) for d in range(2, n_col, 2)], axis=0)
        return jnp.concatenate([x, swap(x, "col", 1)], axis=0)

    msg_rows = -(-(slots * (depth + 1) + 1) // 8) * 8
    hbm = [pltpu.with_memory_space_constraint(x, pltpu.HBM) for x in (far_pairs, points, density.reshape(-1, LANES))]
    msg, far_own, near_own, weight = pl.pallas_call(
        prep_kernel,
        out_shape=(
            f32(msg_rows, BLK),
            f32(blocks + 1, 4, BLK),
            f32(blocks, depth + 8, BLK),
            f32(blocks, BLK),
        ),
        in_specs=[SMEM, SMEM, HBM, HBM, HBM],
        out_specs=(VMEM, VMEM, VMEM, VMEM),
        scratch_shapes=[
            pltpu.VMEM(far_pairs.shape, jnp.int32),
            pltpu.VMEM(points.shape, jnp.float32),
            pltpu.VMEM((density.shape[0] // LANES, LANES), jnp.float32),
            pltpu.SemaphoreType.DMA((QUARTERS + 2,)),
        ],
        compiler_params=PARAMS,
        cost_estimate=cost(1.2),
        name="prep",
    )(near_pairs, near_count, *hbm)
    row_far = col_gather(far_own)
    col_far = row_gather(far_own)
    msg, *col_far = lax.optimization_barrier((msg, *[col_far[d] for d in direct])) + tuple(col_far[d] for d in late)
    col_far = dict(zip(direct + late, col_far))
    col_far = [far_own] + [col_far[d] for d in range(1, n_row)]
    got = row_gather(msg)[1:]

    bufs = [
        pltpu.VMEM((quad * BLK, TERMS), jnp.bfloat16),
        pltpu.VMEM((TERMS, quad * BLK), jnp.bfloat16),
        pltpu.VMEM((BLK, LANES), jnp.float32),
        pltpu.VMEM((8, BLK), jnp.float32),
    ]
    near0 = pl.pallas_call(
        near_own_kernel,
        out_shape=f32(blocks, BLK),
        in_specs=[SMEM, VMEM],
        out_specs=VMEM,
        scratch_shapes=bufs,
        compiler_params=PARAMS,
        cost_estimate=cost(5.0),
        name="near_own",
    )(near_pairs, near_own)

    far_rows, far_cols = pl.pallas_call(
        functools.partial(far_kernel, blocks=blocks, n_row=n_row, n_col=n_col),
        out_shape=[f32(nfar, BLK), f32(nfar, BLK)],
        in_specs=[SMEM, SMEM] + [VMEM] * (n_row + 1) + [ANY],
        out_specs=[VMEM, VMEM],
        scratch_shapes=[
            pltpu.VMEM((2, 4, BLK), jnp.float32),
            pltpu.VMEM((2, BLK, TERMS), jnp.bfloat16),
            pltpu.VMEM((2, TERMS, BLK), jnp.bfloat16),
            pltpu.VMEM((2, BLK, LANES), jnp.float32),
        ],
        compiler_params=PARAMS,
        cost_estimate=cost(4.0),
        name="far",
    )(far_pairs, far_count, row_far, *col_far, near0)
    both = jnp.concatenate([far_rows, swap(far_rows, "col", 1)], axis=0)
    rows = [both] + [swap(both, "col", d) for d in range(2, n_col, 2)]

    def near_call(ways, outs, extra, after, merge, name):
        away = [d for d in ways if d > 0]
        return pl.pallas_call(
            functools.partial(near_kernel, ways=ways, merge=merge),
            out_shape=[f32(blocks, BLK)] + outs,
            in_specs=[SMEM, SMEM] + [VMEM] * (len(away) + 1 + len(extra)) + [ANY] * len(after),
            out_specs=[VMEM] * (len(outs) + 1),
            scratch_shapes=[
                pltpu.VMEM((depth + 8, BLK), jnp.float32),
                pltpu.SMEM((len(away), 8, LANES), jnp.float32),
                pltpu.SemaphoreType.DMA((len(away),)),
            ]
            + bufs,
            compiler_params=PARAMS,
            cost_estimate=cost(5.0),
            name=name,
        )(near_pairs, near_count, near_own, *[got[d - 1] for d in away], *extra, *after)

    field, *backs = near_call([0] + direct, [f32(8, BLK)] * len(direct), [near0], rows, 0, "near_direct")
    outs = [f32(nfar + 8, BLK)] * (n_row - 1)
    field, *messages = near_call(late, outs, [field, far_cols, *backs], [], n_row - 1, "near_late")
    messages = dict(zip(direct + late, messages))
    messages = [swap(messages[d], "row", d) for d in range(1, n_row)]
    args = [weight, field, row_far, *col_far, *rows, far_cols, *messages]
    out = pl.pallas_call(
        functools.partial(final_kernel, n_row=n_row, n_col=n_col),
        out_shape=f32(blocks * BLK // LANES, LANES),
        in_specs=[SMEM] + [VMEM] * len(args),
        out_specs=VMEM,
        scratch_shapes=[pltpu.VMEM((blocks, BLK), jnp.float32)],
        compiler_params=PARAMS,
        name="final",
    )(near_pairs, *args)
    return out.reshape(-1)


def solution(mesh):
    in_specs = (
        P(None, None, ("row", "col")),
        P(("row", "col")),
        P(("row", "col"), None),
        P(("row", "col"), None),
        P(("row", "col")),
        P(("row", "col")),
    )
    out_specs = P(("row", "col"))
    kernel = functools.partial(body, n_row=mesh.shape["row"], n_col=mesh.shape["col"])
    return jax.shard_map(kernel, mesh=mesh, in_specs=in_specs, out_specs=out_specs, check_vma=False)
```

```python
import functools

import jax
import jax.numpy as jnp
from jax import lax
from jax.experimental import pallas as pl
from jax.experimental.pallas import tpu as pltpu
from jax.sharding import PartitionSpec as P

BLK = 512
LANES = 128
SOFT_SQ = 0.0004
TERMS = 64
SPLIT = 48
HALF = 512
QUARTERS = 4
SLOTS = 5
NEAR_SCRATCH = 4 * [None]
GROUP = 16
CHUNK = 512
VMEM = pl.BlockSpec(memory_space=pltpu.VMEM)
SMEM = pl.BlockSpec(memory_space=pltpu.SMEM)
ANY = pl.BlockSpec(memory_space=pl.ANY)
HBM = pl.BlockSpec(memory_space=pltpu.HBM)
PARAMS = pltpu.CompilerParams(vmem_limit_bytes=40 * 1024 * 1024)


def prep_kernel(near_ref, count, far_hbm, pts_hbm, dens_hbm, msg, far_out, near_out, weight_out, *scratch):
    far_ref, pts_ref, dens_ref, sems = scratch
    blocks = near_out.shape[0]
    quad = pts_ref.shape[1]
    slots, body = near_ref.shape[1] - 1, quad * 4
    base = near_lines(slots, quad)
    width = pts_ref.shape[2] // QUARTERS
    copies = [
        pltpu.make_async_copy(dens_hbm, dens_ref, sems.at[QUARTERS]),
        pltpu.make_async_copy(far_hbm, far_ref, sems.at[QUARTERS + 1]),
    ]
    for i in range(QUARTERS):
        part = slice(i * width, (i + 1) * width)
        copies.append(pltpu.make_async_copy(pts_hbm.at[:, :, part], pts_ref.at[:, :, part], sems.at[i]))
    for copy in copies:
        copy.start()
    copies.pop(0).wait()
    copies.pop(0).wait()

    def put_far(k, value):
        far_out[k] = value
        msg[base + 4 * k : base + 4 * k + 4, :] = value

    for k in range(blocks):
        cols = slice(k * BLK, (k + 1) * BLK)
        if k % (blocks // QUARTERS) == 0:
            copies.pop(0).wait()
        w = pts_ref[3, :, cols]
        total = jnp.sum(w, axis=0, keepdims=True)
        dens = jnp.concatenate([dens_ref[4 * k + q : 4 * k + q + 1, :] for q in range(4)], axis=1)
        lines = []
        for c in range(3):
            x = pts_ref[c, :, cols]
            lines.append(jnp.sum(x * w, axis=0, keepdims=True) / total)
            near_out[k, quad * c : quad * c + quad, :] = x
        near_out[k, quad * 3 : quad * 4, :] = w
        near_out[k, quad * 4 : quad * 4 + 8, :] = jnp.broadcast_to(dens, (8, BLK))
        put_far(k, jnp.concatenate(lines + [total * dens], axis=0))
        weight_out[k : k + 1, :] = total
    pairs = jnp.concatenate([far_ref[...].astype(jnp.float32), jnp.full((2, LANES - far_ref.shape[1]), -1.0)], axis=1)
    pairs = jnp.concatenate([pairs] * (BLK // LANES), axis=1)
    put_far(blocks, jnp.concatenate([pairs, jnp.zeros((2, BLK), jnp.float32)], axis=0))
    lane = lax.broadcasted_iota(jnp.int32, (1, BLK), 1)
    line = jnp.full((1, BLK), -1.0, jnp.float32)
    for t in range(slots):
        k = lax.rem(near_ref[0, t + 1], blocks)
        msg[t * body : (t + 1) * body, :] = near_out[k, 0:body, :]
        msg[slots * body + t : slots * body + t + 1, :] = near_out[k, body : body + 1, :]
        source = jnp.where(t + 1 < count[0], near_ref[1, t + 1], -1)
        line = jnp.where(lane == t, source.astype(jnp.float32), line)
    first = slots * (body + 1)
    msg[first:base, :] = jnp.broadcast_to(line, (base - first, BLK))


def near_lines(slots, quad):
    return -(-(slots * (4 * quad + 1) + 1) // 8) * 8


def three(value):
    one = value.astype(jnp.bfloat16).astype(jnp.float32)
    two = (value - one).astype(jnp.bfloat16).astype(jnp.float32)
    return one, two, value - one - two


def pick_row(row, values):
    out = jnp.zeros(row.shape, jnp.float32)
    for k, value in enumerate(values):
        out = jnp.where(row == k, value, out)
    return out


def parts(x):
    row = lax.broadcasted_iota(jnp.int32, x.shape, 0)
    live = row < 3
    centred = jnp.where(live, x - 0.5, 0.0)
    head = jnp.round(centred * 256.0) * (1.0 / 256.0)
    rest = centred - head
    rest1 = rest.astype(jnp.bfloat16).astype(jnp.float32)
    big = pick_row(row, three(jnp.sum(head * head, axis=0, keepdims=True)))
    small = pick_row(row, three(jnp.sum(rest * (2.0 * head + rest), axis=0, keepdims=True) + 0.5 * SOFT_SQ))
    return head, rest1, rest - rest1, big, small, jnp.where(live, 1.0, 0.0)


def left_terms(x, columns):
    head, rest1, rest2, big, small, ones = parts(x)
    h2, a2, b2 = -2.0 * head, -2.0 * rest1, -2.0 * rest2
    groups = [h2, big, ones, small, ones, h2, h2, a2, b2, a2, a2, b2]
    row = lax.broadcasted_iota(jnp.int32, (TERMS - SPLIT, x.shape[1]), 0)
    groups.append(pick_row(row, [part for column in columns for part in three(column)]))
    return jnp.concatenate(groups, axis=0)


def right_terms(x):
    head, rest1, rest2, big, small, ones = parts(x)
    groups = [head, ones, big, ones, small, rest1, rest2, head, head, rest1, rest2, rest1]
    groups.append(jnp.zeros((TERMS - SPLIT, x.shape[1]), jnp.float32))
    return jnp.concatenate(groups, axis=0).astype(jnp.bfloat16)


def column_of(lhs, which):
    row = lax.broadcasted_iota(jnp.int32, (TERMS, LANES), 0) - SPLIT - 3 * which
    pick = jnp.where((row >= 0) & (row < 3), 1.0, 0.0).astype(jnp.bfloat16)
    return jnp.dot(lhs, pick, preferred_element_type=jnp.float32)


def fold_lanes(tile, row):
    part = tile[:, :LANES] * row[:, :LANES]
    for q in range(1, tile.shape[1] // LANES):
        part = part + tile[:, q * LANES : (q + 1) * LANES] * row[:, q * LANES : (q + 1) * LANES]
    return part


def twice(col):
    return jnp.concatenate([col] * (HALF // LANES), axis=1)


def far_tiles(pairs, count, row_in, own_in, col_in, rows_out, cols_out, right_buf, lhs_buf, rhs_buf, part_buf, base):
    blocks = own_in.shape[0] - 1
    rows_out[...] = jnp.zeros_like(rows_out)
    cols_out[...] = jnp.zeros_like(cols_out)
    my_row, my_col = lax.axis_index("row"), lax.axis_index("col")

    def step(s, _):
        a, b = pairs[0, s], pairs[1, s]
        a_way, b_way = jnp.bitwise_xor(lax.div(a, blocks), my_col), jnp.bitwise_xor(lax.div(b, blocks), my_row)
        ka, kb = lax.rem(a, blocks), lax.rem(b, blocks)
        same = (a_way == 0) & (b_way == 0) & (ka == kb)

        @pl.when(b_way == 0)
        def _():
            right_buf[...] = own_in[kb]

        for d, other in enumerate(col_in):

            @pl.when(b_way == d + 1)
            def _():
                lines = [other[pl.ds(base + 4 * kb + c, 1), :] for c in range(4)]
                right_buf[...] = jnp.concatenate(lines, axis=0)

        left, right = row_in[a_way * (blocks + 1) + ka], right_buf[...]
        lhs_buf[...] = jnp.transpose(left_terms(left, [left[3:4]])).astype(jnp.bfloat16)
        rhs_buf[...] = right_terms(right)
        lhs = lhs_buf[...]
        zcol = column_of(lhs, 0)
        total = []
        for h in range(BLK // HALF):
            cols = slice(h * HALF, (h + 1) * HALF)
            dist = jnp.dot(lhs, rhs_buf[:, cols], preferred_element_type=jnp.float32)
            acc = jnp.zeros((8, HALF), jnp.float32)
            for g in range(BLK // 8):
                rows = slice(g * 8, (g + 1) * 8)
                tile = lax.rsqrt(dist[rows, :])
                part = fold_lanes(tile, right[3:4, cols])
                part_buf[rows, :] = part if h == 0 else part_buf[rows, :] + part
                acc = acc + tile * twice(zcol[rows, :])
            total.append(jnp.sum(acc, axis=0, keepdims=True))
        rows_out[pl.ds(s, 1), :] = jnp.sum(jnp.transpose(part_buf[...]), axis=0, keepdims=True)
        cols_out[pl.ds(s, 1), :] = jnp.concatenate(total, axis=1) * jnp.where(same, 0.0, 1.0)
        return 0

    lax.fori_loop(0, count[0], step, 0)


def points(tall):
    quad = tall.shape[0] // 4
    sides = [[tall[quad * c + u : quad * c + u + 1, :] for c in range(4)] for u in range(quad)]
    return jnp.concatenate([jnp.concatenate(side, axis=0) for side in sides], axis=1)


def near_tile(left, dens_i, right, dens_j, lhs_buf, rhs_buf, part_buf, acc_buf):
    quad = left.shape[1] // BLK
    terms = jnp.transpose(left_terms(left, [left[3:4], jnp.concatenate([dens_i] * quad, axis=1)]))
    terms = terms.astype(jnp.bfloat16)
    for g in range(BLK // GROUP):
        for u in range(quad):
            to, at = (g * quad + u) * GROUP, u * BLK + g * GROUP
            lhs_buf[to : to + GROUP, :] = terms[at : at + GROUP, :]
    rhs_buf[...] = right_terms(right)
    weights = right[3:4]
    acc_buf[...] = jnp.zeros_like(acc_buf)

    def chunk(i, _):
        at = pl.multiple_of(i * CHUNK * quad, CHUNK * quad)
        lhs = lhs_buf[pl.ds(at, CHUNK * quad), :]
        wcol = column_of(lhs, 0)
        groups = CHUNK // GROUP
        first_rows = [lhs[g * quad * GROUP : g * quad * GROUP + GROUP, :] for g in range(groups)]
        dcol = column_of(jnp.concatenate(first_rows, axis=0), 1)
        part = None
        for h in range(BLK // HALF):
            tiles = [None] * groups
            for v in range(quad):
                cols = slice(v * BLK + h * HALF, v * BLK + (h + 1) * HALF)
                dist = jnp.dot(lhs, rhs_buf[:, cols], preferred_element_type=jnp.float32)
                for g in range(groups):
                    inner = None
                    for u in range(quad):
                        rows = slice((g * quad + u) * GROUP, (g * quad + u + 1) * GROUP)
                        term = lax.rsqrt(dist[rows, :]) * twice(wcol[rows, :])
                        inner = term if inner is None else inner + term
                    inner = inner * weights[:, cols]
                    tiles[g] = inner if tiles[g] is None else tiles[g] + inner
            tile = jnp.concatenate(tiles, axis=0)
            cols = slice(h * HALF, (h + 1) * HALF)
            more = fold_lanes(tile, dens_j[:, cols])
            part = more if part is None else part + more
            acc_buf[:, cols] += jnp.sum((tile * twice(dcol)).reshape(-1, 8, HALF), axis=0)
        part_buf[pl.ds(pl.multiple_of(i * CHUNK, CHUNK), CHUNK), :] = part
        return 0

    lax.fori_loop(0, BLK // CHUNK, chunk, 0)
    rows = jnp.sum(jnp.transpose(part_buf[...]), axis=0, keepdims=True)
    return rows, jnp.sum(acc_buf[...], axis=0, keepdims=True)


def near_own_kernel(pairs, count, near_ref, field, *bufs):
    blocks, depth, _ = near_ref.shape
    body = depth - 8
    my_row = lax.axis_index("row")
    field[...] = jnp.zeros_like(field)

    def step(s, _):
        ka, kb = lax.rem(pairs[0, s], blocks), pairs[1, s] - my_row * blocks

        @pl.when((kb >= 0) & (kb < blocks))
        def _():
            left, right = points(near_ref[ka, 0:body, :]), points(near_ref[kb, 0:body, :])
            dens_i, dens_j = near_ref[ka, body : body + 1, :], near_ref[kb, body : body + 1, :]
            rows, cols = near_tile(left, dens_i, right, dens_j, *bufs)
            field[pl.ds(ka, 1), :] += rows
            field[pl.ds(kb, 1), :] += cols * jnp.where(ka == kb, 0.0, 1.0)

        return 0

    lax.fori_loop(0, count[0], step, 0)


def near_tiles(near_ref, got, field, backs, first, right_buf, tags, sems, *bufs):
    blocks, depth, _ = near_ref.shape
    body = depth - 8
    base = near_lines(SLOTS, body // 4)
    my_row = lax.axis_index("row")
    copies = [
        pltpu.make_async_copy(g.at[base - 8 : base, 0:LANES], tags.at[d], sems.at[d]) for d, g in enumerate(got)
    ]
    for copy in copies:
        copy.start()
    for copy in copies:
        copy.wait()

    def step(i, _):
        way, t = lax.div(i, SLOTS), lax.rem(i, SLOTS)
        kb = tags[way, 7, t].astype(jnp.int32) - my_row * blocks

        @pl.when((kb >= 0) & (kb < blocks))
        def _():
            for d, other in enumerate(got):

                @pl.when(way == d)
                def _():
                    at = pl.multiple_of(t * body, 8)
                    right_buf[0:body, :] = other[pl.ds(at, body), :]
                    right_buf[body : body + 1, :] = other[pl.ds(SLOTS * body + t, 1), :]

            left, right = points(near_ref[kb, 0:body, :]), points(right_buf[0:body, :])
            dens_i, dens_j = near_ref[kb, body : body + 1, :], right_buf[body : body + 1, :]
            rows, cols = near_tile(left, dens_i, right, dens_j, *bufs)
            field[pl.ds(kb, 1), :] += rows
            for d, back in enumerate(backs):

                @pl.when(way == d)
                def _():
                    back[pl.ds(first + t, 1), :] = cols

        return 0

    lax.fori_loop(0, len(got) * SLOTS, step, 0)


def direct_kernel(near_ref, start, *refs, ways):
    got, (field, *backs), scratch = refs[:ways], refs[ways : 2 * ways + 1], refs[2 * ways + 1 :]
    field[...] = start[...]
    for back in backs:
        back[...] = jnp.zeros_like(back)
    near_tiles(near_ref, got, field, backs, 0, *scratch)


def late_kernel(pairs, count, near_ref, start, row_in, own_in, *refs, n_row, direct, late):
    refs = list(refs)
    take = lambda n: [refs.pop(0) for _ in range(n)]
    got, backs = take(n_row - 1), take(len(direct))
    field, rows_out, cols_out, *messages = take(n_row + 2)
    near_scratch, far_scratch = take(len(NEAR_SCRATCH) + 3), refs
    nfar = cols_out.shape[0]
    field[...] = start[...]
    for message in messages:
        message[nfar:, :] = jnp.zeros((8, BLK), jnp.float32)
    for d, back in zip(direct, backs):
        messages[d - 1][nfar:, :] = back[...]
    back_to = [messages[d - 1] for d in late]
    near_tiles(near_ref, [got[d - 1] for d in late], field, back_to, nfar, *near_scratch)
    base = near_lines(SLOTS, near_ref.shape[1] // 4 - 2)
    far_tiles(pairs, count, row_in, own_in, got, rows_out, cols_out, *far_scratch, base)
    for message in messages:
        message[0:nfar, :] = cols_out[...]


def final_kernel(*refs, n_row, n_col, base):
    refs = list(refs)
    take = lambda n: [refs.pop(0) for _ in range(n)]
    pairs, weight, near, row_far, own_far = take(5)
    col_far, rows, (own_cols,), messages = take(n_row - 1), take(n_col // 2), take(1), take(n_row - 1)
    out, field = refs
    blocks, nfar = weight.shape[0], own_cols.shape[0]
    my_row, my_col = lax.axis_index("row"), lax.axis_index("col")
    field[...] = near[...]
    for d, message in enumerate(messages):
        for t in range(pairs.shape[1] - 1):
            k = lax.rem(pairs[0, t + 1], blocks)
            field[pl.ds(k, 1), :] += message[nfar + t : nfar + t + 1, :]

    def hot(index, base):
        want = lax.broadcasted_iota(jnp.int32, (blocks, nfar), 0) + base * blocks
        return jnp.where(index[:, 0:nfar] == want.astype(jnp.float32), 1.0, 0.0)

    pick = [hot(row_far[d * (blocks + 1) + blocks, 0:1, :], my_col) for d in range(n_col)]
    pick += [hot(own_far[blocks, 1:2, :], my_row)]
    line = base + 4 * blocks + 1
    pick += [hot(other[line : line + 1, :], my_row) for other in col_far]
    pick = jnp.concatenate(pick * 3, axis=1).astype(jnp.bfloat16)
    slots = jnp.concatenate([r[...] for r in rows] + [own_cols[...]] + [m[0:nfar, :] for m in messages], axis=0)
    slots = jnp.concatenate(three(slots), axis=0).astype(jnp.bfloat16)
    far = jnp.dot(pick, slots, preferred_element_type=jnp.float32)
    total = field[...] + far * weight[...]
    for q in range(BLK // LANES):
        out[pl.ds(q, blocks, stride=BLK // LANES), :] = total[:, q * LANES : (q + 1) * LANES]


def f32(*shape):
    return jax.ShapeDtypeStruct(shape, jnp.float32)


def cost(micros):
    return pl.CostEstimate(flops=int(micros * 1.1e9), bytes_accessed=1 << 16, transcendentals=0)


def body(points, density, near_pairs, far_pairs, near_count, far_count, *, n_row, n_col):
    quad = points.shape[1]
    blocks = points.shape[2] // BLK
    nnear, nfar = near_pairs.shape[0], far_pairs.shape[0]
    depth, slots = 4 * quad, nnear - 1
    near_pairs, far_pairs = near_pairs.T, far_pairs.T

    def swap(x, axis, d):
        n = {"row": n_row, "col": n_col}[axis]
        return lax.ppermute(x, axis, [(i, i ^ d) for i in range(n)])

    def halves(n):
        return [1 << j for j in reversed(range(n.bit_length() - 1))]

    def row_gather(x):
        known = {0: x}
        for d in halves(n_row):
            known.update({k ^ d: swap(v, "row", d) for k, v in known.items()})
        return [known[k] for k in range(n_row)]

    def col_gather(x):
        for d in reversed(halves(n_col)):
            x = jnp.concatenate([x, swap(x, "col", d)], axis=0)
        return x

    base = near_lines(slots, quad)
    msg_rows = -(-(base + 4 * (blocks + 1)) // 8) * 8
    hbm = [pltpu.with_memory_space_constraint(x, pltpu.HBM) for x in (far_pairs, points, density.reshape(-1, LANES))]
    msg, far_own, near_own, weight = pl.pallas_call(
        prep_kernel,
        out_shape=(
            f32(msg_rows, BLK),
            f32(blocks + 1, 4, BLK),
            f32(blocks, depth + 8, BLK),
            f32(blocks, BLK),
        ),
        in_specs=[SMEM, SMEM, HBM, HBM, HBM],
        out_specs=(VMEM, VMEM, VMEM, VMEM),
        scratch_shapes=[
            pltpu.VMEM(far_pairs.shape, jnp.int32),
            pltpu.VMEM(points.shape, jnp.float32),
            pltpu.VMEM((density.shape[0] // LANES, LANES), jnp.float32),
            pltpu.SemaphoreType.DMA((QUARTERS + 2,)),
        ],
        compiler_params=PARAMS,
        cost_estimate=cost(1.2),
        name="prep",
    )(near_pairs, near_count, *hbm)
    got = row_gather(msg)[1:]
    row_far = col_gather(far_own)

    bufs = [
        pltpu.VMEM((quad * BLK, TERMS), jnp.bfloat16),
        pltpu.VMEM((TERMS, quad * BLK), jnp.bfloat16),
        pltpu.VMEM((BLK, LANES), jnp.float32),
        pltpu.VMEM((8, BLK), jnp.float32),
    ]
    near0 = pl.pallas_call(
        near_own_kernel,
        out_shape=f32(blocks, BLK),
        in_specs=[SMEM, SMEM, VMEM],
        out_specs=VMEM,
        scratch_shapes=bufs,
        compiler_params=PARAMS,
        cost_estimate=cost(5.0),
        name="near_own",
    )(near_pairs, near_count, near_own)

    def near_scratch(n):
        return [
            pltpu.VMEM((depth + 8, BLK), jnp.float32),
            pltpu.SMEM((n, 8, LANES), jnp.float32),
            pltpu.SemaphoreType.DMA((n,)),
        ] + bufs

    direct = [d for d in range(1, n_row) if d & (d - 1) == 0]
    late = [d for d in range(1, n_row) if d & (d - 1) != 0]
    field, *backs = pl.pallas_call(
        functools.partial(direct_kernel, ways=len(direct)),
        out_shape=[f32(blocks, BLK)] + [f32(8, BLK)] * len(direct),
        in_specs=[VMEM] * (len(direct) + 2),
        out_specs=[VMEM] * (len(direct) + 1),
        scratch_shapes=near_scratch(len(direct)),
        compiler_params=PARAMS,
        cost_estimate=cost(5.0),
        name="near_direct",
    )(near_own, near0, *[got[d - 1] for d in direct])
    field, far_rows, far_cols, *messages = pl.pallas_call(
        functools.partial(late_kernel, n_row=n_row, direct=direct, late=late),
        out_shape=[f32(blocks, BLK)] + [f32(nfar, BLK)] * 2 + [f32(nfar + 8, BLK)] * (n_row - 1),
        in_specs=[SMEM, SMEM] + [VMEM] * (4 + n_row - 1 + len(direct)),
        out_specs=[VMEM] * (n_row + 2),
        scratch_shapes=near_scratch(len(late))
        + [
            pltpu.VMEM((4, BLK), jnp.float32),
            pltpu.VMEM((BLK, TERMS), jnp.bfloat16),
            pltpu.VMEM((TERMS, BLK), jnp.bfloat16),
            pltpu.VMEM((BLK, LANES), jnp.float32),
        ],
        compiler_params=PARAMS,
        cost_estimate=cost(8.0),
        name="late",
    )(far_pairs, far_count, near_own, field, row_far, far_own, *got, *backs)

    messages = [swap(x, "row", d + 1) for d, x in enumerate(messages)]
    both = jnp.concatenate([far_rows, swap(far_rows, "col", 1)], axis=0)
    rows = [both] + [swap(both, "col", d) for d in range(2, n_col, 2)]
    args = [weight, field, row_far, far_own, *got, *rows, far_cols, *messages]
    out = pl.pallas_call(
        functools.partial(final_kernel, n_row=n_row, n_col=n_col, base=base),
        out_shape=f32(blocks * BLK // LANES, LANES),
        in_specs=[SMEM] + [VMEM] * len(args),
        out_specs=VMEM,
        scratch_shapes=[pltpu.VMEM((blocks, BLK), jnp.float32)],
        compiler_params=PARAMS,
        name="final",
    )(near_pairs, *args)
    return out.reshape(-1)


def solution(mesh):
    in_specs = (
        P(None, None, ("row", "col")),
        P(("row", "col")),
        P(("row", "col"), None),
        P(("row", "col"), None),
        P(("row", "col")),
        P(("row", "col")),
    )
    out_specs = P(("row", "col"))
    kernel = functools.partial(body, n_row=mesh.shape["row"], n_col=mesh.shape["col"])
    return jax.shard_map(kernel, mesh=mesh, in_specs=in_specs, out_specs=out_specs, check_vma=False)
```

```python
import functools

import jax
import jax.numpy as jnp
from jax import lax
from jax.experimental import pallas as pl
from jax.experimental.pallas import tpu as pltpu
from jax.sharding import PartitionSpec as P

BLK = 512
LANES = 128
SOFT_SQ = 0.0004
TERMS = 64
SPLIT = 48
HALF = 512
QUARTERS = 4
SLOTS = 5
NEAR_SCRATCH = 4 * [None]
GROUP = 16
CHUNK = 512
VMEM = pl.BlockSpec(memory_space=pltpu.VMEM)
SMEM = pl.BlockSpec(memory_space=pltpu.SMEM)
ANY = pl.BlockSpec(memory_space=pl.ANY)
HBM = pl.BlockSpec(memory_space=pltpu.HBM)
PARAMS = pltpu.CompilerParams(vmem_limit_bytes=40 * 1024 * 1024)


def prep_kernel(near_hbm, count, far_hbm, pts_hbm, dens_hbm, msg, far_out, near_out, weight_out, *scratch):
    near_ref, far_ref, pts_ref, dens_ref, sems = scratch
    blocks = near_out.shape[0]
    quad = pts_ref.shape[1]
    slots, body = near_ref.shape[1] - 1, quad * 4
    base = near_lines(slots, quad)
    width = pts_ref.shape[2] // QUARTERS
    copies = [
        pltpu.make_async_copy(dens_hbm, dens_ref, sems.at[QUARTERS]),
        pltpu.make_async_copy(far_hbm, far_ref, sems.at[QUARTERS + 1]),
        pltpu.make_async_copy(near_hbm, near_ref, sems.at[QUARTERS + 2]),
    ]
    for i in range(QUARTERS):
        part = slice(i * width, (i + 1) * width)
        copies.append(pltpu.make_async_copy(pts_hbm.at[:, :, part], pts_ref.at[:, :, part], sems.at[i]))
    for copy in copies:
        copy.start()
    copies.pop(0).wait()
    copies.pop(0).wait()
    copies.pop(0).wait()

    def put_far(k, value):
        far_out[k] = value
        msg[base + 4 * k : base + 4 * k + 4, :] = value

    for k in range(blocks):
        cols = slice(k * BLK, (k + 1) * BLK)
        if k % (blocks // QUARTERS) == 0:
            copies.pop(0).wait()
        w = pts_ref[3, :, cols]
        total = jnp.sum(w, axis=0, keepdims=True)
        dens = jnp.concatenate([dens_ref[4 * k + q : 4 * k + q + 1, :] for q in range(4)], axis=1)
        lines = []
        for c in range(3):
            x = pts_ref[c, :, cols]
            lines.append(jnp.sum(x * w, axis=0, keepdims=True) / total)
            near_out[k, quad * c : quad * c + quad, :] = x
        near_out[k, quad * 3 : quad * 4, :] = w
        near_out[k, quad * 4 : quad * 4 + 8, :] = jnp.broadcast_to(dens, (8, BLK))
        put_far(k, jnp.concatenate(lines + [total * dens], axis=0))
        weight_out[k : k + 1, :] = total
    pairs = jnp.concatenate([far_ref[...].astype(jnp.float32), jnp.full((2, LANES - far_ref.shape[1]), -1.0)], axis=1)
    pairs = jnp.concatenate([pairs] * (BLK // LANES), axis=1)
    put_far(blocks, jnp.concatenate([pairs, jnp.zeros((2, BLK), jnp.float32)], axis=0))
    lane = lax.broadcasted_iota(jnp.int32, (1, BLK), 1)
    line = jnp.full((1, BLK), -1.0, jnp.float32)
    for t in range(slots):
        k = lax.rem(near_ref[0, t + 1], blocks)
        msg[t * body : (t + 1) * body, :] = near_out[k, 0:body, :]
        msg[slots * body + t : slots * body + t + 1, :] = near_out[k, body : body + 1, :]
        source = jnp.where(t + 1 < count[0], near_ref[1, t + 1], -1)
        line = jnp.where(lane == t, source.astype(jnp.float32), line)
    first = slots * (body + 1)
    msg[first:base, :] = jnp.broadcast_to(line, (base - first, BLK))


def near_lines(slots, quad):
    return -(-(slots * (4 * quad + 1) + 1) // 8) * 8


def three(value):
    one = value.astype(jnp.bfloat16).astype(jnp.float32)
    two = (value - one).astype(jnp.bfloat16).astype(jnp.float32)
    return one, two, value - one - two


def pick_row(row, values):
    out = jnp.zeros(row.shape, jnp.float32)
    for k, value in enumerate(values):
        out = jnp.where(row == k, value, out)
    return out


def parts(x):
    row = lax.broadcasted_iota(jnp.int32, x.shape, 0)
    live = row < 3
    centred = jnp.where(live, x - 0.5, 0.0)
    head = jnp.round(centred * 256.0) * (1.0 / 256.0)
    rest = centred - head
    rest1 = rest.astype(jnp.bfloat16).astype(jnp.float32)
    big = pick_row(row, three(jnp.sum(head * head, axis=0, keepdims=True)))
    small = pick_row(row, three(jnp.sum(rest * (2.0 * head + rest), axis=0, keepdims=True) + 0.5 * SOFT_SQ))
    return head, rest1, rest - rest1, big, small, jnp.where(live, 1.0, 0.0)


def left_terms(x, columns):
    head, rest1, rest2, big, small, ones = parts(x)
    h2, a2, b2 = -2.0 * head, -2.0 * rest1, -2.0 * rest2
    groups = [h2, big, ones, small, ones, h2, h2, a2, b2, a2, a2, b2]
    row = lax.broadcasted_iota(jnp.int32, (TERMS - SPLIT, x.shape[1]), 0)
    groups.append(pick_row(row, [part for column in columns for part in three(column)]))
    return jnp.concatenate(groups, axis=0)


def right_terms(x):
    head, rest1, rest2, big, small, ones = parts(x)
    groups = [head, ones, big, ones, small, rest1, rest2, head, head, rest1, rest2, rest1]
    groups.append(jnp.zeros((TERMS - SPLIT, x.shape[1]), jnp.float32))
    return jnp.concatenate(groups, axis=0).astype(jnp.bfloat16)


def column_of(lhs, which):
    row = lax.broadcasted_iota(jnp.int32, (TERMS, LANES), 0) - SPLIT - 3 * which
    pick = jnp.where((row >= 0) & (row < 3), 1.0, 0.0).astype(jnp.bfloat16)
    return jnp.dot(lhs, pick, preferred_element_type=jnp.float32)


def fold_lanes(tile, row):
    part = tile[:, :LANES] * row[:, :LANES]
    for q in range(1, tile.shape[1] // LANES):
        part = part + tile[:, q * LANES : (q + 1) * LANES] * row[:, q * LANES : (q + 1) * LANES]
    return part


def twice(col):
    return jnp.concatenate([col] * (HALF // LANES), axis=1)


def place(x, n):
    bits = n.bit_length() - 1
    div, rem = (lambda a, b: a // b, lambda a, b: a % b) if isinstance(x, int) else (lax.div, lax.rem)
    return sum(rem(div(x, 1 << (bits - 1 - j)), 2) * (1 << j) for j in range(bits))


def far_tiles(pairs, count, row_in, own_in, col_in, rows_out, cols_out, right_buf, lhs_buf, rhs_buf, part_buf, base):
    blocks = own_in.shape[0] - 1
    rows_out[...] = jnp.zeros_like(rows_out)
    cols_out[...] = jnp.zeros_like(cols_out)
    my_row, my_col = lax.axis_index("row"), lax.axis_index("col")

    def step(s, _):
        a, b = pairs[0, s], pairs[1, s]
        a_way, b_way = jnp.bitwise_xor(lax.div(a, blocks), my_col), jnp.bitwise_xor(lax.div(b, blocks), my_row)
        ka, kb = lax.rem(a, blocks), lax.rem(b, blocks)
        same = (a_way == 0) & (b_way == 0) & (ka == kb)

        @pl.when(b_way == 0)
        def _():
            right_buf[...] = own_in[kb]

        for d, other in enumerate(col_in):

            @pl.when(b_way == d + 1)
            def _():
                lines = [other[pl.ds(base + 4 * kb + c, 1), :] for c in range(4)]
                right_buf[...] = jnp.concatenate(lines, axis=0)

        left, right = row_in[place(a_way, row_in.shape[0] // (blocks + 1)) * (blocks + 1) + ka], right_buf[...]
        lhs_buf[...] = jnp.transpose(left_terms(left, [left[3:4]])).astype(jnp.bfloat16)
        rhs_buf[...] = right_terms(right)
        lhs = lhs_buf[...]
        zcol = column_of(lhs, 0)
        total = []
        for h in range(BLK // HALF):
            cols = slice(h * HALF, (h + 1) * HALF)
            dist = jnp.dot(lhs, rhs_buf[:, cols], preferred_element_type=jnp.float32)
            acc = jnp.zeros((8, HALF), jnp.float32)
            for g in range(BLK // 8):
                rows = slice(g * 8, (g + 1) * 8)
                tile = lax.rsqrt(dist[rows, :])
                part = fold_lanes(tile, right[3:4, cols])
                part_buf[rows, :] = part if h == 0 else part_buf[rows, :] + part
                acc = acc + tile * twice(zcol[rows, :])
            total.append(jnp.sum(acc, axis=0, keepdims=True))
        rows_out[pl.ds(s, 1), :] = jnp.sum(jnp.transpose(part_buf[...]), axis=0, keepdims=True)
        cols_out[pl.ds(s, 1), :] = jnp.concatenate(total, axis=1) * jnp.where(same, 0.0, 1.0)
        return 0

    lax.fori_loop(0, count[0], step, 0)


def points(tall):
    quad = tall.shape[0] // 4
    sides = [[tall[quad * c + u : quad * c + u + 1, :] for c in range(4)] for u in range(quad)]
    return jnp.concatenate([jnp.concatenate(side, axis=0) for side in sides], axis=1)


def near_tile(left, dens_i, right, dens_j, lhs_buf, rhs_buf, part_buf, acc_buf):
    quad = left.shape[1] // BLK
    terms = jnp.transpose(left_terms(left, [left[3:4], jnp.concatenate([dens_i] * quad, axis=1)]))
    terms = terms.astype(jnp.bfloat16)
    for g in range(BLK // GROUP):
        for u in range(quad):
            to, at = (g * quad + u) * GROUP, u * BLK + g * GROUP
            lhs_buf[to : to + GROUP, :] = terms[at : at + GROUP, :]
    rhs_buf[...] = right_terms(right)
    weights = right[3:4]
    acc_buf[...] = jnp.zeros_like(acc_buf)

    def chunk(i, _):
        at = pl.multiple_of(i * CHUNK * quad, CHUNK * quad)
        lhs = lhs_buf[pl.ds(at, CHUNK * quad), :]
        wcol = column_of(lhs, 0)
        groups = CHUNK // GROUP
        first_rows = [lhs[g * quad * GROUP : g * quad * GROUP + GROUP, :] for g in range(groups)]
        dcol = column_of(jnp.concatenate(first_rows, axis=0), 1)
        part = None
        for h in range(BLK // HALF):
            tiles = [None] * groups
            for v in range(quad):
                cols = slice(v * BLK + h * HALF, v * BLK + (h + 1) * HALF)
                dist = jnp.dot(lhs, rhs_buf[:, cols], preferred_element_type=jnp.float32)
                for g in range(groups):
                    inner = None
                    for u in range(quad):
                        rows = slice((g * quad + u) * GROUP, (g * quad + u + 1) * GROUP)
                        term = lax.rsqrt(dist[rows, :]) * twice(wcol[rows, :])
                        inner = term if inner is None else inner + term
                    inner = inner * weights[:, cols]
                    tiles[g] = inner if tiles[g] is None else tiles[g] + inner
            tile = jnp.concatenate(tiles, axis=0)
            cols = slice(h * HALF, (h + 1) * HALF)
            more = fold_lanes(tile, dens_j[:, cols])
            part = more if part is None else part + more
            acc_buf[:, cols] += jnp.sum((tile * twice(dcol)).reshape(-1, 8, HALF), axis=0)
        part_buf[pl.ds(pl.multiple_of(i * CHUNK, CHUNK), CHUNK), :] = part
        return 0

    lax.fori_loop(0, BLK // CHUNK, chunk, 0)
    rows = jnp.sum(jnp.transpose(part_buf[...]), axis=0, keepdims=True)
    return rows, jnp.sum(acc_buf[...], axis=0, keepdims=True)


def near_own_kernel(pairs, count, near_ref, field, *bufs):
    blocks, depth, _ = near_ref.shape
    body = depth - 8
    my_row = lax.axis_index("row")
    field[...] = jnp.zeros_like(field)

    def step(s, _):
        ka, kb = lax.rem(pairs[0, s], blocks), pairs[1, s] - my_row * blocks

        @pl.when((kb >= 0) & (kb < blocks))
        def _():
            left, right = points(near_ref[ka, 0:body, :]), points(near_ref[kb, 0:body, :])
            dens_i, dens_j = near_ref[ka, body : body + 1, :], near_ref[kb, body : body + 1, :]
            rows, cols = near_tile(left, dens_i, right, dens_j, *bufs)
            field[pl.ds(ka, 1), :] += rows
            field[pl.ds(kb, 1), :] += cols * jnp.where(ka == kb, 0.0, 1.0)

        return 0

    lax.fori_loop(0, count[0], step, 0)


def near_tiles(near_ref, got, field, backs, first, right_buf, tags, sems, *bufs):
    blocks, depth, _ = near_ref.shape
    body = depth - 8
    base = near_lines(SLOTS, body // 4)
    my_row = lax.axis_index("row")
    copies = [
        pltpu.make_async_copy(g.at[base - 8 : base, 0:LANES], tags.at[d], sems.at[d]) for d, g in enumerate(got)
    ]
    for copy in copies:
        copy.start()
    for copy in copies:
        copy.wait()

    def step(i, _):
        way, t = lax.div(i, SLOTS), lax.rem(i, SLOTS)
        kb = tags[way, 7, t].astype(jnp.int32) - my_row * blocks

        @pl.when((kb >= 0) & (kb < blocks))
        def _():
            for d, other in enumerate(got):

                @pl.when(way == d)
                def _():
                    at = pl.multiple_of(t * body, 8)
                    right_buf[0:body, :] = other[pl.ds(at, body), :]
                    right_buf[body : body + 1, :] = other[pl.ds(SLOTS * body + t, 1), :]

            left, right = points(near_ref[kb, 0:body, :]), points(right_buf[0:body, :])
            dens_i, dens_j = near_ref[kb, body : body + 1, :], right_buf[body : body + 1, :]
            rows, cols = near_tile(left, dens_i, right, dens_j, *bufs)
            field[pl.ds(kb, 1), :] += rows
            for d, back in enumerate(backs):

                @pl.when(way == d)
                def _():
                    back[pl.ds(first + t, 1), :] = cols

        return 0

    lax.fori_loop(0, len(got) * SLOTS, step, 0)


def direct_kernel(near_ref, start, *refs, ways):
    got, (field, *backs), scratch = refs[:ways], refs[ways : 2 * ways + 1], refs[2 * ways + 1 :]
    field[...] = start[...]
    for back in backs:
        back[...] = jnp.zeros_like(back)
    near_tiles(near_ref, got, field, backs, 0, *scratch)


def late_kernel(pairs, count, near_ref, start, row_in, own_in, *refs, n_row, direct, late):
    refs = list(refs)
    take = lambda n: [refs.pop(0) for _ in range(n)]
    got, backs = take(n_row - 1), take(len(direct))
    field, rows_out, cols_out, *messages = take(n_row + 2)
    near_scratch, far_scratch = take(len(NEAR_SCRATCH) + 3), refs
    nfar = cols_out.shape[0]
    field[...] = start[...]
    for message in messages:
        message[nfar:, :] = jnp.zeros((8, BLK), jnp.float32)
    for d, back in zip(direct, backs):
        messages[d - 1][nfar:, :] = back[...]
    back_to = [messages[d - 1] for d in late]
    near_tiles(near_ref, [got[d - 1] for d in late], field, back_to, nfar, *near_scratch)
    base = near_lines(SLOTS, near_ref.shape[1] // 4 - 2)
    far_tiles(pairs, count, row_in, own_in, got, rows_out, cols_out, *far_scratch, base)
    for message in messages:
        message[0:nfar, :] = cols_out[...]


def hot(index, blocks, slots, base):
    want = lax.broadcasted_iota(jnp.int32, (blocks, slots), 0) + base * blocks
    return jnp.where(index[:, 0:slots] == want.astype(jnp.float32), 1.0, 0.0)


def spread(pick, slots, weight):
    pick = jnp.concatenate(pick * 3, axis=1).astype(jnp.bfloat16)
    slots = jnp.concatenate(three(jnp.concatenate(slots, axis=0)), axis=0).astype(jnp.bfloat16)
    return jnp.dot(pick, slots, preferred_element_type=jnp.float32) * weight[...]


def cols_kernel(pairs, weight, near, own_far, own_cols, *refs, n_row, base):
    col_far, messages, field = refs[: n_row - 1], refs[n_row - 1 : -1], refs[-1]
    blocks, nfar = weight.shape[0], own_cols.shape[0]
    my_row = lax.axis_index("row")
    line = base + 4 * blocks + 1
    pick = [hot(own_far[blocks, 1:2, :], blocks, nfar, my_row)]
    pick += [hot(other[line : line + 1, :], blocks, nfar, my_row) for other in col_far]
    field[...] = near[...] + spread(pick, [own_cols[...]] + [m[0:nfar, :] for m in messages], weight)
    for message in messages:
        for t in range(pairs.shape[1] - 1):
            k = lax.rem(pairs[0, t + 1], blocks)
            field[pl.ds(k, 1), :] += message[nfar + t : nfar + t + 1, :]


def rows_kernel(weight, field, row_far, *refs, n_col):
    rows, out = refs[:-1], refs[-1]
    blocks, nfar = weight.shape[0], rows[0].shape[0] // 2
    my_col = lax.axis_index("col")
    tags = [place(d, n_col) * (blocks + 1) + blocks for d in range(n_col)]
    pick = [hot(row_far[tag, 0:1, :], blocks, nfar, my_col) for tag in tags]
    total = field[...] + spread(pick, [r[...] for r in rows], weight)
    for q in range(BLK // LANES):
        out[pl.ds(q, blocks, stride=BLK // LANES), :] = total[:, q * LANES : (q + 1) * LANES]


def f32(*shape):
    return jax.ShapeDtypeStruct(shape, jnp.float32)


def cost(micros):
    return pl.CostEstimate(flops=int(micros * 1.1e9), bytes_accessed=1 << 16, transcendentals=0)


def body(points, density, near_pairs, far_pairs, near_count, far_count, *, n_row, n_col):
    quad = points.shape[1]
    blocks = points.shape[2] // BLK
    nnear, nfar = near_pairs.shape[0], far_pairs.shape[0]
    depth, slots = 4 * quad, nnear - 1
    near_pairs, far_pairs = near_pairs.T, far_pairs.T

    def swap(x, axis, d):
        n = {"row": n_row, "col": n_col}[axis]
        return lax.ppermute(x, axis, [(i, i ^ d) for i in range(n)])

    def halves(n):
        return [1 << j for j in reversed(range(n.bit_length() - 1))]

    def row_gather(x):
        known = {0: x}
        for d in halves(n_row):
            known.update({k ^ d: swap(v, "row", d) for k, v in known.items()})
        return [known[k] for k in range(n_row)]

    def col_gather(x):
        steps = [x]
        for d in halves(n_col):
            steps.append(jnp.concatenate([steps[-1], swap(steps[-1], "col", d)], axis=0))
        return steps[-1], steps[-2]

    base = near_lines(slots, quad)
    msg_rows = -(-(base + 4 * (blocks + 1)) // 8) * 8
    hbm = (near_pairs, far_pairs, points, density.reshape(-1, LANES))
    hbm = [pltpu.with_memory_space_constraint(x, pltpu.HBM) for x in hbm]
    msg, far_own, near_own, weight = pl.pallas_call(
        prep_kernel,
        out_shape=(
            f32(msg_rows, BLK),
            f32(blocks + 1, 4, BLK),
            f32(blocks, depth + 8, BLK),
            f32(blocks, BLK),
        ),
        in_specs=[HBM, SMEM, HBM, HBM, HBM],
        out_specs=(VMEM, VMEM, VMEM, VMEM),
        scratch_shapes=[
            pltpu.SMEM(near_pairs.shape, jnp.int32),
            pltpu.VMEM(far_pairs.shape, jnp.int32),
            pltpu.VMEM(points.shape, jnp.float32),
            pltpu.VMEM((density.shape[0] // LANES, LANES), jnp.float32),
            pltpu.SemaphoreType.DMA((QUARTERS + 3,)),
        ],
        compiler_params=PARAMS,
        cost_estimate=cost(1.2),
        name="prep",
    )(hbm[0], near_count, *hbm[1:])
    got = row_gather(msg)[1:]
    row_far, row_part = col_gather(far_own)

    bufs = [
        pltpu.VMEM((quad * BLK, TERMS), jnp.bfloat16),
        pltpu.VMEM((TERMS, quad * BLK), jnp.bfloat16),
        pltpu.VMEM((BLK, LANES), jnp.float32),
        pltpu.VMEM((8, BLK), jnp.float32),
    ]
    near0 = pl.pallas_call(
        near_own_kernel,
        out_shape=f32(blocks, BLK),
        in_specs=[SMEM, SMEM, VMEM],
        out_specs=VMEM,
        scratch_shapes=bufs,
        compiler_params=PARAMS,
        cost_estimate=cost(5.0),
        name="near_own",
    )(near_pairs, near_count, near_own)

    def near_scratch(n):
        return [
            pltpu.VMEM((depth + 8, BLK), jnp.float32),
            pltpu.SMEM((n, 8, LANES), jnp.float32),
            pltpu.SemaphoreType.DMA((n,)),
        ] + bufs

    direct = [d for d in range(1, n_row) if d & (d - 1) == 0]
    late = [d for d in range(1, n_row) if d & (d - 1) != 0]
    field, *backs = pl.pallas_call(
        functools.partial(direct_kernel, ways=len(direct)),
        out_shape=[f32(blocks, BLK)] + [f32(8, BLK)] * len(direct),
        in_specs=[VMEM] * (len(direct) + 2),
        out_specs=[VMEM] * (len(direct) + 1),
        scratch_shapes=near_scratch(len(direct)),
        compiler_params=PARAMS,
        cost_estimate=cost(5.0),
        name="near_direct",
    )(near_own, near0, *[got[d - 1] for d in direct])
    field, far_rows, far_cols, *messages = pl.pallas_call(
        functools.partial(late_kernel, n_row=n_row, direct=direct, late=late),
        out_shape=[f32(blocks, BLK)] + [f32(nfar, BLK)] * 2 + [f32(nfar + 8, BLK)] * (n_row - 1),
        in_specs=[SMEM, SMEM] + [VMEM] * (4 + n_row - 1 + len(direct)),
        out_specs=[VMEM] * (n_row + 2),
        scratch_shapes=near_scratch(len(late))
        + [
            pltpu.VMEM((4, BLK), jnp.float32),
            pltpu.VMEM((BLK, TERMS), jnp.bfloat16),
            pltpu.VMEM((TERMS, BLK), jnp.bfloat16),
            pltpu.VMEM((BLK, LANES), jnp.float32),
        ],
        compiler_params=PARAMS,
        cost_estimate=cost(8.0),
        name="late",
    )(far_pairs, far_count, near_own, field, row_far, far_own, *got, *backs)

    messages = [swap(x, "row", d + 1) for d, x in enumerate(messages)]
    both = jnp.concatenate([far_rows, swap(far_rows, "col", 1)], axis=0)
    rows = [both] + [swap(both, "col", d) for d in range(2, n_col, 2)]
    field = pl.pallas_call(
        functools.partial(cols_kernel, n_row=n_row, base=base),
        out_shape=f32(blocks, BLK),
        in_specs=[SMEM] + [VMEM] * (2 * n_row + 2),
        out_specs=VMEM,
        compiler_params=PARAMS,
        cost_estimate=cost(1.0),
        name="final_cols",
    )(near_pairs, weight, field, far_own, far_cols, *got, *messages)
    out = pl.pallas_call(
        functools.partial(rows_kernel, n_col=n_col),
        out_shape=f32(blocks * BLK // LANES, LANES),
        in_specs=[VMEM] * (3 + len(rows)),
        out_specs=VMEM,
        compiler_params=PARAMS,
        cost_estimate=cost(1.0),
        name="final_rows",
    )(weight, field, row_far, *rows)
    return out.reshape(-1)


def solution(mesh):
    in_specs = (
        P(None, None, ("row", "col")),
        P(("row", "col")),
        P(("row", "col"), None),
        P(("row", "col"), None),
        P(("row", "col")),
        P(("row", "col")),
    )
    out_specs = P(("row", "col"))
    kernel = functools.partial(body, n_row=mesh.shape["row"], n_col=mesh.shape["col"])
    return jax.shard_map(kernel, mesh=mesh, in_specs=in_specs, out_specs=out_specs, check_vma=False)
```

```python
import functools

import jax
import jax.numpy as jnp
from jax import lax
from jax.experimental import pallas as pl
from jax.experimental.pallas import tpu as pltpu
from jax.sharding import PartitionSpec as P

BLK = 512
LANES = 128
SOFT_SQ = 0.0004
TERMS = 64
SPLIT = 48
HALF = 512
QUARTERS = 4
SLOTS = 5
NEAR_SCRATCH = 4 * [None]
GROUP = 16
CHUNK = 512
VMEM = pl.BlockSpec(memory_space=pltpu.VMEM)
SMEM = pl.BlockSpec(memory_space=pltpu.SMEM)
ANY = pl.BlockSpec(memory_space=pl.ANY)
HBM = pl.BlockSpec(memory_space=pltpu.HBM)
PARAMS = pltpu.CompilerParams(vmem_limit_bytes=40 * 1024 * 1024)


def prep_kernel(near_hbm, count, far_hbm, pts_hbm, dens_hbm, msg, far_out, near_out, weight_out, *scratch):
    near_ref, far_ref, pts_ref, dens_ref, sems = scratch
    blocks = near_out.shape[0]
    quad = pts_ref.shape[1]
    slots, body = near_ref.shape[1] - 1, quad * 4
    base = near_lines(slots, quad)
    width = pts_ref.shape[2] // QUARTERS
    copies = [
        pltpu.make_async_copy(dens_hbm, dens_ref, sems.at[QUARTERS]),
        pltpu.make_async_copy(far_hbm, far_ref, sems.at[QUARTERS + 1]),
        pltpu.make_async_copy(near_hbm, near_ref, sems.at[QUARTERS + 2]),
    ]
    for i in range(QUARTERS):
        part = slice(i * width, (i + 1) * width)
        copies.append(pltpu.make_async_copy(pts_hbm.at[:, :, part], pts_ref.at[:, :, part], sems.at[i]))
    for copy in copies:
        copy.start()
    copies.pop(0).wait()
    copies.pop(0).wait()
    copies.pop(0).wait()

    def put_far(k, value):
        far_out[k] = value
        msg[base + 4 * k : base + 4 * k + 4, :] = value

    for k in range(blocks):
        cols = slice(k * BLK, (k + 1) * BLK)
        if k % (blocks // QUARTERS) == 0:
            copies.pop(0).wait()
        w = pts_ref[3, :, cols]
        total = jnp.sum(w, axis=0, keepdims=True)
        dens = jnp.concatenate([dens_ref[4 * k + q : 4 * k + q + 1, :] for q in range(4)], axis=1)
        lines = []
        for c in range(3):
            x = pts_ref[c, :, cols]
            lines.append(jnp.sum(x * w, axis=0, keepdims=True) / total)
            near_out[k, quad * c : quad * c + quad, :] = x
        near_out[k, quad * 3 : quad * 4, :] = w
        near_out[k, quad * 4 : quad * 4 + 8, :] = jnp.broadcast_to(dens, (8, BLK))
        put_far(k, jnp.concatenate(lines + [total * dens], axis=0))
        weight_out[k : k + 1, :] = total
    pairs = jnp.concatenate([far_ref[...].astype(jnp.float32), jnp.full((2, LANES - far_ref.shape[1]), -1.0)], axis=1)
    pairs = jnp.concatenate([pairs] * (BLK // LANES), axis=1)
    put_far(blocks, jnp.concatenate([pairs, jnp.zeros((2, BLK), jnp.float32)], axis=0))
    lane = lax.broadcasted_iota(jnp.int32, (1, BLK), 1)
    line = jnp.full((1, BLK), -1.0, jnp.float32)
    for t in range(slots):
        k = lax.rem(near_ref[0, t + 1], blocks)
        msg[t * body : (t + 1) * body, :] = near_out[k, 0:body, :]
        msg[slots * body + t : slots * body + t + 1, :] = near_out[k, body : body + 1, :]
        source = jnp.where(t + 1 < count[0], near_ref[1, t + 1], -1)
        line = jnp.where(lane == t, source.astype(jnp.float32), line)
    first = slots * (body + 1)
    msg[first:base, :] = jnp.broadcast_to(line, (base - first, BLK))


def near_lines(slots, quad):
    return -(-(slots * (4 * quad + 1) + 1) // 8) * 8


def three(value):
    one = value.astype(jnp.bfloat16).astype(jnp.float32)
    two = (value - one).astype(jnp.bfloat16).astype(jnp.float32)
    return one, two, value - one - two


def pick_row(row, values):
    out = jnp.zeros(row.shape, jnp.float32)
    for k, value in enumerate(values):
        out = jnp.where(row == k, value, out)
    return out


def parts(x):
    row = lax.broadcasted_iota(jnp.int32, x.shape, 0)
    live = row < 3
    centred = jnp.where(live, x - 0.5, 0.0)
    head = jnp.round(centred * 256.0) * (1.0 / 256.0)
    rest = centred - head
    rest1 = rest.astype(jnp.bfloat16).astype(jnp.float32)
    big = pick_row(row, three(jnp.sum(head * head, axis=0, keepdims=True)))
    small = pick_row(row, three(jnp.sum(rest * (2.0 * head + rest), axis=0, keepdims=True) + 0.5 * SOFT_SQ))
    return head, rest1, rest - rest1, big, small, jnp.where(live, 1.0, 0.0)


def left_terms(x, columns):
    head, rest1, rest2, big, small, ones = parts(x)
    h2, a2, b2 = -2.0 * head, -2.0 * rest1, -2.0 * rest2
    groups = [h2, big, ones, small, ones, h2, h2, a2, b2, a2, a2, b2]
    row = lax.broadcasted_iota(jnp.int32, (TERMS - SPLIT, x.shape[1]), 0)
    groups.append(pick_row(row, [part for column in columns for part in three(column)]))
    return jnp.concatenate(groups, axis=0)


def right_terms(x):
    head, rest1, rest2, big, small, ones = parts(x)
    groups = [head, ones, big, ones, small, rest1, rest2, head, head, rest1, rest2, rest1]
    groups.append(jnp.zeros((TERMS - SPLIT, x.shape[1]), jnp.float32))
    return jnp.concatenate(groups, axis=0).astype(jnp.bfloat16)


def column_of(lhs, which):
    row = lax.broadcasted_iota(jnp.int32, (TERMS, LANES), 0) - SPLIT - 3 * which
    pick = jnp.where((row >= 0) & (row < 3), 1.0, 0.0).astype(jnp.bfloat16)
    return jnp.dot(lhs, pick, preferred_element_type=jnp.float32)


def fold_lanes(tile, row):
    part = tile[:, :LANES] * row[:, :LANES]
    for q in range(1, tile.shape[1] // LANES):
        part = part + tile[:, q * LANES : (q + 1) * LANES] * row[:, q * LANES : (q + 1) * LANES]
    return part


def twice(col):
    return jnp.concatenate([col] * (HALF // LANES), axis=1)


def place(x, n):
    bits = n.bit_length() - 1
    div, rem = (lambda a, b: a // b, lambda a, b: a % b) if isinstance(x, int) else (lax.div, lax.rem)
    return sum(rem(div(x, 1 << (bits - 1 - j)), 2) * (1 << j) for j in range(bits))


def far_tiles(pairs, count, row_in, sources, rows_out, cols_out, right_buf, lhs_buf, rhs_buf, part_buf, base):
    row_step = row_in.shape[0] // lax.axis_size("col")
    blocks = row_step - 1
    my_row, my_col = lax.axis_index("row"), lax.axis_index("col")

    def step(s, _):
        a, b = pairs[0, s], pairs[1, s]
        a_way, b_way = jnp.bitwise_xor(lax.div(a, blocks), my_col), jnp.bitwise_xor(lax.div(b, blocks), my_row)
        here = functools.reduce(jnp.logical_or, [b_way == d for d in sources])
        pl.when(here)(lambda: tile(s, a_way, b_way, lax.rem(a, blocks), lax.rem(b, blocks)))
        return 0

    def tile(s, a_way, b_way, ka, kb):
        same = (a_way == 0) & (b_way == 0) & (ka == kb)
        for d, other in sources.items():

            @pl.when(b_way == d)
            def _():
                if d == 0:
                    right_buf[...] = other[kb]
                else:
                    lines = [other[pl.ds(base + 4 * kb + c, 1), :] for c in range(4)]
                    right_buf[...] = jnp.concatenate(lines, axis=0)

        left, right = row_in[place(a_way, lax.axis_size("col")) * row_step + ka], right_buf[...]
        lhs_buf[...] = jnp.transpose(left_terms(left, [left[3:4]])).astype(jnp.bfloat16)
        rhs_buf[...] = right_terms(right)
        lhs = lhs_buf[...]
        zcol = column_of(lhs, 0)
        total = []
        for h in range(BLK // HALF):
            cols = slice(h * HALF, (h + 1) * HALF)
            dist = jnp.dot(lhs, rhs_buf[:, cols], preferred_element_type=jnp.float32)
            acc = jnp.zeros((8, HALF), jnp.float32)
            for g in range(BLK // 8):
                rows = slice(g * 8, (g + 1) * 8)
                tile = lax.rsqrt(dist[rows, :])
                part = fold_lanes(tile, right[3:4, cols])
                part_buf[rows, :] = part if h == 0 else part_buf[rows, :] + part
                acc = acc + tile * twice(zcol[rows, :])
            total.append(jnp.sum(acc, axis=0, keepdims=True))
        rows_out[pl.ds(s, 1), :] = jnp.sum(jnp.transpose(part_buf[...]), axis=0, keepdims=True)
        cols_out[pl.ds(s, 1), :] = jnp.concatenate(total, axis=1) * jnp.where(same, 0.0, 1.0)

    lax.fori_loop(0, count[0], step, 0)


def points(tall):
    quad = tall.shape[0] // 4
    sides = [[tall[quad * c + u : quad * c + u + 1, :] for c in range(4)] for u in range(quad)]
    return jnp.concatenate([jnp.concatenate(side, axis=0) for side in sides], axis=1)


def near_tile(left, dens_i, right, dens_j, lhs_buf, rhs_buf, part_buf, acc_buf):
    quad = left.shape[1] // BLK
    terms = jnp.transpose(left_terms(left, [left[3:4], jnp.concatenate([dens_i] * quad, axis=1)]))
    terms = terms.astype(jnp.bfloat16)
    for g in range(BLK // GROUP):
        for u in range(quad):
            to, at = (g * quad + u) * GROUP, u * BLK + g * GROUP
            lhs_buf[to : to + GROUP, :] = terms[at : at + GROUP, :]
    rhs_buf[...] = right_terms(right)
    weights = right[3:4]
    acc_buf[...] = jnp.zeros_like(acc_buf)

    def chunk(i, _):
        at = pl.multiple_of(i * CHUNK * quad, CHUNK * quad)
        lhs = lhs_buf[pl.ds(at, CHUNK * quad), :]
        wcol = column_of(lhs, 0)
        groups = CHUNK // GROUP
        first_rows = [lhs[g * quad * GROUP : g * quad * GROUP + GROUP, :] for g in range(groups)]
        dcol = column_of(jnp.concatenate(first_rows, axis=0), 1)
        part = None
        for h in range(BLK // HALF):
            tiles = [None] * groups
            for v in range(quad):
                cols = slice(v * BLK + h * HALF, v * BLK + (h + 1) * HALF)
                dist = jnp.dot(lhs, rhs_buf[:, cols], preferred_element_type=jnp.float32)
                for g in range(groups):
                    inner = None
                    for u in range(quad):
                        rows = slice((g * quad + u) * GROUP, (g * quad + u + 1) * GROUP)
                        term = lax.rsqrt(dist[rows, :]) * twice(wcol[rows, :])
                        inner = term if inner is None else inner + term
                    inner = inner * weights[:, cols]
                    tiles[g] = inner if tiles[g] is None else tiles[g] + inner
            tile = jnp.concatenate(tiles, axis=0)
            cols = slice(h * HALF, (h + 1) * HALF)
            more = fold_lanes(tile, dens_j[:, cols])
            part = more if part is None else part + more
            acc_buf[:, cols] += jnp.sum((tile * twice(dcol)).reshape(-1, 8, HALF), axis=0)
        part_buf[pl.ds(pl.multiple_of(i * CHUNK, CHUNK), CHUNK), :] = part
        return 0

    lax.fori_loop(0, BLK // CHUNK, chunk, 0)
    rows = jnp.sum(jnp.transpose(part_buf[...]), axis=0, keepdims=True)
    return rows, jnp.sum(acc_buf[...], axis=0, keepdims=True)


def near_own_kernel(pairs, count, near_ref, field, *bufs):
    blocks, depth, _ = near_ref.shape
    body = depth - 8
    my_row = lax.axis_index("row")
    field[...] = jnp.zeros_like(field)

    def step(s, _):
        ka, kb = lax.rem(pairs[0, s], blocks), pairs[1, s] - my_row * blocks

        @pl.when((kb >= 0) & (kb < blocks))
        def _():
            left, right = points(near_ref[ka, 0:body, :]), points(near_ref[kb, 0:body, :])
            dens_i, dens_j = near_ref[ka, body : body + 1, :], near_ref[kb, body : body + 1, :]
            rows, cols = near_tile(left, dens_i, right, dens_j, *bufs)
            field[pl.ds(ka, 1), :] += rows
            field[pl.ds(kb, 1), :] += cols * jnp.where(ka == kb, 0.0, 1.0)

        return 0

    lax.fori_loop(0, count[0], step, 0)


def near_tiles(near_ref, got, field, backs, first, right_buf, tags, sems, *bufs):
    blocks, depth, _ = near_ref.shape
    body = depth - 8
    base = near_lines(SLOTS, body // 4)
    my_row = lax.axis_index("row")
    copies = [
        pltpu.make_async_copy(g.at[base - 8 : base, 0:LANES], tags.at[d], sems.at[d]) for d, g in enumerate(got)
    ]
    for copy in copies:
        copy.start()
    for copy in copies:
        copy.wait()

    def step(i, _):
        way, t = lax.div(i, SLOTS), lax.rem(i, SLOTS)
        kb = tags[way, 7, t].astype(jnp.int32) - my_row * blocks

        @pl.when((kb >= 0) & (kb < blocks))
        def _():
            for d, other in enumerate(got):

                @pl.when(way == d)
                def _():
                    at = pl.multiple_of(t * body, 8)
                    right_buf[0:body, :] = other[pl.ds(at, body), :]
                    right_buf[body : body + 1, :] = other[pl.ds(SLOTS * body + t, 1), :]

            left, right = points(near_ref[kb, 0:body, :]), points(right_buf[0:body, :])
            dens_i, dens_j = near_ref[kb, body : body + 1, :], right_buf[body : body + 1, :]
            rows, cols = near_tile(left, dens_i, right, dens_j, *bufs)
            field[pl.ds(kb, 1), :] += rows
            for d, back in enumerate(backs):

                @pl.when(way == d)
                def _():
                    back[pl.ds(first + t, 1), :] = cols

        return 0

    lax.fori_loop(0, len(got) * SLOTS, step, 0)


def direct_kernel(near_ref, start, *refs, ways):
    got, (field, *backs), scratch = refs[:ways], refs[ways : 2 * ways + 1], refs[2 * ways + 1 :]
    field[...] = start[...]
    for back in backs:
        back[...] = jnp.zeros_like(back)
    near_tiles(near_ref, got, field, backs, 0, *scratch)


def far_kernel(pairs, count, row_in, own_in, *refs, direct, base):
    got, (rows_out, cols_out), scratch = refs[: len(direct)], refs[len(direct) : -4], refs[-4:]
    rows_out[...] = jnp.zeros_like(rows_out)
    cols_out[...] = jnp.zeros_like(cols_out)
    far_tiles(pairs, count, row_in, {0: own_in, **dict(zip(direct, got))}, rows_out, cols_out, *scratch, base)


def late_kernel(pairs, count, near_ref, start, row_in, rows_in, cols_in, *refs, n_row, direct, late):
    refs = list(refs)
    take = lambda n: [refs.pop(0) for _ in range(n)]
    got, backs = take(len(late)), take(len(direct))
    field, rows_out, cols_out, *messages = take(n_row + 2)
    near_scratch, far_scratch = take(len(NEAR_SCRATCH) + 3), refs
    nfar = cols_out.shape[0]
    field[...] = start[...]
    rows_out[...] = rows_in[...]
    cols_out[...] = cols_in[...]
    for message in messages:
        message[nfar:, :] = jnp.zeros((8, BLK), jnp.float32)
    for d, back in zip(direct, backs):
        messages[d - 1][nfar:, :] = back[...]
    near_tiles(near_ref, got, field, [messages[d - 1] for d in late], nfar, *near_scratch)
    base = near_lines(SLOTS, near_ref.shape[1] // 4 - 2)
    far_tiles(pairs, count, row_in, dict(zip(late, got)), rows_out, cols_out, *far_scratch, base)
    for message in messages:
        message[0:nfar, :] = cols_out[...]


def hot(index, blocks, slots, base):
    want = lax.broadcasted_iota(jnp.int32, (blocks, slots), 0) + base * blocks
    return jnp.where(index[:, 0:slots] == want.astype(jnp.float32), 1.0, 0.0)


def spread(pick, slots, weight):
    pick = jnp.concatenate(pick * 3, axis=1).astype(jnp.bfloat16)
    slots = jnp.concatenate(three(jnp.concatenate(slots, axis=0)), axis=0).astype(jnp.bfloat16)
    return jnp.dot(pick, slots, preferred_element_type=jnp.float32) * weight[...]


def cols_kernel(pairs, weight, near, own_far, own_cols, *refs, n_row, base):
    col_far, messages, field = refs[: n_row - 1], refs[n_row - 1 : -1], refs[-1]
    blocks, nfar = weight.shape[0], own_cols.shape[0]
    my_row = lax.axis_index("row")
    line = base + 4 * blocks + 1
    pick = [hot(own_far[blocks, 1:2, :], blocks, nfar, my_row)]
    pick += [hot(other[line : line + 1, :], blocks, nfar, my_row) for other in col_far]
    field[...] = near[...] + spread(pick, [own_cols[...]] + [m[0:nfar, :] for m in messages], weight)
    for message in messages:
        for t in range(pairs.shape[1] - 1):
            k = lax.rem(pairs[0, t + 1], blocks)
            field[pl.ds(k, 1), :] += message[nfar + t : nfar + t + 1, :]


def rows_kernel(weight, field, row_far, *refs, n_col):
    rows, out = refs[:-1], refs[-1]
    blocks, nfar = weight.shape[0], rows[0].shape[0] // 2
    my_col = lax.axis_index("col")
    tags = [place(d, n_col) * (blocks + 1) + blocks for d in range(n_col)]
    pick = [hot(row_far[tag, 0:1, :], blocks, nfar, my_col) for tag in tags]
    total = field[...] + spread(pick, [r[...] for r in rows], weight)
    for q in range(BLK // LANES):
        out[pl.ds(q, blocks, stride=BLK // LANES), :] = total[:, q * LANES : (q + 1) * LANES]


def f32(*shape):
    return jax.ShapeDtypeStruct(shape, jnp.float32)


def cost(micros):
    return pl.CostEstimate(flops=int(micros * 1.1e9), bytes_accessed=1 << 16, transcendentals=0)


def body(points, density, near_pairs, far_pairs, near_count, far_count, *, n_row, n_col):
    quad = points.shape[1]
    blocks = points.shape[2] // BLK
    nnear, nfar = near_pairs.shape[0], far_pairs.shape[0]
    depth, slots = 4 * quad, nnear - 1
    near_pairs, far_pairs = near_pairs.T, far_pairs.T

    def swap(x, axis, d):
        n = {"row": n_row, "col": n_col}[axis]
        return lax.ppermute(x, axis, [(i, i ^ d) for i in range(n)])

    def halves(n):
        return [1 << j for j in reversed(range(n.bit_length() - 1))]

    def row_gather(x):
        known = {0: x}
        for d in halves(n_row):
            known.update({k ^ d: swap(v, "row", d) for k, v in known.items()})
        return [known[k] for k in range(n_row)]

    def col_gather(x):
        steps = [x]
        for d in halves(n_col):
            steps.append(jnp.concatenate([steps[-1], swap(steps[-1], "col", d)], axis=0))
        return steps[-1], steps[-2]

    base = near_lines(slots, quad)
    msg_rows = -(-(base + 4 * (blocks + 1)) // 8) * 8
    hbm = (near_pairs, far_pairs, points, density.reshape(-1, LANES))
    hbm = [pltpu.with_memory_space_constraint(x, pltpu.HBM) for x in hbm]
    msg, far_own, near_own, weight = pl.pallas_call(
        prep_kernel,
        out_shape=(
            f32(msg_rows, BLK),
            f32(blocks + 1, 4, BLK),
            f32(blocks, depth + 8, BLK),
            f32(blocks, BLK),
        ),
        in_specs=[HBM, SMEM, HBM, HBM, HBM],
        out_specs=(VMEM, VMEM, VMEM, VMEM),
        scratch_shapes=[
            pltpu.SMEM(near_pairs.shape, jnp.int32),
            pltpu.VMEM(far_pairs.shape, jnp.int32),
            pltpu.VMEM(points.shape, jnp.float32),
            pltpu.VMEM((density.shape[0] // LANES, LANES), jnp.float32),
            pltpu.SemaphoreType.DMA((QUARTERS + 3,)),
        ],
        compiler_params=PARAMS,
        cost_estimate=cost(1.2),
        name="prep",
    )(hbm[0], near_count, *hbm[1:])
    got = row_gather(msg)[1:]
    row_far, row_part = col_gather(far_own)

    bufs = [
        pltpu.VMEM((quad * BLK, TERMS), jnp.bfloat16),
        pltpu.VMEM((TERMS, quad * BLK), jnp.bfloat16),
        pltpu.VMEM((BLK, LANES), jnp.float32),
        pltpu.VMEM((8, BLK), jnp.float32),
    ]
    near0 = pl.pallas_call(
        near_own_kernel,
        out_shape=f32(blocks, BLK),
        in_specs=[SMEM, SMEM, VMEM],
        out_specs=VMEM,
        scratch_shapes=bufs,
        compiler_params=PARAMS,
        cost_estimate=cost(5.0),
        name="near_own",
    )(near_pairs, near_count, near_own)

    def near_scratch(n):
        return [
            pltpu.VMEM((depth + 8, BLK), jnp.float32),
            pltpu.SMEM((n, 8, LANES), jnp.float32),
            pltpu.SemaphoreType.DMA((n,)),
        ] + bufs

    direct = [d for d in range(1, n_row) if d & (d - 1) == 0]
    late = [d for d in range(1, n_row) if d & (d - 1) != 0]
    field, *backs = pl.pallas_call(
        functools.partial(direct_kernel, ways=len(direct)),
        out_shape=[f32(blocks, BLK)] + [f32(8, BLK)] * len(direct),
        in_specs=[VMEM] * (len(direct) + 2),
        out_specs=[VMEM] * (len(direct) + 1),
        scratch_shapes=near_scratch(len(direct)),
        compiler_params=PARAMS,
        cost_estimate=cost(5.0),
        name="near_direct",
    )(near_own, near0, *[got[d - 1] for d in direct])
    far_scratch = [
        pltpu.VMEM((4, BLK), jnp.float32),
        pltpu.VMEM((BLK, TERMS), jnp.bfloat16),
        pltpu.VMEM((TERMS, BLK), jnp.bfloat16),
        pltpu.VMEM((BLK, LANES), jnp.float32),
    ]
    far_rows, far_cols = pl.pallas_call(
        functools.partial(far_kernel, direct=direct, base=base),
        out_shape=[f32(nfar, BLK)] * 2,
        in_specs=[SMEM, SMEM] + [VMEM] * (2 + len(direct)),
        out_specs=[VMEM] * 2,
        scratch_shapes=far_scratch,
        compiler_params=PARAMS,
        cost_estimate=cost(3.0),
        name="far_direct",
    )(far_pairs, far_count, row_far, far_own, *[got[d - 1] for d in direct])
    field, far_rows, far_cols, *messages = pl.pallas_call(
        functools.partial(late_kernel, n_row=n_row, direct=direct, late=late),
        out_shape=[f32(blocks, BLK)] + [f32(nfar, BLK)] * 2 + [f32(nfar + 8, BLK)] * (n_row - 1),
        in_specs=[SMEM, SMEM] + [VMEM] * (5 + n_row - 1),
        out_specs=[VMEM] * (n_row + 2),
        scratch_shapes=near_scratch(len(late)) + far_scratch,
        compiler_params=PARAMS,
        cost_estimate=cost(8.0),
        name="late",
    )(far_pairs, far_count, near_own, field, row_far, far_rows, far_cols, *[got[d - 1] for d in late], *backs)

    messages = [swap(x, "row", d + 1) for d, x in enumerate(messages)]
    both = jnp.concatenate([far_rows, swap(far_rows, "col", 1)], axis=0)
    rows = [both] + [swap(both, "col", d) for d in range(2, n_col, 2)]
    field = pl.pallas_call(
        functools.partial(cols_kernel, n_row=n_row, base=base),
        out_shape=f32(blocks, BLK),
        in_specs=[SMEM] + [VMEM] * (2 * n_row + 2),
        out_specs=VMEM,
        compiler_params=PARAMS,
        cost_estimate=cost(1.0),
        name="final_cols",
    )(near_pairs, weight, field, far_own, far_cols, *got, *messages)
    out = pl.pallas_call(
        functools.partial(rows_kernel, n_col=n_col),
        out_shape=f32(blocks * BLK // LANES, LANES),
        in_specs=[VMEM] * (3 + len(rows)),
        out_specs=VMEM,
        compiler_params=PARAMS,
        cost_estimate=cost(1.0),
        name="final_rows",
    )(weight, field, row_far, *rows)
    return out.reshape(-1)


def solution(mesh):
    in_specs = (
        P(None, None, ("row", "col")),
        P(("row", "col")),
        P(("row", "col"), None),
        P(("row", "col"), None),
        P(("row", "col")),
        P(("row", "col")),
    )
    out_specs = P(("row", "col"))
    kernel = functools.partial(body, n_row=mesh.shape["row"], n_col=mesh.shape["col"])
    return jax.shard_map(kernel, mesh=mesh, in_specs=in_specs, out_specs=out_specs, check_vma=False)
```

```python
import functools

import jax
import jax.numpy as jnp
from jax import lax
from jax.experimental import pallas as pl
from jax.experimental.pallas import tpu as pltpu
from jax.sharding import PartitionSpec as P

BLK = 512
LANES = 128
SOFT_SQ = 0.0004
TERMS = 64
SPLIT = 48
HALF = 512
QUARTERS = 4
SLOTS = 5
NEAR_SCRATCH = 4 * [None]
GROUP = 16
CHUNK = 512
VMEM = pl.BlockSpec(memory_space=pltpu.VMEM)
SMEM = pl.BlockSpec(memory_space=pltpu.SMEM)
ANY = pl.BlockSpec(memory_space=pl.ANY)
HBM = pl.BlockSpec(memory_space=pltpu.HBM)
PARAMS = pltpu.CompilerParams(vmem_limit_bytes=40 * 1024 * 1024)


def prep_kernel(near_hbm, count, far_hbm, pts_hbm, dens_hbm, msg, far_out, near_out, weight_out, *scratch):
    near_ref, far_ref, pts_ref, dens_ref, sems = scratch
    blocks = near_out.shape[0]
    quad = pts_ref.shape[1]
    slots, body = near_ref.shape[1] - 1, quad * 4
    base = near_lines(slots, quad)
    width = pts_ref.shape[2] // QUARTERS
    copies = [
        pltpu.make_async_copy(dens_hbm, dens_ref, sems.at[QUARTERS]),
        pltpu.make_async_copy(far_hbm, far_ref, sems.at[QUARTERS + 1]),
        pltpu.make_async_copy(near_hbm, near_ref, sems.at[QUARTERS + 2]),
    ]
    for i in range(QUARTERS):
        part = slice(i * width, (i + 1) * width)
        copies.append(pltpu.make_async_copy(pts_hbm.at[:, :, part], pts_ref.at[:, :, part], sems.at[i]))
    for copy in copies:
        copy.start()
    copies.pop(0).wait()
    copies.pop(0).wait()
    copies.pop(0).wait()

    for k in range(blocks):
        cols = slice(k * BLK, (k + 1) * BLK)
        if k % (blocks // QUARTERS) == 0:
            copies.pop(0).wait()
        w = pts_ref[3, :, cols]
        total = jnp.sum(w, axis=0, keepdims=True)
        dens = jnp.concatenate([dens_ref[4 * k + q : 4 * k + q + 1, :] for q in range(4)], axis=1)
        lines = []
        for c in range(3):
            x = pts_ref[c, :, cols]
            lines.append(jnp.sum(x * w, axis=0, keepdims=True) / total)
            near_out[k, quad * c : quad * c + quad, :] = x
        near_out[k, quad * 3 : quad * 4, :] = w
        near_out[k, quad * 4 : quad * 4 + 8, :] = jnp.broadcast_to(dens, (8, BLK))
        far_out[k] = jnp.concatenate(lines + [total * dens], axis=0)
        weight_out[k : k + 1, :] = total
    pairs = jnp.concatenate([far_ref[...].astype(jnp.float32), jnp.full((2, LANES - far_ref.shape[1]), -1.0)], axis=1)
    pairs = jnp.concatenate([pairs] * (BLK // LANES), axis=1)
    far_out[blocks] = jnp.concatenate([pairs, jnp.zeros((2, BLK), jnp.float32)], axis=0)
    lane = lax.broadcasted_iota(jnp.int32, (1, BLK), 1)
    line = jnp.full((1, BLK), -1.0, jnp.float32)
    for t in range(slots):
        k = lax.rem(near_ref[0, t + 1], blocks)
        msg[t * body : (t + 1) * body, :] = near_out[k, 0:body, :]
        msg[slots * body + t : slots * body + t + 1, :] = near_out[k, body : body + 1, :]
        source = jnp.where(t + 1 < count[0], near_ref[1, t + 1], -1)
        line = jnp.where(lane == t, source.astype(jnp.float32), line)
    first = slots * (body + 1)
    msg[first:base, :] = jnp.broadcast_to(line, (base - first, BLK))


def near_lines(slots, quad):
    return -(-(slots * (4 * quad + 1) + 1) // 8) * 8


def three(value):
    one = value.astype(jnp.bfloat16).astype(jnp.float32)
    two = (value - one).astype(jnp.bfloat16).astype(jnp.float32)
    return one, two, value - one - two


def pick_row(row, values):
    out = jnp.zeros(row.shape, jnp.float32)
    for k, value in enumerate(values):
        out = jnp.where(row == k, value, out)
    return out


def parts(x):
    row = lax.broadcasted_iota(jnp.int32, x.shape, 0)
    live = row < 3
    centred = jnp.where(live, x - 0.5, 0.0)
    head = jnp.round(centred * 256.0) * (1.0 / 256.0)
    rest = centred - head
    rest1 = rest.astype(jnp.bfloat16).astype(jnp.float32)
    big = pick_row(row, three(jnp.sum(head * head, axis=0, keepdims=True)))
    small = pick_row(row, three(jnp.sum(rest * (2.0 * head + rest), axis=0, keepdims=True) + 0.5 * SOFT_SQ))
    return head, rest1, rest - rest1, big, small, jnp.where(live, 1.0, 0.0)


def left_terms(x, columns):
    head, rest1, rest2, big, small, ones = parts(x)
    h2, a2, b2 = -2.0 * head, -2.0 * rest1, -2.0 * rest2
    groups = [h2, big, ones, small, ones, h2, h2, a2, b2, a2, a2, b2]
    row = lax.broadcasted_iota(jnp.int32, (TERMS - SPLIT, x.shape[1]), 0)
    groups.append(pick_row(row, [part for column in columns for part in three(column)]))
    return jnp.concatenate(groups, axis=0)


def right_terms(x):
    head, rest1, rest2, big, small, ones = parts(x)
    groups = [head, ones, big, ones, small, rest1, rest2, head, head, rest1, rest2, rest1]
    groups.append(jnp.zeros((TERMS - SPLIT, x.shape[1]), jnp.float32))
    return jnp.concatenate(groups, axis=0).astype(jnp.bfloat16)


def column_of(lhs, which):
    row = lax.broadcasted_iota(jnp.int32, (TERMS, LANES), 0) - SPLIT - 3 * which
    pick = jnp.where((row >= 0) & (row < 3), 1.0, 0.0).astype(jnp.bfloat16)
    return jnp.dot(lhs, pick, preferred_element_type=jnp.float32)


def fold_lanes(tile, row):
    part = tile[:, :LANES] * row[:, :LANES]
    for q in range(1, tile.shape[1] // LANES):
        part = part + tile[:, q * LANES : (q + 1) * LANES] * row[:, q * LANES : (q + 1) * LANES]
    return part


def twice(col):
    return jnp.concatenate([col] * (HALF // LANES), axis=1)


def place(x, n):
    bits = n.bit_length() - 1
    div, rem = (lambda a, b: a // b, lambda a, b: a % b) if isinstance(x, int) else (lax.div, lax.rem)
    return sum(rem(div(x, 1 << (bits - 1 - j)), 2) * (1 << j) for j in range(bits))


def far_tiles(pairs, count, row_in, sources, rows_out, cols_out, left_buf, right_buf, lhs_buf, rhs_buf, part_buf):
    n_col = lax.axis_size("col")
    row_step = 2 * row_in[0].shape[0] // n_col
    blocks = row_step - 1
    my_row, my_col = lax.axis_index("row"), lax.axis_index("col")

    def step(s, _):
        a, b = pairs[0, s], pairs[1, s]
        a_way, b_way = jnp.bitwise_xor(lax.div(a, blocks), my_col), jnp.bitwise_xor(lax.div(b, blocks), my_row)
        here = functools.reduce(jnp.logical_or, [b_way == d for d in sources])
        pl.when(here)(lambda: tile(s, a_way, b_way, lax.rem(a, blocks), lax.rem(b, blocks)))
        return 0

    def tile(s, a_way, b_way, ka, kb):
        same = (a_way == 0) & (b_way == 0) & (ka == kb)
        for d, other in sources.items():

            @pl.when(b_way == d)
            def _():
                right_buf[...] = other[kb]

        for core, half in enumerate(row_in):

            @pl.when(lax.rem(a_way, 2) == core)
            def _():
                left_buf[...] = half[place(lax.div(a_way, 2), n_col // 2) * row_step + ka]

        left, right = left_buf[...], right_buf[...]
        lhs_buf[...] = jnp.transpose(left_terms(left, [left[3:4]])).astype(jnp.bfloat16)
        rhs_buf[...] = right_terms(right)
        lhs = lhs_buf[...]
        zcol = column_of(lhs, 0)
        total = []
        for h in range(BLK // HALF):
            cols = slice(h * HALF, (h + 1) * HALF)
            dist = jnp.dot(lhs, rhs_buf[:, cols], preferred_element_type=jnp.float32)
            acc = jnp.zeros((8, HALF), jnp.float32)
            for g in range(BLK // 8):
                rows = slice(g * 8, (g + 1) * 8)
                tile = lax.rsqrt(dist[rows, :])
                part = fold_lanes(tile, right[3:4, cols])
                part_buf[rows, :] = part if h == 0 else part_buf[rows, :] + part
                acc = acc + tile * twice(zcol[rows, :])
            total.append(jnp.sum(acc, axis=0, keepdims=True))
        rows_out[pl.ds(s, 1), :] = jnp.sum(jnp.transpose(part_buf[...]), axis=0, keepdims=True)
        cols_out[pl.ds(s, 1), :] = jnp.concatenate(total, axis=1) * jnp.where(same, 0.0, 1.0)

    lax.fori_loop(0, count[0], step, 0)


def points(tall):
    quad = tall.shape[0] // 4
    sides = [[tall[quad * c + u : quad * c + u + 1, :] for c in range(4)] for u in range(quad)]
    return jnp.concatenate([jnp.concatenate(side, axis=0) for side in sides], axis=1)


def near_tile(left, dens_i, right, dens_j, lhs_buf, rhs_buf, part_buf, acc_buf):
    quad = left.shape[1] // BLK
    terms = jnp.transpose(left_terms(left, [left[3:4], jnp.concatenate([dens_i] * quad, axis=1)]))
    terms = terms.astype(jnp.bfloat16)
    for g in range(BLK // GROUP):
        for u in range(quad):
            to, at = (g * quad + u) * GROUP, u * BLK + g * GROUP
            lhs_buf[to : to + GROUP, :] = terms[at : at + GROUP, :]
    rhs_buf[...] = right_terms(right)
    weights = right[3:4]
    acc_buf[...] = jnp.zeros_like(acc_buf)

    def chunk(i, _):
        at = pl.multiple_of(i * CHUNK * quad, CHUNK * quad)
        lhs = lhs_buf[pl.ds(at, CHUNK * quad), :]
        wcol = column_of(lhs, 0)
        groups = CHUNK // GROUP
        first_rows = [lhs[g * quad * GROUP : g * quad * GROUP + GROUP, :] for g in range(groups)]
        dcol = column_of(jnp.concatenate(first_rows, axis=0), 1)
        part = None
        for h in range(BLK // HALF):
            tiles = [None] * groups
            for v in range(quad):
                cols = slice(v * BLK + h * HALF, v * BLK + (h + 1) * HALF)
                dist = jnp.dot(lhs, rhs_buf[:, cols], preferred_element_type=jnp.float32)
                for g in range(groups):
                    inner = None
                    for u in range(quad):
                        rows = slice((g * quad + u) * GROUP, (g * quad + u + 1) * GROUP)
                        term = lax.rsqrt(dist[rows, :]) * twice(wcol[rows, :])
                        inner = term if inner is None else inner + term
                    inner = inner * weights[:, cols]
                    tiles[g] = inner if tiles[g] is None else tiles[g] + inner
            tile = jnp.concatenate(tiles, axis=0)
            cols = slice(h * HALF, (h + 1) * HALF)
            more = fold_lanes(tile, dens_j[:, cols])
            part = more if part is None else part + more
            acc_buf[:, cols] += jnp.sum((tile * twice(dcol)).reshape(-1, 8, HALF), axis=0)
        part_buf[pl.ds(pl.multiple_of(i * CHUNK, CHUNK), CHUNK), :] = part
        return 0

    lax.fori_loop(0, BLK // CHUNK, chunk, 0)
    rows = jnp.sum(jnp.transpose(part_buf[...]), axis=0, keepdims=True)
    return rows, jnp.sum(acc_buf[...], axis=0, keepdims=True)


def near_own_kernel(pairs, count, near_ref, field, *bufs):
    blocks, depth, _ = near_ref.shape
    body = depth - 8
    my_row = lax.axis_index("row")
    field[...] = jnp.zeros_like(field)

    def step(s, _):
        ka, kb = lax.rem(pairs[0, s], blocks), pairs[1, s] - my_row * blocks

        @pl.when((kb >= 0) & (kb < blocks))
        def _():
            left, right = points(near_ref[ka, 0:body, :]), points(near_ref[kb, 0:body, :])
            dens_i, dens_j = near_ref[ka, body : body + 1, :], near_ref[kb, body : body + 1, :]
            rows, cols = near_tile(left, dens_i, right, dens_j, *bufs)
            field[pl.ds(ka, 1), :] += rows
            field[pl.ds(kb, 1), :] += cols * jnp.where(ka == kb, 0.0, 1.0)

        return 0

    lax.fori_loop(0, count[0], step, 0)


def near_tiles(near_ref, got, field, backs, first, right_buf, tags, sems, *bufs):
    blocks, depth, _ = near_ref.shape
    body = depth - 8
    base = near_lines(SLOTS, body // 4)
    my_row = lax.axis_index("row")
    copies = [
        pltpu.make_async_copy(g.at[base - 8 : base, 0:LANES], tags.at[d], sems.at[d]) for d, g in enumerate(got)
    ]
    for copy in copies:
        copy.start()
    for copy in copies:
        copy.wait()

    def step(i, _):
        way, t = lax.div(i, SLOTS), lax.rem(i, SLOTS)
        kb = tags[way, 7, t].astype(jnp.int32) - my_row * blocks

        @pl.when((kb >= 0) & (kb < blocks))
        def _():
            for d, other in enumerate(got):

                @pl.when(way == d)
                def _():
                    at = pl.multiple_of(t * body, 8)
                    right_buf[0:body, :] = other[pl.ds(at, body), :]
                    right_buf[body : body + 1, :] = other[pl.ds(SLOTS * body + t, 1), :]

            left, right = points(near_ref[kb, 0:body, :]), points(right_buf[0:body, :])
            dens_i, dens_j = near_ref[kb, body : body + 1, :], right_buf[body : body + 1, :]
            rows, cols = near_tile(left, dens_i, right, dens_j, *bufs)
            field[pl.ds(kb, 1), :] += rows
            for d, back in enumerate(backs):

                @pl.when(way == d)
                def _():
                    back[pl.ds(first + t, 1), :] = cols

        return 0

    lax.fori_loop(0, len(got) * SLOTS, step, 0)


def direct_kernel(near_ref, start, *refs, ways):
    got, (field, *backs), scratch = refs[:ways], refs[ways : 2 * ways + 1], refs[2 * ways + 1 :]
    field[...] = start[...]
    for back in backs:
        back[...] = jnp.zeros_like(back)
    near_tiles(near_ref, got, field, backs, 0, *scratch)


def far_kernel(pairs, count, row0, row1, *refs, ways):
    got, (rows_out, cols_out), scratch = refs[: len(ways)], refs[len(ways) : -5], refs[-5:]
    rows_out[...] = jnp.zeros_like(rows_out)
    cols_out[...] = jnp.zeros_like(cols_out)
    far_tiles(pairs, count, (row0, row1), dict(zip(ways, got)), rows_out, cols_out, *scratch)


def late_kernel(pairs, count, near_ref, start, row0, row1, rows_in, cols_in, *refs, n_row, direct, late):
    refs = list(refs)
    take = lambda n: [refs.pop(0) for _ in range(n)]
    got, far, backs = take(len(late)), take(len(late)), take(len(direct))
    field, rows_out, cols_out, *messages = take(n_row + 2)
    near_scratch, far_scratch = take(len(NEAR_SCRATCH) + 3), refs
    nfar = cols_out.shape[0]
    field[...] = start[...]
    rows_out[...] = rows_in[...]
    cols_out[...] = cols_in[...]
    for message in messages:
        message[nfar:, :] = jnp.zeros((8, BLK), jnp.float32)
    for d, back in zip(direct, backs):
        messages[d - 1][nfar:, :] = back[...]
    near_tiles(near_ref, got, field, [messages[d - 1] for d in late], nfar, *near_scratch)
    far_tiles(pairs, count, (row0, row1), dict(zip(late, far)), rows_out, cols_out, *far_scratch)
    for message in messages:
        message[0:nfar, :] = cols_out[...]


def hot(index, blocks, slots, base):
    want = lax.broadcasted_iota(jnp.int32, (blocks, slots), 0) + base * blocks
    return jnp.where(index[:, 0:slots] == want.astype(jnp.float32), 1.0, 0.0)


def spread(pick, slots, weight):
    pick = jnp.concatenate(pick * 3, axis=1).astype(jnp.bfloat16)
    slots = jnp.concatenate(three(jnp.concatenate(slots, axis=0)), axis=0).astype(jnp.bfloat16)
    return jnp.dot(pick, slots, preferred_element_type=jnp.float32) * weight[...]


def cols_kernel(pairs, weight, near, own_cols, *refs, n_row):
    col_far, messages, field = refs[:n_row], refs[n_row:-1], refs[-1]
    blocks, nfar = weight.shape[0], own_cols.shape[0]
    my_row = lax.axis_index("row")
    pick = [hot(other[blocks, 1:2, :], blocks, nfar, my_row) for other in col_far]
    field[...] = near[...] + spread(pick, [own_cols[...]] + [m[0:nfar, :] for m in messages], weight)
    for message in messages:
        for t in range(pairs.shape[1] - 1):
            k = lax.rem(pairs[0, t + 1], blocks)
            field[pl.ds(k, 1), :] += message[nfar + t : nfar + t + 1, :]


def rows_kernel(weight, field, row0, row1, *refs, n_col):
    rows, out = refs[:-1], refs[-1]
    blocks, nfar = weight.shape[0], rows[0].shape[0] // 2
    my_col = lax.axis_index("col")
    tags = [place(d // 2, n_col // 2) * (blocks + 1) + blocks for d in range(n_col)]
    pick = [hot((row0, row1)[d % 2][tag, 0:1, :], blocks, nfar, my_col) for d, tag in enumerate(tags)]
    total = field[...] + spread(pick, [r[...] for r in rows], weight)
    for q in range(BLK // LANES):
        out[pl.ds(q, blocks, stride=BLK // LANES), :] = total[:, q * LANES : (q + 1) * LANES]


def f32(*shape):
    return jax.ShapeDtypeStruct(shape, jnp.float32)


def cost(micros):
    return pl.CostEstimate(flops=int(micros * 1.1e9), bytes_accessed=1 << 16, transcendentals=0)


def body(points, density, near_pairs, far_pairs, near_count, far_count, *, n_row, n_col):
    quad = points.shape[1]
    blocks = points.shape[2] // BLK
    nnear, nfar = near_pairs.shape[0], far_pairs.shape[0]
    depth, slots = 4 * quad, nnear - 1
    near_pairs, far_pairs = near_pairs.T, far_pairs.T

    def swap(x, axis, d):
        n = {"row": n_row, "col": n_col}[axis]
        return lax.ppermute(x, axis, [(i, i ^ d) for i in range(n)])

    direct = [d for d in range(1, n_row) if d & (d - 1) == 0]
    late = [d for d in range(1, n_row) if d & (d - 1) != 0]

    def halves(n):
        return [1 << j for j in reversed(range(n.bit_length() - 1))]

    def row_gather(x):
        known = {0: x}
        for d in halves(n_row):
            known.update({k ^ d: swap(v, "row", d) for k, v in known.items()})
        return [known[k] for k in range(n_row)]

    base = near_lines(slots, quad)
    hbm = (near_pairs, far_pairs, points, density.reshape(-1, LANES))
    hbm = [pltpu.with_memory_space_constraint(x, pltpu.HBM) for x in hbm]
    msg, far_own, near_own, weight = pl.pallas_call(
        prep_kernel,
        out_shape=(
            f32(base, BLK),
            f32(blocks + 1, 4, BLK),
            f32(blocks, depth + 8, BLK),
            f32(blocks, BLK),
        ),
        in_specs=[HBM, SMEM, HBM, HBM, HBM],
        out_specs=(VMEM, VMEM, VMEM, VMEM),
        scratch_shapes=[
            pltpu.SMEM(near_pairs.shape, jnp.int32),
            pltpu.VMEM(far_pairs.shape, jnp.int32),
            pltpu.VMEM(points.shape, jnp.float32),
            pltpu.VMEM((density.shape[0] // LANES, LANES), jnp.float32),
            pltpu.SemaphoreType.DMA((QUARTERS + 3,)),
        ],
        compiler_params=PARAMS,
        cost_estimate=cost(1.2),
        name="prep",
    )(hbm[0], near_count, *hbm[1:])
    got = row_gather(msg)[1:]
    row_part = far_own
    for i, d in enumerate(halves(n_col)[:-1]):
        row_part = jnp.concatenate([row_part, swap(row_part, "col", d)], axis=0)
        if i == 0:
            row_part, far_next = lax.optimization_barrier((row_part, far_own))
    row_far = (row_part, swap(row_part, "col", 1))
    col_far = {0: far_own, **{d: swap(far_next, "row", d) for d in direct}}

    bufs = [
        pltpu.VMEM((quad * BLK, TERMS), jnp.bfloat16),
        pltpu.VMEM((TERMS, quad * BLK), jnp.bfloat16),
        pltpu.VMEM((BLK, LANES), jnp.float32),
        pltpu.VMEM((8, BLK), jnp.float32),
    ]
    near0 = pl.pallas_call(
        near_own_kernel,
        out_shape=f32(blocks, BLK),
        in_specs=[SMEM, SMEM, VMEM],
        out_specs=VMEM,
        scratch_shapes=bufs,
        compiler_params=PARAMS,
        cost_estimate=cost(5.0),
        name="near_own",
    )(near_pairs, near_count, near_own)

    def near_scratch(n):
        return [
            pltpu.VMEM((depth + 8, BLK), jnp.float32),
            pltpu.SMEM((n, 8, LANES), jnp.float32),
            pltpu.SemaphoreType.DMA((n,)),
        ] + bufs

    field, *backs = pl.pallas_call(
        functools.partial(direct_kernel, ways=len(direct)),
        out_shape=[f32(blocks, BLK)] + [f32(8, BLK)] * len(direct),
        in_specs=[VMEM] * (len(direct) + 2),
        out_specs=[VMEM] * (len(direct) + 1),
        scratch_shapes=near_scratch(len(direct)),
        compiler_params=PARAMS,
        cost_estimate=cost(10.0),
        name="near_direct",
    )(near_own, near0, *[got[d - 1] for d in direct])
    *onward, field = lax.optimization_barrier((*[col_far[d] for d in direct], field))
    onward = dict(zip(direct, onward))
    for d in late:
        bit = d & -d
        onward[d] = swap(onward[d ^ bit], "row", bit)
    col_far.update({d: onward[d] for d in late})

    far_scratch = [
        pltpu.VMEM((4, BLK), jnp.float32),
        pltpu.VMEM((4, BLK), jnp.float32),
        pltpu.VMEM((BLK, TERMS), jnp.bfloat16),
        pltpu.VMEM((TERMS, BLK), jnp.bfloat16),
        pltpu.VMEM((BLK, LANES), jnp.float32),
    ]
    far_rows, far_cols = pl.pallas_call(
        functools.partial(far_kernel, ways=[0] + direct),
        out_shape=[f32(nfar, BLK)] * 2,
        in_specs=[SMEM, SMEM] + [VMEM] * (3 + len(direct)),
        out_specs=[VMEM] * 2,
        scratch_shapes=far_scratch,
        compiler_params=PARAMS,
        cost_estimate=cost(3.0),
        name="far_direct",
    )(far_pairs, far_count, *row_far, *[col_far[d] for d in [0] + direct])
    field, far_rows, far_cols, *messages = pl.pallas_call(
        functools.partial(late_kernel, n_row=n_row, direct=direct, late=late),
        out_shape=[f32(blocks, BLK)] + [f32(nfar, BLK)] * 2 + [f32(nfar + 8, BLK)] * (n_row - 1),
        in_specs=[SMEM, SMEM] + [VMEM] * (6 + n_row - 1 + len(late)),
        out_specs=[VMEM] * (n_row + 2),
        scratch_shapes=near_scratch(len(late)) + far_scratch,
        compiler_params=PARAMS,
        cost_estimate=cost(8.0),
        name="late",
    )(
        *(far_pairs, far_count, near_own, field, *row_far, far_rows, far_cols),
        *[got[d - 1] for d in late],
        *[col_far[d] for d in late],
        *backs,
    )

    messages = [swap(x, "row", d + 1) for d, x in enumerate(messages)]
    both = jnp.concatenate([far_rows, swap(far_rows, "col", 1)], axis=0)
    rows = [both] + [swap(both, "col", d) for d in range(2, n_col, 2)]
    field = pl.pallas_call(
        functools.partial(cols_kernel, n_row=n_row),
        out_shape=f32(blocks, BLK),
        in_specs=[SMEM] + [VMEM] * (2 * n_row + 2),
        out_specs=VMEM,
        compiler_params=PARAMS,
        cost_estimate=cost(1.0),
        name="final_cols",
    )(near_pairs, weight, field, far_cols, *[col_far[d] for d in range(n_row)], *messages)
    out = pl.pallas_call(
        functools.partial(rows_kernel, n_col=n_col),
        out_shape=f32(blocks * BLK // LANES, LANES),
        in_specs=[VMEM] * (4 + len(rows)),
        out_specs=VMEM,
        compiler_params=PARAMS,
        cost_estimate=cost(1.0),
        name="final_rows",
    )(weight, field, *row_far, *rows)
    return out.reshape(-1)


def solution(mesh):
    in_specs = (
        P(None, None, ("row", "col")),
        P(("row", "col")),
        P(("row", "col"), None),
        P(("row", "col"), None),
        P(("row", "col")),
        P(("row", "col")),
    )
    out_specs = P(("row", "col"))
    kernel = functools.partial(body, n_row=mesh.shape["row"], n_col=mesh.shape["col"])
    return jax.shard_map(kernel, mesh=mesh, in_specs=in_specs, out_specs=out_specs, check_vma=False)
```

```python
import functools

import jax
import jax.numpy as jnp
from jax import lax
from jax.experimental import pallas as pl
from jax.experimental.pallas import tpu as pltpu
from jax.sharding import PartitionSpec as P

BLK = 512
LANES = 128
SOFT_SQ = 0.0004
TERMS = 64
SPLIT = 48
HALF = 512
QUARTERS = 4
SLOTS = 5
NEAR_SCRATCH = 4 * [None]
GROUP = 16
CHUNK = 512
VMEM = pl.BlockSpec(memory_space=pltpu.VMEM)
SMEM = pl.BlockSpec(memory_space=pltpu.SMEM)
ANY = pl.BlockSpec(memory_space=pl.ANY)
HBM = pl.BlockSpec(memory_space=pltpu.HBM)
PARAMS = pltpu.CompilerParams(vmem_limit_bytes=40 * 1024 * 1024)


def prep_kernel(near_hbm, count, far_hbm, pts_hbm, dens_hbm, msg, far_out, near_out, weight_out, *scratch):
    near_ref, far_ref, pts_ref, dens_ref, sems = scratch
    blocks = near_out.shape[0]
    quad = pts_ref.shape[1]
    slots, body = near_ref.shape[1] - 1, quad * 4
    base = near_lines(slots, quad)
    width = pts_ref.shape[2] // QUARTERS
    copies = [
        pltpu.make_async_copy(dens_hbm, dens_ref, sems.at[QUARTERS]),
        pltpu.make_async_copy(far_hbm, far_ref, sems.at[QUARTERS + 1]),
        pltpu.make_async_copy(near_hbm, near_ref, sems.at[QUARTERS + 2]),
    ]
    for i in range(QUARTERS):
        part = slice(i * width, (i + 1) * width)
        copies.append(pltpu.make_async_copy(pts_hbm.at[:, :, part], pts_ref.at[:, :, part], sems.at[i]))
    for copy in copies:
        copy.start()
    copies.pop(0).wait()
    copies.pop(0).wait()
    copies.pop(0).wait()

    def put_far(k, value):
        far_out[k] = value
        msg[base + 4 * k : base + 4 * k + 4, :] = value

    for k in range(blocks):
        cols = slice(k * BLK, (k + 1) * BLK)
        if k % (blocks // QUARTERS) == 0:
            copies.pop(0).wait()
        w = pts_ref[3, :, cols]
        total = jnp.sum(w, axis=0, keepdims=True)
        dens = jnp.concatenate([dens_ref[4 * k + q : 4 * k + q + 1, :] for q in range(4)], axis=1)
        lines = []
        for c in range(3):
            x = pts_ref[c, :, cols]
            lines.append(jnp.sum(x * w, axis=0, keepdims=True) / total)
            near_out[k, quad * c : quad * c + quad, :] = x
        near_out[k, quad * 3 : quad * 4, :] = w
        near_out[k, quad * 4 : quad * 4 + 8, :] = jnp.broadcast_to(dens, (8, BLK))
        put_far(k, jnp.concatenate(lines + [total * dens], axis=0))
        weight_out[k : k + 1, :] = total
    pairs = jnp.concatenate([far_ref[...].astype(jnp.float32), jnp.full((2, LANES - far_ref.shape[1]), -1.0)], axis=1)
    pairs = jnp.concatenate([pairs] * (BLK // LANES), axis=1)
    put_far(blocks, jnp.concatenate([pairs, jnp.zeros((2, BLK), jnp.float32)], axis=0))
    lane = lax.broadcasted_iota(jnp.int32, (1, BLK), 1)
    line = jnp.full((1, BLK), -1.0, jnp.float32)
    for t in range(slots):
        k = lax.rem(near_ref[0, t + 1], blocks)
        msg[t * body : (t + 1) * body, :] = near_out[k, 0:body, :]
        msg[slots * body + t : slots * body + t + 1, :] = near_out[k, body : body + 1, :]
        source = jnp.where(t + 1 < count[0], near_ref[1, t + 1], -1)
        line = jnp.where(lane == t, source.astype(jnp.float32), line)
    first = slots * (body + 1)
    msg[first:base, :] = jnp.broadcast_to(line, (base - first, BLK))


def near_lines(slots, quad):
    return -(-(slots * (4 * quad + 1) + 1) // 8) * 8


def three(value):
    one = value.astype(jnp.bfloat16).astype(jnp.float32)
    two = (value - one).astype(jnp.bfloat16).astype(jnp.float32)
    return one, two, value - one - two


def pick_row(row, values):
    out = jnp.zeros(row.shape, jnp.float32)
    for k, value in enumerate(values):
        out = jnp.where(row == k, value, out)
    return out


def parts(x):
    row = lax.broadcasted_iota(jnp.int32, x.shape, 0)
    live = row < 3
    centred = jnp.where(live, x - 0.5, 0.0)
    head = jnp.round(centred * 256.0) * (1.0 / 256.0)
    rest = centred - head
    rest1 = rest.astype(jnp.bfloat16).astype(jnp.float32)
    big = pick_row(row, three(jnp.sum(head * head, axis=0, keepdims=True)))
    small = pick_row(row, three(jnp.sum(rest * (2.0 * head + rest), axis=0, keepdims=True) + 0.5 * SOFT_SQ))
    return head, rest1, rest - rest1, big, small, jnp.where(live, 1.0, 0.0)


def left_terms(x, columns):
    head, rest1, rest2, big, small, ones = parts(x)
    h2, a2, b2 = -2.0 * head, -2.0 * rest1, -2.0 * rest2
    groups = [h2, big, ones, small, ones, h2, h2, a2, b2, a2, a2, b2]
    row = lax.broadcasted_iota(jnp.int32, (TERMS - SPLIT, x.shape[1]), 0)
    groups.append(pick_row(row, [part for column in columns for part in three(column)]))
    return jnp.concatenate(groups, axis=0)


def right_terms(x):
    head, rest1, rest2, big, small, ones = parts(x)
    groups = [head, ones, big, ones, small, rest1, rest2, head, head, rest1, rest2, rest1]
    groups.append(jnp.zeros((TERMS - SPLIT, x.shape[1]), jnp.float32))
    return jnp.concatenate(groups, axis=0).astype(jnp.bfloat16)


def column_of(lhs, which):
    row = lax.broadcasted_iota(jnp.int32, (TERMS, LANES), 0) - SPLIT - 3 * which
    pick = jnp.where((row >= 0) & (row < 3), 1.0, 0.0).astype(jnp.bfloat16)
    return jnp.dot(lhs, pick, preferred_element_type=jnp.float32)


def fold_lanes(tile, row):
    part = tile[:, :LANES] * row[:, :LANES]
    for q in range(1, tile.shape[1] // LANES):
        part = part + tile[:, q * LANES : (q + 1) * LANES] * row[:, q * LANES : (q + 1) * LANES]
    return part


def twice(col):
    return jnp.concatenate([col] * (HALF // LANES), axis=1)


def place(x, n):
    bits = n.bit_length() - 1
    div, rem = (lambda a, b: a // b, lambda a, b: a % b) if isinstance(x, int) else (lax.div, lax.rem)
    return sum(rem(div(x, 1 << (bits - 1 - j)), 2) * (1 << j) for j in range(bits))


def far_tiles(pairs, count, row_in, sources, rows_out, cols_out, base, left_buf, right_buf, lhs_buf, rhs_buf, part_buf):
    n_col = lax.axis_size("col")
    row_step = 2 * row_in[0].shape[0] // n_col
    blocks = row_step - 1
    my_row, my_col = lax.axis_index("row"), lax.axis_index("col")

    def step(s, _):
        a, b = pairs[0, s], pairs[1, s]
        a_way, b_way = jnp.bitwise_xor(lax.div(a, blocks), my_col), jnp.bitwise_xor(lax.div(b, blocks), my_row)
        here = functools.reduce(jnp.logical_or, [b_way == d for d in sources])
        pl.when(here)(lambda: tile(s, a_way, b_way, lax.rem(a, blocks), lax.rem(b, blocks)))
        return 0

    def tile(s, a_way, b_way, ka, kb):
        same = (a_way == 0) & (b_way == 0) & (ka == kb)
        for d, other in sources.items():

            @pl.when(b_way == d)
            def _():
                if d == 0:
                    right_buf[...] = other[kb]
                else:
                    lines = [other[pl.ds(base + 4 * kb + c, 1), :] for c in range(4)]
                    right_buf[...] = jnp.concatenate(lines, axis=0)

        for core, half in enumerate(row_in):

            @pl.when(lax.rem(a_way, 2) == core)
            def _():
                left_buf[...] = half[place(lax.div(a_way, 2), n_col // 2) * row_step + ka]

        left, right = left_buf[...], right_buf[...]
        lhs_buf[...] = jnp.transpose(left_terms(left, [left[3:4]])).astype(jnp.bfloat16)
        rhs_buf[...] = right_terms(right)
        lhs = lhs_buf[...]
        zcol = column_of(lhs, 0)
        total = []
        for h in range(BLK // HALF):
            cols = slice(h * HALF, (h + 1) * HALF)
            dist = jnp.dot(lhs, rhs_buf[:, cols], preferred_element_type=jnp.float32)
            acc = jnp.zeros((8, HALF), jnp.float32)
            for g in range(BLK // 8):
                rows = slice(g * 8, (g + 1) * 8)
                tile = lax.rsqrt(dist[rows, :])
                part = fold_lanes(tile, right[3:4, cols])
                part_buf[rows, :] = part if h == 0 else part_buf[rows, :] + part
                acc = acc + tile * twice(zcol[rows, :])
            total.append(jnp.sum(acc, axis=0, keepdims=True))
        rows_out[pl.ds(s, 1), :] = jnp.sum(jnp.transpose(part_buf[...]), axis=0, keepdims=True)
        cols_out[pl.ds(s, 1), :] = jnp.concatenate(total, axis=1) * jnp.where(same, 0.0, 1.0)

    lax.fori_loop(0, count[0], step, 0)


def points(tall):
    quad = tall.shape[0] // 4
    sides = [[tall[quad * c + u : quad * c + u + 1, :] for c in range(4)] for u in range(quad)]
    return jnp.concatenate([jnp.concatenate(side, axis=0) for side in sides], axis=1)


def near_tile(left, dens_i, right, dens_j, lhs_buf, rhs_buf, part_buf, acc_buf):
    quad = left.shape[1] // BLK
    terms = jnp.transpose(left_terms(left, [left[3:4], jnp.concatenate([dens_i] * quad, axis=1)]))
    terms = terms.astype(jnp.bfloat16)
    for g in range(BLK // GROUP):
        for u in range(quad):
            to, at = (g * quad + u) * GROUP, u * BLK + g * GROUP
            lhs_buf[to : to + GROUP, :] = terms[at : at + GROUP, :]
    rhs_buf[...] = right_terms(right)
    weights = right[3:4]
    acc_buf[...] = jnp.zeros_like(acc_buf)

    def chunk(i, _):
        at = pl.multiple_of(i * CHUNK * quad, CHUNK * quad)
        lhs = lhs_buf[pl.ds(at, CHUNK * quad), :]
        wcol = column_of(lhs, 0)
        groups = CHUNK // GROUP
        first_rows = [lhs[g * quad * GROUP : g * quad * GROUP + GROUP, :] for g in range(groups)]
        dcol = column_of(jnp.concatenate(first_rows, axis=0), 1)
        part = None
        for h in range(BLK // HALF):
            tiles = [None] * groups
            for v in range(quad):
                cols = slice(v * BLK + h * HALF, v * BLK + (h + 1) * HALF)
                dist = jnp.dot(lhs, rhs_buf[:, cols], preferred_element_type=jnp.float32)
                for g in range(groups):
                    inner = None
                    for u in range(quad):
                        rows = slice((g * quad + u) * GROUP, (g * quad + u + 1) * GROUP)
                        term = lax.rsqrt(dist[rows, :]) * twice(wcol[rows, :])
                        inner = term if inner is None else inner + term
                    inner = inner * weights[:, cols]
                    tiles[g] = inner if tiles[g] is None else tiles[g] + inner
            tile = jnp.concatenate(tiles, axis=0)
            cols = slice(h * HALF, (h + 1) * HALF)
            more = fold_lanes(tile, dens_j[:, cols])
            part = more if part is None else part + more
            acc_buf[:, cols] += jnp.sum((tile * twice(dcol)).reshape(-1, 8, HALF), axis=0)
        part_buf[pl.ds(pl.multiple_of(i * CHUNK, CHUNK), CHUNK), :] = part
        return 0

    lax.fori_loop(0, BLK // CHUNK, chunk, 0)
    rows = jnp.sum(jnp.transpose(part_buf[...]), axis=0, keepdims=True)
    return rows, jnp.sum(acc_buf[...], axis=0, keepdims=True)


def near_own_kernel(pairs, count, near_ref, field, *bufs):
    blocks, depth, _ = near_ref.shape
    body = depth - 8
    my_row = lax.axis_index("row")
    field[...] = jnp.zeros_like(field)

    def step(s, _):
        ka, kb = lax.rem(pairs[0, s], blocks), pairs[1, s] - my_row * blocks

        @pl.when((kb >= 0) & (kb < blocks))
        def _():
            left, right = points(near_ref[ka, 0:body, :]), points(near_ref[kb, 0:body, :])
            dens_i, dens_j = near_ref[ka, body : body + 1, :], near_ref[kb, body : body + 1, :]
            rows, cols = near_tile(left, dens_i, right, dens_j, *bufs)
            field[pl.ds(ka, 1), :] += rows
            field[pl.ds(kb, 1), :] += cols * jnp.where(ka == kb, 0.0, 1.0)

        return 0

    lax.fori_loop(0, count[0], step, 0)


def near_tiles(meanwhile, near_ref, got, field, put, right_buf, tags, sems, *bufs):
    blocks, depth, _ = near_ref.shape
    body = depth - 8
    base = near_lines(SLOTS, body // 4)
    my_row = lax.axis_index("row")
    copies = [
        pltpu.make_async_copy(g.at[base - 8 : base, 0:LANES], tags.at[d], sems.at[d]) for d, g in enumerate(got)
    ]
    for copy in copies:
        copy.start()
    meanwhile()
    for copy in copies:
        copy.wait()

    def step(i, _):
        way, t = lax.div(i, SLOTS), lax.rem(i, SLOTS)
        kb = tags[way, 7, t].astype(jnp.int32) - my_row * blocks

        @pl.when((kb >= 0) & (kb < blocks))
        def _():
            for d, other in enumerate(got):

                @pl.when(way == d)
                def _():
                    at = pl.multiple_of(t * body, 8)
                    right_buf[0:body, :] = other[pl.ds(at, body), :]
                    right_buf[body : body + 1, :] = other[pl.ds(SLOTS * body + t, 1), :]

            left, right = points(near_ref[kb, 0:body, :]), points(right_buf[0:body, :])
            dens_i, dens_j = near_ref[kb, body : body + 1, :], right_buf[body : body + 1, :]
            rows, cols = near_tile(left, dens_i, right, dens_j, *bufs)
            field[pl.ds(kb, 1), :] += rows
            put(way, t, cols)

        return 0

    lax.fori_loop(0, len(got) * SLOTS, step, 0)


def direct_kernel(near_ref, start, *refs, ways):
    got, (field, *backs), scratch = refs[:ways], refs[ways : 2 * ways + 1], refs[2 * ways + 1 :]

    def clear():
        field[...] = start[...]
        for back in backs:
            back[...] = jnp.zeros_like(back)

    def put(way, t, result):
        for i, back in enumerate(backs):

            @pl.when(way == i)
            def _():
                back[pl.ds(t, 1), :] = result

    near_tiles(clear, near_ref, got, field, put, *scratch)


def far_kernel(pairs, count, row0, row1, own_in, *refs, direct, base):
    got, (rows_out, cols_out), scratch = refs[: len(direct)], refs[len(direct) : -5], refs[-5:]
    rows_out[...] = jnp.zeros_like(rows_out)
    cols_out[...] = jnp.zeros_like(cols_out)
    sources = {0: own_in, **dict(zip(direct, got))}
    far_tiles(pairs, count, (row0, row1), sources, rows_out, cols_out, base, *scratch)


def late_kernel(pairs, count, near_ref, start, row0, row1, rows_in, cols_in, *refs, n_row, direct, late):
    refs = list(refs)
    take = lambda n: [refs.pop(0) for _ in range(n)]
    got, backs = take(len(late)), take(len(direct))
    field, rows_out, cols_out, *messages = take(n_row + 2)
    near_scratch, far_scratch = take(len(NEAR_SCRATCH) + 3), refs
    nfar = cols_out.shape[0]
    base = near_lines(SLOTS, near_ref.shape[1] // 4 - 2)
    my_row = lax.axis_index("row")

    def to_peer(d, lines, value):
        k = lax.rem(jnp.bitwise_xor(my_row, d) - my_row + n_row - 1, n_row)
        for i, message in enumerate(messages):

            @pl.when(k == i)
            def _():
                message[lines, :] = value

    def put(way, t, result):
        for i, d in enumerate(late):
            pl.when(way == i)(lambda: to_peer(d, pl.ds(nfar + t, 1), result))

    def far():
        field[...] = start[...]
        rows_out[...] = rows_in[...]
        cols_out[...] = cols_in[...]
        for message in messages:
            message[nfar:, :] = jnp.zeros((8, BLK), jnp.float32)
        for d, back in zip(direct, backs):
            to_peer(d, slice(nfar, nfar + 8), back[...])
        far_tiles(pairs, count, (row0, row1), dict(zip(late, got)), rows_out, cols_out, base, *far_scratch)
        for message in messages:
            message[0:nfar, :] = cols_out[...]

    near_tiles(far, near_ref, got, field, put, *near_scratch)


def hot(index, blocks, slots, base):
    want = lax.broadcasted_iota(jnp.int32, (blocks, slots), 0) + base * blocks
    return jnp.where(index[:, 0:slots] == want.astype(jnp.float32), 1.0, 0.0)


def spread(pick, slots, weight):
    pick = jnp.concatenate(pick * 3, axis=1).astype(jnp.bfloat16)
    slots = jnp.concatenate(three(jnp.concatenate(slots, axis=0)), axis=0).astype(jnp.bfloat16)
    return jnp.dot(pick, slots, preferred_element_type=jnp.float32) * weight[...]


def cols_kernel(pairs, weight, near, own_far, own_cols, *refs, n_row, base):
    col_far, messages, field = refs[: n_row - 1], refs[n_row - 1 : -1], refs[-1]
    blocks, nfar = weight.shape[0], own_cols.shape[0]
    my_row = lax.axis_index("row")
    line = base + 4 * blocks + 1
    pick = [hot(own_far[blocks, 1:2, :], blocks, nfar, my_row)]
    for k in range(1, n_row):
        way = jnp.bitwise_xor(my_row, lax.rem(my_row + n_row - k, n_row))
        index = jnp.zeros((1, BLK), jnp.float32)
        for d, other in enumerate(col_far):
            index = jnp.where(way == d + 1, other[line : line + 1, :], index)
        pick.append(hot(index, blocks, nfar, my_row))
    field[...] = near[...] + spread(pick, [own_cols[...]] + [m[0:nfar, :] for m in messages], weight)
    for message in messages:
        for t in range(pairs.shape[1] - 1):
            k = lax.rem(pairs[0, t + 1], blocks)
            field[pl.ds(k, 1), :] += message[nfar + t : nfar + t + 1, :]


def rows_kernel(weight, field, row0, row1, *refs, n_col):
    rows, out = refs[:-1], refs[-1]
    blocks, nfar = weight.shape[0], rows[0].shape[0] // 2
    my_col = lax.axis_index("col")
    chips = n_col // 2
    chip = lax.div(my_col, 2)
    pick = []
    for k in range(chips):
        way = jnp.bitwise_xor(chip, lax.rem(chip + chips - k, chips))
        tag = place(way, chips) * (blocks + 1) + blocks
        pick += [hot(half[tag, 0:1, :], blocks, nfar, my_col) for half in (row0, row1)]
    total = field[...] + spread(pick, [r[...] for r in rows], weight)
    for q in range(BLK // LANES):
        out[pl.ds(q, blocks, stride=BLK // LANES), :] = total[:, q * LANES : (q + 1) * LANES]


def f32(*shape):
    return jax.ShapeDtypeStruct(shape, jnp.float32)


def cost(micros):
    return pl.CostEstimate(flops=int(micros * 1.1e9), bytes_accessed=1 << 16, transcendentals=0)


def body(points, density, near_pairs, far_pairs, near_count, far_count, *, n_row, n_col):
    quad = points.shape[1]
    blocks = points.shape[2] // BLK
    nnear, nfar = near_pairs.shape[0], far_pairs.shape[0]
    depth, slots = 4 * quad, nnear - 1
    near_pairs, far_pairs = near_pairs.T, far_pairs.T

    def swap(x, axis, d):
        n = {"row": n_row, "col": n_col}[axis]
        return lax.ppermute(x, axis, [(i, i ^ d) for i in range(n)])

    def halves(n):
        return [1 << j for j in reversed(range(n.bit_length() - 1))]

    def row_gather(x):
        known = {0: x}
        for d in halves(n_row):
            known.update({k ^ d: swap(v, "row", d) for k, v in known.items()})
        return [known[k] for k in range(n_row)]

    def col_gather(x):
        for d in halves(n_col)[:-1]:
            x = jnp.concatenate([x, swap(x, "col", d)], axis=0)
        return x, swap(x, "col", 1)

    base = near_lines(slots, quad)
    msg_rows = -(-(base + 4 * (blocks + 1)) // 8) * 8
    hbm = (near_pairs, far_pairs, points, density.reshape(-1, LANES))
    hbm = [pltpu.with_memory_space_constraint(x, pltpu.HBM) for x in hbm]
    msg, far_own, near_own, weight = pl.pallas_call(
        prep_kernel,
        out_shape=(
            f32(msg_rows, BLK),
            f32(blocks + 1, 4, BLK),
            f32(blocks, depth + 8, BLK),
            f32(blocks, BLK),
        ),
        in_specs=[HBM, SMEM, HBM, HBM, HBM],
        out_specs=(VMEM, VMEM, VMEM, VMEM),
        scratch_shapes=[
            pltpu.SMEM(near_pairs.shape, jnp.int32),
            pltpu.VMEM(far_pairs.shape, jnp.int32),
            pltpu.VMEM(points.shape, jnp.float32),
            pltpu.VMEM((density.shape[0] // LANES, LANES), jnp.float32),
            pltpu.SemaphoreType.DMA((QUARTERS + 3,)),
        ],
        compiler_params=PARAMS,
        cost_estimate=cost(1.2),
        name="prep",
    )(hbm[0], near_count, *hbm[1:])
    got = row_gather(msg)[1:]
    row_far = col_gather(far_own)

    bufs = [
        pltpu.VMEM((quad * BLK, TERMS), jnp.bfloat16),
        pltpu.VMEM((TERMS, quad * BLK), jnp.bfloat16),
        pltpu.VMEM((BLK, LANES), jnp.float32),
        pltpu.VMEM((8, BLK), jnp.float32),
    ]
    near0 = pl.pallas_call(
        near_own_kernel,
        out_shape=f32(blocks, BLK),
        in_specs=[SMEM, SMEM, VMEM],
        out_specs=VMEM,
        scratch_shapes=bufs,
        compiler_params=PARAMS,
        cost_estimate=cost(5.0),
        name="near_own",
    )(near_pairs, near_count, near_own)

    def near_scratch(n):
        return [
            pltpu.VMEM((depth + 8, BLK), jnp.float32),
            pltpu.SMEM((n, 8, LANES), jnp.float32),
            pltpu.SemaphoreType.DMA((n,)),
        ] + bufs

    direct = [d for d in range(1, n_row) if d & (d - 1) == 0]
    late = [d for d in range(1, n_row) if d & (d - 1) != 0]
    far_scratch = [
        pltpu.VMEM((4, BLK), jnp.float32),
        pltpu.VMEM((4, BLK), jnp.float32),
        pltpu.VMEM((BLK, TERMS), jnp.bfloat16),
        pltpu.VMEM((TERMS, BLK), jnp.bfloat16),
        pltpu.VMEM((BLK, LANES), jnp.float32),
    ]
    field, *backs = pl.pallas_call(
        functools.partial(direct_kernel, ways=len(direct)),
        out_shape=[f32(blocks, BLK)] + [f32(8, BLK)] * len(direct),
        in_specs=[VMEM] * (2 + len(direct)),
        out_specs=[VMEM] * (len(direct) + 1),
        scratch_shapes=near_scratch(len(direct)),
        compiler_params=PARAMS,
        cost_estimate=cost(30.0),
        name="near_direct",
    )(near_own, near0, *[got[d - 1] for d in direct])
    far_rows, far_cols = pl.pallas_call(
        functools.partial(far_kernel, direct=direct, base=base),
        out_shape=[f32(nfar, BLK)] * 2,
        in_specs=[SMEM, SMEM] + [VMEM] * (3 + len(direct)),
        out_specs=[VMEM] * 2,
        scratch_shapes=far_scratch,
        compiler_params=PARAMS,
        cost_estimate=cost(3.0),
        name="far_direct",
    )(far_pairs, far_count, *row_far, far_own, *[got[d - 1] for d in direct])
    field, far_rows, far_cols, *messages = pl.pallas_call(
        functools.partial(late_kernel, n_row=n_row, direct=direct, late=late),
        out_shape=[f32(blocks, BLK)] + [f32(nfar, BLK)] * 2 + [f32(nfar + 8, BLK)] * (n_row - 1),
        in_specs=[SMEM, SMEM] + [VMEM] * (6 + n_row - 1),
        out_specs=[VMEM] * (n_row + 2),
        scratch_shapes=near_scratch(len(late)) + far_scratch,
        compiler_params=PARAMS,
        cost_estimate=cost(8.0),
        name="late",
    )(far_pairs, far_count, near_own, field, *row_far, far_rows, far_cols, *[got[d - 1] for d in late], *backs)

    messages = [
        lax.ppermute(x, "row", [(i, (i + k + 1) % n_row) for i in range(n_row)]) for k, x in enumerate(messages)
    ]
    both = jnp.concatenate([far_rows, swap(far_rows, "col", 1)], axis=0)
    rows = [both]
    for k in range(2, n_col, 2):
        rows.append(lax.ppermute(both, "col", [(i, (i + k) % n_col) for i in range(n_col)]))
    field = pl.pallas_call(
        functools.partial(cols_kernel, n_row=n_row, base=base),
        out_shape=f32(blocks, BLK),
        in_specs=[SMEM] + [VMEM] * (2 * n_row + 2),
        out_specs=VMEM,
        compiler_params=PARAMS,
        cost_estimate=cost(1.0),
        name="final_cols",
    )(near_pairs, weight, field, far_own, far_cols, *got, *messages)
    out = pl.pallas_call(
        functools.partial(rows_kernel, n_col=n_col),
        out_shape=f32(blocks * BLK // LANES, LANES),
        in_specs=[VMEM] * (4 + len(rows)),
        out_specs=VMEM,
        compiler_params=PARAMS,
        cost_estimate=cost(1.0),
        name="final_rows",
    )(weight, field, *row_far, *rows)
    return out.reshape(-1)


def solution(mesh):
    in_specs = (
        P(None, None, ("row", "col")),
        P(("row", "col")),
        P(("row", "col"), None),
        P(("row", "col"), None),
        P(("row", "col")),
        P(("row", "col")),
    )
    out_specs = P(("row", "col"))
    kernel = functools.partial(body, n_row=mesh.shape["row"], n_col=mesh.shape["col"])
    return jax.shard_map(kernel, mesh=mesh, in_specs=in_specs, out_specs=out_specs, check_vma=False)
```

```python
import functools

import jax
import jax.numpy as jnp
from jax import lax
from jax.experimental import pallas as pl
from jax.experimental.pallas import tpu as pltpu
from jax.sharding import PartitionSpec as P

BLK = 512
LANES = 128
SOFT_SQ = 0.0004
TERMS = 64
SPLIT = 48
HALF = 512
QUARTERS = 4
SLOTS = 5
NEAR_SCRATCH = 4 * [None]
GROUP = 16
CHUNK = 512
VMEM = pl.BlockSpec(memory_space=pltpu.VMEM)
SMEM = pl.BlockSpec(memory_space=pltpu.SMEM)
ANY = pl.BlockSpec(memory_space=pl.ANY)
HBM = pl.BlockSpec(memory_space=pltpu.HBM)
PARAMS = pltpu.CompilerParams(vmem_limit_bytes=40 * 1024 * 1024)


def prep_kernel(near_hbm, count, far_hbm, pts_hbm, dens_hbm, msg, far_out, near_out, weight_out, *scratch):
    near_ref, far_ref, pts_ref, dens_ref, sems = scratch
    blocks = near_out.shape[0]
    quad = pts_ref.shape[1]
    slots, body = near_ref.shape[1] - 1, quad * 4
    base = near_lines(slots, quad)
    width = pts_ref.shape[2] // QUARTERS
    copies = [
        pltpu.make_async_copy(dens_hbm, dens_ref, sems.at[QUARTERS]),
        pltpu.make_async_copy(far_hbm, far_ref, sems.at[QUARTERS + 1]),
        pltpu.make_async_copy(near_hbm, near_ref, sems.at[QUARTERS + 2]),
    ]
    for i in range(QUARTERS):
        part = slice(i * width, (i + 1) * width)
        copies.append(pltpu.make_async_copy(pts_hbm.at[:, :, part], pts_ref.at[:, :, part], sems.at[i]))
    for copy in copies:
        copy.start()
    copies.pop(0).wait()
    copies.pop(0).wait()
    copies.pop(0).wait()

    def put_far(k, value):
        far_out[k] = value
        msg[base + 4 * k : base + 4 * k + 4, :] = value

    for k in range(blocks):
        cols = slice(k * BLK, (k + 1) * BLK)
        if k % (blocks // QUARTERS) == 0:
            copies.pop(0).wait()
        w = pts_ref[3, :, cols]
        total = jnp.sum(w, axis=0, keepdims=True)
        dens = jnp.concatenate([dens_ref[4 * k + q : 4 * k + q + 1, :] for q in range(4)], axis=1)
        lines = []
        for c in range(3):
            x = pts_ref[c, :, cols]
            lines.append(jnp.sum(x * w, axis=0, keepdims=True) / total)
            near_out[k, quad * c : quad * c + quad, :] = x
        near_out[k, quad * 3 : quad * 4, :] = w
        near_out[k, quad * 4 : quad * 4 + 8, :] = jnp.broadcast_to(dens, (8, BLK))
        put_far(k, jnp.concatenate(lines + [total * dens], axis=0))
        weight_out[k : k + 1, :] = total
    lane = lax.broadcasted_iota(jnp.int32, (1, LANES), 1)
    lines = [jnp.full((1, LANES), -1.0, jnp.float32)] * 2
    for t in range(slots):
        k = lax.rem(near_ref[0, t + 1], blocks)
        msg[t * body : (t + 1) * body, :] = near_out[k, 0:body, :]
        source = jnp.where(t + 1 < count[0], near_ref[1, t + 1], -1)
        lines[0] = jnp.where(lane == t, k.astype(jnp.float32), lines[0])
        lines[1] = jnp.where(lane == t, source.astype(jnp.float32), lines[1])
    pairs = jnp.concatenate([far_ref[...].astype(jnp.float32), jnp.full((2, LANES - far_ref.shape[1]), -1.0)], axis=1)
    pairs = jnp.concatenate([pairs] + lines, axis=0)
    put_far(blocks, jnp.concatenate([pairs] * (BLK // LANES), axis=1))
    used = base + 4 * (blocks + 1)
    if used < msg.shape[0]:
        msg[used:, :] = jnp.zeros((msg.shape[0] - used, BLK), jnp.float32)


def near_lines(slots, quad):
    return slots * 4 * quad


def three(value):
    one = value.astype(jnp.bfloat16).astype(jnp.float32)
    two = (value - one).astype(jnp.bfloat16).astype(jnp.float32)
    return one, two, value - one - two


def pick_row(row, values):
    out = jnp.zeros(row.shape, jnp.float32)
    for k, value in enumerate(values):
        out = jnp.where(row == k, value, out)
    return out


def parts(x):
    row = lax.broadcasted_iota(jnp.int32, x.shape, 0)
    live = row < 3
    centred = jnp.where(live, x - 0.5, 0.0)
    head = jnp.round(centred * 256.0) * (1.0 / 256.0)
    rest = centred - head
    rest1 = rest.astype(jnp.bfloat16).astype(jnp.float32)
    big = pick_row(row, three(jnp.sum(head * head, axis=0, keepdims=True)))
    small = pick_row(row, three(jnp.sum(rest * (2.0 * head + rest), axis=0, keepdims=True) + 0.5 * SOFT_SQ))
    return head, rest1, rest - rest1, big, small, jnp.where(live, 1.0, 0.0)


def left_terms(x, columns):
    head, rest1, rest2, big, small, ones = parts(x)
    h2, a2, b2 = -2.0 * head, -2.0 * rest1, -2.0 * rest2
    groups = [h2, big, ones, small, ones, h2, h2, a2, b2, a2, a2, b2]
    row = lax.broadcasted_iota(jnp.int32, (TERMS - SPLIT, x.shape[1]), 0)
    groups.append(pick_row(row, [part for column in columns for part in three(column)]))
    return jnp.concatenate(groups, axis=0)


def right_terms(x):
    head, rest1, rest2, big, small, ones = parts(x)
    groups = [head, ones, big, ones, small, rest1, rest2, head, head, rest1, rest2, rest1]
    groups.append(jnp.zeros((TERMS - SPLIT, x.shape[1]), jnp.float32))
    return jnp.concatenate(groups, axis=0).astype(jnp.bfloat16)


def column_of(lhs, which):
    row = lax.broadcasted_iota(jnp.int32, (TERMS, LANES), 0) - SPLIT - 3 * which
    pick = jnp.where((row >= 0) & (row < 3), 1.0, 0.0).astype(jnp.bfloat16)
    return jnp.dot(lhs, pick, preferred_element_type=jnp.float32)


def fold_lanes(tile, row):
    part = tile[:, :LANES] * row[:, :LANES]
    for q in range(1, tile.shape[1] // LANES):
        part = part + tile[:, q * LANES : (q + 1) * LANES] * row[:, q * LANES : (q + 1) * LANES]
    return part


def twice(col):
    return jnp.concatenate([col] * (HALF // LANES), axis=1)


def place(x, n):
    bits = n.bit_length() - 1
    div, rem = (lambda a, b: a // b, lambda a, b: a % b) if isinstance(x, int) else (lax.div, lax.rem)
    return sum(rem(div(x, 1 << (bits - 1 - j)), 2) * (1 << j) for j in range(bits))


def far_tiles(pairs, count, row_in, sources, rows_out, cols_out, base, left_buf, right_buf, lhs_buf, rhs_buf, part_buf):
    n_col = lax.axis_size("col")
    row_step = 2 * row_in[0].shape[0] // n_col
    blocks = row_step - 1
    my_row, my_col = lax.axis_index("row"), lax.axis_index("col")

    def step(s, _):
        a, b = pairs[0, s], pairs[1, s]
        a_way, b_way = jnp.bitwise_xor(lax.div(a, blocks), my_col), jnp.bitwise_xor(lax.div(b, blocks), my_row)
        here = functools.reduce(jnp.logical_or, [b_way == d for d in sources])
        pl.when(here)(lambda: tile(s, a_way, b_way, lax.rem(a, blocks), lax.rem(b, blocks)))
        return 0

    def tile(s, a_way, b_way, ka, kb):
        same = (a_way == 0) & (b_way == 0) & (ka == kb)
        for d, other in sources.items():

            @pl.when(b_way == d)
            def _():
                if d == 0:
                    right_buf[...] = other[kb]
                else:
                    lines = [other[pl.ds(base + 4 * kb + c, 1), :] for c in range(4)]
                    right_buf[...] = jnp.concatenate(lines, axis=0)

        for core, half in enumerate(row_in):

            @pl.when(lax.rem(a_way, 2) == core)
            def _():
                left_buf[...] = half[place(lax.div(a_way, 2), n_col // 2) * row_step + ka]

        left, right = left_buf[...], right_buf[...]
        lhs_buf[...] = jnp.transpose(left_terms(left, [left[3:4]])).astype(jnp.bfloat16)
        rhs_buf[...] = right_terms(right)
        lhs = lhs_buf[...]
        zcol = column_of(lhs, 0)
        total = []
        for h in range(BLK // HALF):
            cols = slice(h * HALF, (h + 1) * HALF)
            dist = jnp.dot(lhs, rhs_buf[:, cols], preferred_element_type=jnp.float32)
            acc = jnp.zeros((8, HALF), jnp.float32)
            for g in range(BLK // 8):
                rows = slice(g * 8, (g + 1) * 8)
                tile = lax.rsqrt(dist[rows, :])
                part = fold_lanes(tile, right[3:4, cols])
                part_buf[rows, :] = part if h == 0 else part_buf[rows, :] + part
                acc = acc + tile * twice(zcol[rows, :])
            total.append(jnp.sum(acc, axis=0, keepdims=True))
        rows_out[pl.ds(s, 1), :] = jnp.sum(jnp.transpose(part_buf[...]), axis=0, keepdims=True)
        cols_out[pl.ds(s, 1), :] = jnp.concatenate(total, axis=1) * jnp.where(same, 0.0, 1.0)

    lax.fori_loop(0, count[0], step, 0)


def points(tall):
    quad = tall.shape[0] // 4
    sides = [[tall[quad * c + u : quad * c + u + 1, :] for c in range(4)] for u in range(quad)]
    return jnp.concatenate([jnp.concatenate(side, axis=0) for side in sides], axis=1)


def near_tile(left, dens_i, right, dens_j, lhs_buf, rhs_buf, part_buf, acc_buf):
    quad = left.shape[1] // BLK
    terms = jnp.transpose(left_terms(left, [left[3:4], jnp.concatenate([dens_i] * quad, axis=1)]))
    terms = terms.astype(jnp.bfloat16)
    for g in range(BLK // GROUP):
        for u in range(quad):
            to, at = (g * quad + u) * GROUP, u * BLK + g * GROUP
            lhs_buf[to : to + GROUP, :] = terms[at : at + GROUP, :]
    rhs_buf[...] = right_terms(right)
    weights = right[3:4]
    acc_buf[...] = jnp.zeros_like(acc_buf)

    def chunk(i, _):
        at = pl.multiple_of(i * CHUNK * quad, CHUNK * quad)
        lhs = lhs_buf[pl.ds(at, CHUNK * quad), :]
        wcol = column_of(lhs, 0)
        groups = CHUNK // GROUP
        first_rows = [lhs[g * quad * GROUP : g * quad * GROUP + GROUP, :] for g in range(groups)]
        dcol = column_of(jnp.concatenate(first_rows, axis=0), 1)
        part = None
        for h in range(BLK // HALF):
            tiles = [None] * groups
            for v in range(quad):
                cols = slice(v * BLK + h * HALF, v * BLK + (h + 1) * HALF)
                dist = jnp.dot(lhs, rhs_buf[:, cols], preferred_element_type=jnp.float32)
                for g in range(groups):
                    inner = None
                    for u in range(quad):
                        rows = slice((g * quad + u) * GROUP, (g * quad + u + 1) * GROUP)
                        term = lax.rsqrt(dist[rows, :]) * twice(wcol[rows, :])
                        inner = term if inner is None else inner + term
                    inner = inner * weights[:, cols]
                    tiles[g] = inner if tiles[g] is None else tiles[g] + inner
            tile = jnp.concatenate(tiles, axis=0)
            cols = slice(h * HALF, (h + 1) * HALF)
            more = fold_lanes(tile, dens_j[:, cols])
            part = more if part is None else part + more
            acc_buf[:, cols] += jnp.sum((tile * twice(dcol)).reshape(-1, 8, HALF), axis=0)
        part_buf[pl.ds(pl.multiple_of(i * CHUNK, CHUNK), CHUNK), :] = part
        return 0

    lax.fori_loop(0, BLK // CHUNK, chunk, 0)
    rows = jnp.sum(jnp.transpose(part_buf[...]), axis=0, keepdims=True)
    return rows, jnp.sum(acc_buf[...], axis=0, keepdims=True)


def near_own_kernel(pairs, count, near_ref, field, *bufs):
    blocks, depth, _ = near_ref.shape
    body = depth - 8
    my_row = lax.axis_index("row")
    field[...] = jnp.zeros_like(field)

    def step(s, _):
        ka, kb = lax.rem(pairs[0, s], blocks), pairs[1, s] - my_row * blocks

        @pl.when((kb >= 0) & (kb < blocks))
        def _():
            left, right = points(near_ref[ka, 0:body, :]), points(near_ref[kb, 0:body, :])
            dens_i, dens_j = near_ref[ka, body : body + 1, :], near_ref[kb, body : body + 1, :]
            rows, cols = near_tile(left, dens_i, right, dens_j, *bufs)
            field[pl.ds(ka, 1), :] += rows
            field[pl.ds(kb, 1), :] += cols * jnp.where(ka == kb, 0.0, 1.0)

        return 0

    lax.fori_loop(0, count[0], step, 0)


def near_tiles(meanwhile, near_ref, got, field, put, right_buf, tags, sems, *bufs):
    blocks, depth, _ = near_ref.shape
    body = depth - 8
    base = near_lines(SLOTS, body // 4)
    my_row = lax.axis_index("row")
    tail = slice(base + 4 * blocks, base + 4 * blocks + 8)
    copies = [pltpu.make_async_copy(g.at[tail, 0:LANES], tags.at[d], sems.at[d]) for d, g in enumerate(got)]
    for copy in copies:
        copy.start()
    meanwhile()
    for copy in copies:
        copy.wait()

    def step(i, _):
        way, t = lax.div(i, SLOTS), lax.rem(i, SLOTS)
        kb = tags[way, 3, t].astype(jnp.int32) - my_row * blocks

        @pl.when((kb >= 0) & (kb < blocks))
        def _():
            for d, other in enumerate(got):

                @pl.when(way == d)
                def _():
                    at = pl.multiple_of(t * body, 8)
                    points_j = other[pl.ds(at, body), :]
                    line = base + 4 * tags[way, 2, t].astype(jnp.int32) + 3
                    total = jnp.sum(points_j[body - body // 4 :], axis=0, keepdims=True)
                    right_buf[0:body, :] = points_j
                    right_buf[body : body + 1, :] = other[pl.ds(line, 1), :] / total

            left, right = points(near_ref[kb, 0:body, :]), points(right_buf[0:body, :])
            dens_i, dens_j = near_ref[kb, body : body + 1, :], right_buf[body : body + 1, :]
            rows, cols = near_tile(left, dens_i, right, dens_j, *bufs)
            field[pl.ds(kb, 1), :] += rows
            put(way, t, cols)

        return 0

    lax.fori_loop(0, len(got) * SLOTS, step, 0)


def direct_kernel(near_ref, start, *refs, ways):
    got, (field, *backs), scratch = refs[:ways], refs[ways : 2 * ways + 1], refs[2 * ways + 1 :]

    def clear():
        field[...] = start[...]
        for back in backs:
            back[...] = jnp.zeros_like(back)

    def put(way, t, result):
        for i, back in enumerate(backs):

            @pl.when(way == i)
            def _():
                back[pl.ds(t, 1), :] = result

    near_tiles(clear, near_ref, got, field, put, *scratch)


def far_kernel(pairs, count, row0, row1, own_in, *refs, direct, base):
    got, (rows_out, cols_out), scratch = refs[: len(direct)], refs[len(direct) : -5], refs[-5:]
    rows_out[...] = jnp.zeros_like(rows_out)
    cols_out[...] = jnp.zeros_like(cols_out)
    sources = {0: own_in, **dict(zip(direct, got))}
    far_tiles(pairs, count, (row0, row1), sources, rows_out, cols_out, base, *scratch)


def late_kernel(pairs, count, near_ref, start, row0, row1, rows_in, cols_in, *refs, n_row, direct, late):
    refs = list(refs)
    take = lambda n: [refs.pop(0) for _ in range(n)]
    got, backs = take(len(late)), take(len(direct))
    field, rows_out, cols_out, *messages = take(n_row + 2)
    near_scratch, far_scratch = take(len(NEAR_SCRATCH) + 3), refs
    nfar = cols_out.shape[0]
    base = near_lines(SLOTS, near_ref.shape[1] // 4 - 2)
    my_row = lax.axis_index("row")

    def to_peer(d, lines, value):
        k = lax.rem(jnp.bitwise_xor(my_row, d) - my_row + n_row - 1, n_row)
        for i, message in enumerate(messages):

            @pl.when(k == i)
            def _():
                message[lines, :] = value

    def put(way, t, result):
        for i, d in enumerate(late):
            pl.when(way == i)(lambda: to_peer(d, pl.ds(nfar + t, 1), result))

    def far():
        field[...] = start[...]
        rows_out[...] = rows_in[...]
        cols_out[...] = cols_in[...]
        for message in messages:
            message[nfar:, :] = jnp.zeros((8, BLK), jnp.float32)
        for d, back in zip(direct, backs):
            to_peer(d, slice(nfar, nfar + 8), back[...])
        far_tiles(pairs, count, (row0, row1), dict(zip(late, got)), rows_out, cols_out, base, *far_scratch)
        for message in messages:
            message[0:nfar, :] = cols_out[...]

    near_tiles(far, near_ref, got, field, put, *near_scratch)


def hot(index, blocks, slots, base):
    want = lax.broadcasted_iota(jnp.int32, (blocks, slots), 0) + base * blocks
    return jnp.where(index[:, 0:slots] == want.astype(jnp.float32), 1.0, 0.0)


def spread(pick, slots, weight):
    pick = jnp.concatenate(pick * 3, axis=1).astype(jnp.bfloat16)
    slots = jnp.concatenate(three(jnp.concatenate(slots, axis=0)), axis=0).astype(jnp.bfloat16)
    return jnp.dot(pick, slots, preferred_element_type=jnp.float32) * weight[...]


def cols_kernel(pairs, weight, near, own_far, own_cols, *refs, n_row, base):
    col_far, messages, field = refs[: n_row - 1], refs[n_row - 1 : -1], refs[-1]
    blocks, nfar = weight.shape[0], own_cols.shape[0]
    my_row = lax.axis_index("row")
    line = base + 4 * blocks + 1
    pick = [hot(own_far[blocks, 1:2, :], blocks, nfar, my_row)]
    for k in range(1, n_row):
        way = jnp.bitwise_xor(my_row, lax.rem(my_row + n_row - k, n_row))
        index = jnp.zeros((1, BLK), jnp.float32)
        for d, other in enumerate(col_far):
            index = jnp.where(way == d + 1, other[line : line + 1, :], index)
        pick.append(hot(index, blocks, nfar, my_row))
    field[...] = near[...] + spread(pick, [own_cols[...]] + [m[0:nfar, :] for m in messages], weight)
    for message in messages:
        for t in range(pairs.shape[1] - 1):
            k = lax.rem(pairs[0, t + 1], blocks)
            field[pl.ds(k, 1), :] += message[nfar + t : nfar + t + 1, :]


def rows_kernel(weight, field, row0, row1, *refs, n_col):
    rows, out = refs[:-1], refs[-1]
    blocks, nfar = weight.shape[0], rows[0].shape[0] // 2
    my_col = lax.axis_index("col")
    chips = n_col // 2
    chip = lax.div(my_col, 2)
    pick = []
    for k in range(chips):
        way = jnp.bitwise_xor(chip, lax.rem(chip + chips - k, chips))
        tag = place(way, chips) * (blocks + 1) + blocks
        pick += [hot(half[tag, 0:1, :], blocks, nfar, my_col) for half in (row0, row1)]
    total = field[...] + spread(pick, [r[...] for r in rows], weight)
    for q in range(BLK // LANES):
        out[pl.ds(q, blocks, stride=BLK // LANES), :] = total[:, q * LANES : (q + 1) * LANES]


def f32(*shape):
    return jax.ShapeDtypeStruct(shape, jnp.float32)


def cost(micros):
    return pl.CostEstimate(flops=int(micros * 1.1e9), bytes_accessed=1 << 16, transcendentals=0)


def body(points, density, near_pairs, far_pairs, near_count, far_count, *, n_row, n_col):
    quad = points.shape[1]
    blocks = points.shape[2] // BLK
    nnear, nfar = near_pairs.shape[0], far_pairs.shape[0]
    depth, slots = 4 * quad, nnear - 1
    near_pairs, far_pairs = near_pairs.T, far_pairs.T

    def swap(x, axis, d):
        n = {"row": n_row, "col": n_col}[axis]
        return lax.ppermute(x, axis, [(i, i ^ d) for i in range(n)])

    direct = [d for d in range(1, n_row) if d & (d - 1) == 0]
    late = [d for d in range(1, n_row) if d & (d - 1) != 0]

    def halves(n):
        return [1 << j for j in reversed(range(n.bit_length() - 1))]

    def col_gather(x):
        for d in halves(n_col)[:-1]:
            x = jnp.concatenate([x, swap(x, "col", d)], axis=0)
        return x, swap(x, "col", 1)

    base = near_lines(slots, quad)
    msg_rows = -(-(base + 4 * (blocks + 1)) // 8) * 8
    hbm = (near_pairs, far_pairs, points, density.reshape(-1, LANES))
    hbm = [pltpu.with_memory_space_constraint(x, pltpu.HBM) for x in hbm]
    msg, far_own, near_own, weight = pl.pallas_call(
        prep_kernel,
        out_shape=(
            f32(msg_rows, BLK),
            f32(blocks + 1, 4, BLK),
            f32(blocks, depth + 8, BLK),
            f32(blocks, BLK),
        ),
        in_specs=[HBM, SMEM, HBM, HBM, HBM],
        out_specs=(VMEM, VMEM, VMEM, VMEM),
        scratch_shapes=[
            pltpu.SMEM(near_pairs.shape, jnp.int32),
            pltpu.VMEM(far_pairs.shape, jnp.int32),
            pltpu.VMEM(points.shape, jnp.float32),
            pltpu.VMEM((density.shape[0] // LANES, LANES), jnp.float32),
            pltpu.SemaphoreType.DMA((QUARTERS + 3,)),
        ],
        compiler_params=PARAMS,
        cost_estimate=cost(1.2),
        name="prep",
    )(hbm[0], near_count, *hbm[1:])
    row_far = col_gather(far_own)
    known = {d: swap(msg, "row", d) for d in direct}
    *onward, last = lax.optimization_barrier((*[known[d] for d in direct], row_far[0]))
    known.update(zip(direct, onward))
    row_far = (last, row_far[1])
    for d in late:
        known[d] = swap(known[d ^ (d & -d)], "row", d & -d)
    got = [known[d] for d in range(1, n_row)]

    bufs = [
        pltpu.VMEM((quad * BLK, TERMS), jnp.bfloat16),
        pltpu.VMEM((TERMS, quad * BLK), jnp.bfloat16),
        pltpu.VMEM((BLK, LANES), jnp.float32),
        pltpu.VMEM((8, BLK), jnp.float32),
    ]
    near0 = pl.pallas_call(
        near_own_kernel,
        out_shape=f32(blocks, BLK),
        in_specs=[SMEM, SMEM, VMEM],
        out_specs=VMEM,
        scratch_shapes=bufs,
        compiler_params=PARAMS,
        cost_estimate=cost(5.0),
        name="near_own",
    )(near_pairs, near_count, near_own)

    def near_scratch(n):
        return [
            pltpu.VMEM((depth + 8, BLK), jnp.float32),
            pltpu.SMEM((n, 8, LANES), jnp.float32),
            pltpu.SemaphoreType.DMA((n,)),
        ] + bufs

    far_scratch = [
        pltpu.VMEM((4, BLK), jnp.float32),
        pltpu.VMEM((4, BLK), jnp.float32),
        pltpu.VMEM((BLK, TERMS), jnp.bfloat16),
        pltpu.VMEM((TERMS, BLK), jnp.bfloat16),
        pltpu.VMEM((BLK, LANES), jnp.float32),
    ]
    field, *backs = pl.pallas_call(
        functools.partial(direct_kernel, ways=len(direct)),
        out_shape=[f32(blocks, BLK)] + [f32(8, BLK)] * len(direct),
        in_specs=[VMEM] * (2 + len(direct)),
        out_specs=[VMEM] * (len(direct) + 1),
        scratch_shapes=near_scratch(len(direct)),
        compiler_params=PARAMS,
        cost_estimate=cost(30.0),
        name="near_direct",
    )(near_own, near0, *[got[d - 1] for d in direct])
    far_rows, far_cols = pl.pallas_call(
        functools.partial(far_kernel, direct=direct, base=base),
        out_shape=[f32(nfar, BLK)] * 2,
        in_specs=[SMEM, SMEM] + [VMEM] * (3 + len(direct)),
        out_specs=[VMEM] * 2,
        scratch_shapes=far_scratch,
        compiler_params=PARAMS,
        cost_estimate=cost(3.0),
        name="far_direct",
    )(far_pairs, far_count, *row_far, far_own, *[got[d - 1] for d in direct])
    field, far_rows, far_cols, *messages = pl.pallas_call(
        functools.partial(late_kernel, n_row=n_row, direct=direct, late=late),
        out_shape=[f32(blocks, BLK)] + [f32(nfar, BLK)] * 2 + [f32(nfar + 8, BLK)] * (n_row - 1),
        in_specs=[SMEM, SMEM] + [VMEM] * (6 + n_row - 1),
        out_specs=[VMEM] * (n_row + 2),
        scratch_shapes=near_scratch(len(late)) + far_scratch,
        compiler_params=PARAMS,
        cost_estimate=cost(8.0),
        name="late",
    )(far_pairs, far_count, near_own, field, *row_far, far_rows, far_cols, *[got[d - 1] for d in late], *backs)

    messages = [
        lax.ppermute(x, "row", [(i, (i + k + 1) % n_row) for i in range(n_row)]) for k, x in enumerate(messages)
    ]
    both = jnp.concatenate([far_rows, swap(far_rows, "col", 1)], axis=0)
    rows = [both]
    for k in range(2, n_col, 2):
        rows.append(lax.ppermute(both, "col", [(i, (i + k) % n_col) for i in range(n_col)]))
    field = pl.pallas_call(
        functools.partial(cols_kernel, n_row=n_row, base=base),
        out_shape=f32(blocks, BLK),
        in_specs=[SMEM] + [VMEM] * (2 * n_row + 2),
        out_specs=VMEM,
        compiler_params=PARAMS,
        cost_estimate=cost(1.0),
        name="final_cols",
    )(near_pairs, weight, field, far_own, far_cols, *got, *messages)
    out = pl.pallas_call(
        functools.partial(rows_kernel, n_col=n_col),
        out_shape=f32(blocks * BLK // LANES, LANES),
        in_specs=[VMEM] * (4 + len(rows)),
        out_specs=VMEM,
        compiler_params=PARAMS,
        cost_estimate=cost(1.0),
        name="final_rows",
    )(weight, field, *row_far, *rows)
    return out.reshape(-1)


def solution(mesh):
    in_specs = (
        P(None, None, ("row", "col")),
        P(("row", "col")),
        P(("row", "col"), None),
        P(("row", "col"), None),
        P(("row", "col")),
        P(("row", "col")),
    )
    out_specs = P(("row", "col"))
    kernel = functools.partial(body, n_row=mesh.shape["row"], n_col=mesh.shape["col"])
    return jax.shard_map(kernel, mesh=mesh, in_specs=in_specs, out_specs=out_specs, check_vma=False)
```

```python
import functools

import jax
import jax.numpy as jnp
from jax import lax
from jax.experimental import pallas as pl
from jax.experimental.pallas import tpu as pltpu
from jax.sharding import PartitionSpec as P

BLK = 512
LANES = 128
SOFT_SQ = 0.0004
TERMS = 64
SPLIT = 48
HALF = 512
QUARTERS = 4
SLOTS = 5
NEAR_SCRATCH = 4 * [None]
GROUP = 16
CHUNK = 512
VMEM = pl.BlockSpec(memory_space=pltpu.VMEM)
SMEM = pl.BlockSpec(memory_space=pltpu.SMEM)
ANY = pl.BlockSpec(memory_space=pl.ANY)
HBM = pl.BlockSpec(memory_space=pltpu.HBM)
PARAMS = pltpu.CompilerParams(vmem_limit_bytes=40 * 1024 * 1024)


def prep_kernel(near_hbm, count, far_hbm, pts_hbm, dens_hbm, msg, far_out, near_out, weight_out, *scratch):
    near_ref, far_ref, pts_ref, dens_ref, sems = scratch
    blocks = near_out.shape[0]
    quad = pts_ref.shape[1]
    slots, body = near_ref.shape[1] - 1, quad * 4
    base = near_lines(slots, quad)
    width = pts_ref.shape[2] // QUARTERS
    copies = [
        pltpu.make_async_copy(dens_hbm, dens_ref, sems.at[QUARTERS]),
        pltpu.make_async_copy(far_hbm, far_ref, sems.at[QUARTERS + 1]),
        pltpu.make_async_copy(near_hbm, near_ref, sems.at[QUARTERS + 2]),
    ]
    for i in range(QUARTERS):
        part = slice(i * width, (i + 1) * width)
        copies.append(pltpu.make_async_copy(pts_hbm.at[:, :, part], pts_ref.at[:, :, part], sems.at[i]))
    for copy in copies:
        copy.start()
    copies.pop(0).wait()
    copies.pop(0).wait()
    copies.pop(0).wait()

    def put_far(k, value):
        far_out[k] = value
        msg[base + 4 * k : base + 4 * k + 4, :] = value

    for k in range(blocks):
        cols = slice(k * BLK, (k + 1) * BLK)
        if k % (blocks // QUARTERS) == 0:
            copies.pop(0).wait()
        w = pts_ref[3, :, cols]
        total = jnp.sum(w, axis=0, keepdims=True)
        dens = jnp.concatenate([dens_ref[4 * k + q : 4 * k + q + 1, :] for q in range(4)], axis=1)
        lines = []
        for c in range(3):
            x = pts_ref[c, :, cols]
            lines.append(jnp.sum(x * w, axis=0, keepdims=True) / total)
            near_out[k, quad * c : quad * c + quad, :] = x
        near_out[k, quad * 3 : quad * 4, :] = w
        near_out[k, quad * 4 : quad * 4 + 8, :] = jnp.broadcast_to(dens, (8, BLK))
        put_far(k, jnp.concatenate(lines + [total * dens], axis=0))
        weight_out[k : k + 1, :] = total
    lane = lax.broadcasted_iota(jnp.int32, (1, LANES), 1)
    lines = [jnp.full((1, LANES), -1.0, jnp.float32)] * 2
    for t in range(slots):
        k = lax.rem(near_ref[0, t + 1], blocks)
        msg[t * body : (t + 1) * body, :] = near_out[k, 0:body, :]
        source = jnp.where(t + 1 < count[0], near_ref[1, t + 1], -1)
        lines[0] = jnp.where(lane == t, k.astype(jnp.float32), lines[0])
        lines[1] = jnp.where(lane == t, source.astype(jnp.float32), lines[1])
    pairs = jnp.concatenate([far_ref[...].astype(jnp.float32), jnp.full((2, LANES - far_ref.shape[1]), -1.0)], axis=1)
    pairs = jnp.concatenate([pairs] + lines, axis=0)
    put_far(blocks, jnp.concatenate([pairs] * (BLK // LANES), axis=1))
    used = base + 4 * (blocks + 1)
    if used < msg.shape[0]:
        msg[used:, :] = jnp.zeros((msg.shape[0] - used, BLK), jnp.float32)


def near_lines(slots, quad):
    return slots * 4 * quad


def three(value):
    one = value.astype(jnp.bfloat16).astype(jnp.float32)
    two = (value - one).astype(jnp.bfloat16).astype(jnp.float32)
    return one, two, value - one - two


def pick_row(row, values):
    out = jnp.zeros(row.shape, jnp.float32)
    for k, value in enumerate(values):
        out = jnp.where(row == k, value, out)
    return out


def parts(x):
    row = lax.broadcasted_iota(jnp.int32, x.shape, 0)
    live = row < 3
    centred = jnp.where(live, x - 0.5, 0.0)
    head = jnp.round(centred * 256.0) * (1.0 / 256.0)
    rest = centred - head
    rest1 = rest.astype(jnp.bfloat16).astype(jnp.float32)
    big = pick_row(row, three(jnp.sum(head * head, axis=0, keepdims=True)))
    small = pick_row(row, three(jnp.sum(rest * (2.0 * head + rest), axis=0, keepdims=True) + 0.5 * SOFT_SQ))
    return head, rest1, rest - rest1, big, small, jnp.where(live, 1.0, 0.0)


def left_terms(x, columns):
    head, rest1, rest2, big, small, ones = parts(x)
    h2, a2, b2 = -2.0 * head, -2.0 * rest1, -2.0 * rest2
    groups = [h2, big, ones, small, ones, h2, h2, a2, b2, a2, a2, b2]
    row = lax.broadcasted_iota(jnp.int32, (TERMS - SPLIT, x.shape[1]), 0)
    groups.append(pick_row(row, [part for column in columns for part in three(column)]))
    return jnp.concatenate(groups, axis=0)


def right_terms(x):
    head, rest1, rest2, big, small, ones = parts(x)
    groups = [head, ones, big, ones, small, rest1, rest2, head, head, rest1, rest2, rest1]
    groups.append(jnp.zeros((TERMS - SPLIT, x.shape[1]), jnp.float32))
    return jnp.concatenate(groups, axis=0).astype(jnp.bfloat16)


def column_of(lhs, which):
    row = lax.broadcasted_iota(jnp.int32, (TERMS, LANES), 0) - SPLIT - 3 * which
    pick = jnp.where((row >= 0) & (row < 3), 1.0, 0.0).astype(jnp.bfloat16)
    return jnp.dot(lhs, pick, preferred_element_type=jnp.float32)


def fold_lanes(tile, row):
    part = tile[:, :LANES] * row[:, :LANES]
    for q in range(1, tile.shape[1] // LANES):
        part = part + tile[:, q * LANES : (q + 1) * LANES] * row[:, q * LANES : (q + 1) * LANES]
    return part


def twice(col):
    return jnp.concatenate([col] * (HALF // LANES), axis=1)


def place(x, n):
    bits = n.bit_length() - 1
    div, rem = (lambda a, b: a // b, lambda a, b: a % b) if isinstance(x, int) else (lax.div, lax.rem)
    return sum(rem(div(x, 1 << (bits - 1 - j)), 2) * (1 << j) for j in range(bits))


def far_tiles(pairs, count, row_in, sources, rows_out, cols_out, base, queue, left_buf, right_buf, lhs_buf, rhs_buf, part_buf):
    n_col = lax.axis_size("col")
    row_step = 2 * row_in[0].shape[0] // n_col
    blocks = row_step - 1
    my_row, my_col = lax.axis_index("row"), lax.axis_index("col")

    def ways(s):
        a, b = pairs[0, s], pairs[1, s]
        return jnp.bitwise_xor(lax.div(a, blocks), my_col), jnp.bitwise_xor(lax.div(b, blocks), my_row)

    def enqueue(s, n):
        b_way = ways(s)[1]
        here = functools.reduce(jnp.logical_or, [b_way == d for d in sources])

        @pl.when(here)
        def _():
            queue[n] = s

        return n + here.astype(jnp.int32)

    def fetch(s, j):
        a_way, b_way = ways(s)
        ka, kb = lax.rem(pairs[0, s], blocks), lax.rem(pairs[1, s], blocks)
        for d, other in sources.items():

            @pl.when(b_way == d)
            def _():
                if d == 0:
                    right_buf[j] = other[kb]
                else:
                    lines = [other[pl.ds(base + 4 * kb + c, 1), :] for c in range(4)]
                    right_buf[j] = jnp.concatenate(lines, axis=0)

        for core, half in enumerate(row_in):

            @pl.when(lax.rem(a_way, 2) == core)
            def _():
                left_buf[j] = half[place(lax.div(a_way, 2), n_col // 2) * row_step + ka]

        return jnp.where((a_way == 0) & (b_way == 0) & (ka == kb), 0.0, 1.0)

    def step(i, _):
        two = (queue[2 * i], queue[jnp.minimum(2 * i + 1, total - 1)])
        mirror = [fetch(s, j) for j, s in enumerate(two)]
        for j in range(2):
            left = left_buf[j]
            lhs_buf[j] = jnp.transpose(left_terms(left, [left[3:4]])).astype(jnp.bfloat16)
            rhs_buf[j] = right_terms(right_buf[j])
        zcol = [column_of(lhs_buf[j], 0) for j in range(2)]
        dist = [jnp.dot(lhs_buf[j], rhs_buf[j], preferred_element_type=jnp.float32) for j in range(2)]
        weights = [right_buf[j, 3:4, :] for j in range(2)]
        acc = [jnp.zeros((8, BLK), jnp.float32)] * 2
        for g in range(BLK // 8):
            rows = slice(g * 8, (g + 1) * 8)
            for j in range(2):
                tile = lax.rsqrt(dist[j][rows, :])
                part_buf[j, rows, :] = fold_lanes(tile, weights[j])
                acc[j] = acc[j] + tile * twice(zcol[j][rows, :])
        for j, s in enumerate(two):
            rows_out[pl.ds(s, 1), :] = jnp.sum(jnp.transpose(part_buf[j]), axis=0, keepdims=True)
            cols_out[pl.ds(s, 1), :] = jnp.sum(acc[j], axis=0, keepdims=True) * mirror[j]
        return 0

    total = lax.fori_loop(0, count[0], enqueue, 0)
    lax.fori_loop(0, lax.div(total + 1, 2), step, 0)


def points(tall):
    quad = tall.shape[0] // 4
    sides = [[tall[quad * c + u : quad * c + u + 1, :] for c in range(4)] for u in range(quad)]
    return jnp.concatenate([jnp.concatenate(side, axis=0) for side in sides], axis=1)


def near_tile(left, dens_i, right, dens_j, lhs_buf, rhs_buf, part_buf, acc_buf):
    quad = left.shape[1] // BLK
    terms = jnp.transpose(left_terms(left, [left[3:4], jnp.concatenate([dens_i] * quad, axis=1)]))
    terms = terms.astype(jnp.bfloat16)
    for g in range(BLK // GROUP):
        for u in range(quad):
            to, at = (g * quad + u) * GROUP, u * BLK + g * GROUP
            lhs_buf[to : to + GROUP, :] = terms[at : at + GROUP, :]
    rhs_buf[...] = right_terms(right)
    weights = right[3:4]
    acc_buf[...] = jnp.zeros_like(acc_buf)

    def chunk(i, _):
        at = pl.multiple_of(i * CHUNK * quad, CHUNK * quad)
        lhs = lhs_buf[pl.ds(at, CHUNK * quad), :]
        wcol = column_of(lhs, 0)
        groups = CHUNK // GROUP
        first_rows = [lhs[g * quad * GROUP : g * quad * GROUP + GROUP, :] for g in range(groups)]
        dcol = column_of(jnp.concatenate(first_rows, axis=0), 1)
        part = None
        for h in range(BLK // HALF):
            tiles = [None] * groups
            for v in range(quad):
                cols = slice(v * BLK + h * HALF, v * BLK + (h + 1) * HALF)
                dist = jnp.dot(lhs, rhs_buf[:, cols], preferred_element_type=jnp.float32)
                for g in range(groups):
                    inner = None
                    for u in range(quad):
                        rows = slice((g * quad + u) * GROUP, (g * quad + u + 1) * GROUP)
                        term = lax.rsqrt(dist[rows, :]) * twice(wcol[rows, :])
                        inner = term if inner is None else inner + term
                    inner = inner * weights[:, cols]
                    tiles[g] = inner if tiles[g] is None else tiles[g] + inner
            tile = jnp.concatenate(tiles, axis=0)
            cols = slice(h * HALF, (h + 1) * HALF)
            more = fold_lanes(tile, dens_j[:, cols])
            part = more if part is None else part + more
            acc_buf[:, cols] += jnp.sum((tile * twice(dcol)).reshape(-1, 8, HALF), axis=0)
        part_buf[pl.ds(pl.multiple_of(i * CHUNK, CHUNK), CHUNK), :] = part
        return 0

    lax.fori_loop(0, BLK // CHUNK, chunk, 0)
    rows = jnp.sum(jnp.transpose(part_buf[...]), axis=0, keepdims=True)
    return rows, jnp.sum(acc_buf[...], axis=0, keepdims=True)


def near_own_kernel(pairs, count, near_ref, field, *bufs):
    blocks, depth, _ = near_ref.shape
    body = depth - 8
    my_row = lax.axis_index("row")
    field[...] = jnp.zeros_like(field)

    def step(s, _):
        ka, kb = lax.rem(pairs[0, s], blocks), pairs[1, s] - my_row * blocks

        @pl.when((kb >= 0) & (kb < blocks))
        def _():
            left, right = points(near_ref[ka, 0:body, :]), points(near_ref[kb, 0:body, :])
            dens_i, dens_j = near_ref[ka, body : body + 1, :], near_ref[kb, body : body + 1, :]
            rows, cols = near_tile(left, dens_i, right, dens_j, *bufs)
            field[pl.ds(ka, 1), :] += rows
            field[pl.ds(kb, 1), :] += cols * jnp.where(ka == kb, 0.0, 1.0)

        return 0

    lax.fori_loop(0, count[0], step, 0)


def near_tiles(meanwhile, near_ref, got, field, put, right_buf, tags, sems, *bufs):
    blocks, depth, _ = near_ref.shape
    body = depth - 8
    base = near_lines(SLOTS, body // 4)
    my_row = lax.axis_index("row")
    tail = slice(base + 4 * blocks, base + 4 * blocks + 8)
    copies = [pltpu.make_async_copy(g.at[tail, 0:LANES], tags.at[d], sems.at[d]) for d, g in enumerate(got)]
    for copy in copies:
        copy.start()
    meanwhile()
    for copy in copies:
        copy.wait()

    def step(i, _):
        way, t = lax.div(i, SLOTS), lax.rem(i, SLOTS)
        kb = tags[way, 3, t].astype(jnp.int32) - my_row * blocks

        @pl.when((kb >= 0) & (kb < blocks))
        def _():
            for d, other in enumerate(got):

                @pl.when(way == d)
                def _():
                    at = pl.multiple_of(t * body, 8)
                    points_j = other[pl.ds(at, body), :]
                    line = base + 4 * tags[way, 2, t].astype(jnp.int32) + 3
                    total = jnp.sum(points_j[body - body // 4 :], axis=0, keepdims=True)
                    right_buf[0:body, :] = points_j
                    right_buf[body : body + 1, :] = other[pl.ds(line, 1), :] / total

            left, right = points(near_ref[kb, 0:body, :]), points(right_buf[0:body, :])
            dens_i, dens_j = near_ref[kb, body : body + 1, :], right_buf[body : body + 1, :]
            rows, cols = near_tile(left, dens_i, right, dens_j, *bufs)
            field[pl.ds(kb, 1), :] += rows
            put(way, t, cols)

        return 0

    lax.fori_loop(0, len(got) * SLOTS, step, 0)


def direct_kernel(near_ref, start, *refs, ways):
    got, (field, *backs), scratch = refs[:ways], refs[ways : 2 * ways + 1], refs[2 * ways + 1 :]

    def clear():
        field[...] = start[...]
        for back in backs:
            back[...] = jnp.zeros_like(back)

    def put(way, t, result):
        for i, back in enumerate(backs):

            @pl.when(way == i)
            def _():
                back[pl.ds(t, 1), :] = result

    near_tiles(clear, near_ref, got, field, put, *scratch)


def far_kernel(pairs, count, row0, row1, own_in, *refs, direct, base):
    got, (rows_out, cols_out), scratch = refs[: len(direct)], refs[len(direct) : -6], refs[-6:]
    rows_out[...] = jnp.zeros_like(rows_out)
    cols_out[...] = jnp.zeros_like(cols_out)
    sources = {0: own_in, **dict(zip(direct, got))}
    far_tiles(pairs, count, (row0, row1), sources, rows_out, cols_out, base, *scratch)


def late_kernel(pairs, count, near_ref, start, row0, row1, rows_in, cols_in, *refs, n_row, direct, late):
    refs = list(refs)
    take = lambda n: [refs.pop(0) for _ in range(n)]
    got, backs = take(len(late)), take(len(direct))
    field, rows_out, cols_out, *messages = take(n_row + 2)
    near_scratch, far_scratch = take(len(NEAR_SCRATCH) + 3), refs
    nfar = cols_out.shape[0]
    base = near_lines(SLOTS, near_ref.shape[1] // 4 - 2)
    my_row = lax.axis_index("row")

    def to_peer(d, lines, value):
        k = lax.rem(jnp.bitwise_xor(my_row, d) - my_row + n_row - 1, n_row)
        for i, message in enumerate(messages):

            @pl.when(k == i)
            def _():
                message[lines, :] = value

    def put(way, t, result):
        for i, d in enumerate(late):
            pl.when(way == i)(lambda: to_peer(d, pl.ds(nfar + t, 1), result))

    def far():
        field[...] = start[...]
        rows_out[...] = rows_in[...]
        cols_out[...] = cols_in[...]
        for message in messages:
            message[nfar:, :] = jnp.zeros((8, BLK), jnp.float32)
        for d, back in zip(direct, backs):
            to_peer(d, slice(nfar, nfar + 8), back[...])
        far_tiles(pairs, count, (row0, row1), dict(zip(late, got)), rows_out, cols_out, base, *far_scratch)
        for message in messages:
            message[0:nfar, :] = cols_out[...]

    near_tiles(far, near_ref, got, field, put, *near_scratch)


def hot(index, blocks, slots, base):
    want = lax.broadcasted_iota(jnp.int32, (blocks, slots), 0) + base * blocks
    return jnp.where(index[:, 0:slots] == want.astype(jnp.float32), 1.0, 0.0)


def spread(pick, slots, weight):
    pick = jnp.concatenate(pick * 3, axis=1).astype(jnp.bfloat16)
    slots = jnp.concatenate(three(jnp.concatenate(slots, axis=0)), axis=0).astype(jnp.bfloat16)
    return jnp.dot(pick, slots, preferred_element_type=jnp.float32) * weight[...]


def cols_kernel(pairs, weight, near, own_far, own_cols, *refs, n_row, base):
    col_far, messages, field = refs[: n_row - 1], refs[n_row - 1 : -1], refs[-1]
    blocks, nfar = weight.shape[0], own_cols.shape[0]
    my_row = lax.axis_index("row")
    line = base + 4 * blocks + 1
    pick = [hot(own_far[blocks, 1:2, :], blocks, nfar, my_row)]
    for k in range(1, n_row):
        way = jnp.bitwise_xor(my_row, lax.rem(my_row + n_row - k, n_row))
        index = jnp.zeros((1, BLK), jnp.float32)
        for d, other in enumerate(col_far):
            index = jnp.where(way == d + 1, other[line : line + 1, :], index)
        pick.append(hot(index, blocks, nfar, my_row))
    field[...] = near[...] + spread(pick, [own_cols[...]] + [m[0:nfar, :] for m in messages], weight)
    for message in messages:
        for t in range(pairs.shape[1] - 1):
            k = lax.rem(pairs[0, t + 1], blocks)
            field[pl.ds(k, 1), :] += message[nfar + t : nfar + t + 1, :]


def rows_kernel(weight, field, row0, row1, *refs, n_col):
    rows, out = refs[:-1], refs[-1]
    blocks, nfar = weight.shape[0], rows[0].shape[0] // 2
    my_col = lax.axis_index("col")
    chips = n_col // 2
    chip = lax.div(my_col, 2)
    pick = []
    for k in range(chips):
        way = jnp.bitwise_xor(chip, lax.rem(chip + chips - k, chips))
        tag = place(way, chips) * (blocks + 1) + blocks
        pick += [hot(half[tag, 0:1, :], blocks, nfar, my_col) for half in (row0, row1)]
    total = field[...] + spread(pick, [r[...] for r in rows], weight)
    for q in range(BLK // LANES):
        out[pl.ds(q, blocks, stride=BLK // LANES), :] = total[:, q * LANES : (q + 1) * LANES]


def f32(*shape):
    return jax.ShapeDtypeStruct(shape, jnp.float32)


def cost(micros):
    return pl.CostEstimate(flops=int(micros * 1.1e9), bytes_accessed=1 << 16, transcendentals=0)


def body(points, density, near_pairs, far_pairs, near_count, far_count, *, n_row, n_col):
    quad = points.shape[1]
    blocks = points.shape[2] // BLK
    nnear, nfar = near_pairs.shape[0], far_pairs.shape[0]
    depth, slots = 4 * quad, nnear - 1
    near_pairs, far_pairs = near_pairs.T, far_pairs.T

    def swap(x, axis, d):
        n = {"row": n_row, "col": n_col}[axis]
        return lax.ppermute(x, axis, [(i, i ^ d) for i in range(n)])

    direct = [d for d in range(1, n_row) if d & (d - 1) == 0]
    late = [d for d in range(1, n_row) if d & (d - 1) != 0]

    def halves(n):
        return [1 << j for j in reversed(range(n.bit_length() - 1))]

    def col_gather(x):
        for d in halves(n_col)[:-1]:
            x = jnp.concatenate([x, swap(x, "col", d)], axis=0)
        return x, swap(x, "col", 1)

    base = near_lines(slots, quad)
    msg_rows = -(-(base + 4 * (blocks + 1)) // 8) * 8
    hbm = (near_pairs, far_pairs, points, density.reshape(-1, LANES))
    hbm = [pltpu.with_memory_space_constraint(x, pltpu.HBM) for x in hbm]
    msg, far_own, near_own, weight = pl.pallas_call(
        prep_kernel,
        out_shape=(
            f32(msg_rows, BLK),
            f32(blocks + 1, 4, BLK),
            f32(blocks, depth + 8, BLK),
            f32(blocks, BLK),
        ),
        in_specs=[HBM, SMEM, HBM, HBM, HBM],
        out_specs=(VMEM, VMEM, VMEM, VMEM),
        scratch_shapes=[
            pltpu.SMEM(near_pairs.shape, jnp.int32),
            pltpu.VMEM(far_pairs.shape, jnp.int32),
            pltpu.VMEM(points.shape, jnp.float32),
            pltpu.VMEM((density.shape[0] // LANES, LANES), jnp.float32),
            pltpu.SemaphoreType.DMA((QUARTERS + 3,)),
        ],
        compiler_params=PARAMS,
        cost_estimate=cost(1.2),
        name="prep",
    )(hbm[0], near_count, *hbm[1:])
    row_far = col_gather(far_own)
    known = {d: swap(msg, "row", d) for d in direct}
    *onward, last = lax.optimization_barrier((*[known[d] for d in direct], row_far[0]))
    known.update(zip(direct, onward))
    row_far = (last, row_far[1])
    for d in late:
        known[d] = swap(known[d ^ (d & -d)], "row", d & -d)
    got = [known[d] for d in range(1, n_row)]

    bufs = [
        pltpu.VMEM((quad * BLK, TERMS), jnp.bfloat16),
        pltpu.VMEM((TERMS, quad * BLK), jnp.bfloat16),
        pltpu.VMEM((BLK, LANES), jnp.float32),
        pltpu.VMEM((8, BLK), jnp.float32),
    ]
    near0 = pl.pallas_call(
        near_own_kernel,
        out_shape=f32(blocks, BLK),
        in_specs=[SMEM, SMEM, VMEM],
        out_specs=VMEM,
        scratch_shapes=bufs,
        compiler_params=PARAMS,
        cost_estimate=cost(5.0),
        name="near_own",
    )(near_pairs, near_count, near_own)

    def near_scratch(n):
        return [
            pltpu.VMEM((depth + 8, BLK), jnp.float32),
            pltpu.SMEM((n, 8, LANES), jnp.float32),
            pltpu.SemaphoreType.DMA((n,)),
        ] + bufs

    far_scratch = [
        pltpu.SMEM((nfar,), jnp.int32),
        pltpu.VMEM((2, 4, BLK), jnp.float32),
        pltpu.VMEM((2, 4, BLK), jnp.float32),
        pltpu.VMEM((2, BLK, TERMS), jnp.bfloat16),
        pltpu.VMEM((2, TERMS, BLK), jnp.bfloat16),
        pltpu.VMEM((2, BLK, LANES), jnp.float32),
    ]
    field, *backs = pl.pallas_call(
        functools.partial(direct_kernel, ways=len(direct)),
        out_shape=[f32(blocks, BLK)] + [f32(8, BLK)] * len(direct),
        in_specs=[VMEM] * (2 + len(direct)),
        out_specs=[VMEM] * (len(direct) + 1),
        scratch_shapes=near_scratch(len(direct)),
        compiler_params=PARAMS,
        cost_estimate=cost(30.0),
        name="near_direct",
    )(near_own, near0, *[got[d - 1] for d in direct])
    far_rows, far_cols = pl.pallas_call(
        functools.partial(far_kernel, direct=direct, base=base),
        out_shape=[f32(nfar, BLK)] * 2,
        in_specs=[SMEM, SMEM] + [VMEM] * (3 + len(direct)),
        out_specs=[VMEM] * 2,
        scratch_shapes=far_scratch,
        compiler_params=PARAMS,
        cost_estimate=cost(3.0),
        name="far_direct",
    )(far_pairs, far_count, *row_far, far_own, *[got[d - 1] for d in direct])
    field, far_rows, far_cols, *messages = pl.pallas_call(
        functools.partial(late_kernel, n_row=n_row, direct=direct, late=late),
        out_shape=[f32(blocks, BLK)] + [f32(nfar, BLK)] * 2 + [f32(nfar + 8, BLK)] * (n_row - 1),
        in_specs=[SMEM, SMEM] + [VMEM] * (6 + n_row - 1),
        out_specs=[VMEM] * (n_row + 2),
        scratch_shapes=near_scratch(len(late)) + far_scratch,
        compiler_params=PARAMS,
        cost_estimate=cost(8.0),
        name="late",
    )(far_pairs, far_count, near_own, field, *row_far, far_rows, far_cols, *[got[d - 1] for d in late], *backs)

    messages = [
        lax.ppermute(x, "row", [(i, (i + k + 1) % n_row) for i in range(n_row)]) for k, x in enumerate(messages)
    ]
    both = jnp.concatenate([far_rows, swap(far_rows, "col", 1)], axis=0)
    rows = [both]
    for k in range(2, n_col, 2):
        rows.append(lax.ppermute(both, "col", [(i, (i + k) % n_col) for i in range(n_col)]))
    field = pl.pallas_call(
        functools.partial(cols_kernel, n_row=n_row, base=base),
        out_shape=f32(blocks, BLK),
        in_specs=[SMEM] + [VMEM] * (2 * n_row + 2),
        out_specs=VMEM,
        compiler_params=PARAMS,
        cost_estimate=cost(1.0),
        name="final_cols",
    )(near_pairs, weight, field, far_own, far_cols, *got, *messages)
    out = pl.pallas_call(
        functools.partial(rows_kernel, n_col=n_col),
        out_shape=f32(blocks * BLK // LANES, LANES),
        in_specs=[VMEM] * (4 + len(rows)),
        out_specs=VMEM,
        compiler_params=PARAMS,
        cost_estimate=cost(1.0),
        name="final_rows",
    )(weight, field, *row_far, *rows)
    return out.reshape(-1)


def solution(mesh):
    in_specs = (
        P(None, None, ("row", "col")),
        P(("row", "col")),
        P(("row", "col"), None),
        P(("row", "col"), None),
        P(("row", "col")),
        P(("row", "col")),
    )
    out_specs = P(("row", "col"))
    kernel = functools.partial(body, n_row=mesh.shape["row"], n_col=mesh.shape["col"])
    return jax.shard_map(kernel, mesh=mesh, in_specs=in_specs, out_specs=out_specs, check_vma=False)
```

```python
import functools

import jax
import jax.numpy as jnp
from jax import lax
from jax.experimental import pallas as pl
from jax.experimental.pallas import tpu as pltpu
from jax.sharding import PartitionSpec as P

BLK = 512
LANES = 128
SOFT_SQ = 0.0004
TERMS = 64
SPLIT = 48
HALF = 512
QUARTERS = 4
SLOTS = 5
NEAR_SCRATCH = 4 * [None]
GROUP = 16
CHUNK = 512
VMEM = pl.BlockSpec(memory_space=pltpu.VMEM)
SMEM = pl.BlockSpec(memory_space=pltpu.SMEM)
ANY = pl.BlockSpec(memory_space=pl.ANY)
HBM = pl.BlockSpec(memory_space=pltpu.HBM)
PARAMS = pltpu.CompilerParams(vmem_limit_bytes=40 * 1024 * 1024)


def prep_kernel(near_hbm, count, far_hbm, pts_hbm, dens_hbm, msg, far_out, near_out, weight_out, *scratch):
    near_ref, far_ref, pts_ref, dens_ref, sems = scratch
    blocks = near_out.shape[0]
    quad = pts_ref.shape[1]
    slots, body = near_ref.shape[1] - 1, quad * 4
    base = near_lines(slots, quad)
    width = pts_ref.shape[2] // QUARTERS
    copies = [
        pltpu.make_async_copy(dens_hbm, dens_ref, sems.at[QUARTERS]),
        pltpu.make_async_copy(far_hbm, far_ref, sems.at[QUARTERS + 1]),
        pltpu.make_async_copy(near_hbm, near_ref, sems.at[QUARTERS + 2]),
    ]
    for i in range(QUARTERS):
        part = slice(i * width, (i + 1) * width)
        copies.append(pltpu.make_async_copy(pts_hbm.at[:, :, part], pts_ref.at[:, :, part], sems.at[i]))
    for copy in copies:
        copy.start()
    copies.pop(0).wait()
    copies.pop(0).wait()
    copies.pop(0).wait()

    def put_far(k, value):
        far_out[k] = value
        msg[base + 4 * k : base + 4 * k + 4, :] = value

    for k in range(blocks):
        cols = slice(k * BLK, (k + 1) * BLK)
        if k % (blocks // QUARTERS) == 0:
            copies.pop(0).wait()
        w = pts_ref[3, :, cols]
        total = jnp.sum(w, axis=0, keepdims=True)
        dens = jnp.concatenate([dens_ref[4 * k + q : 4 * k + q + 1, :] for q in range(4)], axis=1)
        lines = []
        for c in range(3):
            x = pts_ref[c, :, cols]
            lines.append(jnp.sum(x * w, axis=0, keepdims=True) / total)
            near_out[k, quad * c : quad * c + quad, :] = x
        near_out[k, quad * 3 : quad * 4, :] = w
        near_out[k, quad * 4 : quad * 4 + 8, :] = jnp.broadcast_to(dens, (8, BLK))
        put_far(k, jnp.concatenate(lines + [total * dens], axis=0))
        weight_out[k : k + 1, :] = total
    lane = lax.broadcasted_iota(jnp.int32, (1, LANES), 1)
    lines = [jnp.full((1, LANES), -1.0, jnp.float32)] * 2
    for t in range(slots):
        k = lax.rem(near_ref[0, t + 1], blocks)
        msg[t * body : (t + 1) * body, :] = near_out[k, 0:body, :]
        source = jnp.where(t + 1 < count[0], near_ref[1, t + 1], -1)
        lines[0] = jnp.where(lane == t, k.astype(jnp.float32), lines[0])
        lines[1] = jnp.where(lane == t, source.astype(jnp.float32), lines[1])
    pairs = jnp.concatenate([far_ref[...].astype(jnp.float32), jnp.full((2, LANES - far_ref.shape[1]), -1.0)], axis=1)
    pairs = jnp.concatenate([pairs] + lines, axis=0)
    put_far(blocks, jnp.concatenate([pairs] * (BLK // LANES), axis=1))
    used = base + 4 * (blocks + 1)
    if used < msg.shape[0]:
        msg[used:, :] = jnp.zeros((msg.shape[0] - used, BLK), jnp.float32)


def near_lines(slots, quad):
    return slots * 4 * quad


def three(value):
    one = value.astype(jnp.bfloat16).astype(jnp.float32)
    two = (value - one).astype(jnp.bfloat16).astype(jnp.float32)
    return one, two, value - one - two


def pick_row(row, values):
    out = jnp.zeros(row.shape, jnp.float32)
    for k, value in enumerate(values):
        out = jnp.where(row == k, value, out)
    return out


def parts(x):
    row = lax.broadcasted_iota(jnp.int32, x.shape, 0)
    live = row < 3
    centred = jnp.where(live, x - 0.5, 0.0)
    head = jnp.round(centred * 256.0) * (1.0 / 256.0)
    rest = centred - head
    rest1 = rest.astype(jnp.bfloat16).astype(jnp.float32)
    big = pick_row(row, three(jnp.sum(head * head, axis=0, keepdims=True)))
    small = pick_row(row, three(jnp.sum(rest * (2.0 * head + rest), axis=0, keepdims=True) + 0.5 * SOFT_SQ))
    return head, rest1, rest - rest1, big, small, jnp.where(live, 1.0, 0.0)


def left_terms(x, columns):
    head, rest1, rest2, big, small, ones = parts(x)
    h2, a2, b2 = -2.0 * head, -2.0 * rest1, -2.0 * rest2
    groups = [h2, big, ones, small, ones, h2, h2, a2, b2, a2, a2, b2]
    row = lax.broadcasted_iota(jnp.int32, (TERMS - SPLIT, x.shape[1]), 0)
    groups.append(pick_row(row, [part for column in columns for part in three(column)]))
    return jnp.concatenate(groups, axis=0)


def right_terms(x):
    head, rest1, rest2, big, small, ones = parts(x)
    groups = [head, ones, big, ones, small, rest1, rest2, head, head, rest1, rest2, rest1]
    groups.append(jnp.zeros((TERMS - SPLIT, x.shape[1]), jnp.float32))
    return jnp.concatenate(groups, axis=0).astype(jnp.bfloat16)


def column_of(lhs, which):
    row = lax.broadcasted_iota(jnp.int32, (TERMS, LANES), 0) - SPLIT - 3 * which
    pick = jnp.where((row >= 0) & (row < 3), 1.0, 0.0).astype(jnp.bfloat16)
    return jnp.dot(lhs, pick, preferred_element_type=jnp.float32)


def fold_lanes(tile, row):
    part = tile[:, :LANES] * row[:, :LANES]
    for q in range(1, tile.shape[1] // LANES):
        part = part + tile[:, q * LANES : (q + 1) * LANES] * row[:, q * LANES : (q + 1) * LANES]
    return part


def twice(col):
    return jnp.concatenate([col] * (HALF // LANES), axis=1)


def place(x, n):
    bits = n.bit_length() - 1
    div, rem = (lambda a, b: a // b, lambda a, b: a % b) if isinstance(x, int) else (lax.div, lax.rem)
    return sum(rem(div(x, 1 << (bits - 1 - j)), 2) * (1 << j) for j in range(bits))


def far_tiles(pairs, count, row_in, sources, rows_out, cols_out, base, queue, left_buf, right_buf, lhs_buf, rhs_buf, part_buf):
    n_col = lax.axis_size("col")
    row_step = 2 * row_in[0].shape[0] // n_col
    blocks = row_step - 1
    my_row, my_col = lax.axis_index("row"), lax.axis_index("col")

    def ways(s):
        a, b = pairs[0, s], pairs[1, s]
        return jnp.bitwise_xor(lax.div(a, blocks), my_col), jnp.bitwise_xor(lax.div(b, blocks), my_row)

    def enqueue(s, n):
        b_way = ways(s)[1]
        here = functools.reduce(jnp.logical_or, [b_way == d for d in sources])

        @pl.when(here)
        def _():
            queue[n] = s

        return n + here.astype(jnp.int32)

    def fetch(s, j):
        a_way, b_way = ways(s)
        ka, kb = lax.rem(pairs[0, s], blocks), lax.rem(pairs[1, s], blocks)
        for d, other in sources.items():

            @pl.when(b_way == d)
            def _():
                if d == 0:
                    right_buf[j] = other[kb]
                else:
                    lines = [other[pl.ds(base + 4 * kb + c, 1), :] for c in range(4)]
                    right_buf[j] = jnp.concatenate(lines, axis=0)

        for core, half in enumerate(row_in):

            @pl.when(lax.rem(a_way, 2) == core)
            def _():
                left_buf[j] = half[place(lax.div(a_way, 2), n_col // 2) * row_step + ka]

        return jnp.where((a_way == 0) & (b_way == 0) & (ka == kb), 0.0, 1.0)

    def tiles(slots):
        many = range(len(slots))
        mirror = [fetch(s, j) for j, s in enumerate(slots)]
        for j in many:
            left = left_buf[j]
            lhs_buf[j] = jnp.transpose(left_terms(left, [left[3:4]])).astype(jnp.bfloat16)
            rhs_buf[j] = right_terms(right_buf[j])
        zcol = [column_of(lhs_buf[j], 0) for j in many]
        dist = [jnp.dot(lhs_buf[j], rhs_buf[j], preferred_element_type=jnp.float32) for j in many]
        weights = [right_buf[j, 3:4, :] for j in many]
        acc = [jnp.zeros((8, BLK), jnp.float32) for _ in many]
        for g in range(BLK // 8):
            rows = slice(g * 8, (g + 1) * 8)
            for j in many:
                tile = lax.rsqrt(dist[j][rows, :])
                part_buf[j, rows, :] = fold_lanes(tile, weights[j])
                acc[j] = acc[j] + tile * twice(zcol[j][rows, :])
        for j, s in enumerate(slots):
            rows_out[pl.ds(s, 1), :] = jnp.sum(jnp.transpose(part_buf[j]), axis=0, keepdims=True)
            cols_out[pl.ds(s, 1), :] = jnp.sum(acc[j], axis=0, keepdims=True) * mirror[j]

    def two(i, _):
        tiles([queue[2 * i], queue[2 * i + 1]])
        return 0

    total = lax.fori_loop(0, count[0], enqueue, 0)
    lax.fori_loop(0, lax.div(total, 2), two, 0)
    pl.when(lax.rem(total, 2) == 1)(lambda: tiles([queue[total - 1]]))


def points(tall):
    quad = tall.shape[0] // 4
    sides = [[tall[quad * c + u : quad * c + u + 1, :] for c in range(4)] for u in range(quad)]
    return jnp.concatenate([jnp.concatenate(side, axis=0) for side in sides], axis=1)


def near_tile(left, dens_i, right, dens_j, lhs_buf, rhs_buf, part_buf, acc_buf):
    quad = left.shape[1] // BLK
    terms = jnp.transpose(left_terms(left, [left[3:4], jnp.concatenate([dens_i] * quad, axis=1)]))
    terms = terms.astype(jnp.bfloat16)
    for g in range(BLK // GROUP):
        for u in range(quad):
            to, at = (g * quad + u) * GROUP, u * BLK + g * GROUP
            lhs_buf[to : to + GROUP, :] = terms[at : at + GROUP, :]
    rhs_buf[...] = right_terms(right)
    weights = right[3:4]
    acc_buf[...] = jnp.zeros_like(acc_buf)

    def chunk(i, _):
        at = pl.multiple_of(i * CHUNK * quad, CHUNK * quad)
        lhs = lhs_buf[pl.ds(at, CHUNK * quad), :]
        wcol = column_of(lhs, 0)
        groups = CHUNK // GROUP
        first_rows = [lhs[g * quad * GROUP : g * quad * GROUP + GROUP, :] for g in range(groups)]
        dcol = column_of(jnp.concatenate(first_rows, axis=0), 1)
        part = None
        for h in range(BLK // HALF):
            tiles = [None] * groups
            for v in range(quad):
                cols = slice(v * BLK + h * HALF, v * BLK + (h + 1) * HALF)
                dist = jnp.dot(lhs, rhs_buf[:, cols], preferred_element_type=jnp.float32)
                for g in range(groups):
                    inner = None
                    for u in range(quad):
                        rows = slice((g * quad + u) * GROUP, (g * quad + u + 1) * GROUP)
                        term = lax.rsqrt(dist[rows, :]) * twice(wcol[rows, :])
                        inner = term if inner is None else inner + term
                    inner = inner * weights[:, cols]
                    tiles[g] = inner if tiles[g] is None else tiles[g] + inner
            tile = jnp.concatenate(tiles, axis=0)
            cols = slice(h * HALF, (h + 1) * HALF)
            more = fold_lanes(tile, dens_j[:, cols])
            part = more if part is None else part + more
            acc_buf[:, cols] += jnp.sum((tile * twice(dcol)).reshape(-1, 8, HALF), axis=0)
        part_buf[pl.ds(pl.multiple_of(i * CHUNK, CHUNK), CHUNK), :] = part
        return 0

    lax.fori_loop(0, BLK // CHUNK, chunk, 0)
    rows = jnp.sum(jnp.transpose(part_buf[...]), axis=0, keepdims=True)
    return rows, jnp.sum(acc_buf[...], axis=0, keepdims=True)


def near_own_kernel(pairs, count, near_ref, field, *bufs):
    blocks, depth, _ = near_ref.shape
    body = depth - 8
    my_row = lax.axis_index("row")
    field[...] = jnp.zeros_like(field)

    def step(s, _):
        ka, kb = lax.rem(pairs[0, s], blocks), pairs[1, s] - my_row * blocks

        @pl.when((kb >= 0) & (kb < blocks))
        def _():
            left, right = points(near_ref[ka, 0:body, :]), points(near_ref[kb, 0:body, :])
            dens_i, dens_j = near_ref[ka, body : body + 1, :], near_ref[kb, body : body + 1, :]
            rows, cols = near_tile(left, dens_i, right, dens_j, *bufs)
            field[pl.ds(ka, 1), :] += rows
            field[pl.ds(kb, 1), :] += cols * jnp.where(ka == kb, 0.0, 1.0)

        return 0

    lax.fori_loop(0, count[0], step, 0)


def near_tiles(meanwhile, near_ref, got, field, put, right_buf, tags, sems, *bufs):
    blocks, depth, _ = near_ref.shape
    body = depth - 8
    base = near_lines(SLOTS, body // 4)
    my_row = lax.axis_index("row")
    tail = slice(base + 4 * blocks, base + 4 * blocks + 8)
    copies = [pltpu.make_async_copy(g.at[tail, 0:LANES], tags.at[d], sems.at[d]) for d, g in enumerate(got)]
    for copy in copies:
        copy.start()
    meanwhile()
    for copy in copies:
        copy.wait()

    def step(i, _):
        way, t = lax.div(i, SLOTS), lax.rem(i, SLOTS)
        kb = tags[way, 3, t].astype(jnp.int32) - my_row * blocks

        @pl.when((kb >= 0) & (kb < blocks))
        def _():
            for d, other in enumerate(got):

                @pl.when(way == d)
                def _():
                    at = pl.multiple_of(t * body, 8)
                    points_j = other[pl.ds(at, body), :]
                    line = base + 4 * tags[way, 2, t].astype(jnp.int32) + 3
                    total = jnp.sum(points_j[body - body // 4 :], axis=0, keepdims=True)
                    right_buf[0:body, :] = points_j
                    right_buf[body : body + 1, :] = other[pl.ds(line, 1), :] / total

            left, right = points(near_ref[kb, 0:body, :]), points(right_buf[0:body, :])
            dens_i, dens_j = near_ref[kb, body : body + 1, :], right_buf[body : body + 1, :]
            rows, cols = near_tile(left, dens_i, right, dens_j, *bufs)
            field[pl.ds(kb, 1), :] += rows
            put(way, t, cols)

        return 0

    lax.fori_loop(0, len(got) * SLOTS, step, 0)


def direct_kernel(near_ref, start, *refs, ways):
    got, (field, *backs), scratch = refs[:ways], refs[ways : 2 * ways + 1], refs[2 * ways + 1 :]

    def clear():
        field[...] = start[...]
        for back in backs:
            back[...] = jnp.zeros_like(back)

    def put(way, t, result):
        for i, back in enumerate(backs):

            @pl.when(way == i)
            def _():
                back[pl.ds(t, 1), :] = result

    near_tiles(clear, near_ref, got, field, put, *scratch)


def far_kernel(pairs, count, row0, row1, own_in, *refs, direct, base):
    got, (rows_out, cols_out), scratch = refs[: len(direct)], refs[len(direct) : -6], refs[-6:]
    rows_out[...] = jnp.zeros_like(rows_out)
    cols_out[...] = jnp.zeros_like(cols_out)
    sources = {0: own_in, **dict(zip(direct, got))}
    far_tiles(pairs, count, (row0, row1), sources, rows_out, cols_out, base, *scratch)


def late_kernel(pairs, count, near_ref, start, row0, row1, rows_in, cols_in, *refs, n_row, direct, late):
    refs = list(refs)
    take = lambda n: [refs.pop(0) for _ in range(n)]
    got, backs = take(len(late)), take(len(direct))
    field, rows_out, cols_out, *messages = take(n_row + 2)
    near_scratch, far_scratch = take(len(NEAR_SCRATCH) + 3), refs
    nfar = cols_out.shape[0]
    base = near_lines(SLOTS, near_ref.shape[1] // 4 - 2)
    my_row = lax.axis_index("row")

    def to_peer(d, lines, value):
        k = lax.rem(jnp.bitwise_xor(my_row, d) - my_row + n_row - 1, n_row)
        for i, message in enumerate(messages):

            @pl.when(k == i)
            def _():
                message[lines, :] = value

    def put(way, t, result):
        for i, d in enumerate(late):
            pl.when(way == i)(lambda: to_peer(d, pl.ds(nfar + t, 1), result))

    def far():
        field[...] = start[...]
        rows_out[...] = rows_in[...]
        cols_out[...] = cols_in[...]
        for message in messages:
            message[nfar:, :] = jnp.zeros((8, BLK), jnp.float32)
        for d, back in zip(direct, backs):
            to_peer(d, slice(nfar, nfar + 8), back[...])
        far_tiles(pairs, count, (row0, row1), dict(zip(late, got)), rows_out, cols_out, base, *far_scratch)
        for message in messages:
            message[0:nfar, :] = cols_out[...]

    near_tiles(far, near_ref, got, field, put, *near_scratch)


def hot(index, blocks, slots, base):
    want = lax.broadcasted_iota(jnp.int32, (blocks, slots), 0) + base * blocks
    return jnp.where(index[:, 0:slots] == want.astype(jnp.float32), 1.0, 0.0)


def spread(pick, slots, weight):
    pick = jnp.concatenate(pick * 3, axis=1).astype(jnp.bfloat16)
    slots = jnp.concatenate(three(jnp.concatenate(slots, axis=0)), axis=0).astype(jnp.bfloat16)
    return jnp.dot(pick, slots, preferred_element_type=jnp.float32) * weight[...]


def cols_kernel(pairs, weight, near, own_far, own_cols, *refs, n_row, base):
    col_far, messages, field = refs[: n_row - 1], refs[n_row - 1 : -1], refs[-1]
    blocks, nfar = weight.shape[0], own_cols.shape[0]
    my_row = lax.axis_index("row")
    line = base + 4 * blocks + 1
    pick = [hot(own_far[blocks, 1:2, :], blocks, nfar, my_row)]
    for k in range(1, n_row):
        way = jnp.bitwise_xor(my_row, lax.rem(my_row + n_row - k, n_row))
        index = jnp.zeros((1, BLK), jnp.float32)
        for d, other in enumerate(col_far):
            index = jnp.where(way == d + 1, other[line : line + 1, :], index)
        pick.append(hot(index, blocks, nfar, my_row))
    field[...] = near[...] + spread(pick, [own_cols[...]] + [m[0:nfar, :] for m in messages], weight)
    for message in messages:
        for t in range(pairs.shape[1] - 1):
            k = lax.rem(pairs[0, t + 1], blocks)
            field[pl.ds(k, 1), :] += message[nfar + t : nfar + t + 1, :]


def rows_kernel(weight, field, row0, row1, *refs, n_col):
    rows, out = refs[:-1], refs[-1]
    blocks, nfar = weight.shape[0], rows[0].shape[0] // 2
    my_col = lax.axis_index("col")
    chips = n_col // 2
    chip = lax.div(my_col, 2)
    pick = []
    for k in range(chips):
        way = jnp.bitwise_xor(chip, lax.rem(chip + chips - k, chips))
        tag = place(way, chips) * (blocks + 1) + blocks
        pick += [hot(half[tag, 0:1, :], blocks, nfar, my_col) for half in (row0, row1)]
    total = field[...] + spread(pick, [r[...] for r in rows], weight)
    for q in range(BLK // LANES):
        out[pl.ds(q, blocks, stride=BLK // LANES), :] = total[:, q * LANES : (q + 1) * LANES]


def f32(*shape):
    return jax.ShapeDtypeStruct(shape, jnp.float32)


def cost(micros):
    return pl.CostEstimate(flops=int(micros * 1.1e9), bytes_accessed=1 << 16, transcendentals=0)


def body(points, density, near_pairs, far_pairs, near_count, far_count, *, n_row, n_col):
    quad = points.shape[1]
    blocks = points.shape[2] // BLK
    nnear, nfar = near_pairs.shape[0], far_pairs.shape[0]
    depth, slots = 4 * quad, nnear - 1
    near_pairs, far_pairs = near_pairs.T, far_pairs.T

    def swap(x, axis, d):
        n = {"row": n_row, "col": n_col}[axis]
        return lax.ppermute(x, axis, [(i, i ^ d) for i in range(n)])

    direct = [d for d in range(1, n_row) if d & (d - 1) == 0]
    late = [d for d in range(1, n_row) if d & (d - 1) != 0]

    def halves(n):
        return [1 << j for j in reversed(range(n.bit_length() - 1))]

    def col_gather(x):
        for d in halves(n_col)[:-1]:
            x = jnp.concatenate([x, swap(x, "col", d)], axis=0)
        return x, swap(x, "col", 1)

    base = near_lines(slots, quad)
    msg_rows = -(-(base + 4 * (blocks + 1)) // 8) * 8
    hbm = (near_pairs, far_pairs, points, density.reshape(-1, LANES))
    hbm = [pltpu.with_memory_space_constraint(x, pltpu.HBM) for x in hbm]
    msg, far_own, near_own, weight = pl.pallas_call(
        prep_kernel,
        out_shape=(
            f32(msg_rows, BLK),
            f32(blocks + 1, 4, BLK),
            f32(blocks, depth + 8, BLK),
            f32(blocks, BLK),
        ),
        in_specs=[HBM, SMEM, HBM, HBM, HBM],
        out_specs=(VMEM, VMEM, VMEM, VMEM),
        scratch_shapes=[
            pltpu.SMEM(near_pairs.shape, jnp.int32),
            pltpu.VMEM(far_pairs.shape, jnp.int32),
            pltpu.VMEM(points.shape, jnp.float32),
            pltpu.VMEM((density.shape[0] // LANES, LANES), jnp.float32),
            pltpu.SemaphoreType.DMA((QUARTERS + 3,)),
        ],
        compiler_params=PARAMS,
        cost_estimate=cost(1.2),
        name="prep",
    )(hbm[0], near_count, *hbm[1:])
    row_far = col_gather(far_own)
    known = {d: swap(msg, "row", d) for d in direct}
    *onward, last = lax.optimization_barrier((*[known[d] for d in direct], row_far[0]))
    known.update(zip(direct, onward))
    row_far = (last, row_far[1])
    for d in late:
        known[d] = swap(known[d ^ (d & -d)], "row", d & -d)
    got = [known[d] for d in range(1, n_row)]

    bufs = [
        pltpu.VMEM((quad * BLK, TERMS), jnp.bfloat16),
        pltpu.VMEM((TERMS, quad * BLK), jnp.bfloat16),
        pltpu.VMEM((BLK, LANES), jnp.float32),
        pltpu.VMEM((8, BLK), jnp.float32),
    ]
    near0 = pl.pallas_call(
        near_own_kernel,
        out_shape=f32(blocks, BLK),
        in_specs=[SMEM, SMEM, VMEM],
        out_specs=VMEM,
        scratch_shapes=bufs,
        compiler_params=PARAMS,
        cost_estimate=cost(5.0),
        name="near_own",
    )(near_pairs, near_count, near_own)

    def near_scratch(n):
        return [
            pltpu.VMEM((depth + 8, BLK), jnp.float32),
            pltpu.SMEM((n, 8, LANES), jnp.float32),
            pltpu.SemaphoreType.DMA((n,)),
        ] + bufs

    far_scratch = [
        pltpu.SMEM((nfar,), jnp.int32),
        pltpu.VMEM((2, 4, BLK), jnp.float32),
        pltpu.VMEM((2, 4, BLK), jnp.float32),
        pltpu.VMEM((2, BLK, TERMS), jnp.bfloat16),
        pltpu.VMEM((2, TERMS, BLK), jnp.bfloat16),
        pltpu.VMEM((2, BLK, LANES), jnp.float32),
    ]
    field, *backs = pl.pallas_call(
        functools.partial(direct_kernel, ways=len(direct)),
        out_shape=[f32(blocks, BLK)] + [f32(8, BLK)] * len(direct),
        in_specs=[VMEM] * (2 + len(direct)),
        out_specs=[VMEM] * (len(direct) + 1),
        scratch_shapes=near_scratch(len(direct)),
        compiler_params=PARAMS,
        cost_estimate=cost(30.0),
        name="near_direct",
    )(near_own, near0, *[got[d - 1] for d in direct])
    far_rows, far_cols = pl.pallas_call(
        functools.partial(far_kernel, direct=direct, base=base),
        out_shape=[f32(nfar, BLK)] * 2,
        in_specs=[SMEM, SMEM] + [VMEM] * (3 + len(direct)),
        out_specs=[VMEM] * 2,
        scratch_shapes=far_scratch,
        compiler_params=PARAMS,
        cost_estimate=cost(3.0),
        name="far_direct",
    )(far_pairs, far_count, *row_far, far_own, *[got[d - 1] for d in direct])
    field, far_rows, far_cols, *messages = pl.pallas_call(
        functools.partial(late_kernel, n_row=n_row, direct=direct, late=late),
        out_shape=[f32(blocks, BLK)] + [f32(nfar, BLK)] * 2 + [f32(nfar + 8, BLK)] * (n_row - 1),
        in_specs=[SMEM, SMEM] + [VMEM] * (6 + n_row - 1),
        out_specs=[VMEM] * (n_row + 2),
        scratch_shapes=near_scratch(len(late)) + far_scratch,
        compiler_params=PARAMS,
        cost_estimate=cost(8.0),
        name="late",
    )(far_pairs, far_count, near_own, field, *row_far, far_rows, far_cols, *[got[d - 1] for d in late], *backs)

    messages = [
        lax.ppermute(x, "row", [(i, (i + k + 1) % n_row) for i in range(n_row)]) for k, x in enumerate(messages)
    ]
    both = jnp.concatenate([far_rows, swap(far_rows, "col", 1)], axis=0)
    rows = [both]
    for k in range(2, n_col, 2):
        rows.append(lax.ppermute(both, "col", [(i, (i + k) % n_col) for i in range(n_col)]))
    field = pl.pallas_call(
        functools.partial(cols_kernel, n_row=n_row, base=base),
        out_shape=f32(blocks, BLK),
        in_specs=[SMEM] + [VMEM] * (2 * n_row + 2),
        out_specs=VMEM,
        compiler_params=PARAMS,
        cost_estimate=cost(1.0),
        name="final_cols",
    )(near_pairs, weight, field, far_own, far_cols, *got, *messages)
    out = pl.pallas_call(
        functools.partial(rows_kernel, n_col=n_col),
        out_shape=f32(blocks * BLK // LANES, LANES),
        in_specs=[VMEM] * (4 + len(rows)),
        out_specs=VMEM,
        compiler_params=PARAMS,
        cost_estimate=cost(1.0),
        name="final_rows",
    )(weight, field, *row_far, *rows)
    return out.reshape(-1)


def solution(mesh):
    in_specs = (
        P(None, None, ("row", "col")),
        P(("row", "col")),
        P(("row", "col"), None),
        P(("row", "col"), None),
        P(("row", "col")),
        P(("row", "col")),
    )
    out_specs = P(("row", "col"))
    kernel = functools.partial(body, n_row=mesh.shape["row"], n_col=mesh.shape["col"])
    return jax.shard_map(kernel, mesh=mesh, in_specs=in_specs, out_specs=out_specs, check_vma=False)
```

```python
import functools

import jax
import jax.numpy as jnp
from jax import lax
from jax.experimental import pallas as pl
from jax.experimental.pallas import tpu as pltpu
from jax.sharding import PartitionSpec as P

BLK = 512
LANES = 128
SOFT_SQ = 0.0004
TERMS = 64
SPLIT = 48
HALF = 512
QUARTERS = 4
SLOTS = 5
NEAR_SCRATCH = 4 * [None]
GROUP = 16
CHUNK = 512
VMEM = pl.BlockSpec(memory_space=pltpu.VMEM)
SMEM = pl.BlockSpec(memory_space=pltpu.SMEM)
ANY = pl.BlockSpec(memory_space=pl.ANY)
HBM = pl.BlockSpec(memory_space=pltpu.HBM)
PARAMS = pltpu.CompilerParams(vmem_limit_bytes=40 * 1024 * 1024)


def prep_kernel(near_hbm, count, far_hbm, pts_hbm, dens_hbm, msg, far_out, near_out, weight_out, *scratch):
    near_ref, far_ref, pts_ref, dens_ref, sems = scratch
    blocks = near_out.shape[0]
    quad = pts_ref.shape[1]
    slots, body = near_ref.shape[1] - 1, quad * 4
    base = near_lines(slots, quad)
    width = pts_ref.shape[2] // QUARTERS
    copies = [
        pltpu.make_async_copy(dens_hbm, dens_ref, sems.at[QUARTERS]),
        pltpu.make_async_copy(far_hbm, far_ref, sems.at[QUARTERS + 1]),
        pltpu.make_async_copy(near_hbm, near_ref, sems.at[QUARTERS + 2]),
    ]
    for i in range(QUARTERS):
        part = slice(i * width, (i + 1) * width)
        copies.append(pltpu.make_async_copy(pts_hbm.at[:, :, part], pts_ref.at[:, :, part], sems.at[i]))
    for copy in copies:
        copy.start()
    copies.pop(0).wait()
    copies.pop(0).wait()
    copies.pop(0).wait()

    def put_far(k, value):
        far_out[k] = value
        msg[base + 4 * k : base + 4 * k + 4, :] = value

    for k in range(blocks):
        cols = slice(k * BLK, (k + 1) * BLK)
        if k % (blocks // QUARTERS) == 0:
            copies.pop(0).wait()
        w = pts_ref[3, :, cols]
        total = jnp.sum(w, axis=0, keepdims=True)
        dens = jnp.concatenate([dens_ref[4 * k + q : 4 * k + q + 1, :] for q in range(4)], axis=1)
        lines = []
        for c in range(3):
            x = pts_ref[c, :, cols]
            lines.append(jnp.sum(x * w, axis=0, keepdims=True) / total)
            near_out[k, quad * c : quad * c + quad, :] = x
        near_out[k, quad * 3 : quad * 4, :] = w
        near_out[k, quad * 4 : quad * 4 + 8, :] = jnp.broadcast_to(dens, (8, BLK))
        put_far(k, jnp.concatenate(lines + [total * dens], axis=0))
        weight_out[k : k + 1, :] = total
    lane = lax.broadcasted_iota(jnp.int32, (1, LANES), 1)
    lines = [jnp.full((1, LANES), -1.0, jnp.float32)] * 2
    for t in range(slots):
        k = lax.rem(near_ref[0, t + 1], blocks)
        msg[t * body : (t + 1) * body, :] = near_out[k, 0:body, :]
        source = jnp.where(t + 1 < count[0], near_ref[1, t + 1], -1)
        lines[0] = jnp.where(lane == t, k.astype(jnp.float32), lines[0])
        lines[1] = jnp.where(lane == t, source.astype(jnp.float32), lines[1])
    pairs = jnp.concatenate([far_ref[...].astype(jnp.float32), jnp.full((2, LANES - far_ref.shape[1]), -1.0)], axis=1)
    pairs = jnp.concatenate([pairs] + lines, axis=0)
    put_far(blocks, jnp.concatenate([pairs] * (BLK // LANES), axis=1))
    used = base + 4 * (blocks + 1)
    if used < msg.shape[0]:
        msg[used:, :] = jnp.zeros((msg.shape[0] - used, BLK), jnp.float32)


def near_lines(slots, quad):
    return slots * 4 * quad


def three(value):
    one = value.astype(jnp.bfloat16).astype(jnp.float32)
    two = (value - one).astype(jnp.bfloat16).astype(jnp.float32)
    return one, two, value - one - two


def pick_row(row, values):
    out = jnp.zeros(row.shape, jnp.float32)
    for k, value in enumerate(values):
        out = jnp.where(row == k, value, out)
    return out


def parts(x):
    row = lax.broadcasted_iota(jnp.int32, x.shape, 0)
    live = row < 3
    centred = jnp.where(live, x - 0.5, 0.0)
    head = jnp.round(centred * 256.0) * (1.0 / 256.0)
    rest = centred - head
    rest1 = rest.astype(jnp.bfloat16).astype(jnp.float32)
    big = pick_row(row, three(jnp.sum(head * head, axis=0, keepdims=True)))
    small = pick_row(row, three(jnp.sum(rest * (2.0 * head + rest), axis=0, keepdims=True) + 0.5 * SOFT_SQ))
    return head, rest1, rest - rest1, big, small, jnp.where(live, 1.0, 0.0)


def left_terms(x, columns):
    head, rest1, rest2, big, small, ones = parts(x)
    h2, a2, b2 = -2.0 * head, -2.0 * rest1, -2.0 * rest2
    groups = [h2, big, ones, small, ones, h2, h2, a2, b2, a2, a2, b2]
    row = lax.broadcasted_iota(jnp.int32, (TERMS - SPLIT, x.shape[1]), 0)
    groups.append(pick_row(row, [part for column in columns for part in three(column)]))
    return jnp.concatenate(groups, axis=0)


def right_terms(x):
    head, rest1, rest2, big, small, ones = parts(x)
    groups = [head, ones, big, ones, small, rest1, rest2, head, head, rest1, rest2, rest1]
    groups.append(jnp.zeros((TERMS - SPLIT, x.shape[1]), jnp.float32))
    return jnp.concatenate(groups, axis=0).astype(jnp.bfloat16)


def column_of(lhs, which):
    row = lax.broadcasted_iota(jnp.int32, (TERMS, LANES), 0) - SPLIT - 3 * which
    pick = jnp.where((row >= 0) & (row < 3), 1.0, 0.0).astype(jnp.bfloat16)
    return jnp.dot(lhs, pick, preferred_element_type=jnp.float32)


def fold_lanes(tile, row):
    part = tile[:, :LANES] * row[:, :LANES]
    for q in range(1, tile.shape[1] // LANES):
        part = part + tile[:, q * LANES : (q + 1) * LANES] * row[:, q * LANES : (q + 1) * LANES]
    return part


def twice(col):
    return jnp.concatenate([col] * (HALF // LANES), axis=1)


def place(x, n):
    bits = n.bit_length() - 1
    div, rem = (lambda a, b: a // b, lambda a, b: a % b) if isinstance(x, int) else (lax.div, lax.rem)
    return sum(rem(div(x, 1 << (bits - 1 - j)), 2) * (1 << j) for j in range(bits))


def far_tiles(pairs, count, row_in, sources, rows_out, cols_out, base, queue, left_buf, right_buf, lhs_buf, rhs_buf, part_buf):
    n_col = lax.axis_size("col")
    row_step = 2 * row_in[0].shape[0] // n_col
    blocks = row_step - 1
    my_row, my_col = lax.axis_index("row"), lax.axis_index("col")

    def ways(s):
        a, b = pairs[0, s], pairs[1, s]
        return jnp.bitwise_xor(lax.div(a, blocks), my_col), jnp.bitwise_xor(lax.div(b, blocks), my_row)

    def enqueue(s, n):
        b_way = ways(s)[1]
        here = functools.reduce(jnp.logical_or, [b_way == d for d in sources])

        @pl.when(here)
        def _():
            queue[n] = s

        return n + here.astype(jnp.int32)

    def fetch(s, j):
        a_way, b_way = ways(s)
        ka, kb = lax.rem(pairs[0, s], blocks), lax.rem(pairs[1, s], blocks)
        for d, other in sources.items():

            @pl.when(b_way == d)
            def _():
                if d == 0:
                    right_buf[j] = other[kb]
                else:
                    lines = [other[pl.ds(base + 4 * kb + c, 1), :] for c in range(4)]
                    right_buf[j] = jnp.concatenate(lines, axis=0)

        for core, half in enumerate(row_in):

            @pl.when(lax.rem(a_way, 2) == core)
            def _():
                left_buf[j] = half[place(lax.div(a_way, 2), n_col // 2) * row_step + ka]

        return jnp.where((a_way == 0) & (b_way == 0) & (ka == kb), 0.0, 1.0)

    def tiles(slots):
        many = range(len(slots))
        mirror = [fetch(s, j) for j, s in enumerate(slots)]
        for j in many:
            left = left_buf[j]
            lhs_buf[j] = jnp.transpose(left_terms(left, [left[3:4]])).astype(jnp.bfloat16)
            rhs_buf[j] = right_terms(right_buf[j])
        zcol = [column_of(lhs_buf[j], 0) for j in many]
        dist = [jnp.dot(lhs_buf[j], rhs_buf[j], preferred_element_type=jnp.float32) for j in many]
        weights = [right_buf[j, 3:4, :] for j in many]
        acc = [jnp.zeros((8, BLK), jnp.float32) for _ in many]
        for g in range(BLK // 8):
            rows = slice(g * 8, (g + 1) * 8)
            for j in many:
                tile = lax.rsqrt(dist[j][rows, :])
                part_buf[j, rows, :] = fold_lanes(tile, weights[j])
                acc[j] = acc[j] + tile * twice(zcol[j][rows, :])
        for j, s in enumerate(slots):
            rows_out[pl.ds(s, 1), :] = jnp.sum(jnp.transpose(part_buf[j]), axis=0, keepdims=True)
            cols_out[pl.ds(s, 1), :] = jnp.sum(acc[j], axis=0, keepdims=True) * mirror[j]

    def two(i, _):
        tiles([queue[2 * i], queue[2 * i + 1]])
        return 0

    total = lax.fori_loop(0, count[0], enqueue, 0)
    lax.fori_loop(0, lax.div(total, 2), two, 0)
    pl.when(lax.rem(total, 2) == 1)(lambda: tiles([queue[total - 1]]))


def points(tall):
    quad = tall.shape[0] // 4
    sides = [[tall[quad * c + u : quad * c + u + 1, :] for c in range(4)] for u in range(quad)]
    return jnp.concatenate([jnp.concatenate(side, axis=0) for side in sides], axis=1)


def near_tile(left, dens_i, right, dens_j, lhs_buf, rhs_buf, part_buf, acc_buf):
    quad = left.shape[1] // BLK
    terms = jnp.transpose(left_terms(left, [left[3:4], jnp.concatenate([dens_i] * quad, axis=1)]))
    terms = terms.astype(jnp.bfloat16)
    for g in range(BLK // GROUP):
        for u in range(quad):
            to, at = (g * quad + u) * GROUP, u * BLK + g * GROUP
            lhs_buf[to : to + GROUP, :] = terms[at : at + GROUP, :]
    rhs_buf[...] = right_terms(right)
    weights = right[3:4]
    acc_buf[...] = jnp.zeros_like(acc_buf)

    def chunk(i, _):
        at = pl.multiple_of(i * CHUNK * quad, CHUNK * quad)
        lhs = lhs_buf[pl.ds(at, CHUNK * quad), :]
        wcol = column_of(lhs, 0)
        groups = CHUNK // GROUP
        first_rows = [lhs[g * quad * GROUP : g * quad * GROUP + GROUP, :] for g in range(groups)]
        dcol = column_of(jnp.concatenate(first_rows, axis=0), 1)
        part = None
        for h in range(BLK // HALF):
            tiles = [None] * groups
            for v in range(quad):
                cols = slice(v * BLK + h * HALF, v * BLK + (h + 1) * HALF)
                dist = jnp.dot(lhs, rhs_buf[:, cols], preferred_element_type=jnp.float32)
                for g in range(groups):
                    inner = None
                    for u in range(quad):
                        rows = slice((g * quad + u) * GROUP, (g * quad + u + 1) * GROUP)
                        term = lax.rsqrt(dist[rows, :]) * twice(wcol[rows, :])
                        inner = term if inner is None else inner + term
                    inner = inner * weights[:, cols]
                    tiles[g] = inner if tiles[g] is None else tiles[g] + inner
            tile = jnp.concatenate(tiles, axis=0)
            cols = slice(h * HALF, (h + 1) * HALF)
            more = fold_lanes(tile, dens_j[:, cols])
            part = more if part is None else part + more
            acc_buf[:, cols] += jnp.sum((tile * twice(dcol)).reshape(-1, 8, HALF), axis=0)
        part_buf[pl.ds(pl.multiple_of(i * CHUNK, CHUNK), CHUNK), :] = part
        return 0

    lax.fori_loop(0, BLK // CHUNK, chunk, 0)
    rows = jnp.sum(jnp.transpose(part_buf[...]), axis=0, keepdims=True)
    return rows, jnp.sum(acc_buf[...], axis=0, keepdims=True)


def near_own_kernel(pairs, count, near_ref, field, *bufs):
    blocks, depth, _ = near_ref.shape
    body = depth - 8
    my_row = lax.axis_index("row")
    field[...] = jnp.zeros_like(field)

    def step(s, _):
        ka, kb = lax.rem(pairs[0, s], blocks), pairs[1, s] - my_row * blocks

        @pl.when((kb >= 0) & (kb < blocks))
        def _():
            left, right = points(near_ref[ka, 0:body, :]), points(near_ref[kb, 0:body, :])
            dens_i, dens_j = near_ref[ka, body : body + 1, :], near_ref[kb, body : body + 1, :]
            rows, cols = near_tile(left, dens_i, right, dens_j, *bufs)
            field[pl.ds(ka, 1), :] += rows
            field[pl.ds(kb, 1), :] += cols * jnp.where(ka == kb, 0.0, 1.0)

        return 0

    lax.fori_loop(0, count[0], step, 0)


def near_tiles(meanwhile, near_ref, got, field, put, right_buf, tags, sems, *bufs):
    blocks, depth, _ = near_ref.shape
    body = depth - 8
    base = near_lines(SLOTS, body // 4)
    my_row = lax.axis_index("row")
    tail = slice(base + 4 * blocks, base + 4 * blocks + 8)
    copies = [pltpu.make_async_copy(g.at[tail, 0:LANES], tags.at[d], sems.at[d]) for d, g in enumerate(got)]
    for copy in copies:
        copy.start()
    meanwhile()
    for copy in copies:
        copy.wait()

    def step(i, _):
        way, t = lax.div(i, SLOTS), lax.rem(i, SLOTS)
        kb = tags[way, 3, t].astype(jnp.int32) - my_row * blocks

        @pl.when((kb >= 0) & (kb < blocks))
        def _():
            for d, other in enumerate(got):

                @pl.when(way == d)
                def _():
                    at = pl.multiple_of(t * body, 8)
                    points_j = other[pl.ds(at, body), :]
                    line = base + 4 * tags[way, 2, t].astype(jnp.int32) + 3
                    total = jnp.sum(points_j[body - body // 4 :], axis=0, keepdims=True)
                    right_buf[0:body, :] = points_j
                    right_buf[body : body + 1, :] = other[pl.ds(line, 1), :] / total

            left, right = points(near_ref[kb, 0:body, :]), points(right_buf[0:body, :])
            dens_i, dens_j = near_ref[kb, body : body + 1, :], right_buf[body : body + 1, :]
            rows, cols = near_tile(left, dens_i, right, dens_j, *bufs)
            field[pl.ds(kb, 1), :] += rows
            put(way, t, cols)

        return 0

    lax.fori_loop(0, len(got) * SLOTS, step, 0)


def direct_kernel(near_ref, start, *refs, ways):
    got, (field, *backs), scratch = refs[:ways], refs[ways : 2 * ways + 1], refs[2 * ways + 1 :]

    def clear():
        field[...] = start[...]
        for back in backs:
            back[...] = jnp.zeros_like(back)

    def put(way, t, result):
        for i, back in enumerate(backs):

            @pl.when(way == i)
            def _():
                back[pl.ds(t, 1), :] = result

    near_tiles(clear, near_ref, got, field, put, *scratch)


def far_kernel(pairs, count, row0, row1, own_in, *refs, direct, base):
    got, (rows_out, cols_out), scratch = refs[: len(direct)], refs[len(direct) : -6], refs[-6:]
    rows_out[...] = jnp.zeros_like(rows_out)
    cols_out[...] = jnp.zeros_like(cols_out)
    sources = {0: own_in, **dict(zip(direct, got))}
    far_tiles(pairs, count, (row0, row1), sources, rows_out, cols_out, base, *scratch)


def late_kernel(pairs, count, near_ref, start, row0, row1, rows_in, cols_in, *refs, n_row, direct, late):
    refs = list(refs)
    take = lambda n: [refs.pop(0) for _ in range(n)]
    got, backs = take(len(late)), take(len(direct))
    field, rows_out, cols_out, *messages = take(n_row + 2)
    near_scratch, far_scratch = take(len(NEAR_SCRATCH) + 3), refs
    nfar = cols_out.shape[0]
    base = near_lines(SLOTS, near_ref.shape[1] // 4 - 2)
    my_row = lax.axis_index("row")

    def to_peer(d, lines, value):
        k = lax.rem(jnp.bitwise_xor(my_row, d) - my_row + n_row - 1, n_row)
        for i, message in enumerate(messages):

            @pl.when(k == i)
            def _():
                message[lines, :] = value

    def put(way, t, result):
        for i, d in enumerate(late):
            pl.when(way == i)(lambda: to_peer(d, pl.ds(nfar + t, 1), result))

    def far():
        field[...] = start[...]
        rows_out[...] = rows_in[...]
        cols_out[...] = cols_in[...]
        for message in messages:
            message[nfar:, :] = jnp.zeros((8, BLK), jnp.float32)
        for d, back in zip(direct, backs):
            to_peer(d, slice(nfar, nfar + 8), back[...])
        far_tiles(pairs, count, (row0, row1), dict(zip(late, got)), rows_out, cols_out, base, *far_scratch)
        for message in messages:
            message[0:nfar, :] = cols_out[...]

    near_tiles(far, near_ref, got, field, put, *near_scratch)


def hot(index, blocks, slots, base):
    want = lax.broadcasted_iota(jnp.int32, (blocks, slots), 0) + base * blocks
    return jnp.where(index[:, 0:slots] == want.astype(jnp.float32), 1.0, 0.0)


def spread(pick, slots, weight):
    pick = jnp.concatenate(pick * 3, axis=1).astype(jnp.bfloat16)
    slots = jnp.concatenate(three(jnp.concatenate(slots, axis=0)), axis=0).astype(jnp.bfloat16)
    return jnp.dot(pick, slots, preferred_element_type=jnp.float32) * weight[...]


def cols_kernel(pairs, weight, near, own_far, own_cols, *refs, n_row, base):
    col_far, messages, field = refs[: n_row - 1], refs[n_row - 1 : -1], refs[-1]
    blocks, nfar = weight.shape[0], own_cols.shape[0]
    my_row = lax.axis_index("row")
    line = base + 4 * blocks + 1
    pick = [hot(own_far[blocks, 1:2, :], blocks, nfar, my_row)]
    for k in range(1, n_row):
        way = jnp.bitwise_xor(my_row, lax.rem(my_row + n_row - k, n_row))
        index = jnp.zeros((1, BLK), jnp.float32)
        for d, other in enumerate(col_far):
            index = jnp.where(way == d + 1, other[line : line + 1, :], index)
        pick.append(hot(index, blocks, nfar, my_row))
    field[...] = near[...] + spread(pick, [own_cols[...]] + [m[0:nfar, :] for m in messages], weight)
    for message in messages:
        for t in range(pairs.shape[1] - 1):
            k = lax.rem(pairs[0, t + 1], blocks)
            field[pl.ds(k, 1), :] += message[nfar + t : nfar + t + 1, :]


def rows_kernel(weight, field, row0, row1, *refs, n_col):
    rows, out = refs[:-1], refs[-1]
    blocks, nfar = weight.shape[0], rows[0].shape[0] // 2
    my_col = lax.axis_index("col")
    chips = n_col // 2
    chip = lax.div(my_col, 2)
    pick = []
    for k in range(chips):
        way = jnp.bitwise_xor(chip, lax.rem(chip + k, chips))
        tag = place(way, chips) * (blocks + 1) + blocks
        pick += [hot(half[tag, 0:1, :], blocks, nfar, my_col) for half in (row0, row1)]
    total = field[...] + spread(pick, [r[...] for r in rows], weight)
    for q in range(BLK // LANES):
        out[pl.ds(q, blocks, stride=BLK // LANES), :] = total[:, q * LANES : (q + 1) * LANES]


def f32(*shape):
    return jax.ShapeDtypeStruct(shape, jnp.float32)


def cost(micros):
    return pl.CostEstimate(flops=int(micros * 1.1e9), bytes_accessed=1 << 16, transcendentals=0)


def body(points, density, near_pairs, far_pairs, near_count, far_count, *, n_row, n_col):
    quad = points.shape[1]
    blocks = points.shape[2] // BLK
    nnear, nfar = near_pairs.shape[0], far_pairs.shape[0]
    depth, slots = 4 * quad, nnear - 1
    near_pairs, far_pairs = near_pairs.T, far_pairs.T

    def swap(x, axis, d):
        n = {"row": n_row, "col": n_col}[axis]
        return lax.ppermute(x, axis, [(i, i ^ d) for i in range(n)])

    direct = [d for d in range(1, n_row) if d & (d - 1) == 0]
    late = [d for d in range(1, n_row) if d & (d - 1) != 0]

    def halves(n):
        return [1 << j for j in reversed(range(n.bit_length() - 1))]

    def col_gather(x):
        for d in halves(n_col)[:-1]:
            x = jnp.concatenate([x, swap(x, "col", d)], axis=0)
        return x, swap(x, "col", 1)

    base = near_lines(slots, quad)
    msg_rows = -(-(base + 4 * (blocks + 1)) // 8) * 8
    hbm = (near_pairs, far_pairs, points, density.reshape(-1, LANES))
    hbm = [pltpu.with_memory_space_constraint(x, pltpu.HBM) for x in hbm]
    msg, far_own, near_own, weight = pl.pallas_call(
        prep_kernel,
        out_shape=(
            f32(msg_rows, BLK),
            f32(blocks + 1, 4, BLK),
            f32(blocks, depth + 8, BLK),
            f32(blocks, BLK),
        ),
        in_specs=[HBM, SMEM, HBM, HBM, HBM],
        out_specs=(VMEM, VMEM, VMEM, VMEM),
        scratch_shapes=[
            pltpu.SMEM(near_pairs.shape, jnp.int32),
            pltpu.VMEM(far_pairs.shape, jnp.int32),
            pltpu.VMEM(points.shape, jnp.float32),
            pltpu.VMEM((density.shape[0] // LANES, LANES), jnp.float32),
            pltpu.SemaphoreType.DMA((QUARTERS + 3,)),
        ],
        compiler_params=PARAMS,
        cost_estimate=cost(1.2),
        name="prep",
    )(hbm[0], near_count, *hbm[1:])
    row_far = col_gather(far_own)
    known = {d: swap(msg, "row", d) for d in direct}
    passed = [d for d in direct if d > 1]
    *onward, first = lax.optimization_barrier((*[known[d] for d in passed], row_far[0]))
    known.update(zip(passed, onward))
    row_far = (first, row_far[1])
    for d in late:
        known[d] = swap(known[d ^ (d & -d)], "row", d & -d)
    got = [known[d] for d in range(1, n_row)]

    bufs = [
        pltpu.VMEM((quad * BLK, TERMS), jnp.bfloat16),
        pltpu.VMEM((TERMS, quad * BLK), jnp.bfloat16),
        pltpu.VMEM((BLK, LANES), jnp.float32),
        pltpu.VMEM((8, BLK), jnp.float32),
    ]
    near0 = pl.pallas_call(
        near_own_kernel,
        out_shape=f32(blocks, BLK),
        in_specs=[SMEM, SMEM, VMEM],
        out_specs=VMEM,
        scratch_shapes=bufs,
        compiler_params=PARAMS,
        cost_estimate=cost(5.0),
        name="near_own",
    )(near_pairs, near_count, near_own)

    def near_scratch(n):
        return [
            pltpu.VMEM((depth + 8, BLK), jnp.float32),
            pltpu.SMEM((n, 8, LANES), jnp.float32),
            pltpu.SemaphoreType.DMA((n,)),
        ] + bufs

    far_scratch = [
        pltpu.SMEM((nfar,), jnp.int32),
        pltpu.VMEM((2, 4, BLK), jnp.float32),
        pltpu.VMEM((2, 4, BLK), jnp.float32),
        pltpu.VMEM((2, BLK, TERMS), jnp.bfloat16),
        pltpu.VMEM((2, TERMS, BLK), jnp.bfloat16),
        pltpu.VMEM((2, BLK, LANES), jnp.float32),
    ]
    field, *backs = pl.pallas_call(
        functools.partial(direct_kernel, ways=len(direct)),
        out_shape=[f32(blocks, BLK)] + [f32(8, BLK)] * len(direct),
        in_specs=[VMEM] * (2 + len(direct)),
        out_specs=[VMEM] * (len(direct) + 1),
        scratch_shapes=near_scratch(len(direct)),
        compiler_params=PARAMS,
        cost_estimate=cost(30.0),
        name="near_direct",
    )(near_own, near0, *[got[d - 1] for d in direct])
    far_rows, far_cols = pl.pallas_call(
        functools.partial(far_kernel, direct=direct, base=base),
        out_shape=[f32(nfar, BLK)] * 2,
        in_specs=[SMEM, SMEM] + [VMEM] * (3 + len(direct)),
        out_specs=[VMEM] * 2,
        scratch_shapes=far_scratch,
        compiler_params=PARAMS,
        cost_estimate=cost(3.0),
        name="far_direct",
    )(far_pairs, far_count, *row_far, far_own, *[got[d - 1] for d in direct])
    field, far_rows, far_cols, *messages = pl.pallas_call(
        functools.partial(late_kernel, n_row=n_row, direct=direct, late=late),
        out_shape=[f32(blocks, BLK)] + [f32(nfar, BLK)] * 2 + [f32(nfar + 8, BLK)] * (n_row - 1),
        in_specs=[SMEM, SMEM] + [VMEM] * (6 + n_row - 1),
        out_specs=[VMEM] * (n_row + 2),
        scratch_shapes=near_scratch(len(late)) + far_scratch,
        compiler_params=PARAMS,
        cost_estimate=cost(8.0),
        name="late",
    )(far_pairs, far_count, near_own, field, *row_far, far_rows, far_cols, *[got[d - 1] for d in late], *backs)

    messages = [
        lax.ppermute(x, "row", [(i, (i + k + 1) % n_row) for i in range(n_row)]) for k, x in enumerate(messages)
    ]
    both = jnp.concatenate([far_rows, swap(far_rows, "col", 1)], axis=0)
    rows = [both]
    for k in range(2, n_col, 2):
        rows.append(lax.ppermute(both, "col", [(i, (i - k) % n_col) for i in range(n_col)]))
    field = pl.pallas_call(
        functools.partial(cols_kernel, n_row=n_row, base=base),
        out_shape=f32(blocks, BLK),
        in_specs=[SMEM] + [VMEM] * (2 * n_row + 2),
        out_specs=VMEM,
        compiler_params=PARAMS,
        cost_estimate=cost(1.0),
        name="final_cols",
    )(near_pairs, weight, field, far_own, far_cols, *got, *messages)
    out = pl.pallas_call(
        functools.partial(rows_kernel, n_col=n_col),
        out_shape=f32(blocks * BLK // LANES, LANES),
        in_specs=[VMEM] * (4 + len(rows)),
        out_specs=VMEM,
        compiler_params=PARAMS,
        cost_estimate=cost(1.0),
        name="final_rows",
    )(weight, field, *row_far, *rows)
    return out.reshape(-1)


def solution(mesh):
    in_specs = (
        P(None, None, ("row", "col")),
        P(("row", "col")),
        P(("row", "col"), None),
        P(("row", "col"), None),
        P(("row", "col")),
        P(("row", "col")),
    )
    out_specs = P(("row", "col"))
    kernel = functools.partial(body, n_row=mesh.shape["row"], n_col=mesh.shape["col"])
    return jax.shard_map(kernel, mesh=mesh, in_specs=in_specs, out_specs=out_specs, check_vma=False)
```

```python
import functools

import jax
import jax.numpy as jnp
from jax import lax
from jax.experimental import pallas as pl
from jax.experimental.pallas import tpu as pltpu
from jax.sharding import PartitionSpec as P

BLK = 512
LANES = 128
SOFT_SQ = 0.0004
TERMS = 64
SPLIT = 48
HALF = 512
QUARTERS = 4
SLOTS = 5
OWN_FIRST = 2
NEAR_SCRATCH = 4 * [None]
GROUP = 16
CHUNK = 512
VMEM = pl.BlockSpec(memory_space=pltpu.VMEM)
SMEM = pl.BlockSpec(memory_space=pltpu.SMEM)
ANY = pl.BlockSpec(memory_space=pl.ANY)
HBM = pl.BlockSpec(memory_space=pltpu.HBM)
PARAMS = pltpu.CompilerParams(vmem_limit_bytes=40 * 1024 * 1024)


def prep_kernel(near_hbm, count, far_hbm, pts_hbm, dens_hbm, msg, far_out, near_out, weight_out, *scratch):
    near_ref, far_ref, pts_ref, dens_ref, sems = scratch
    blocks = near_out.shape[0]
    quad = pts_ref.shape[1]
    slots, body = near_ref.shape[1] - 1, quad * 4
    base = near_lines(slots, quad)
    width = pts_ref.shape[2] // QUARTERS
    copies = [
        pltpu.make_async_copy(dens_hbm, dens_ref, sems.at[QUARTERS]),
        pltpu.make_async_copy(far_hbm, far_ref, sems.at[QUARTERS + 1]),
        pltpu.make_async_copy(near_hbm, near_ref, sems.at[QUARTERS + 2]),
    ]
    for i in range(QUARTERS):
        part = slice(i * width, (i + 1) * width)
        copies.append(pltpu.make_async_copy(pts_hbm.at[:, :, part], pts_ref.at[:, :, part], sems.at[i]))
    for copy in copies:
        copy.start()
    copies.pop(0).wait()
    copies.pop(0).wait()
    copies.pop(0).wait()

    def put_far(k, value):
        far_out[k] = value
        msg[base + 4 * k : base + 4 * k + 4, :] = value

    for k in range(blocks):
        cols = slice(k * BLK, (k + 1) * BLK)
        if k % (blocks // QUARTERS) == 0:
            copies.pop(0).wait()
        w = pts_ref[3, :, cols]
        total = jnp.sum(w, axis=0, keepdims=True)
        dens = jnp.concatenate([dens_ref[4 * k + q : 4 * k + q + 1, :] for q in range(4)], axis=1)
        lines = []
        for c in range(3):
            x = pts_ref[c, :, cols]
            lines.append(jnp.sum(x * w, axis=0, keepdims=True) / total)
            near_out[k, quad * c : quad * c + quad, :] = x
        near_out[k, quad * 3 : quad * 4, :] = w
        near_out[k, quad * 4 : quad * 4 + 8, :] = jnp.broadcast_to(dens, (8, BLK))
        put_far(k, jnp.concatenate(lines + [total * dens], axis=0))
        weight_out[k : k + 1, :] = total
    lane = lax.broadcasted_iota(jnp.int32, (1, LANES), 1)
    lines = [jnp.full((1, LANES), -1.0, jnp.float32)] * 2
    for t in range(slots):
        k = lax.rem(near_ref[0, t + 1], blocks)
        msg[t * body : (t + 1) * body, :] = near_out[k, 0:body, :]
        source = jnp.where(t + 1 < count[0], near_ref[1, t + 1], -1)
        lines[0] = jnp.where(lane == t, k.astype(jnp.float32), lines[0])
        lines[1] = jnp.where(lane == t, source.astype(jnp.float32), lines[1])
    pairs = jnp.concatenate([far_ref[...].astype(jnp.float32), jnp.full((2, LANES - far_ref.shape[1]), -1.0)], axis=1)
    pairs = jnp.concatenate([pairs] + lines, axis=0)
    put_far(blocks, jnp.concatenate([pairs] * (BLK // LANES), axis=1))
    used = base + 4 * (blocks + 1)
    if used < msg.shape[0]:
        msg[used:, :] = jnp.zeros((msg.shape[0] - used, BLK), jnp.float32)


def near_lines(slots, quad):
    return slots * 4 * quad


def three(value):
    one = value.astype(jnp.bfloat16).astype(jnp.float32)
    two = (value - one).astype(jnp.bfloat16).astype(jnp.float32)
    return one, two, value - one - two


def pick_row(row, values):
    out = jnp.zeros(row.shape, jnp.float32)
    for k, value in enumerate(values):
        out = jnp.where(row == k, value, out)
    return out


def parts(x):
    row = lax.broadcasted_iota(jnp.int32, x.shape, 0)
    live = row < 3
    centred = jnp.where(live, x - 0.5, 0.0)
    head = jnp.round(centred * 256.0) * (1.0 / 256.0)
    rest = centred - head
    rest1 = rest.astype(jnp.bfloat16).astype(jnp.float32)
    big = pick_row(row, three(jnp.sum(head * head, axis=0, keepdims=True)))
    small = pick_row(row, three(jnp.sum(rest * (2.0 * head + rest), axis=0, keepdims=True) + 0.5 * SOFT_SQ))
    return head, rest1, rest - rest1, big, small, jnp.where(live, 1.0, 0.0)


def left_terms(x, columns):
    head, rest1, rest2, big, small, ones = parts(x)
    h2, a2, b2 = -2.0 * head, -2.0 * rest1, -2.0 * rest2
    groups = [h2, big, ones, small, ones, h2, h2, a2, b2, a2, a2, b2]
    row = lax.broadcasted_iota(jnp.int32, (TERMS - SPLIT, x.shape[1]), 0)
    groups.append(pick_row(row, [part for column in columns for part in three(column)]))
    return jnp.concatenate(groups, axis=0)


def right_terms(x):
    head, rest1, rest2, big, small, ones = parts(x)
    groups = [head, ones, big, ones, small, rest1, rest2, head, head, rest1, rest2, rest1]
    groups.append(jnp.zeros((TERMS - SPLIT, x.shape[1]), jnp.float32))
    return jnp.concatenate(groups, axis=0).astype(jnp.bfloat16)


def column_of(lhs, which):
    row = lax.broadcasted_iota(jnp.int32, (TERMS, LANES), 0) - SPLIT - 3 * which
    pick = jnp.where((row >= 0) & (row < 3), 1.0, 0.0).astype(jnp.bfloat16)
    return jnp.dot(lhs, pick, preferred_element_type=jnp.float32)


def fold_lanes(tile, row):
    part = tile[:, :LANES] * row[:, :LANES]
    for q in range(1, tile.shape[1] // LANES):
        part = part + tile[:, q * LANES : (q + 1) * LANES] * row[:, q * LANES : (q + 1) * LANES]
    return part


def twice(col):
    return jnp.concatenate([col] * (HALF // LANES), axis=1)


def place(x, n):
    bits = n.bit_length() - 1
    div, rem = (lambda a, b: a // b, lambda a, b: a % b) if isinstance(x, int) else (lax.div, lax.rem)
    return sum(rem(div(x, 1 << (bits - 1 - j)), 2) * (1 << j) for j in range(bits))


def far_tiles(pairs, count, row_in, sources, rows_out, cols_out, base, queue, left_buf, right_buf, lhs_buf, rhs_buf, part_buf):
    n_col = lax.axis_size("col")
    row_step = 2 * row_in[0].shape[0] // n_col
    blocks = row_step - 1
    my_row, my_col = lax.axis_index("row"), lax.axis_index("col")

    def ways(s):
        a, b = pairs[0, s], pairs[1, s]
        return jnp.bitwise_xor(lax.div(a, blocks), my_col), jnp.bitwise_xor(lax.div(b, blocks), my_row)

    def enqueue(s, n):
        b_way = ways(s)[1]
        here = functools.reduce(jnp.logical_or, [b_way == d for d in sources])

        @pl.when(here)
        def _():
            queue[n] = s

        return n + here.astype(jnp.int32)

    def fetch(s, j):
        a_way, b_way = ways(s)
        ka, kb = lax.rem(pairs[0, s], blocks), lax.rem(pairs[1, s], blocks)
        for d, other in sources.items():

            @pl.when(b_way == d)
            def _():
                if d == 0:
                    right_buf[j] = other[kb]
                else:
                    lines = [other[pl.ds(base + 4 * kb + c, 1), :] for c in range(4)]
                    right_buf[j] = jnp.concatenate(lines, axis=0)

        for core, half in enumerate(row_in):

            @pl.when(lax.rem(a_way, 2) == core)
            def _():
                left_buf[j] = half[place(lax.div(a_way, 2), n_col // 2) * row_step + ka]

        return jnp.where((a_way == 0) & (b_way == 0) & (ka == kb), 0.0, 1.0)

    def tiles(slots):
        many = range(len(slots))
        mirror = [fetch(s, j) for j, s in enumerate(slots)]
        for j in many:
            left = left_buf[j]
            lhs_buf[j] = jnp.transpose(left_terms(left, [left[3:4]])).astype(jnp.bfloat16)
            rhs_buf[j] = right_terms(right_buf[j])
        zcol = [column_of(lhs_buf[j], 0) for j in many]
        dist = [jnp.dot(lhs_buf[j], rhs_buf[j], preferred_element_type=jnp.float32) for j in many]
        weights = [right_buf[j, 3:4, :] for j in many]
        acc = [jnp.zeros((8, BLK), jnp.float32) for _ in many]
        for g in range(BLK // 8):
            rows = slice(g * 8, (g + 1) * 8)
            for j in many:
                tile = lax.rsqrt(dist[j][rows, :])
                part_buf[j, rows, :] = fold_lanes(tile, weights[j])
                acc[j] = acc[j] + tile * twice(zcol[j][rows, :])
        for j, s in enumerate(slots):
            rows_out[pl.ds(s, 1), :] = jnp.sum(jnp.transpose(part_buf[j]), axis=0, keepdims=True)
            cols_out[pl.ds(s, 1), :] = jnp.sum(acc[j], axis=0, keepdims=True) * mirror[j]

    def two(i, _):
        tiles([queue[2 * i], queue[2 * i + 1]])
        return 0

    total = lax.fori_loop(0, count[0], enqueue, 0)
    lax.fori_loop(0, lax.div(total, 2), two, 0)
    pl.when(lax.rem(total, 2) == 1)(lambda: tiles([queue[total - 1]]))


def points(tall):
    quad = tall.shape[0] // 4
    sides = [[tall[quad * c + u : quad * c + u + 1, :] for c in range(4)] for u in range(quad)]
    return jnp.concatenate([jnp.concatenate(side, axis=0) for side in sides], axis=1)


def near_tile(left, dens_i, right, dens_j, lhs_buf, rhs_buf, part_buf, acc_buf):
    quad = left.shape[1] // BLK
    terms = jnp.transpose(left_terms(left, [left[3:4], jnp.concatenate([dens_i] * quad, axis=1)]))
    terms = terms.astype(jnp.bfloat16)
    for g in range(BLK // GROUP):
        for u in range(quad):
            to, at = (g * quad + u) * GROUP, u * BLK + g * GROUP
            lhs_buf[to : to + GROUP, :] = terms[at : at + GROUP, :]
    rhs_buf[...] = right_terms(right)
    weights = right[3:4]
    acc_buf[...] = jnp.zeros_like(acc_buf)

    def chunk(i, _):
        at = pl.multiple_of(i * CHUNK * quad, CHUNK * quad)
        lhs = lhs_buf[pl.ds(at, CHUNK * quad), :]
        wcol = column_of(lhs, 0)
        groups = CHUNK // GROUP
        first_rows = [lhs[g * quad * GROUP : g * quad * GROUP + GROUP, :] for g in range(groups)]
        dcol = column_of(jnp.concatenate(first_rows, axis=0), 1)
        part = None
        for h in range(BLK // HALF):
            tiles = [None] * groups
            for v in range(quad):
                cols = slice(v * BLK + h * HALF, v * BLK + (h + 1) * HALF)
                dist = jnp.dot(lhs, rhs_buf[:, cols], preferred_element_type=jnp.float32)
                for g in range(groups):
                    inner = None
                    for u in range(quad):
                        rows = slice((g * quad + u) * GROUP, (g * quad + u + 1) * GROUP)
                        term = lax.rsqrt(dist[rows, :]) * twice(wcol[rows, :])
                        inner = term if inner is None else inner + term
                    inner = inner * weights[:, cols]
                    tiles[g] = inner if tiles[g] is None else tiles[g] + inner
            tile = jnp.concatenate(tiles, axis=0)
            cols = slice(h * HALF, (h + 1) * HALF)
            more = fold_lanes(tile, dens_j[:, cols])
            part = more if part is None else part + more
            acc_buf[:, cols] += jnp.sum((tile * twice(dcol)).reshape(-1, 8, HALF), axis=0)
        part_buf[pl.ds(pl.multiple_of(i * CHUNK, CHUNK), CHUNK), :] = part
        return 0

    lax.fori_loop(0, BLK // CHUNK, chunk, 0)
    rows = jnp.sum(jnp.transpose(part_buf[...]), axis=0, keepdims=True)
    return rows, jnp.sum(acc_buf[...], axis=0, keepdims=True)


def near_own_kernel(pairs, count, near_ref, field, *bufs):
    blocks, depth, _ = near_ref.shape
    body = depth - 8
    my_row = lax.axis_index("row")
    field[...] = jnp.zeros_like(field)

    def step(s, n):
        ka, kb = lax.rem(pairs[0, s], blocks), pairs[1, s] - my_row * blocks
        own = (kb >= 0) & (kb < blocks)

        @pl.when(own & (n < OWN_FIRST))
        def _():
            left, right = points(near_ref[ka, 0:body, :]), points(near_ref[kb, 0:body, :])
            dens_i, dens_j = near_ref[ka, body : body + 1, :], near_ref[kb, body : body + 1, :]
            rows, cols = near_tile(left, dens_i, right, dens_j, *bufs)
            field[pl.ds(ka, 1), :] += rows
            field[pl.ds(kb, 1), :] += cols * jnp.where(ka == kb, 0.0, 1.0)

        return n + own.astype(jnp.int32)

    lax.fori_loop(0, count[0], step, jnp.int32(0))


def near_tiles(meanwhile, near_ref, got, field, put, right_buf, tags, sems, *bufs, own=None):
    blocks, depth, _ = near_ref.shape
    body = depth - 8
    base = near_lines(SLOTS, body // 4)
    my_row = lax.axis_index("row")
    tail = slice(base + 4 * blocks, base + 4 * blocks + 8)
    copies = [pltpu.make_async_copy(g.at[tail, 0:LANES], tags.at[d], sems.at[d]) for d, g in enumerate(got)]
    for copy in copies:
        copy.start()
    meanwhile()
    for copy in copies:
        copy.wait()

    def step(i, _):
        way, t = lax.div(i, SLOTS), lax.rem(i, SLOTS)
        kb = tags[jnp.minimum(way, len(got) - 1), 3, t].astype(jnp.int32) - my_row * blocks
        if own is not None:
            pairs, count = own
            before = jnp.int32(0)
            for s in range(SLOTS + 1):
                inside = (pairs[1, s] >= my_row * blocks) & (pairs[1, s] < (my_row + 1) * blocks)
                before = before + jnp.where(inside & (s <= t), 1, 0)
            left_over = (t + 1 < count[0]) & (before >= OWN_FIRST)
            own_kb = jnp.where(left_over, pairs[1, t + 1] - my_row * blocks, -1)
            kb = jnp.where(way == len(got), own_kb, kb)

        @pl.when((kb >= 0) & (kb < blocks))
        def _():
            if own is not None:

                @pl.when(way == len(got))
                def _():
                    right_buf[...] = near_ref[lax.rem(own[0][0, t + 1], blocks)]

            for d, other in enumerate(got):

                @pl.when(way == d)
                def _():
                    at = pl.multiple_of(t * body, 8)
                    points_j = other[pl.ds(at, body), :]
                    line = base + 4 * tags[way, 2, t].astype(jnp.int32) + 3
                    total = jnp.sum(points_j[body - body // 4 :], axis=0, keepdims=True)
                    right_buf[0:body, :] = points_j
                    right_buf[body : body + 1, :] = other[pl.ds(line, 1), :] / total

            left, right = points(near_ref[kb, 0:body, :]), points(right_buf[0:body, :])
            dens_i, dens_j = near_ref[kb, body : body + 1, :], right_buf[body : body + 1, :]
            rows, cols = near_tile(left, dens_i, right, dens_j, *bufs)
            field[pl.ds(kb, 1), :] += rows
            put(way, t, cols)
            if own is not None:
                ka = lax.rem(own[0][0, t + 1], blocks)

                @pl.when(way == len(got))
                def _():
                    field[pl.ds(ka, 1), :] += cols * jnp.where(ka == kb, 0.0, 1.0)

        return 0

    lax.fori_loop(0, (len(got) + (own is not None)) * SLOTS, step, 0)


def direct_kernel(pairs, count, near_ref, start, *refs, ways):
    got, (field, *backs), scratch = refs[:ways], refs[ways : 2 * ways + 1], refs[2 * ways + 1 :]

    def clear():
        field[...] = start[...]
        for back in backs:
            back[...] = jnp.zeros_like(back)

    def put(way, t, result):
        for i, back in enumerate(backs):

            @pl.when(way == i)
            def _():
                back[pl.ds(t, 1), :] = result

    near_tiles(clear, near_ref, got, field, put, *scratch, own=(pairs, count))


def far_kernel(pairs, count, row0, row1, own_in, *refs, direct, base):
    got, (rows_out, cols_out), scratch = refs[: len(direct)], refs[len(direct) : -6], refs[-6:]
    rows_out[...] = jnp.zeros_like(rows_out)
    cols_out[...] = jnp.zeros_like(cols_out)
    sources = {0: own_in, **dict(zip(direct, got))}
    far_tiles(pairs, count, (row0, row1), sources, rows_out, cols_out, base, *scratch)


def late_kernel(pairs, count, near_ref, start, row0, row1, rows_in, cols_in, *refs, n_row, direct, late):
    refs = list(refs)
    take = lambda n: [refs.pop(0) for _ in range(n)]
    got, backs = take(len(late)), take(len(direct))
    field, rows_out, cols_out, *messages = take(n_row + 2)
    near_scratch, far_scratch = take(len(NEAR_SCRATCH) + 3), refs
    nfar = cols_out.shape[0]
    base = near_lines(SLOTS, near_ref.shape[1] // 4 - 2)
    my_row = lax.axis_index("row")

    def to_peer(d, lines, value):
        k = lax.rem(jnp.bitwise_xor(my_row, d) - my_row + n_row - 1, n_row)
        for i, message in enumerate(messages):

            @pl.when(k == i)
            def _():
                message[lines, :] = value

    def put(way, t, result):
        for i, d in enumerate(late):
            pl.when(way == i)(lambda: to_peer(d, pl.ds(nfar + t, 1), result))

    def far():
        field[...] = start[...]
        rows_out[...] = rows_in[...]
        cols_out[...] = cols_in[...]
        for message in messages:
            message[nfar:, :] = jnp.zeros((8, BLK), jnp.float32)
        for d, back in zip(direct, backs):
            to_peer(d, slice(nfar, nfar + 8), back[...])
        far_tiles(pairs, count, (row0, row1), dict(zip(late, got)), rows_out, cols_out, base, *far_scratch)
        for message in messages:
            message[0:nfar, :] = cols_out[...]

    near_tiles(far, near_ref, got, field, put, *near_scratch)


def hot(index, blocks, slots, base):
    want = lax.broadcasted_iota(jnp.int32, (blocks, slots), 0) + base * blocks
    return jnp.where(index[:, 0:slots] == want.astype(jnp.float32), 1.0, 0.0)


def spread(pick, slots, weight):
    pick = jnp.concatenate(pick * 3, axis=1).astype(jnp.bfloat16)
    slots = jnp.concatenate(three(jnp.concatenate(slots, axis=0)), axis=0).astype(jnp.bfloat16)
    return jnp.dot(pick, slots, preferred_element_type=jnp.float32) * weight[...]


def cols_kernel(pairs, weight, near, own_far, own_cols, *refs, n_row, base):
    col_far, messages, field = refs[: n_row - 1], refs[n_row - 1 : -1], refs[-1]
    blocks, nfar = weight.shape[0], own_cols.shape[0]
    my_row = lax.axis_index("row")
    line = base + 4 * blocks + 1
    pick = [hot(own_far[blocks, 1:2, :], blocks, nfar, my_row)]
    for k in range(1, n_row):
        way = jnp.bitwise_xor(my_row, lax.rem(my_row + n_row - k, n_row))
        index = jnp.zeros((1, BLK), jnp.float32)
        for d, other in enumerate(col_far):
            index = jnp.where(way == d + 1, other[line : line + 1, :], index)
        pick.append(hot(index, blocks, nfar, my_row))
    field[...] = near[...] + spread(pick, [own_cols[...]] + [m[0:nfar, :] for m in messages], weight)
    for message in messages:
        for t in range(pairs.shape[1] - 1):
            k = lax.rem(pairs[0, t + 1], blocks)
            field[pl.ds(k, 1), :] += message[nfar + t : nfar + t + 1, :]


def rows_kernel(weight, field, row0, row1, *refs, n_col):
    rows, out = refs[:-1], refs[-1]
    blocks, nfar = weight.shape[0], rows[0].shape[0] // 2
    my_col = lax.axis_index("col")
    chips = n_col // 2
    chip = lax.div(my_col, 2)
    pick = []
    for k in range(chips):
        way = jnp.bitwise_xor(chip, lax.rem(chip + k, chips))
        tag = place(way, chips) * (blocks + 1) + blocks
        pick += [hot(half[tag, 0:1, :], blocks, nfar, my_col) for half in (row0, row1)]
    total = field[...] + spread(pick, [r[...] for r in rows], weight)
    for q in range(BLK // LANES):
        out[pl.ds(q, blocks, stride=BLK // LANES), :] = total[:, q * LANES : (q + 1) * LANES]


def f32(*shape):
    return jax.ShapeDtypeStruct(shape, jnp.float32)


def cost(micros):
    return pl.CostEstimate(flops=int(micros * 1.1e9), bytes_accessed=1 << 16, transcendentals=0)


def body(points, density, near_pairs, far_pairs, near_count, far_count, *, n_row, n_col):
    quad = points.shape[1]
    blocks = points.shape[2] // BLK
    nnear, nfar = near_pairs.shape[0], far_pairs.shape[0]
    depth, slots = 4 * quad, nnear - 1
    near_pairs, far_pairs = near_pairs.T, far_pairs.T

    def swap(x, axis, d):
        n = {"row": n_row, "col": n_col}[axis]
        return lax.ppermute(x, axis, [(i, i ^ d) for i in range(n)])

    direct = [d for d in range(1, n_row) if d & (d - 1) == 0]
    late = [d for d in range(1, n_row) if d & (d - 1) != 0]

    def halves(n):
        return [1 << j for j in reversed(range(n.bit_length() - 1))]

    def col_gather(x):
        for d in halves(n_col)[:-1]:
            x = jnp.concatenate([x, swap(x, "col", d)], axis=0)
        return x, swap(x, "col", 1)

    base = near_lines(slots, quad)
    msg_rows = -(-(base + 4 * (blocks + 1)) // 8) * 8
    hbm = (near_pairs, far_pairs, points, density.reshape(-1, LANES))
    hbm = [pltpu.with_memory_space_constraint(x, pltpu.HBM) for x in hbm]
    msg, far_own, near_own, weight = pl.pallas_call(
        prep_kernel,
        out_shape=(
            f32(msg_rows, BLK),
            f32(blocks + 1, 4, BLK),
            f32(blocks, depth + 8, BLK),
            f32(blocks, BLK),
        ),
        in_specs=[HBM, SMEM, HBM, HBM, HBM],
        out_specs=(VMEM, VMEM, VMEM, VMEM),
        scratch_shapes=[
            pltpu.SMEM(near_pairs.shape, jnp.int32),
            pltpu.VMEM(far_pairs.shape, jnp.int32),
            pltpu.VMEM(points.shape, jnp.float32),
            pltpu.VMEM((density.shape[0] // LANES, LANES), jnp.float32),
            pltpu.SemaphoreType.DMA((QUARTERS + 3,)),
        ],
        compiler_params=PARAMS,
        cost_estimate=cost(1.2),
        name="prep",
    )(hbm[0], near_count, *hbm[1:])
    row_far = col_gather(far_own)
    known = {d: swap(msg, "row", d) for d in direct}
    passed = [d for d in direct if d > 1]
    *onward, first = lax.optimization_barrier((*[known[d] for d in passed], row_far[0]))
    known.update(zip(passed, onward))
    row_far = (first, row_far[1])
    for d in late:
        known[d] = swap(known[d ^ (d & -d)], "row", d & -d)
    got = [known[d] for d in range(1, n_row)]

    bufs = [
        pltpu.VMEM((quad * BLK, TERMS), jnp.bfloat16),
        pltpu.VMEM((TERMS, quad * BLK), jnp.bfloat16),
        pltpu.VMEM((BLK, LANES), jnp.float32),
        pltpu.VMEM((8, BLK), jnp.float32),
    ]
    near0 = pl.pallas_call(
        near_own_kernel,
        out_shape=f32(blocks, BLK),
        in_specs=[SMEM, SMEM, VMEM],
        out_specs=VMEM,
        scratch_shapes=bufs,
        compiler_params=PARAMS,
        cost_estimate=cost(5.0),
        name="near_own",
    )(near_pairs, near_count, near_own)

    def near_scratch(n):
        return [
            pltpu.VMEM((depth + 8, BLK), jnp.float32),
            pltpu.SMEM((n, 8, LANES), jnp.float32),
            pltpu.SemaphoreType.DMA((n,)),
        ] + bufs

    far_scratch = [
        pltpu.SMEM((nfar,), jnp.int32),
        pltpu.VMEM((2, 4, BLK), jnp.float32),
        pltpu.VMEM((2, 4, BLK), jnp.float32),
        pltpu.VMEM((2, BLK, TERMS), jnp.bfloat16),
        pltpu.VMEM((2, TERMS, BLK), jnp.bfloat16),
        pltpu.VMEM((2, BLK, LANES), jnp.float32),
    ]
    field, *backs = pl.pallas_call(
        functools.partial(direct_kernel, ways=len(direct)),
        out_shape=[f32(blocks, BLK)] + [f32(8, BLK)] * len(direct),
        in_specs=[SMEM, SMEM] + [VMEM] * (2 + len(direct)),
        out_specs=[VMEM] * (len(direct) + 1),
        scratch_shapes=near_scratch(len(direct)),
        compiler_params=PARAMS,
        cost_estimate=cost(30.0),
        name="near_direct",
    )(near_pairs, near_count, near_own, near0, *[got[d - 1] for d in direct])
    far_rows, far_cols = pl.pallas_call(
        functools.partial(far_kernel, direct=direct, base=base),
        out_shape=[f32(nfar, BLK)] * 2,
        in_specs=[SMEM, SMEM] + [VMEM] * (3 + len(direct)),
        out_specs=[VMEM] * 2,
        scratch_shapes=far_scratch,
        compiler_params=PARAMS,
        cost_estimate=cost(3.0),
        name="far_direct",
    )(far_pairs, far_count, *row_far, far_own, *[got[d - 1] for d in direct])
    field, far_rows, far_cols, *messages = pl.pallas_call(
        functools.partial(late_kernel, n_row=n_row, direct=direct, late=late),
        out_shape=[f32(blocks, BLK)] + [f32(nfar, BLK)] * 2 + [f32(nfar + 8, BLK)] * (n_row - 1),
        in_specs=[SMEM, SMEM] + [VMEM] * (6 + n_row - 1),
        out_specs=[VMEM] * (n_row + 2),
        scratch_shapes=near_scratch(len(late)) + far_scratch,
        compiler_params=PARAMS,
        cost_estimate=cost(8.0),
        name="late",
    )(far_pairs, far_count, near_own, field, *row_far, far_rows, far_cols, *[got[d - 1] for d in late], *backs)

    messages = [
        lax.ppermute(x, "row", [(i, (i + k + 1) % n_row) for i in range(n_row)]) for k, x in enumerate(messages)
    ]
    both = jnp.concatenate([far_rows, swap(far_rows, "col", 1)], axis=0)
    rows = [both]
    for k in range(2, n_col, 2):
        rows.append(lax.ppermute(both, "col", [(i, (i - k) % n_col) for i in range(n_col)]))
    field = pl.pallas_call(
        functools.partial(cols_kernel, n_row=n_row, base=base),
        out_shape=f32(blocks, BLK),
        in_specs=[SMEM] + [VMEM] * (2 * n_row + 2),
        out_specs=VMEM,
        compiler_params=PARAMS,
        cost_estimate=cost(1.0),
        name="final_cols",
    )(near_pairs, weight, field, far_own, far_cols, *got, *messages)
    out = pl.pallas_call(
        functools.partial(rows_kernel, n_col=n_col),
        out_shape=f32(blocks * BLK // LANES, LANES),
        in_specs=[VMEM] * (4 + len(rows)),
        out_specs=VMEM,
        compiler_params=PARAMS,
        cost_estimate=cost(1.0),
        name="final_rows",
    )(weight, field, *row_far, *rows)
    return out.reshape(-1)


def solution(mesh):
    in_specs = (
        P(None, None, ("row", "col")),
        P(("row", "col")),
        P(("row", "col"), None),
        P(("row", "col"), None),
        P(("row", "col")),
        P(("row", "col")),
    )
    out_specs = P(("row", "col"))
    kernel = functools.partial(body, n_row=mesh.shape["row"], n_col=mesh.shape["col"])
    return jax.shard_map(kernel, mesh=mesh, in_specs=in_specs, out_specs=out_specs, check_vma=False)
```

```python
import functools

import jax
import jax.numpy as jnp
from jax import lax
from jax.experimental import pallas as pl
from jax.experimental.pallas import tpu as pltpu
from jax.sharding import PartitionSpec as P

BLK = 512
LANES = 128
SOFT_SQ = 0.0004
TERMS = 64
SPLIT = 48
HALF = 512
QUARTERS = 4
SLOTS = 5
OWN_FIRST = 2
NEAR_SCRATCH = 4 * [None]
GROUP = 16
CHUNK = 512
VMEM = pl.BlockSpec(memory_space=pltpu.VMEM)
SMEM = pl.BlockSpec(memory_space=pltpu.SMEM)
ANY = pl.BlockSpec(memory_space=pl.ANY)
HBM = pl.BlockSpec(memory_space=pltpu.HBM)
PARAMS = pltpu.CompilerParams(vmem_limit_bytes=40 * 1024 * 1024)


def prep_kernel(near_hbm, count, far_hbm, pts_hbm, dens_hbm, msg, far_out, near_out, weight_out, *scratch):
    near_ref, far_ref, pts_ref, dens_ref, sems = scratch
    blocks = near_out.shape[0]
    quad = pts_ref.shape[1]
    slots, body = near_ref.shape[1] - 1, quad * 4
    base = near_lines(slots, quad)
    width = pts_ref.shape[2] // QUARTERS
    copies = [
        pltpu.make_async_copy(dens_hbm, dens_ref, sems.at[QUARTERS]),
        pltpu.make_async_copy(far_hbm, far_ref, sems.at[QUARTERS + 1]),
        pltpu.make_async_copy(near_hbm, near_ref, sems.at[QUARTERS + 2]),
    ]
    for i in range(QUARTERS):
        part = slice(i * width, (i + 1) * width)
        copies.append(pltpu.make_async_copy(pts_hbm.at[:, :, part], pts_ref.at[:, :, part], sems.at[i]))
    for copy in copies:
        copy.start()
    copies.pop(0).wait()
    copies.pop(0).wait()
    copies.pop(0).wait()

    def put_far(k, value):
        far_out[k] = value
        msg[base + 4 * k : base + 4 * k + 4, :] = value

    for k in range(blocks):
        cols = slice(k * BLK, (k + 1) * BLK)
        if k % (blocks // QUARTERS) == 0:
            copies.pop(0).wait()
        w = pts_ref[3, :, cols]
        total = jnp.sum(w, axis=0, keepdims=True)
        dens = jnp.concatenate([dens_ref[4 * k + q : 4 * k + q + 1, :] for q in range(4)], axis=1)
        lines = []
        for c in range(3):
            x = pts_ref[c, :, cols]
            lines.append(jnp.sum(x * w, axis=0, keepdims=True) / total)
            near_out[k, quad * c : quad * c + quad, :] = x
        near_out[k, quad * 3 : quad * 4, :] = w
        near_out[k, quad * 4 : quad * 4 + 8, :] = jnp.broadcast_to(dens, (8, BLK))
        put_far(k, jnp.concatenate(lines + [total * dens], axis=0))
        weight_out[k : k + 1, :] = total
    lane = lax.broadcasted_iota(jnp.int32, (1, LANES), 1)
    lines = [jnp.full((1, LANES), -1.0, jnp.float32)] * 2
    for t in range(slots):
        k = lax.rem(near_ref[0, t + 1], blocks)
        msg[t * body : (t + 1) * body, :] = near_out[k, 0:body, :]
        source = jnp.where(t + 1 < count[0], near_ref[1, t + 1], -1)
        lines[0] = jnp.where(lane == t, k.astype(jnp.float32), lines[0])
        lines[1] = jnp.where(lane == t, source.astype(jnp.float32), lines[1])
    pairs = jnp.concatenate([far_ref[...].astype(jnp.float32), jnp.full((2, LANES - far_ref.shape[1]), -1.0)], axis=1)
    pairs = jnp.concatenate([pairs] + lines, axis=0)
    put_far(blocks, jnp.concatenate([pairs] * (BLK // LANES), axis=1))
    used = base + 4 * (blocks + 1)
    if used < msg.shape[0]:
        msg[used:, :] = jnp.zeros((msg.shape[0] - used, BLK), jnp.float32)


def near_lines(slots, quad):
    return slots * 4 * quad


def three(value):
    one = value.astype(jnp.bfloat16).astype(jnp.float32)
    two = (value - one).astype(jnp.bfloat16).astype(jnp.float32)
    return one, two, value - one - two


def pick_row(row, values):
    out = jnp.zeros(row.shape, jnp.float32)
    for k, value in enumerate(values):
        out = jnp.where(row == k, value, out)
    return out


def parts(x):
    row = lax.broadcasted_iota(jnp.int32, x.shape, 0)
    live = row < 3
    centred = jnp.where(live, x - 0.5, 0.0)
    head = jnp.round(centred * 256.0) * (1.0 / 256.0)
    rest = centred - head
    rest1 = rest.astype(jnp.bfloat16).astype(jnp.float32)
    big = pick_row(row, three(jnp.sum(head * head, axis=0, keepdims=True)))
    small = pick_row(row, three(jnp.sum(rest * (2.0 * head + rest), axis=0, keepdims=True) + 0.5 * SOFT_SQ))
    return head, rest1, rest - rest1, big, small, jnp.where(live, 1.0, 0.0)


def left_terms(x, columns):
    head, rest1, rest2, big, small, ones = parts(x)
    h2, a2, b2 = -2.0 * head, -2.0 * rest1, -2.0 * rest2
    groups = [h2, big, ones, small, ones, h2, h2, a2, b2, a2, a2, b2]
    row = lax.broadcasted_iota(jnp.int32, (TERMS - SPLIT, x.shape[1]), 0)
    groups.append(pick_row(row, [part for column in columns for part in three(column)]))
    return jnp.concatenate(groups, axis=0)


def right_terms(x):
    head, rest1, rest2, big, small, ones = parts(x)
    groups = [head, ones, big, ones, small, rest1, rest2, head, head, rest1, rest2, rest1]
    groups.append(jnp.zeros((TERMS - SPLIT, x.shape[1]), jnp.float32))
    return jnp.concatenate(groups, axis=0).astype(jnp.bfloat16)


def column_of(lhs, which):
    row = lax.broadcasted_iota(jnp.int32, (TERMS, LANES), 0) - SPLIT - 3 * which
    pick = jnp.where((row >= 0) & (row < 3), 1.0, 0.0).astype(jnp.bfloat16)
    return jnp.dot(lhs, pick, preferred_element_type=jnp.float32)


def fold_lanes(tile, row):
    part = tile[:, :LANES] * row[:, :LANES]
    for q in range(1, tile.shape[1] // LANES):
        part = part + tile[:, q * LANES : (q + 1) * LANES] * row[:, q * LANES : (q + 1) * LANES]
    return part


def twice(col):
    return jnp.concatenate([col] * (HALF // LANES), axis=1)


def place(x, n):
    bits = n.bit_length() - 1
    div, rem = (lambda a, b: a // b, lambda a, b: a % b) if isinstance(x, int) else (lax.div, lax.rem)
    return sum(rem(div(x, 1 << (bits - 1 - j)), 2) * (1 << j) for j in range(bits))


def far_tiles(pairs, count, row_in, sources, rows_out, cols_out, base, queue, left_buf, right_buf, lhs_buf, rhs_buf, part_buf):
    n_col = lax.axis_size("col")
    row_step = 2 * row_in[0].shape[0] // n_col
    blocks = row_step - 1
    my_row, my_col = lax.axis_index("row"), lax.axis_index("col")

    def ways(s):
        a, b = pairs[0, s], pairs[1, s]
        return jnp.bitwise_xor(lax.div(a, blocks), my_col), jnp.bitwise_xor(lax.div(b, blocks), my_row)

    def enqueue(s, n):
        b_way = ways(s)[1]
        here = functools.reduce(jnp.logical_or, [b_way == d for d in sources])

        @pl.when(here)
        def _():
            queue[n] = s

        return n + here.astype(jnp.int32)

    def fetch(s, j):
        a_way, b_way = ways(s)
        ka, kb = lax.rem(pairs[0, s], blocks), lax.rem(pairs[1, s], blocks)
        for d, other in sources.items():

            @pl.when(b_way == d)
            def _():
                if d == 0:
                    right_buf[j] = other[kb]
                else:
                    lines = [other[pl.ds(base + 4 * kb + c, 1), :] for c in range(4)]
                    right_buf[j] = jnp.concatenate(lines, axis=0)

        for core, half in enumerate(row_in):

            @pl.when(lax.rem(a_way, 2) == core)
            def _():
                left_buf[j] = half[place(lax.div(a_way, 2), n_col // 2) * row_step + ka]

        return jnp.where((a_way == 0) & (b_way == 0) & (ka == kb), 0.0, 1.0)

    def tiles(slots):
        many = range(len(slots))
        mirror = [fetch(s, j) for j, s in enumerate(slots)]
        for j in many:
            left = left_buf[j]
            lhs_buf[j] = jnp.transpose(left_terms(left, [left[3:4]])).astype(jnp.bfloat16)
            rhs_buf[j] = right_terms(right_buf[j])
        zcol = [column_of(lhs_buf[j], 0) for j in many]
        dist = [jnp.dot(lhs_buf[j], rhs_buf[j], preferred_element_type=jnp.float32) for j in many]
        weights = [right_buf[j, 3:4, :] for j in many]
        acc = [jnp.zeros((8, BLK), jnp.float32) for _ in many]
        for g in range(BLK // 8):
            rows = slice(g * 8, (g + 1) * 8)
            for j in many:
                tile = lax.rsqrt(dist[j][rows, :])
                part_buf[j, rows, :] = fold_lanes(tile, weights[j])
                acc[j] = acc[j] + tile * twice(zcol[j][rows, :])
        for j, s in enumerate(slots):
            rows_out[pl.ds(s, 1), :] = jnp.sum(jnp.transpose(part_buf[j]), axis=0, keepdims=True)
            cols_out[pl.ds(s, 1), :] = jnp.sum(acc[j], axis=0, keepdims=True) * mirror[j]

    def two(i, _):
        tiles([queue[2 * i], queue[2 * i + 1]])
        return 0

    total = lax.fori_loop(0, count[0], enqueue, 0)
    lax.fori_loop(0, lax.div(total, 2), two, 0)
    pl.when(lax.rem(total, 2) == 1)(lambda: tiles([queue[total - 1]]))


def points(tall):
    quad = tall.shape[0] // 4
    sides = [[tall[quad * c + u : quad * c + u + 1, :] for c in range(4)] for u in range(quad)]
    return jnp.concatenate([jnp.concatenate(side, axis=0) for side in sides], axis=1)


def near_tile(left, dens_i, right, dens_j, lhs_buf, rhs_buf, part_buf, acc_buf):
    quad = left.shape[1] // BLK
    terms = jnp.transpose(left_terms(left, [left[3:4], jnp.concatenate([dens_i] * quad, axis=1)]))
    terms = terms.astype(jnp.bfloat16)
    for g in range(BLK // GROUP):
        for u in range(quad):
            to, at = (g * quad + u) * GROUP, u * BLK + g * GROUP
            lhs_buf[to : to + GROUP, :] = terms[at : at + GROUP, :]
    rhs_buf[...] = right_terms(right)
    weights = right[3:4]
    acc_buf[...] = jnp.zeros_like(acc_buf)

    def chunk(i, _):
        at = pl.multiple_of(i * CHUNK * quad, CHUNK * quad)
        lhs = lhs_buf[pl.ds(at, CHUNK * quad), :]
        wcol = column_of(lhs, 0)
        groups = CHUNK // GROUP
        first_rows = [lhs[g * quad * GROUP : g * quad * GROUP + GROUP, :] for g in range(groups)]
        dcol = column_of(jnp.concatenate(first_rows, axis=0), 1)
        part = None
        for h in range(BLK // HALF):
            tiles = [None] * groups
            for v in range(quad):
                cols = slice(v * BLK + h * HALF, v * BLK + (h + 1) * HALF)
                dist = jnp.dot(lhs, rhs_buf[:, cols], preferred_element_type=jnp.float32)
                for g in range(groups):
                    inner = None
                    for u in range(quad):
                        rows = slice((g * quad + u) * GROUP, (g * quad + u + 1) * GROUP)
                        term = lax.rsqrt(dist[rows, :]) * twice(wcol[rows, :])
                        inner = term if inner is None else inner + term
                    inner = inner * weights[:, cols]
                    tiles[g] = inner if tiles[g] is None else tiles[g] + inner
            tile = jnp.concatenate(tiles, axis=0)
            cols = slice(h * HALF, (h + 1) * HALF)
            more = fold_lanes(tile, dens_j[:, cols])
            part = more if part is None else part + more
            acc_buf[:, cols] += jnp.sum((tile * twice(dcol)).reshape(-1, 8, HALF), axis=0)
        part_buf[pl.ds(pl.multiple_of(i * CHUNK, CHUNK), CHUNK), :] = part
        return 0

    lax.fori_loop(0, BLK // CHUNK, chunk, 0)
    rows = jnp.sum(jnp.transpose(part_buf[...]), axis=0, keepdims=True)
    return rows, jnp.sum(acc_buf[...], axis=0, keepdims=True)


def near_own_kernel(pairs, count, near_ref, field, *bufs):
    blocks, depth, _ = near_ref.shape
    body = depth - 8
    my_row = lax.axis_index("row")
    field[...] = jnp.zeros_like(field)

    def step(s, n):
        ka, kb = lax.rem(pairs[0, s], blocks), pairs[1, s] - my_row * blocks
        own = (kb >= 0) & (kb < blocks)

        @pl.when(own & (n < OWN_FIRST))
        def _():
            left, right = points(near_ref[ka, 0:body, :]), points(near_ref[kb, 0:body, :])
            dens_i, dens_j = near_ref[ka, body : body + 1, :], near_ref[kb, body : body + 1, :]
            rows, cols = near_tile(left, dens_i, right, dens_j, *bufs)
            field[pl.ds(ka, 1), :] += rows
            field[pl.ds(kb, 1), :] += cols * jnp.where(ka == kb, 0.0, 1.0)

        return n + own.astype(jnp.int32)

    lax.fori_loop(0, count[0], step, jnp.int32(0))


def near_tiles(meanwhile, near_ref, got, field, put, right_buf, tags, sems, *bufs, own=None):
    blocks, depth, _ = near_ref.shape
    body = depth - 8
    base = near_lines(SLOTS, body // 4)
    my_row = lax.axis_index("row")
    tail = slice(base + 4 * blocks, base + 4 * blocks + 8)
    copies = [pltpu.make_async_copy(g.at[tail, 0:LANES], tags.at[d], sems.at[d]) for d, g in enumerate(got)]
    for copy in copies:
        copy.start()
    meanwhile()
    for copy in copies:
        copy.wait()

    def own_source(s):
        kb = own[0][1, s] - my_row * blocks
        return jnp.where((s < own[1][0]) & (kb >= 0) & (kb < blocks), kb, -1)

    def step(i, seen):
        way, t = lax.div(i, SLOTS), lax.rem(i, SLOTS)
        kb = tags[jnp.minimum(way, len(got) - 1), 3, t].astype(jnp.int32) - my_row * blocks
        if own is not None:
            own_kb = own_source(t + 1)
            kb = jnp.where(way == len(got), jnp.where(seen >= OWN_FIRST, own_kb, -1), kb)
            seen = seen + jnp.where((way == len(got)) & (own_kb >= 0), 1, 0)

        @pl.when((kb >= 0) & (kb < blocks))
        def _():
            if own is not None:

                @pl.when(way == len(got))
                def _():
                    right_buf[...] = near_ref[lax.rem(own[0][0, t + 1], blocks)]

            for d, other in enumerate(got):

                @pl.when(way == d)
                def _():
                    at = pl.multiple_of(t * body, 8)
                    points_j = other[pl.ds(at, body), :]
                    line = base + 4 * tags[way, 2, t].astype(jnp.int32) + 3
                    total = jnp.sum(points_j[body - body // 4 :], axis=0, keepdims=True)
                    right_buf[0:body, :] = points_j
                    right_buf[body : body + 1, :] = other[pl.ds(line, 1), :] / total

            left, right = points(near_ref[kb, 0:body, :]), points(right_buf[0:body, :])
            dens_i, dens_j = near_ref[kb, body : body + 1, :], right_buf[body : body + 1, :]
            rows, cols = near_tile(left, dens_i, right, dens_j, *bufs)
            field[pl.ds(kb, 1), :] += rows
            put(way, t, cols)
            if own is not None:
                ka = lax.rem(own[0][0, t + 1], blocks)

                @pl.when(way == len(got))
                def _():
                    field[pl.ds(ka, 1), :] += cols * jnp.where(ka == kb, 0.0, 1.0)

        return seen

    seen = jnp.int32(0) if own is None else jnp.where(own_source(0) >= 0, 1, 0)
    lax.fori_loop(0, (len(got) + (own is not None)) * SLOTS, step, seen)


def direct_kernel(pairs, count, near_ref, start, *refs, ways):
    got, (field, *backs), scratch = refs[:ways], refs[ways : 2 * ways + 1], refs[2 * ways + 1 :]

    def clear():
        field[...] = start[...]
        for back in backs:
            back[...] = jnp.zeros_like(back)

    def put(way, t, result):
        for i, back in enumerate(backs):

            @pl.when(way == i)
            def _():
                back[pl.ds(t, 1), :] = result

    near_tiles(clear, near_ref, got, field, put, *scratch, own=(pairs, count))


def far_kernel(pairs, count, row0, row1, own_in, *refs, direct, base):
    got, (rows_out, cols_out), scratch = refs[: len(direct)], refs[len(direct) : -6], refs[-6:]
    rows_out[...] = jnp.zeros_like(rows_out)
    cols_out[...] = jnp.zeros_like(cols_out)
    sources = {0: own_in, **dict(zip(direct, got))}
    far_tiles(pairs, count, (row0, row1), sources, rows_out, cols_out, base, *scratch)


def late_kernel(pairs, count, near_ref, start, row0, row1, rows_in, cols_in, *refs, n_row, direct, late):
    refs = list(refs)
    take = lambda n: [refs.pop(0) for _ in range(n)]
    got, backs = take(len(late)), take(len(direct))
    field, rows_out, cols_out, *messages = take(n_row + 2)
    near_scratch, far_scratch = take(len(NEAR_SCRATCH) + 3), refs
    nfar = cols_out.shape[0]
    base = near_lines(SLOTS, near_ref.shape[1] // 4 - 2)
    my_row = lax.axis_index("row")

    def to_peer(d, lines, value):
        k = lax.rem(jnp.bitwise_xor(my_row, d) - my_row + n_row - 1, n_row)
        for i, message in enumerate(messages):

            @pl.when(k == i)
            def _():
                message[lines, :] = value

    def put(way, t, result):
        for i, d in enumerate(late):
            pl.when(way == i)(lambda: to_peer(d, pl.ds(nfar + t, 1), result))

    def far():
        field[...] = start[...]
        rows_out[...] = rows_in[...]
        cols_out[...] = cols_in[...]
        for message in messages:
            message[nfar:, :] = jnp.zeros((8, BLK), jnp.float32)
        for d, back in zip(direct, backs):
            to_peer(d, slice(nfar, nfar + 8), back[...])
        far_tiles(pairs, count, (row0, row1), dict(zip(late, got)), rows_out, cols_out, base, *far_scratch)
        for message in messages:
            message[0:nfar, :] = cols_out[...]

    near_tiles(far, near_ref, got, field, put, *near_scratch)


def hot(index, blocks, slots, base):
    want = lax.broadcasted_iota(jnp.int32, (blocks, slots), 0) + base * blocks
    return jnp.where(index[:, 0:slots] == want.astype(jnp.float32), 1.0, 0.0)


def spread(pick, slots, weight):
    pick = jnp.concatenate(pick * 3, axis=1).astype(jnp.bfloat16)
    slots = jnp.concatenate(three(jnp.concatenate(slots, axis=0)), axis=0).astype(jnp.bfloat16)
    return jnp.dot(pick, slots, preferred_element_type=jnp.float32) * weight[...]


def cols_kernel(pairs, weight, near, own_far, own_cols, *refs, n_row, base):
    col_far, messages, field = refs[: n_row - 1], refs[n_row - 1 : -1], refs[-1]
    blocks, nfar = weight.shape[0], own_cols.shape[0]
    my_row = lax.axis_index("row")
    line = base + 4 * blocks + 1
    pick = [hot(own_far[blocks, 1:2, :], blocks, nfar, my_row)]
    for k in range(1, n_row):
        way = jnp.bitwise_xor(my_row, lax.rem(my_row + n_row - k, n_row))
        index = jnp.zeros((1, BLK), jnp.float32)
        for d, other in enumerate(col_far):
            index = jnp.where(way == d + 1, other[line : line + 1, :], index)
        pick.append(hot(index, blocks, nfar, my_row))
    field[...] = near[...] + spread(pick, [own_cols[...]] + [m[0:nfar, :] for m in messages], weight)
    for message in messages:
        for t in range(pairs.shape[1] - 1):
            k = lax.rem(pairs[0, t + 1], blocks)
            field[pl.ds(k, 1), :] += message[nfar + t : nfar + t + 1, :]


def rows_kernel(weight, field, row0, row1, *refs, n_col):
    rows, out = refs[:-1], refs[-1]
    blocks, nfar = weight.shape[0], rows[0].shape[0] // 2
    my_col = lax.axis_index("col")
    chips = n_col // 2
    chip = lax.div(my_col, 2)
    pick = []
    for k in range(chips):
        way = jnp.bitwise_xor(chip, lax.rem(chip + k, chips))
        tag = place(way, chips) * (blocks + 1) + blocks
        pick += [hot(half[tag, 0:1, :], blocks, nfar, my_col) for half in (row0, row1)]
    total = field[...] + spread(pick, [r[...] for r in rows], weight)
    for q in range(BLK // LANES):
        out[pl.ds(q, blocks, stride=BLK // LANES), :] = total[:, q * LANES : (q + 1) * LANES]


def f32(*shape):
    return jax.ShapeDtypeStruct(shape, jnp.float32)


def cost(micros):
    return pl.CostEstimate(flops=int(micros * 1.1e9), bytes_accessed=1 << 16, transcendentals=0)


def body(points, density, near_pairs, far_pairs, near_count, far_count, *, n_row, n_col):
    quad = points.shape[1]
    blocks = points.shape[2] // BLK
    nnear, nfar = near_pairs.shape[0], far_pairs.shape[0]
    depth, slots = 4 * quad, nnear - 1
    near_pairs, far_pairs = near_pairs.T, far_pairs.T

    def swap(x, axis, d):
        n = {"row": n_row, "col": n_col}[axis]
        return lax.ppermute(x, axis, [(i, i ^ d) for i in range(n)])

    direct = [d for d in range(1, n_row) if d & (d - 1) == 0]
    late = [d for d in range(1, n_row) if d & (d - 1) != 0]

    def halves(n):
        return [1 << j for j in reversed(range(n.bit_length() - 1))]

    def col_gather(x):
        for d in halves(n_col)[:-1]:
            x = jnp.concatenate([x, swap(x, "col", d)], axis=0)
        return x, swap(x, "col", 1)

    base = near_lines(slots, quad)
    msg_rows = -(-(base + 4 * (blocks + 1)) // 8) * 8
    hbm = (near_pairs, far_pairs, points, density.reshape(-1, LANES))
    hbm = [pltpu.with_memory_space_constraint(x, pltpu.HBM) for x in hbm]
    msg, far_own, near_own, weight = pl.pallas_call(
        prep_kernel,
        out_shape=(
            f32(msg_rows, BLK),
            f32(blocks + 1, 4, BLK),
            f32(blocks, depth + 8, BLK),
            f32(blocks, BLK),
        ),
        in_specs=[HBM, SMEM, HBM, HBM, HBM],
        out_specs=(VMEM, VMEM, VMEM, VMEM),
        scratch_shapes=[
            pltpu.SMEM(near_pairs.shape, jnp.int32),
            pltpu.VMEM(far_pairs.shape, jnp.int32),
            pltpu.VMEM(points.shape, jnp.float32),
            pltpu.VMEM((density.shape[0] // LANES, LANES), jnp.float32),
            pltpu.SemaphoreType.DMA((QUARTERS + 3,)),
        ],
        compiler_params=PARAMS,
        cost_estimate=cost(1.2),
        name="prep",
    )(hbm[0], near_count, *hbm[1:])
    row_far = col_gather(far_own)
    known = {d: swap(msg, "row", d) for d in direct}
    passed = [d for d in direct if d > 1]
    *onward, first = lax.optimization_barrier((*[known[d] for d in passed], row_far[0]))
    known.update(zip(passed, onward))
    row_far = (first, row_far[1])
    for d in late:
        known[d] = swap(known[d ^ (d & -d)], "row", d & -d)
    got = [known[d] for d in range(1, n_row)]

    bufs = [
        pltpu.VMEM((quad * BLK, TERMS), jnp.bfloat16),
        pltpu.VMEM((TERMS, quad * BLK), jnp.bfloat16),
        pltpu.VMEM((BLK, LANES), jnp.float32),
        pltpu.VMEM((8, BLK), jnp.float32),
    ]
    near0 = pl.pallas_call(
        near_own_kernel,
        out_shape=f32(blocks, BLK),
        in_specs=[SMEM, SMEM, VMEM],
        out_specs=VMEM,
        scratch_shapes=bufs,
        compiler_params=PARAMS,
        cost_estimate=cost(5.0),
        name="near_own",
    )(near_pairs, near_count, near_own)

    def near_scratch(n):
        return [
            pltpu.VMEM((depth + 8, BLK), jnp.float32),
            pltpu.SMEM((n, 8, LANES), jnp.float32),
            pltpu.SemaphoreType.DMA((n,)),
        ] + bufs

    far_scratch = [
        pltpu.SMEM((nfar,), jnp.int32),
        pltpu.VMEM((2, 4, BLK), jnp.float32),
        pltpu.VMEM((2, 4, BLK), jnp.float32),
        pltpu.VMEM((2, BLK, TERMS), jnp.bfloat16),
        pltpu.VMEM((2, TERMS, BLK), jnp.bfloat16),
        pltpu.VMEM((2, BLK, LANES), jnp.float32),
    ]
    field, *backs = pl.pallas_call(
        functools.partial(direct_kernel, ways=len(direct)),
        out_shape=[f32(blocks, BLK)] + [f32(8, BLK)] * len(direct),
        in_specs=[SMEM, SMEM] + [VMEM] * (2 + len(direct)),
        out_specs=[VMEM] * (len(direct) + 1),
        scratch_shapes=near_scratch(len(direct)),
        compiler_params=PARAMS,
        cost_estimate=cost(30.0),
        name="near_direct",
    )(near_pairs, near_count, near_own, near0, *[got[d - 1] for d in direct])
    far_rows, far_cols = pl.pallas_call(
        functools.partial(far_kernel, direct=direct, base=base),
        out_shape=[f32(nfar, BLK)] * 2,
        in_specs=[SMEM, SMEM] + [VMEM] * (3 + len(direct)),
        out_specs=[VMEM] * 2,
        scratch_shapes=far_scratch,
        compiler_params=PARAMS,
        cost_estimate=cost(3.0),
        name="far_direct",
    )(far_pairs, far_count, *row_far, far_own, *[got[d - 1] for d in direct])
    field, far_rows, far_cols, *messages = pl.pallas_call(
        functools.partial(late_kernel, n_row=n_row, direct=direct, late=late),
        out_shape=[f32(blocks, BLK)] + [f32(nfar, BLK)] * 2 + [f32(nfar + 8, BLK)] * (n_row - 1),
        in_specs=[SMEM, SMEM] + [VMEM] * (6 + n_row - 1),
        out_specs=[VMEM] * (n_row + 2),
        scratch_shapes=near_scratch(len(late)) + far_scratch,
        compiler_params=PARAMS,
        cost_estimate=cost(8.0),
        name="late",
    )(far_pairs, far_count, near_own, field, *row_far, far_rows, far_cols, *[got[d - 1] for d in late], *backs)

    messages = [
        lax.ppermute(x, "row", [(i, (i + k + 1) % n_row) for i in range(n_row)]) for k, x in enumerate(messages)
    ]
    both = jnp.concatenate([far_rows, swap(far_rows, "col", 1)], axis=0)
    rows = [both]
    for k in range(2, n_col, 2):
        rows.append(lax.ppermute(both, "col", [(i, (i - k) % n_col) for i in range(n_col)]))
    field = pl.pallas_call(
        functools.partial(cols_kernel, n_row=n_row, base=base),
        out_shape=f32(blocks, BLK),
        in_specs=[SMEM] + [VMEM] * (2 * n_row + 2),
        out_specs=VMEM,
        compiler_params=PARAMS,
        cost_estimate=cost(1.0),
        name="final_cols",
    )(near_pairs, weight, field, far_own, far_cols, *got, *messages)
    out = pl.pallas_call(
        functools.partial(rows_kernel, n_col=n_col),
        out_shape=f32(blocks * BLK // LANES, LANES),
        in_specs=[VMEM] * (4 + len(rows)),
        out_specs=VMEM,
        compiler_params=PARAMS,
        cost_estimate=cost(1.0),
        name="final_rows",
    )(weight, field, *row_far, *rows)
    return out.reshape(-1)


def solution(mesh):
    in_specs = (
        P(None, None, ("row", "col")),
        P(("row", "col")),
        P(("row", "col"), None),
        P(("row", "col"), None),
        P(("row", "col")),
        P(("row", "col")),
    )
    out_specs = P(("row", "col"))
    kernel = functools.partial(body, n_row=mesh.shape["row"], n_col=mesh.shape["col"])
    return jax.shard_map(kernel, mesh=mesh, in_specs=in_specs, out_specs=out_specs, check_vma=False)
```

```python
import functools

import jax
import jax.numpy as jnp
from jax import lax
from jax.experimental import pallas as pl
from jax.experimental.pallas import tpu as pltpu
from jax.sharding import PartitionSpec as P

BLK = 512
LANES = 128
SOFT_SQ = 0.0004
TERMS = 64
SPLIT = 48
HALF = 512
QUARTERS = 4
SLOTS = 5
OWN_FIRST = 2
NEAR_SCRATCH = 4 * [None]
GROUP = 16
CHUNK = 512
VMEM = pl.BlockSpec(memory_space=pltpu.VMEM)
SMEM = pl.BlockSpec(memory_space=pltpu.SMEM)
ANY = pl.BlockSpec(memory_space=pl.ANY)
HBM = pl.BlockSpec(memory_space=pltpu.HBM)
PARAMS = pltpu.CompilerParams(vmem_limit_bytes=40 * 1024 * 1024)


def prep_kernel(near_hbm, count, far_hbm, pts_hbm, dens_hbm, msg, far_out, near_out, weight_out, *scratch):
    near_ref, far_ref, pts_ref, dens_ref, sems = scratch
    blocks = near_out.shape[0]
    quad = pts_ref.shape[1]
    slots, body = near_ref.shape[1] - 1, quad * 4
    base = near_lines(slots, quad)
    width = pts_ref.shape[2] // QUARTERS
    copies = [
        pltpu.make_async_copy(dens_hbm, dens_ref, sems.at[QUARTERS]),
        pltpu.make_async_copy(far_hbm, far_ref, sems.at[QUARTERS + 1]),
        pltpu.make_async_copy(near_hbm, near_ref, sems.at[QUARTERS + 2]),
    ]
    for i in range(QUARTERS):
        part = slice(i * width, (i + 1) * width)
        copies.append(pltpu.make_async_copy(pts_hbm.at[:, :, part], pts_ref.at[:, :, part], sems.at[i]))
    for copy in copies:
        copy.start()
    copies.pop(0).wait()
    copies.pop(0).wait()
    copies.pop(0).wait()

    def put_far(k, value):
        far_out[k] = value
        msg[base + 4 * k : base + 4 * k + 4, :] = value

    for k in range(blocks):
        cols = slice(k * BLK, (k + 1) * BLK)
        if k % (blocks // QUARTERS) == 0:
            copies.pop(0).wait()
        w = pts_ref[3, :, cols]
        total = jnp.sum(w, axis=0, keepdims=True)
        dens = jnp.concatenate([dens_ref[4 * k + q : 4 * k + q + 1, :] for q in range(4)], axis=1)
        lines = []
        for c in range(3):
            x = pts_ref[c, :, cols]
            lines.append(jnp.sum(x * w, axis=0, keepdims=True) / total)
            near_out[k, quad * c : quad * c + quad, :] = x
        near_out[k, quad * 3 : quad * 4, :] = w
        near_out[k, quad * 4 : quad * 4 + 8, :] = jnp.broadcast_to(dens, (8, BLK))
        put_far(k, jnp.concatenate(lines + [total * dens], axis=0))
        weight_out[k : k + 1, :] = total
    lane = lax.broadcasted_iota(jnp.int32, (1, LANES), 1)
    lines = [jnp.full((1, LANES), -1.0, jnp.float32)] * 2
    for t in range(slots):
        k = lax.rem(near_ref[0, t + 1], blocks)
        msg[t * body : (t + 1) * body, :] = near_out[k, 0:body, :]
        source = jnp.where(t + 1 < count[0], near_ref[1, t + 1], -1)
        lines[0] = jnp.where(lane == t, k.astype(jnp.float32), lines[0])
        lines[1] = jnp.where(lane == t, source.astype(jnp.float32), lines[1])
    pairs = jnp.concatenate([far_ref[...].astype(jnp.float32), jnp.full((2, LANES - far_ref.shape[1]), -1.0)], axis=1)
    pairs = jnp.concatenate([pairs] + lines, axis=0)
    put_far(blocks, jnp.concatenate([pairs] * (BLK // LANES), axis=1))
    used = base + 4 * (blocks + 1)
    if used < msg.shape[0]:
        msg[used:, :] = jnp.zeros((msg.shape[0] - used, BLK), jnp.float32)


def near_lines(slots, quad):
    return slots * 4 * quad


def three(value):
    one = value.astype(jnp.bfloat16).astype(jnp.float32)
    two = (value - one).astype(jnp.bfloat16).astype(jnp.float32)
    return one, two, value - one - two


def pick_row(row, values):
    out = jnp.zeros(row.shape, jnp.float32)
    for k, value in enumerate(values):
        out = jnp.where(row == k, value, out)
    return out


def parts(x):
    row = lax.broadcasted_iota(jnp.int32, x.shape, 0)
    live = row < 3
    centred = jnp.where(live, x - 0.5, 0.0)
    head = jnp.round(centred * 256.0) * (1.0 / 256.0)
    rest = centred - head
    rest1 = rest.astype(jnp.bfloat16).astype(jnp.float32)
    big = pick_row(row, three(jnp.sum(head * head, axis=0, keepdims=True)))
    small = pick_row(row, three(jnp.sum(rest * (2.0 * head + rest), axis=0, keepdims=True) + 0.5 * SOFT_SQ))
    return head, rest1, rest - rest1, big, small, jnp.where(live, 1.0, 0.0)


def left_terms(x, columns):
    head, rest1, rest2, big, small, ones = parts(x)
    h2, a2, b2 = -2.0 * head, -2.0 * rest1, -2.0 * rest2
    groups = [h2, big, ones, small, ones, h2, h2, a2, b2, a2, a2, b2]
    row = lax.broadcasted_iota(jnp.int32, (TERMS - SPLIT, x.shape[1]), 0)
    groups.append(pick_row(row, [part for column in columns for part in three(column)]))
    return jnp.concatenate(groups, axis=0)


def right_terms(x):
    head, rest1, rest2, big, small, ones = parts(x)
    groups = [head, ones, big, ones, small, rest1, rest2, head, head, rest1, rest2, rest1]
    groups.append(jnp.zeros((TERMS - SPLIT, x.shape[1]), jnp.float32))
    return jnp.concatenate(groups, axis=0).astype(jnp.bfloat16)


def column_of(lhs, which):
    row = lax.broadcasted_iota(jnp.int32, (TERMS, LANES), 0) - SPLIT - 3 * which
    pick = jnp.where((row >= 0) & (row < 3), 1.0, 0.0).astype(jnp.bfloat16)
    return jnp.dot(lhs, pick, preferred_element_type=jnp.float32)


def fold_lanes(tile, row):
    part = tile[:, :LANES] * row[:, :LANES]
    for q in range(1, tile.shape[1] // LANES):
        part = part + tile[:, q * LANES : (q + 1) * LANES] * row[:, q * LANES : (q + 1) * LANES]
    return part


def twice(col):
    return jnp.concatenate([col] * (HALF // LANES), axis=1)


def place(x, n):
    bits = n.bit_length() - 1
    div, rem = (lambda a, b: a // b, lambda a, b: a % b) if isinstance(x, int) else (lax.div, lax.rem)
    return sum(rem(div(x, 1 << (bits - 1 - j)), 2) * (1 << j) for j in range(bits))


def far_tiles(pairs, count, row_in, sources, rows_out, cols_out, base, queue, left_buf, right_buf, lhs_buf, rhs_buf, part_buf):
    n_col = lax.axis_size("col")
    row_step = 2 * row_in[0].shape[0] // n_col
    blocks = row_step - 1
    my_row, my_col = lax.axis_index("row"), lax.axis_index("col")

    def ways(s):
        a, b = pairs[0, s], pairs[1, s]
        return jnp.bitwise_xor(lax.div(a, blocks), my_col), jnp.bitwise_xor(lax.div(b, blocks), my_row)

    def enqueue(s, n):
        b_way = ways(s)[1]
        here = functools.reduce(jnp.logical_or, [b_way == d for d in sources])

        @pl.when(here)
        def _():
            queue[n] = s

        return n + here.astype(jnp.int32)

    def fetch(s, j):
        a_way, b_way = ways(s)
        ka, kb = lax.rem(pairs[0, s], blocks), lax.rem(pairs[1, s], blocks)
        for d, other in sources.items():

            @pl.when(b_way == d)
            def _():
                if d == 0:
                    right_buf[j] = other[kb]
                else:
                    lines = [other[pl.ds(base + 4 * kb + c, 1), :] for c in range(4)]
                    right_buf[j] = jnp.concatenate(lines, axis=0)

        for core, half in enumerate(row_in):

            @pl.when(lax.rem(a_way, 2) == core)
            def _():
                left_buf[j] = half[place(lax.div(a_way, 2), n_col // 2) * row_step + ka]

        return jnp.where((a_way == 0) & (b_way == 0) & (ka == kb), 0.0, 1.0)

    def tiles(slots):
        many = range(len(slots))
        mirror = [fetch(s, j) for j, s in enumerate(slots)]
        for j in many:
            left = left_buf[j]
            lhs_buf[j] = jnp.transpose(left_terms(left, [left[3:4]])).astype(jnp.bfloat16)
            rhs_buf[j] = right_terms(right_buf[j])
        zcol = [column_of(lhs_buf[j], 0) for j in many]
        dist = [jnp.dot(lhs_buf[j], rhs_buf[j], preferred_element_type=jnp.float32) for j in many]
        weights = [right_buf[j, 3:4, :] for j in many]
        acc = [jnp.zeros((8, BLK), jnp.float32) for _ in many]
        for g in range(BLK // 8):
            rows = slice(g * 8, (g + 1) * 8)
            for j in many:
                tile = lax.rsqrt(dist[j][rows, :])
                part_buf[j, rows, :] = fold_lanes(tile, weights[j])
                acc[j] = acc[j] + tile * twice(zcol[j][rows, :])
        for j, s in enumerate(slots):
            rows_out[pl.ds(s, 1), :] = jnp.sum(jnp.transpose(part_buf[j]), axis=0, keepdims=True)
            cols_out[pl.ds(s, 1), :] = jnp.sum(acc[j], axis=0, keepdims=True) * mirror[j]

    def two(i, _):
        tiles([queue[2 * i], queue[2 * i + 1]])
        return 0

    total = lax.fori_loop(0, count[0], enqueue, 0)
    lax.fori_loop(0, lax.div(total, 2), two, 0)
    pl.when(lax.rem(total, 2) == 1)(lambda: tiles([queue[total - 1]]))


def points(tall):
    quad = tall.shape[0] // 4
    sides = [[tall[quad * c + u : quad * c + u + 1, :] for c in range(4)] for u in range(quad)]
    return jnp.concatenate([jnp.concatenate(side, axis=0) for side in sides], axis=1)


def near_tile(left, dens_i, right, dens_j, lhs_buf, rhs_buf, part_buf, acc_buf):
    quad = left.shape[1] // BLK
    terms = jnp.transpose(left_terms(left, [left[3:4], jnp.concatenate([dens_i] * quad, axis=1)]))
    terms = terms.astype(jnp.bfloat16)
    for g in range(BLK // GROUP):
        for u in range(quad):
            to, at = (g * quad + u) * GROUP, u * BLK + g * GROUP
            lhs_buf[to : to + GROUP, :] = terms[at : at + GROUP, :]
    rhs_buf[...] = right_terms(right)
    weights = right[3:4]
    acc_buf[...] = jnp.zeros_like(acc_buf)

    def chunk(i, _):
        at = pl.multiple_of(i * CHUNK * quad, CHUNK * quad)
        lhs = lhs_buf[pl.ds(at, CHUNK * quad), :]
        wcol = column_of(lhs, 0)
        groups = CHUNK // GROUP
        first_rows = [lhs[g * quad * GROUP : g * quad * GROUP + GROUP, :] for g in range(groups)]
        dcol = column_of(jnp.concatenate(first_rows, axis=0), 1)
        part = None
        for h in range(BLK // HALF):
            tiles = [None] * groups
            for v in range(quad):
                cols = slice(v * BLK + h * HALF, v * BLK + (h + 1) * HALF)
                dist = jnp.dot(lhs, rhs_buf[:, cols], preferred_element_type=jnp.float32)
                for g in range(groups):
                    inner = None
                    for u in range(quad):
                        rows = slice((g * quad + u) * GROUP, (g * quad + u + 1) * GROUP)
                        term = lax.rsqrt(dist[rows, :]) * twice(wcol[rows, :])
                        inner = term if inner is None else inner + term
                    inner = inner * weights[:, cols]
                    tiles[g] = inner if tiles[g] is None else tiles[g] + inner
            tile = jnp.concatenate(tiles, axis=0)
            cols = slice(h * HALF, (h + 1) * HALF)
            more = fold_lanes(tile, dens_j[:, cols])
            part = more if part is None else part + more
            acc_buf[:, cols] += jnp.sum((tile * twice(dcol)).reshape(-1, 8, HALF), axis=0)
        part_buf[pl.ds(pl.multiple_of(i * CHUNK, CHUNK), CHUNK), :] = part
        return 0

    lax.fori_loop(0, BLK // CHUNK, chunk, 0)
    rows = jnp.sum(jnp.transpose(part_buf[...]), axis=0, keepdims=True)
    return rows, jnp.sum(acc_buf[...], axis=0, keepdims=True)


def near_own_kernel(pairs, count, near_ref, field, *bufs):
    blocks, depth, _ = near_ref.shape
    body = depth - 8
    my_row = lax.axis_index("row")
    field[...] = jnp.zeros_like(field)

    def step(s, n):
        ka, kb = lax.rem(pairs[0, s], blocks), pairs[1, s] - my_row * blocks
        own = (kb >= 0) & (kb < blocks)

        @pl.when(own & (n < OWN_FIRST))
        def _():
            left, right = points(near_ref[ka, 0:body, :]), points(near_ref[kb, 0:body, :])
            dens_i, dens_j = near_ref[ka, body : body + 1, :], near_ref[kb, body : body + 1, :]
            rows, cols = near_tile(left, dens_i, right, dens_j, *bufs)
            field[pl.ds(ka, 1), :] += rows
            field[pl.ds(kb, 1), :] += cols * jnp.where(ka == kb, 0.0, 1.0)

        return n + own.astype(jnp.int32)

    lax.fori_loop(0, count[0], step, jnp.int32(0))


def near_tiles(meanwhile, near_ref, got, field, put, right_buf, tags, sems, *bufs, own=None):
    blocks, depth, _ = near_ref.shape
    body = depth - 8
    base = near_lines(SLOTS, body // 4)
    my_row = lax.axis_index("row")
    tail = slice(base + 4 * blocks, base + 4 * blocks + 8)
    copies = [pltpu.make_async_copy(g.at[tail, 0:LANES], tags.at[d], sems.at[d]) for d, g in enumerate([*got] if own is None else [*got, own])]
    for copy in copies:
        copy.start()
    meanwhile()
    for copy in copies:
        copy.wait()

    def step(i, seen):
        way, t = lax.div(i, SLOTS), lax.rem(i, SLOTS)
        kb = tags[way, 3, t].astype(jnp.int32) - my_row * blocks
        if own is not None:
            is_own = (way == len(got)) & (kb >= 0) & (kb < blocks)
            kb = jnp.where(is_own & (seen < OWN_FIRST), -1, kb)
            seen = seen + jnp.where(is_own, 1, 0)

        @pl.when((kb >= 0) & (kb < blocks))
        def _():
            if own is not None:

                @pl.when(way == len(got))
                def _():
                    right_buf[...] = near_ref[tags[way, 2, t].astype(jnp.int32)]

            for d, other in enumerate(got):

                @pl.when(way == d)
                def _():
                    at = pl.multiple_of(t * body, 8)
                    points_j = other[pl.ds(at, body), :]
                    line = base + 4 * tags[way, 2, t].astype(jnp.int32) + 3
                    total = jnp.sum(points_j[body - body // 4 :], axis=0, keepdims=True)
                    right_buf[0:body, :] = points_j
                    right_buf[body : body + 1, :] = other[pl.ds(line, 1), :] / total

            left, right = points(near_ref[kb, 0:body, :]), points(right_buf[0:body, :])
            dens_i, dens_j = near_ref[kb, body : body + 1, :], right_buf[body : body + 1, :]
            rows, cols = near_tile(left, dens_i, right, dens_j, *bufs)
            field[pl.ds(kb, 1), :] += rows
            put(way, t, cols)
            if own is not None:

                @pl.when(way == len(got))
                def _():
                    ka = tags[way, 2, t].astype(jnp.int32)
                    field[pl.ds(ka, 1), :] += cols * jnp.where(ka == kb, 0.0, 1.0)

        return seen

    lax.fori_loop(0, (len(got) + (own is not None)) * SLOTS, step, jnp.int32(1))


def direct_kernel(msg, near_ref, start, *refs, ways):
    got, (field, *backs), scratch = refs[:ways], refs[ways : 2 * ways + 1], refs[2 * ways + 1 :]

    def clear():
        field[...] = start[...]
        for back in backs:
            back[...] = jnp.zeros_like(back)

    def put(way, t, result):
        for i, back in enumerate(backs):

            @pl.when(way == i)
            def _():
                back[pl.ds(t, 1), :] = result

    near_tiles(clear, near_ref, got, field, put, *scratch, own=msg)


def far_kernel(pairs, count, row0, row1, own_in, *refs, direct, base):
    got, (rows_out, cols_out), scratch = refs[: len(direct)], refs[len(direct) : -6], refs[-6:]
    rows_out[...] = jnp.zeros_like(rows_out)
    cols_out[...] = jnp.zeros_like(cols_out)
    sources = {0: own_in, **dict(zip(direct, got))}
    far_tiles(pairs, count, (row0, row1), sources, rows_out, cols_out, base, *scratch)


def late_kernel(pairs, count, near_ref, start, row0, row1, rows_in, cols_in, *refs, n_row, direct, late):
    refs = list(refs)
    take = lambda n: [refs.pop(0) for _ in range(n)]
    got, backs = take(len(late)), take(len(direct))
    field, rows_out, cols_out, *messages = take(n_row + 2)
    near_scratch, far_scratch = take(len(NEAR_SCRATCH) + 3), refs
    nfar = cols_out.shape[0]
    base = near_lines(SLOTS, near_ref.shape[1] // 4 - 2)
    my_row = lax.axis_index("row")

    def to_peer(d, lines, value):
        k = lax.rem(jnp.bitwise_xor(my_row, d) - my_row + n_row - 1, n_row)
        for i, message in enumerate(messages):

            @pl.when(k == i)
            def _():
                message[lines, :] = value

    def put(way, t, result):
        for i, d in enumerate(late):
            pl.when(way == i)(lambda: to_peer(d, pl.ds(nfar + t, 1), result))

    def far():
        field[...] = start[...]
        rows_out[...] = rows_in[...]
        cols_out[...] = cols_in[...]
        for message in messages:
            message[nfar:, :] = jnp.zeros((8, BLK), jnp.float32)
        for d, back in zip(direct, backs):
            to_peer(d, slice(nfar, nfar + 8), back[...])
        far_tiles(pairs, count, (row0, row1), dict(zip(late, got)), rows_out, cols_out, base, *far_scratch)
        for message in messages:
            message[0:nfar, :] = cols_out[...]

    near_tiles(far, near_ref, got, field, put, *near_scratch)


def hot(index, blocks, slots, base):
    want = lax.broadcasted_iota(jnp.int32, (blocks, slots), 0) + base * blocks
    return jnp.where(index[:, 0:slots] == want.astype(jnp.float32), 1.0, 0.0)


def spread(pick, slots, weight):
    pick = jnp.concatenate(pick * 3, axis=1).astype(jnp.bfloat16)
    slots = jnp.concatenate(three(jnp.concatenate(slots, axis=0)), axis=0).astype(jnp.bfloat16)
    return jnp.dot(pick, slots, preferred_element_type=jnp.float32) * weight[...]


def cols_kernel(pairs, weight, near, own_far, own_cols, *refs, n_row, base):
    col_far, messages, field = refs[: n_row - 1], refs[n_row - 1 : -1], refs[-1]
    blocks, nfar = weight.shape[0], own_cols.shape[0]
    my_row = lax.axis_index("row")
    line = base + 4 * blocks + 1
    pick = [hot(own_far[blocks, 1:2, :], blocks, nfar, my_row)]
    for k in range(1, n_row):
        way = jnp.bitwise_xor(my_row, lax.rem(my_row + n_row - k, n_row))
        index = jnp.zeros((1, BLK), jnp.float32)
        for d, other in enumerate(col_far):
            index = jnp.where(way == d + 1, other[line : line + 1, :], index)
        pick.append(hot(index, blocks, nfar, my_row))
    field[...] = near[...] + spread(pick, [own_cols[...]] + [m[0:nfar, :] for m in messages], weight)
    for message in messages:
        for t in range(pairs.shape[1] - 1):
            k = lax.rem(pairs[0, t + 1], blocks)
            field[pl.ds(k, 1), :] += message[nfar + t : nfar + t + 1, :]


def rows_kernel(weight, field, row0, row1, *refs, n_col):
    rows, out = refs[:-1], refs[-1]
    blocks, nfar = weight.shape[0], rows[0].shape[0] // 2
    my_col = lax.axis_index("col")
    chips = n_col // 2
    chip = lax.div(my_col, 2)
    pick = []
    for k in range(chips):
        way = jnp.bitwise_xor(chip, lax.rem(chip + k, chips))
        tag = place(way, chips) * (blocks + 1) + blocks
        pick += [hot(half[tag, 0:1, :], blocks, nfar, my_col) for half in (row0, row1)]
    total = field[...] + spread(pick, [r[...] for r in rows], weight)
    for q in range(BLK // LANES):
        out[pl.ds(q, blocks, stride=BLK // LANES), :] = total[:, q * LANES : (q + 1) * LANES]


def f32(*shape):
    return jax.ShapeDtypeStruct(shape, jnp.float32)


def cost(micros):
    return pl.CostEstimate(flops=int(micros * 1.1e9), bytes_accessed=1 << 16, transcendentals=0)


def body(points, density, near_pairs, far_pairs, near_count, far_count, *, n_row, n_col):
    quad = points.shape[1]
    blocks = points.shape[2] // BLK
    nnear, nfar = near_pairs.shape[0], far_pairs.shape[0]
    depth, slots = 4 * quad, nnear - 1
    near_pairs, far_pairs = near_pairs.T, far_pairs.T

    def swap(x, axis, d):
        n = {"row": n_row, "col": n_col}[axis]
        return lax.ppermute(x, axis, [(i, i ^ d) for i in range(n)])

    direct = [d for d in range(1, n_row) if d & (d - 1) == 0]
    late = [d for d in range(1, n_row) if d & (d - 1) != 0]

    def halves(n):
        return [1 << j for j in reversed(range(n.bit_length() - 1))]

    def col_gather(x):
        for d in halves(n_col)[:-1]:
            x = jnp.concatenate([x, swap(x, "col", d)], axis=0)
        return x, swap(x, "col", 1)

    base = near_lines(slots, quad)
    msg_rows = -(-(base + 4 * (blocks + 1)) // 8) * 8
    hbm = (near_pairs, far_pairs, points, density.reshape(-1, LANES))
    hbm = [pltpu.with_memory_space_constraint(x, pltpu.HBM) for x in hbm]
    msg, far_own, near_own, weight = pl.pallas_call(
        prep_kernel,
        out_shape=(
            f32(msg_rows, BLK),
            f32(blocks + 1, 4, BLK),
            f32(blocks, depth + 8, BLK),
            f32(blocks, BLK),
        ),
        in_specs=[HBM, SMEM, HBM, HBM, HBM],
        out_specs=(VMEM, VMEM, VMEM, VMEM),
        scratch_shapes=[
            pltpu.SMEM(near_pairs.shape, jnp.int32),
            pltpu.VMEM(far_pairs.shape, jnp.int32),
            pltpu.VMEM(points.shape, jnp.float32),
            pltpu.VMEM((density.shape[0] // LANES, LANES), jnp.float32),
            pltpu.SemaphoreType.DMA((QUARTERS + 3,)),
        ],
        compiler_params=PARAMS,
        cost_estimate=cost(1.2),
        name="prep",
    )(hbm[0], near_count, *hbm[1:])
    row_far = col_gather(far_own)
    known = {d: swap(msg, "row", d) for d in direct}
    passed = [d for d in direct if d > 1]
    *onward, first = lax.optimization_barrier((*[known[d] for d in passed], row_far[0]))
    known.update(zip(passed, onward))
    row_far = (first, row_far[1])
    for d in late:
        known[d] = swap(known[d ^ (d & -d)], "row", d & -d)
    got = [known[d] for d in range(1, n_row)]

    bufs = [
        pltpu.VMEM((quad * BLK, TERMS), jnp.bfloat16),
        pltpu.VMEM((TERMS, quad * BLK), jnp.bfloat16),
        pltpu.VMEM((BLK, LANES), jnp.float32),
        pltpu.VMEM((8, BLK), jnp.float32),
    ]
    near0 = pl.pallas_call(
        near_own_kernel,
        out_shape=f32(blocks, BLK),
        in_specs=[SMEM, SMEM, VMEM],
        out_specs=VMEM,
        scratch_shapes=bufs,
        compiler_params=PARAMS,
        cost_estimate=cost(5.0),
        name="near_own",
    )(near_pairs, near_count, near_own)

    def near_scratch(n):
        return [
            pltpu.VMEM((depth + 8, BLK), jnp.float32),
            pltpu.SMEM((n, 8, LANES), jnp.float32),
            pltpu.SemaphoreType.DMA((n,)),
        ] + bufs

    far_scratch = [
        pltpu.SMEM((nfar,), jnp.int32),
        pltpu.VMEM((2, 4, BLK), jnp.float32),
        pltpu.VMEM((2, 4, BLK), jnp.float32),
        pltpu.VMEM((2, BLK, TERMS), jnp.bfloat16),
        pltpu.VMEM((2, TERMS, BLK), jnp.bfloat16),
        pltpu.VMEM((2, BLK, LANES), jnp.float32),
    ]
    field, *backs = pl.pallas_call(
        functools.partial(direct_kernel, ways=len(direct)),
        out_shape=[f32(blocks, BLK)] + [f32(8, BLK)] * len(direct),
        in_specs=[VMEM] * (3 + len(direct)),
        out_specs=[VMEM] * (len(direct) + 1),
        scratch_shapes=near_scratch(len(direct) + 1),
        compiler_params=PARAMS,
        cost_estimate=cost(30.0),
        name="near_direct",
    )(msg, near_own, near0, *[got[d - 1] for d in direct])
    far_rows, far_cols = pl.pallas_call(
        functools.partial(far_kernel, direct=direct, base=base),
        out_shape=[f32(nfar, BLK)] * 2,
        in_specs=[SMEM, SMEM] + [VMEM] * (3 + len(direct)),
        out_specs=[VMEM] * 2,
        scratch_shapes=far_scratch,
        compiler_params=PARAMS,
        cost_estimate=cost(3.0),
        name="far_direct",
    )(far_pairs, far_count, *row_far, far_own, *[got[d - 1] for d in direct])
    field, far_rows, far_cols, *messages = pl.pallas_call(
        functools.partial(late_kernel, n_row=n_row, direct=direct, late=late),
        out_shape=[f32(blocks, BLK)] + [f32(nfar, BLK)] * 2 + [f32(nfar + 8, BLK)] * (n_row - 1),
        in_specs=[SMEM, SMEM] + [VMEM] * (6 + n_row - 1),
        out_specs=[VMEM] * (n_row + 2),
        scratch_shapes=near_scratch(len(late)) + far_scratch,
        compiler_params=PARAMS,
        cost_estimate=cost(8.0),
        name="late",
    )(far_pairs, far_count, near_own, field, *row_far, far_rows, far_cols, *[got[d - 1] for d in late], *backs)

    messages = [
        lax.ppermute(x, "row", [(i, (i + k + 1) % n_row) for i in range(n_row)]) for k, x in enumerate(messages)
    ]
    both = jnp.concatenate([far_rows, swap(far_rows, "col", 1)], axis=0)
    rows = [both]
    for k in range(2, n_col, 2):
        rows.append(lax.ppermute(both, "col", [(i, (i - k) % n_col) for i in range(n_col)]))
    field = pl.pallas_call(
        functools.partial(cols_kernel, n_row=n_row, base=base),
        out_shape=f32(blocks, BLK),
        in_specs=[SMEM] + [VMEM] * (2 * n_row + 2),
        out_specs=VMEM,
        compiler_params=PARAMS,
        cost_estimate=cost(1.0),
        name="final_cols",
    )(near_pairs, weight, field, far_own, far_cols, *got, *messages)
    out = pl.pallas_call(
        functools.partial(rows_kernel, n_col=n_col),
        out_shape=f32(blocks * BLK // LANES, LANES),
        in_specs=[VMEM] * (4 + len(rows)),
        out_specs=VMEM,
        compiler_params=PARAMS,
        cost_estimate=cost(1.0),
        name="final_rows",
    )(weight, field, *row_far, *rows)
    return out.reshape(-1)


def solution(mesh):
    in_specs = (
        P(None, None, ("row", "col")),
        P(("row", "col")),
        P(("row", "col"), None),
        P(("row", "col"), None),
        P(("row", "col")),
        P(("row", "col")),
    )
    out_specs = P(("row", "col"))
    kernel = functools.partial(body, n_row=mesh.shape["row"], n_col=mesh.shape["col"])
    return jax.shard_map(kernel, mesh=mesh, in_specs=in_specs, out_specs=out_specs, check_vma=False)
```

```python
import functools

import jax
import jax.numpy as jnp
from jax import lax
from jax.experimental import pallas as pl
from jax.experimental.pallas import tpu as pltpu
from jax.sharding import PartitionSpec as P

BLK = 512
LANES = 128
SOFT_SQ = 0.0004
TERMS = 64
SPLIT = 48
HALF = 512
QUARTERS = 4
SLOTS = 5
OWN_FIRST = 2
NEAR_SCRATCH = 4 * [None]
GROUP = 16
CHUNK = 512
VMEM = pl.BlockSpec(memory_space=pltpu.VMEM)
SMEM = pl.BlockSpec(memory_space=pltpu.SMEM)
ANY = pl.BlockSpec(memory_space=pl.ANY)
HBM = pl.BlockSpec(memory_space=pltpu.HBM)
PARAMS = pltpu.CompilerParams(vmem_limit_bytes=40 * 1024 * 1024)


def prep_kernel(near_hbm, count, far_hbm, pts_hbm, dens_hbm, msg, far_out, near_out, weight_out, *scratch):
    near_ref, far_ref, pts_ref, dens_ref, sems = scratch
    blocks = near_out.shape[0]
    quad = pts_ref.shape[1]
    slots, body = near_ref.shape[1] - 1, quad * 4
    base = near_lines(slots, quad)
    width = pts_ref.shape[2] // QUARTERS
    copies = [
        pltpu.make_async_copy(dens_hbm, dens_ref, sems.at[QUARTERS]),
        pltpu.make_async_copy(far_hbm, far_ref, sems.at[QUARTERS + 1]),
        pltpu.make_async_copy(near_hbm, near_ref, sems.at[QUARTERS + 2]),
    ]
    for i in range(QUARTERS):
        part = slice(i * width, (i + 1) * width)
        copies.append(pltpu.make_async_copy(pts_hbm.at[:, :, part], pts_ref.at[:, :, part], sems.at[i]))
    for copy in copies:
        copy.start()
    copies.pop(0).wait()
    copies.pop(0).wait()
    copies.pop(0).wait()

    def put_far(k, value):
        far_out[k] = value
        msg[base + 4 * k : base + 4 * k + 4, :] = value

    for k in range(blocks):
        cols = slice(k * BLK, (k + 1) * BLK)
        if k % (blocks // QUARTERS) == 0:
            copies.pop(0).wait()
        w = pts_ref[3, :, cols]
        total = jnp.sum(w, axis=0, keepdims=True)
        dens = jnp.concatenate([dens_ref[4 * k + q : 4 * k + q + 1, :] for q in range(4)], axis=1)
        lines = []
        for c in range(3):
            x = pts_ref[c, :, cols]
            lines.append(jnp.sum(x * w, axis=0, keepdims=True) / total)
            near_out[k, quad * c : quad * c + quad, :] = x
        near_out[k, quad * 3 : quad * 4, :] = w
        near_out[k, quad * 4 : quad * 4 + 8, :] = jnp.broadcast_to(dens, (8, BLK))
        put_far(k, jnp.concatenate(lines + [total * dens], axis=0))
        weight_out[k : k + 1, :] = total
    lane = lax.broadcasted_iota(jnp.int32, (1, LANES), 1)
    lines = [jnp.full((1, LANES), -1.0, jnp.float32)] * 2
    for t in range(slots):
        k = lax.rem(near_ref[0, t + 1], blocks)
        msg[t * body : (t + 1) * body, :] = near_out[k, 0:body, :]
        source = jnp.where(t + 1 < count[0], near_ref[1, t + 1], -1)
        lines[0] = jnp.where(lane == t, k.astype(jnp.float32), lines[0])
        lines[1] = jnp.where(lane == t, source.astype(jnp.float32), lines[1])
    pairs = jnp.concatenate([far_ref[...].astype(jnp.float32), jnp.full((2, LANES - far_ref.shape[1]), -1.0)], axis=1)
    pairs = jnp.concatenate([pairs] + lines, axis=0)
    put_far(blocks, jnp.concatenate([pairs] * (BLK // LANES), axis=1))
    used = base + 4 * (blocks + 1)
    if used < msg.shape[0]:
        msg[used:, :] = jnp.zeros((msg.shape[0] - used, BLK), jnp.float32)


def near_lines(slots, quad):
    return slots * 4 * quad


def three(value):
    one = value.astype(jnp.bfloat16).astype(jnp.float32)
    two = (value - one).astype(jnp.bfloat16).astype(jnp.float32)
    return one, two, value - one - two


def pick_row(row, values):
    out = jnp.zeros(row.shape, jnp.float32)
    for k, value in enumerate(values):
        out = jnp.where(row == k, value, out)
    return out


def parts(x):
    row = lax.broadcasted_iota(jnp.int32, x.shape, 0)
    live = row < 3
    centred = jnp.where(live, x - 0.5, 0.0)
    head = jnp.round(centred * 256.0) * (1.0 / 256.0)
    rest = centred - head
    rest1 = rest.astype(jnp.bfloat16).astype(jnp.float32)
    big = pick_row(row, three(jnp.sum(head * head, axis=0, keepdims=True)))
    small = pick_row(row, three(jnp.sum(rest * (2.0 * head + rest), axis=0, keepdims=True) + 0.5 * SOFT_SQ))
    return head, rest1, rest - rest1, big, small, jnp.where(live, 1.0, 0.0)


def left_terms(x, columns):
    head, rest1, rest2, big, small, ones = parts(x)
    h2, a2, b2 = -2.0 * head, -2.0 * rest1, -2.0 * rest2
    groups = [h2, big, ones, small, ones, h2, h2, a2, b2, a2, a2, b2]
    row = lax.broadcasted_iota(jnp.int32, (TERMS - SPLIT, x.shape[1]), 0)
    groups.append(pick_row(row, [part for column in columns for part in three(column)]))
    return jnp.concatenate(groups, axis=0)


def right_terms(x):
    head, rest1, rest2, big, small, ones = parts(x)
    groups = [head, ones, big, ones, small, rest1, rest2, head, head, rest1, rest2, rest1]
    groups.append(jnp.zeros((TERMS - SPLIT, x.shape[1]), jnp.float32))
    return jnp.concatenate(groups, axis=0).astype(jnp.bfloat16)


def column_of(lhs, which):
    row = lax.broadcasted_iota(jnp.int32, (TERMS, LANES), 0) - SPLIT - 3 * which
    pick = jnp.where((row >= 0) & (row < 3), 1.0, 0.0).astype(jnp.bfloat16)
    return jnp.dot(lhs, pick, preferred_element_type=jnp.float32)


def fold_lanes(tile, row):
    part = tile[:, :LANES] * row[:, :LANES]
    for q in range(1, tile.shape[1] // LANES):
        part = part + tile[:, q * LANES : (q + 1) * LANES] * row[:, q * LANES : (q + 1) * LANES]
    return part


def twice(col):
    return jnp.concatenate([col] * (HALF // LANES), axis=1)


def place(x, n):
    bits = n.bit_length() - 1
    div, rem = (lambda a, b: a // b, lambda a, b: a % b) if isinstance(x, int) else (lax.div, lax.rem)
    return sum(rem(div(x, 1 << (bits - 1 - j)), 2) * (1 << j) for j in range(bits))


def far_tiles(pairs, count, row_in, sources, rows_out, cols_out, base, queue, left_buf, right_buf, lhs_buf, rhs_buf, part_buf):
    n_col = lax.axis_size("col")
    row_step = 2 * row_in[0].shape[0] // n_col
    blocks = row_step - 1
    my_row, my_col = lax.axis_index("row"), lax.axis_index("col")

    def ways(s):
        a, b = pairs[0, s], pairs[1, s]
        return jnp.bitwise_xor(lax.div(a, blocks), my_col), jnp.bitwise_xor(lax.div(b, blocks), my_row)

    def enqueue(s, n):
        b_way = ways(s)[1]
        here = functools.reduce(jnp.logical_or, [b_way == d for d in sources])

        @pl.when(here)
        def _():
            queue[n] = s

        return n + here.astype(jnp.int32)

    def fetch(s, j):
        a_way, b_way = ways(s)
        ka, kb = lax.rem(pairs[0, s], blocks), lax.rem(pairs[1, s], blocks)
        for d, other in sources.items():

            @pl.when(b_way == d)
            def _():
                if d == 0:
                    right_buf[j] = other[kb]
                else:
                    lines = [other[pl.ds(base + 4 * kb + c, 1), :] for c in range(4)]
                    right_buf[j] = jnp.concatenate(lines, axis=0)

        for core, half in enumerate(row_in):

            @pl.when(lax.rem(a_way, 2) == core)
            def _():
                left_buf[j] = half[place(lax.div(a_way, 2), n_col // 2) * row_step + ka]

        return jnp.where((a_way == 0) & (b_way == 0) & (ka == kb), 0.0, 1.0)

    def tiles(slots):
        many = range(len(slots))
        mirror = [fetch(s, j) for j, s in enumerate(slots)]
        for j in many:
            left = left_buf[j]
            lhs_buf[j] = jnp.transpose(left_terms(left, [left[3:4]])).astype(jnp.bfloat16)
            rhs_buf[j] = right_terms(right_buf[j])
        zcol = [column_of(lhs_buf[j], 0) for j in many]
        dist = [jnp.dot(lhs_buf[j], rhs_buf[j], preferred_element_type=jnp.float32) for j in many]
        weights = [right_buf[j, 3:4, :] for j in many]
        acc = [jnp.zeros((8, BLK), jnp.float32) for _ in many]
        for g in range(BLK // 8):
            rows = slice(g * 8, (g + 1) * 8)
            for j in many:
                tile = lax.rsqrt(dist[j][rows, :])
                part_buf[j, rows, :] = fold_lanes(tile, weights[j])
                acc[j] = acc[j] + tile * twice(zcol[j][rows, :])
        for j, s in enumerate(slots):
            rows_out[pl.ds(s, 1), :] = jnp.sum(jnp.transpose(part_buf[j]), axis=0, keepdims=True)
            cols_out[pl.ds(s, 1), :] = jnp.sum(acc[j], axis=0, keepdims=True) * mirror[j]

    def two(i, _):
        tiles([queue[2 * i], queue[2 * i + 1]])
        return 0

    total = lax.fori_loop(0, count[0], enqueue, 0)
    lax.fori_loop(0, lax.div(total, 2), two, 0)
    pl.when(lax.rem(total, 2) == 1)(lambda: tiles([queue[total - 1]]))


def points(tall):
    quad = tall.shape[0] // 4
    sides = [[tall[quad * c + u : quad * c + u + 1, :] for c in range(4)] for u in range(quad)]
    return jnp.concatenate([jnp.concatenate(side, axis=0) for side in sides], axis=1)


def near_tile(left, dens_i, right, dens_j, lhs_buf, rhs_buf, part_buf, acc_buf):
    quad = left.shape[1] // BLK
    terms = jnp.transpose(left_terms(left, [left[3:4], jnp.concatenate([dens_i] * quad, axis=1)]))
    terms = terms.astype(jnp.bfloat16)
    for g in range(BLK // GROUP):
        for u in range(quad):
            to, at = (g * quad + u) * GROUP, u * BLK + g * GROUP
            lhs_buf[to : to + GROUP, :] = terms[at : at + GROUP, :]
    rhs_buf[...] = right_terms(right)
    weights = right[3:4]
    acc_buf[...] = jnp.zeros_like(acc_buf)

    def chunk(i, _):
        at = pl.multiple_of(i * CHUNK * quad, CHUNK * quad)
        lhs = lhs_buf[pl.ds(at, CHUNK * quad), :]
        wcol = column_of(lhs, 0)
        groups = CHUNK // GROUP
        first_rows = [lhs[g * quad * GROUP : g * quad * GROUP + GROUP, :] for g in range(groups)]
        dcol = column_of(jnp.concatenate(first_rows, axis=0), 1)
        part = None
        for h in range(BLK // HALF):
            tiles = [None] * groups
            for v in range(quad):
                cols = slice(v * BLK + h * HALF, v * BLK + (h + 1) * HALF)
                dist = jnp.dot(lhs, rhs_buf[:, cols], preferred_element_type=jnp.float32)
                for g in range(groups):
                    inner = None
                    for u in range(quad):
                        rows = slice((g * quad + u) * GROUP, (g * quad + u + 1) * GROUP)
                        term = lax.rsqrt(dist[rows, :]) * twice(wcol[rows, :])
                        inner = term if inner is None else inner + term
                    inner = inner * weights[:, cols]
                    tiles[g] = inner if tiles[g] is None else tiles[g] + inner
            tile = jnp.concatenate(tiles, axis=0)
            cols = slice(h * HALF, (h + 1) * HALF)
            more = fold_lanes(tile, dens_j[:, cols])
            part = more if part is None else part + more
            acc_buf[:, cols] += jnp.sum((tile * twice(dcol)).reshape(-1, 8, HALF), axis=0)
        part_buf[pl.ds(pl.multiple_of(i * CHUNK, CHUNK), CHUNK), :] = part
        return 0

    lax.fori_loop(0, BLK // CHUNK, chunk, 0)
    rows = jnp.sum(jnp.transpose(part_buf[...]), axis=0, keepdims=True)
    return rows, jnp.sum(acc_buf[...], axis=0, keepdims=True)


def near_own_kernel(pairs, count, near_ref, field, *bufs):
    blocks, depth, _ = near_ref.shape
    body = depth - 8
    my_row = lax.axis_index("row")
    field[...] = jnp.zeros_like(field)

    def step(s, n):
        ka, kb = lax.rem(pairs[0, s], blocks), pairs[1, s] - my_row * blocks
        own = (kb >= 0) & (kb < blocks)

        @pl.when(own & (n < OWN_FIRST))
        def _():
            left, right = points(near_ref[ka, 0:body, :]), points(near_ref[kb, 0:body, :])
            dens_i, dens_j = near_ref[ka, body : body + 1, :], near_ref[kb, body : body + 1, :]
            rows, cols = near_tile(left, dens_i, right, dens_j, *bufs)
            field[pl.ds(ka, 1), :] += rows
            field[pl.ds(kb, 1), :] += cols * jnp.where(ka == kb, 0.0, 1.0)

        return n + own.astype(jnp.int32)

    lax.fori_loop(0, count[0], step, jnp.int32(0))


def near_tiles(meanwhile, near_ref, got, field, put, right_buf, tags, sems, *bufs, own=None):
    blocks, depth, _ = near_ref.shape
    body = depth - 8
    base = near_lines(SLOTS, body // 4)
    my_row = lax.axis_index("row")
    tail = slice(base + 4 * blocks, base + 4 * blocks + 8)
    copies = [pltpu.make_async_copy(g.at[tail, 0:LANES], tags.at[d], sems.at[d]) for d, g in enumerate([*got] if own is None else [*got, own])]
    for copy in copies:
        copy.start()
    meanwhile()
    for copy in copies:
        copy.wait()

    def step(i, seen):
        way, t = lax.div(i, SLOTS), lax.rem(i, SLOTS)
        kb = tags[way, 3, t].astype(jnp.int32) - my_row * blocks
        if own is not None:
            is_own = (way == len(got)) & (kb >= 0) & (kb < blocks)
            kb = jnp.where(is_own & (seen < OWN_FIRST), -1, kb)
            seen = seen + jnp.where(is_own, 1, 0)

        @pl.when((kb >= 0) & (kb < blocks))
        def _():
            if own is not None:

                @pl.when(way == len(got))
                def _():
                    right_buf[...] = near_ref[tags[way, 2, t].astype(jnp.int32)]

            for d, other in enumerate(got):

                @pl.when(way == d)
                def _():
                    at = pl.multiple_of(t * body, 8)
                    points_j = other[pl.ds(at, body), :]
                    line = base + 4 * tags[way, 2, t].astype(jnp.int32) + 3
                    total = jnp.sum(points_j[body - body // 4 :], axis=0, keepdims=True)
                    right_buf[0:body, :] = points_j
                    right_buf[body : body + 1, :] = other[pl.ds(line, 1), :] / total

            left, right = points(near_ref[kb, 0:body, :]), points(right_buf[0:body, :])
            dens_i, dens_j = near_ref[kb, body : body + 1, :], right_buf[body : body + 1, :]
            rows, cols = near_tile(left, dens_i, right, dens_j, *bufs)
            field[pl.ds(kb, 1), :] += rows
            put(way, t, cols)
            if own is not None:

                @pl.when(way == len(got))
                def _():
                    ka = tags[way, 2, t].astype(jnp.int32)
                    field[pl.ds(ka, 1), :] += cols * jnp.where(ka == kb, 0.0, 1.0)

        return seen

    lax.fori_loop(0, (len(got) + (own is not None)) * SLOTS, step, jnp.int32(1))


def direct_kernel(msg, near_ref, start, *refs, ways):
    got, (field, *backs), scratch = refs[:ways], refs[ways : 2 * ways + 1], refs[2 * ways + 1 :]

    def clear():
        field[...] = start[...]
        for back in backs:
            back[...] = jnp.zeros_like(back)

    def put(way, t, result):
        for i, back in enumerate(backs):

            @pl.when(way == i)
            def _():
                back[pl.ds(t, 1), :] = result

    near_tiles(clear, near_ref, got, field, put, *scratch, own=msg)


def far_kernel(pairs, count, row0, row1, own_in, *refs, direct, base):
    got, (rows_out, cols_out), scratch = refs[: len(direct)], refs[len(direct) : -6], refs[-6:]
    rows_out[...] = jnp.zeros_like(rows_out)
    cols_out[...] = jnp.zeros_like(cols_out)
    sources = {0: own_in, **dict(zip(direct, got))}
    far_tiles(pairs, count, (row0, row1), sources, rows_out, cols_out, base, *scratch)


def late_kernel(pairs, count, near_ref, start, row0, row1, rows_in, cols_in, *refs, n_row, direct, late):
    refs = list(refs)
    take = lambda n: [refs.pop(0) for _ in range(n)]
    got, backs = take(len(late)), take(len(direct))
    field, rows_out, cols_out, *messages = take(n_row + 2)
    near_scratch, far_scratch = take(len(NEAR_SCRATCH) + 3), refs
    nfar = cols_out.shape[0]
    base = near_lines(SLOTS, near_ref.shape[1] // 4 - 2)
    my_row = lax.axis_index("row")

    def to_peer(d, lines, value):
        k = lax.rem(jnp.bitwise_xor(my_row, d) - my_row + n_row - 1, n_row)
        for i, message in enumerate(messages):

            @pl.when(k == i)
            def _():
                message[lines, :] = value

    def put(way, t, result):
        for i, d in enumerate(late):
            pl.when(way == i)(lambda: to_peer(d, pl.ds(nfar + t, 1), result))

    def far():
        field[...] = start[...]
        rows_out[...] = rows_in[...]
        cols_out[...] = cols_in[...]
        for message in messages:
            message[nfar:, :] = jnp.zeros((8, BLK), jnp.float32)
        for d, back in zip(direct, backs):
            to_peer(d, slice(nfar, nfar + 8), back[...])
        far_tiles(pairs, count, (row0, row1), dict(zip(late, got)), rows_out, cols_out, base, *far_scratch)
        for message in messages:
            message[0:nfar, :] = cols_out[...]

    near_tiles(far, near_ref, got, field, put, *near_scratch)


def hot(index, blocks, slots, base):
    want = lax.broadcasted_iota(jnp.int32, (blocks, slots), 0) + base * blocks
    return jnp.where(index[:, 0:slots] == want.astype(jnp.float32), 1.0, 0.0)


def spread(pick, slots, weight):
    pick = jnp.concatenate(pick * 3, axis=1).astype(jnp.bfloat16)
    slots = jnp.concatenate(three(jnp.concatenate(slots, axis=0)), axis=0).astype(jnp.bfloat16)
    return jnp.dot(pick, slots, preferred_element_type=jnp.float32) * weight[...]


def cols_kernel(pairs, weight, near, own_far, own_cols, *refs, n_row, base):
    col_far, messages, field = refs[: n_row - 1], refs[n_row - 1 : -1], refs[-1]
    blocks, nfar = weight.shape[0], own_cols.shape[0]
    my_row = lax.axis_index("row")
    line = base + 4 * blocks + 1
    pick = [hot(own_far[blocks, 1:2, :], blocks, nfar, my_row)]
    for k in range(1, n_row):
        way = jnp.bitwise_xor(my_row, lax.rem(my_row + n_row - k, n_row))
        index = jnp.zeros((1, BLK), jnp.float32)
        for d, other in enumerate(col_far):
            index = jnp.where(way == d + 1, other[line : line + 1, :], index)
        pick.append(hot(index, blocks, nfar, my_row))
    field[...] = near[...] + spread(pick, [own_cols[...]] + [m[0:nfar, :] for m in messages], weight)
    for message in messages:
        for t in range(pairs.shape[1] - 1):
            k = lax.rem(pairs[0, t + 1], blocks)
            field[pl.ds(k, 1), :] += message[nfar + t : nfar + t + 1, :]


def rows_kernel(weight, field, row0, row1, *refs, n_col):
    rows, out = refs[:-1], refs[-1]
    blocks, nfar = weight.shape[0], rows[0].shape[0] // 2
    my_col = lax.axis_index("col")
    chips = n_col // 2
    chip = lax.div(my_col, 2)
    pick = []
    for k in range(chips):
        way = jnp.bitwise_xor(chip, lax.rem(chip + chips - k, chips))
        tag = place(way, chips) * (blocks + 1) + blocks
        pick += [hot(half[tag, 0:1, :], blocks, nfar, my_col) for half in (row0, row1)]
    total = field[...] + spread(pick, [r[...] for r in rows], weight)
    for q in range(BLK // LANES):
        out[pl.ds(q, blocks, stride=BLK // LANES), :] = total[:, q * LANES : (q + 1) * LANES]


def f32(*shape):
    return jax.ShapeDtypeStruct(shape, jnp.float32)


def cost(micros):
    return pl.CostEstimate(flops=int(micros * 1.1e9), bytes_accessed=1 << 16, transcendentals=0)


def body(points, density, near_pairs, far_pairs, near_count, far_count, *, n_row, n_col):
    quad = points.shape[1]
    blocks = points.shape[2] // BLK
    nnear, nfar = near_pairs.shape[0], far_pairs.shape[0]
    depth, slots = 4 * quad, nnear - 1
    near_pairs, far_pairs = near_pairs.T, far_pairs.T

    def swap(x, axis, d):
        n = {"row": n_row, "col": n_col}[axis]
        return lax.ppermute(x, axis, [(i, i ^ d) for i in range(n)])

    direct = [d for d in range(1, n_row) if d & (d - 1) == 0]
    late = [d for d in range(1, n_row) if d & (d - 1) != 0]

    def halves(n):
        return [1 << j for j in reversed(range(n.bit_length() - 1))]

    def col_gather(x):
        for d in halves(n_col)[:-1]:
            x = jnp.concatenate([x, swap(x, "col", d)], axis=0)
        return x, swap(x, "col", 1)

    base = near_lines(slots, quad)
    msg_rows = -(-(base + 4 * (blocks + 1)) // 8) * 8
    hbm = (near_pairs, far_pairs, points, density.reshape(-1, LANES))
    hbm = [pltpu.with_memory_space_constraint(x, pltpu.HBM) for x in hbm]
    msg, far_own, near_own, weight = pl.pallas_call(
        prep_kernel,
        out_shape=(
            f32(msg_rows, BLK),
            f32(blocks + 1, 4, BLK),
            f32(blocks, depth + 8, BLK),
            f32(blocks, BLK),
        ),
        in_specs=[HBM, SMEM, HBM, HBM, HBM],
        out_specs=(VMEM, VMEM, VMEM, VMEM),
        scratch_shapes=[
            pltpu.SMEM(near_pairs.shape, jnp.int32),
            pltpu.VMEM(far_pairs.shape, jnp.int32),
            pltpu.VMEM(points.shape, jnp.float32),
            pltpu.VMEM((density.shape[0] // LANES, LANES), jnp.float32),
            pltpu.SemaphoreType.DMA((QUARTERS + 3,)),
        ],
        compiler_params=PARAMS,
        cost_estimate=cost(1.2),
        name="prep",
    )(hbm[0], near_count, *hbm[1:])
    row_far = col_gather(far_own)
    known = {d: swap(msg, "row", d) for d in direct}
    passed = [d for d in direct if d > 1]
    *onward, first = lax.optimization_barrier((*[known[d] for d in passed], row_far[0]))
    known.update(zip(passed, onward))
    row_far = (first, row_far[1])
    for d in late:
        known[d] = swap(known[d ^ (d & -d)], "row", d & -d)
    got = [known[d] for d in range(1, n_row)]

    bufs = [
        pltpu.VMEM((quad * BLK, TERMS), jnp.bfloat16),
        pltpu.VMEM((TERMS, quad * BLK), jnp.bfloat16),
        pltpu.VMEM((BLK, LANES), jnp.float32),
        pltpu.VMEM((8, BLK), jnp.float32),
    ]
    near0 = pl.pallas_call(
        near_own_kernel,
        out_shape=f32(blocks, BLK),
        in_specs=[SMEM, SMEM, VMEM],
        out_specs=VMEM,
        scratch_shapes=bufs,
        compiler_params=PARAMS,
        cost_estimate=cost(5.0),
        name="near_own",
    )(near_pairs, near_count, near_own)

    def near_scratch(n):
        return [
            pltpu.VMEM((depth + 8, BLK), jnp.float32),
            pltpu.SMEM((n, 8, LANES), jnp.float32),
            pltpu.SemaphoreType.DMA((n,)),
        ] + bufs

    far_scratch = [
        pltpu.SMEM((nfar,), jnp.int32),
        pltpu.VMEM((2, 4, BLK), jnp.float32),
        pltpu.VMEM((2, 4, BLK), jnp.float32),
        pltpu.VMEM((2, BLK, TERMS), jnp.bfloat16),
        pltpu.VMEM((2, TERMS, BLK), jnp.bfloat16),
        pltpu.VMEM((2, BLK, LANES), jnp.float32),
    ]
    field, *backs = pl.pallas_call(
        functools.partial(direct_kernel, ways=len(direct)),
        out_shape=[f32(blocks, BLK)] + [f32(8, BLK)] * len(direct),
        in_specs=[VMEM] * (3 + len(direct)),
        out_specs=[VMEM] * (len(direct) + 1),
        scratch_shapes=near_scratch(len(direct) + 1),
        compiler_params=PARAMS,
        cost_estimate=cost(30.0),
        name="near_direct",
    )(msg, near_own, near0, *[got[d - 1] for d in direct])
    far_rows, far_cols = pl.pallas_call(
        functools.partial(far_kernel, direct=direct, base=base),
        out_shape=[f32(nfar, BLK)] * 2,
        in_specs=[SMEM, SMEM] + [VMEM] * (3 + len(direct)),
        out_specs=[VMEM] * 2,
        scratch_shapes=far_scratch,
        compiler_params=PARAMS,
        cost_estimate=cost(3.0),
        name="far_direct",
    )(far_pairs, far_count, *row_far, far_own, *[got[d - 1] for d in direct])
    field, far_rows, far_cols, *messages = pl.pallas_call(
        functools.partial(late_kernel, n_row=n_row, direct=direct, late=late),
        out_shape=[f32(blocks, BLK)] + [f32(nfar, BLK)] * 2 + [f32(nfar + 8, BLK)] * (n_row - 1),
        in_specs=[SMEM, SMEM] + [VMEM] * (6 + n_row - 1),
        out_specs=[VMEM] * (n_row + 2),
        scratch_shapes=near_scratch(len(late)) + far_scratch,
        compiler_params=PARAMS,
        cost_estimate=cost(8.0),
        name="late",
    )(far_pairs, far_count, near_own, field, *row_far, far_rows, far_cols, *[got[d - 1] for d in late], *backs)

    messages = [
        lax.ppermute(x, "row", [(i, (i + k + 1) % n_row) for i in range(n_row)]) for k, x in enumerate(messages)
    ]
    both = jnp.concatenate([far_rows, swap(far_rows, "col", 1)], axis=0)
    rows = [both]
    for k in range(2, n_col, 2):
        rows.append(lax.ppermute(both, "col", [(i, (i + k) % n_col) for i in range(n_col)]))
    field = pl.pallas_call(
        functools.partial(cols_kernel, n_row=n_row, base=base),
        out_shape=f32(blocks, BLK),
        in_specs=[SMEM] + [VMEM] * (2 * n_row + 2),
        out_specs=VMEM,
        compiler_params=PARAMS,
        cost_estimate=cost(1.0),
        name="final_cols",
    )(near_pairs, weight, field, far_own, far_cols, *got, *messages)
    out = pl.pallas_call(
        functools.partial(rows_kernel, n_col=n_col),
        out_shape=f32(blocks * BLK // LANES, LANES),
        in_specs=[VMEM] * (4 + len(rows)),
        out_specs=VMEM,
        compiler_params=PARAMS,
        cost_estimate=cost(1.0),
        name="final_rows",
    )(weight, field, *row_far, *rows)
    return out.reshape(-1)


def solution(mesh):
    in_specs = (
        P(None, None, ("row", "col")),
        P(("row", "col")),
        P(("row", "col"), None),
        P(("row", "col"), None),
        P(("row", "col")),
        P(("row", "col")),
    )
    out_specs = P(("row", "col"))
    kernel = functools.partial(body, n_row=mesh.shape["row"], n_col=mesh.shape["col"])
    return jax.shard_map(kernel, mesh=mesh, in_specs=in_specs, out_specs=out_specs, check_vma=False)
```
